32 devices in a mesh: dp: 4 (over z), row: 4 (over y, x), col: 2 (over core).
Axes of the slice: x: 2, y: 2, z: 4, core: 2. Of those that a mesh axis runs over, the one named last changes fastest.
Arguments:
- tokens: bfloat16 [3072, 2048], P(('dp', 'row'), 'col'), may hold values from -6 to 6
- gain_one: bfloat16 [2048], P('col'), may hold values from 0.25 to 1.75
- in_weight: bfloat16 [2048, 3, 2048], P('col', None, 'row'), may hold values from -0.125 to 0.125
- conv_weight: bfloat16 [3, 2048], P(None, ('row', 'col')), may hold values from -3.5 to 3.5
- out_weight: bfloat16 [2048, 2048], P('row', 'col'), may hold values from -0.125 to 0.125
- gain_two: bfloat16 [2048], P('col'), may hold values from 0.25 to 1.75
- gate_up_weight: bfloat16 [2048, 2, 8192], P('col', None, 'row'), may hold values from -0.125 to 0.125
- down_weight: bfloat16 [8192, 2048], P('row', 'col'), may hold values from -0.125 to 0.125
- cotangent: bfloat16 [3072, 2048], P(('dp', 'row'), 'col'), may hold values from -6 to 6
- lengths: int32 [3], replicated, may hold values from 507 to 1541, as said below
Outputs:
- block_out: bfloat16 [3072, 2048], P(('dp', 'row'), 'col')
- d_tokens: float32 [3072, 2048], P(('dp', 'row'), 'col')
- d_gain_one: float32 [2048], P('col')
- d_in_weight: float32 [2048, 3, 4, 4, 128], P('col', None, 'row', 'dp')
- d_conv_weight: float32 [3, 8, 4, 64], P(None, ('row', 'col'), 'dp')
- d_out_weight: float32 [4, 4, 128, 2048], P('row', 'dp', None, 'col')
- d_gain_two: float32 [2048], P('col')
- d_gate_up_weight: float32 [2048, 2, 4, 4, 512], P('col', None, 'row', 'dp')
- d_down_weight: float32 [4, 4, 512, 2048], P('row', 'dp', None, 'col')
The draws below stay inside these ranges and needn't reach their ends.
Inputs may be any that keep to these rules, and one draw needn't show every extreme that they name: lengths of the 3 sequences packed one after another into the 3072 tokens; they sum to 3072; the first is the longest, and every later sequence begins at a position that leaves 5 when divided by 8.
All inputs are finite; a program needn't handle non-finite values.
Results may differ from the reference program's by a relative error of at most 0.014.
Values may be sent and summed in bfloat16 or wider, within the bound.
A program may use at most 192 MiB of HBM per device.

```python
import jax
import jax.numpy as jnp
from jax import lax

D = 2048
FF = 8192
TOK_GRP = 768
AVG_LEN = 1024
SPREAD = 512
TOKENS = 3072
NSEQ = 3
N_DP = 4
N_ROW = 4
N_COL = 2


def draw_lengths(key, part):
    key = jax.random.fold_in(key, 11)
    shift_key, order_key = jax.random.split(key)
    pair_count = NSEQ // 2
    steps_count = SPREAD // 8
    shifts = 8 * jax.random.randint(shift_key, (pair_count,), -steps_count, steps_count + 1)
    shifts = shifts.at[0].set(SPREAD)
    paired = jnp.concatenate([AVG_LEN + shifts, AVG_LEN - shifts, jnp.full((NSEQ - 2 * pair_count,), AVG_LEN, jnp.int32)])
    others = paired[1:][jax.random.permutation(order_key, NSEQ - 1)]
    lengths = jnp.concatenate([paired[:1], others])
    place = jnp.arange(NSEQ)
    lengths = lengths + 5 * (place == 0).astype(jnp.int32) - 5 * (place == NSEQ - 1).astype(jnp.int32)
    return lengths.astype(jnp.int32)


def levels(stream_key, extent, pieces, low, top_value):
    def one(dim, blocks):
        heights = jax.random.uniform(jax.random.fold_in(jax.random.fold_in(stream_key, 6), dim), (blocks,), jnp.float32, low / len(pieces), top_value / len(pieces))
        return jnp.repeat(jnp.exp(heights), extent[dim] // blocks).reshape((-1,) + (1,) * (len(extent) - dim - 1))

    loudness = one(*pieces[0])
    for cut in pieces[1:]:
        loudness = loudness * one(*cut)
    return loudness


def centred(rng, extent, scale, bound, pieces=(), kind=jnp.bfloat16):
    values = scale * jax.random.normal(rng, extent, jnp.float32)
    if pieces:
        values = values * levels(rng, extent, pieces, -0.22, 0.18)
    return jnp.clip(values, -bound, bound).astype(kind)


def setup_inputs(seed: int = 0) -> dict:
    splits = jax.random.split(jax.random.key(seed), 11)
    return {
        "tokens": centred(splits[0], (TOKENS, D), 1.0, 6.0, ((0, 16), (1, 2))),
        "gain_one": jnp.clip(1.0 + 0.15 * jax.random.normal(splits[1], (D,), jnp.float32), 0.25, 1.75).astype(jnp.bfloat16),
        "in_weight": centred(splits[2], (D, 3, D), D ** -0.5, 0.125, ((0, 2), (2, 4))),
        "conv_weight": centred(splits[3], (3, D), 3 ** -0.5, 3.5, ((1, 8),)),
        "out_weight": centred(splits[4], (D, D), D ** -0.5, 0.125, ((0, 4), (1, 2))),
        "gain_two": jnp.clip(1.0 + 0.15 * jax.random.normal(splits[5], (D,), jnp.float32), 0.25, 1.75).astype(jnp.bfloat16),
        "gate_up_weight": centred(splits[6], (D, 2, FF), D ** -0.5, 0.125, ((0, 2), (2, 4))),
        "down_weight": centred(splits[7], (FF, D), (FF // 4) ** -0.5, 0.125, ((0, 4), (1, 2))),
        "cotangent": centred(splits[8], (TOKENS, D), 1.0, 6.0, ((0, 16), (1, 2))),
        "lengths": draw_lengths(jax.random.fold_in(splits[10], 71), 0),
    }


@jax.custom_vjp
def low(v):
    return lax.optimization_barrier(v.astype(jnp.bfloat16)).astype(jnp.float32)

@jax.custom_vjp
def low_back(v):
    return v

def low_keep(v):
    return (low(v), None)

def low_pass(kept, grad):
    return (grad,)

def back_keep(v):
    return (v, None)

def back_low(kept, grad):
    return (low(grad),)
low.defvjp(low_keep, low_pass)
low_back.defvjp(back_keep, back_low)

def sequence_offsets(lengths, index):
    ends = jnp.cumsum(lengths).astype(jnp.int32)
    starts = ends - lengths.astype(jnp.int32)
    reached = starts[None, :] <= index[:, None]
    return index - lax.optimization_barrier(jnp.max(jnp.where(reached, starts[None, :], 0), axis=1)).astype(jnp.int32)

def rms_scale(values):
    return lax.rsqrt(lax.optimization_barrier(jnp.mean(values * values, axis=-1, keepdims=True)) + 1e-05)

def layer(lengths, tokens, gain_one, in_weight, conv_weight, out_weight, gain_two, gate_up_weight, down_weight):
    highest = lax.Precision.HIGHEST
    number_blocks = tokens.shape[0] // TOK_GRP
    blocks = tokens.reshape(number_blocks, TOK_GRP, D)

    def block_step(carried, item):
        block_rows, number = item
        index = number * TOK_GRP + jnp.arange(TOK_GRP, dtype=jnp.int32)
        offset = sequence_offsets(lengths, index)
        normed_one = low(block_rows * rms_scale(block_rows) * gain_one)
        projected = low_back(jnp.einsum('ti,ikc->tkc', normed_one, in_weight, precision=highest))
        in_gate = projected[:, 0]
        out_gate = projected[:, 1]
        values = projected[:, 2]
        mixed = in_gate * values
        extended = jnp.concatenate([carried, mixed], axis=0)
        conv_out = jnp.zeros_like(mixed)
        for lag in range(3):
            usable = (offset >= lag).astype(jnp.float32)[:, None]
            conv_out = conv_out + conv_weight[lag] * usable * extended[2 - lag:2 - lag + TOK_GRP]
        gated = low(out_gate * conv_out)
        resid = block_rows + low_back(jnp.dot(gated, out_weight, precision=highest))
        normed_two = low(resid * rms_scale(resid) * gain_two)
        hidden = low_back(jnp.einsum('ti,ikf->tkf', normed_two, gate_up_weight, precision=highest))
        act = low(jax.nn.silu(hidden[:, 0]) * hidden[:, 1])
        result = resid + low_back(jnp.dot(act, down_weight, precision=highest))
        return (mixed[-2:], result)
    start_tail = jnp.zeros((2, D), jnp.float32)
    numbers = jnp.arange(number_blocks, dtype=jnp.int32)
    final_tail, results = lax.scan(jax.checkpoint(block_step), start_tail, (blocks, numbers))
    return results.reshape(number_blocks * TOK_GRP, D)

def reference(tokens, gain_one, in_weight, conv_weight, out_weight, gain_two, gate_up_weight, down_weight, cotangent, lengths):
    inputs = tuple((array.astype(jnp.float32) for array in (tokens, gain_one, in_weight, conv_weight, out_weight, gain_two, gate_up_weight, down_weight)))

    def forward(*arrays):
        return layer(lengths, *arrays)
    block, pullback = jax.vjp(forward, *inputs)
    grads = pullback(cotangent.astype(jnp.float32))
    grad_tokens, grad_gain_one, grad_in, grad_conv, grad_out, grad_gain_two, grad_gate_up, grad_down = grads
    return (block.astype(jnp.bfloat16), grad_tokens, grad_gain_one, grad_in.reshape(D, 3, N_ROW, N_DP, D // (N_ROW * N_DP)), grad_conv.reshape(3, N_ROW * N_COL, N_DP, D // (N_ROW * N_COL * N_DP)), grad_out.reshape(N_ROW, N_DP, D // (N_ROW * N_DP), D), grad_gain_two, grad_gate_up.reshape(D, 2, N_ROW, N_DP, FF // (N_ROW * N_DP)), grad_down.reshape(N_ROW, N_DP, FF // (N_ROW * N_DP), D))
```

```python
import functools

import jax
import jax.numpy as jnp
from jax import lax
from jax.experimental import pallas as pl
from jax.experimental.pallas import tpu as pltpu
from jax.sharding import PartitionSpec as P

MESH = pl.DeviceIdType.MESH
BF = jnp.bfloat16
F32 = jnp.float32
EPS = 1e-05
VMEM_LIMIT = 63 * 2**20


def nn(a, b):
    return lax.dot_general(a, b, (((1,), (0,)), ((), ())), preferred_element_type=F32)


def nt(a, b):
    return lax.dot_general(a, b, (((1,), (1,)), ((), ())), preferred_element_type=F32)


class Links:
    def __init__(self, send_sems, recv_sems):
        self.send_sems, self.recv_sems = send_sems, recv_sems
        self.count = 0
        self.open = []

    def slot(self):
        self.count += 1
        return self.count - 1

    def copy(self, src, dst, to, slot=None):
        if slot is None:
            slot = self.slot()
        return pltpu.make_async_remote_copy(
            src_ref=src,
            dst_ref=dst,
            send_sem=self.send_sems.at[slot],
            recv_sem=self.recv_sems.at[slot],
            device_id=to,
            device_id_type=MESH,
        )

    def send(self, src, dst, to):
        c = self.copy(src, dst, to)
        c.start()
        self.open.append(c)
        return c

    def sent(self, *copies):
        for c in copies:
            c.wait_send()
            self.open = [o for o in self.open if o is not c]

    def close(self):
        for c in self.open:
            c.wait_send()
        self.open = []


def rows_loop(count, step, body):
    def one(i, carry):
        body(pl.multiple_of(i * step, step))
        return carry

    lax.fori_loop(0, count // step, one, 0)


def block_kernel(n_dp, width, *refs):
    (
        tok, g1, w_in, cw, w_out, g2, w_gu, w_dn, cot, mask1, mask2,
        block_out, d_tok, d_gain, d_conv, n1_h, n2_h, cot_h, gb_h, gat_h, act_h, gh_h, gp_h,
        w_in_v, w_out_v, w_gu_v, w_dn_v,
        xall, call, gat, act, gh, gp,
        proj_o, proj_r, mext, halo_b, cout, gext, halo_a, gg_s, gg_r, gg_o,
        hid_o, hid_r, ga_o, ga_r,
        rs_s, rs_r, rt_s, rt_r, acc_b, acc_o,
        resid, gres, ss_s, ss_r, red_s, red_r, red_z,
        send_sems, recv_sems, local_sems,
    ) = refs
    R, B, Dl = xall.shape
    Uc = w_out_v.shape[1]
    Fc = w_dn_v.shape[1]
    T = R * B
    dp, row, col = lax.axis_index("dp"), lax.axis_index("row"), lax.axis_index("col")
    other = 1 - col
    low = row + 1 - 2 * lax.rem(row, 2)
    high = row + 2 - 4 * lax.rem(row // 2, 2)
    row_a = low * other + high * col
    row_b = high * other + low * col
    row_d = low + high - row
    to_a, to_b, to_col = {"row": row_a}, {"row": row_b}, {"col": other}
    links = Links(send_sems, recv_sems)

    loads = {"in": [], "out": [], "gu": [], "dn": []}
    n_local = 0

    def local(src, dst):
        nonlocal n_local
        c = pltpu.make_async_copy(src, dst, local_sems.at[n_local])
        n_local += 1
        c.start()
        return c

    for c in range(2):
        for k in range(3):
            loads["in"].append(local(w_in.at[k, :, pl.ds(c * Uc, Uc)], w_in_v.at[c, k]))
    for c in range(2):
        loads["dn"].append(local(w_dn.at[pl.ds(c * Fc, Fc), :], w_dn_v.at[c]))
        loads["out"].append(local(w_out.at[pl.ds(c * Uc, Uc), :], w_out_v.at[c]))
    for c in range(2):
        for k in range(2):
            loads["gu"].append(local(w_gu.at[k, :, pl.ds(c * Fc, Fc)], w_gu_v.at[c, k]))

    def loaded(name):
        for c in loads[name]:
            c.wait()

    barrier = pltpu.get_barrier_semaphore()
    for to in (to_col, {"row": low}, {"row": high}):
        pl.semaphore_signal(barrier, inc=1, device_id=to, device_id_type=MESH)
    for k in range(1, n_dp):
        pl.semaphore_signal(
            barrier, inc=1, device_id={"dp": lax.rem(dp + k, n_dp)}, device_id_type=MESH
        )

    def col_total(place):
        c = links.send(ss_s.at[place], ss_r.at[place], to_col)
        c.wait_recv()

    def gather(buf):
        first = links.send(buf.at[row], buf.at[row], to_a)
        second = links.send(buf.at[row], buf.at[row], to_b)
        state = {}

        def relay():
            first.wait_recv()
            state["third"] = links.send(buf.at[row_a], buf.at[row_a], to_b)

        def second_in():
            second.wait_recv()

        def third_in():
            state["third"].wait_recv()

        def all_sent():
            links.sent(first, second, state["third"])

        return relay, second_in, third_in, all_sent

    def row_sum(sends, recvs, partial, filler=None):
        def to_bf(slot):
            def put(n0, value):
                sends[slot, :, n0 : n0 + value.shape[1]] = value.astype(BF)

            return put

        def to_f32(acc):
            def put(n0, value):
                acc[:, n0 : n0 + value.shape[1]] = value

            return put

        partial(row_d, to_bf(0))
        c0 = links.send(sends.at[0], recvs.at[0], to_a)
        partial(row_a, to_bf(1))
        c1 = links.send(sends.at[1], recvs.at[1], to_a)
        partial(row_b, to_f32(acc_b))
        c0.wait_recv()

        def combine(r0):
            at = pl.ds(r0, 16)
            sends[2, at, :] = (acc_b[at, :] + recvs[0, at, :].astype(F32)).astype(BF)

        rows_loop(B, 16, combine)
        c2 = links.send(sends.at[2], recvs.at[2], to_b)
        partial(row, to_f32(acc_o))
        if filler is not None:
            filler()
        c1.wait_recv()
        c2.wait_recv()
        return c0, c1, c2

    def row_total(recvs, at):
        return acc_o[at, :] + recvs[1, at, :].astype(F32) + recvs[2, at, :].astype(F32)

    def lanes(x):
        return jnp.broadcast_to(x, (x.shape[0], 128))

    def squares(r0):
        at = pl.ds(r0, 16)
        x = tok[at, :].astype(F32)
        ss_s[0, at, :] = lanes(jnp.sum(x * x, axis=1, keepdims=True))

    rows_loop(B, 16, squares)
    pl.semaphore_wait(barrier, 3 + n_dp - 1)
    col_total(0)

    def scale_of(place, at):
        return lax.rsqrt((ss_s[place, at, :] + ss_r[place, at, :]) / width + EPS)[:, :1]

    def normed_one(r0):
        at = pl.ds(r0, 16)
        x = tok[at, :].astype(F32)
        xall[row, at, :] = (x * scale_of(0, at) * g1[...]).astype(BF)

    rows_loop(B, 16, normed_one)
    relay, second_in, third_in, all_sent = gather(xall)

    def project(blk):
        x = xall[blk]
        for k in range(3):
            gp[col, blk, k] = nn(x, w_in_v[other, k]).astype(BF)
        c = links.send(gp.at[col, blk], proj_r.at[blk], to_col)
        for k in range(3):
            proj_o[k, pl.ds(pl.multiple_of(blk * B, B), B), :] = nn(x, w_in_v[col, k])
        return c

    loaded("in")
    sent = [project(row)]
    relay()
    sent.append(project(row_a))
    second_in()
    sent.append(project(row_b))
    third_in()
    call[row] = cot[...]
    cot_relay, cot_second, cot_third, _ = gather(call)
    sent.append(project(row_d))
    n1_out = local(xall, n1_h)

    for blk, c in zip((row, row_b, row_a, row_d), sent):
        c.wait_recv()
        base = blk * B

        def add(r0, blk=blk, base=base):
            at = pl.ds(r0, 32)
            to = pl.ds(pl.multiple_of(base + r0, 32), 32)
            g = [proj_o[k, to, :] + proj_r[blk, k, at, :].astype(F32) for k in range(3)]
            for k in range(3):
                proj_o[k, to, :] = g[k]
            mext[pl.ds(pl.multiple_of(base + r0 + 8, 8), 32), :] = g[0] * g[2]

        rows_loop(B, 32, add)
    links.sent(*sent)

    behind = links.slot()

    @pl.when(dp < n_dp - 1)
    def _():
        links.copy(mext.at[pl.ds(T, 8), :], halo_b, {"dp": lax.rem(dp + 1, n_dp)}, behind).start()

    @pl.when(dp > 0)
    def _():
        links.copy(mext.at[pl.ds(T, 8), :], halo_b, {"dp": lax.rem(dp + 1, n_dp)}, behind).wait_recv()
        mext[0:8, :] = halo_b[...]

    @pl.when(dp == 0)
    def _():
        mext[0:8, :] = jnp.zeros((8, Uc), F32)

    CH = B // 2

    def mask_of(mask, at):
        return jnp.concatenate([mask[at, :]] * (Uc // 128), axis=1)

    for i in range(T // CH):
        at = pl.ds(i * CH, CH)
        x = mext[pl.ds(i * CH, CH + 8), :]
        y = cw[0:1, :] * x[8 : 8 + CH]
        y = y + cw[1:2, :] * mask_of(mask1, at) * x[7 : 7 + CH]
        y = y + cw[2:3, :] * mask_of(mask2, at) * x[6 : 6 + CH]
        cout[at, :] = y
        gat[col, i * CH // B, i * CH % B : i * CH % B + CH, :] = (proj_o[1, at, :] * y).astype(BF)
    gated_in = links.send(gat.at[col], gat.at[col], to_col)
    gated_in.wait_recv()

    loaded("out")
    n1_out.wait()
    all_sent()

    def out_partial(blk, put):
        for n0 in range(0, Dl, Dl // 2):
            n = slice(n0, n0 + Dl // 2)
            put(n0, nn(gat[0, blk], w_out_v[0, :, n]) + nn(gat[1, blk], w_out_v[1, :, n]))

    sent = row_sum(rs_s, rs_r, out_partial, filler=cot_relay)

    def residual(r0):
        at = pl.ds(r0, 16)
        x = tok[at, :].astype(F32) + row_total(rs_r, at)
        resid[at, :] = x
        ss_s[1, at, :] = lanes(jnp.sum(x * x, axis=1, keepdims=True))

    rows_loop(B, 16, residual)
    links.sent(*sent)
    col_total(1)

    def normed_two(r0):
        at = pl.ds(r0, 16)
        xall[row, at, :] = (resid[at, :] * scale_of(1, at) * g2[...]).astype(BF)

    rows_loop(B, 16, normed_two)
    relay, second_in, third_in, all_sent = gather(xall)

    cot_second()
    cot_third()
    loaded("dn")
    ga_sent = []
    for blk in (row, row_a, row_b, row_d):
        x = call[blk]
        for n0 in range(0, Fc, Fc // 2):
            n = slice(n0, n0 + Fc // 2)
            act[col, blk, :, n] = nt(x, w_dn_v[other, n, :]).astype(BF)
        ga_sent.append(links.send(act.at[col, blk], ga_r.at[blk], to_col))
    relay()
    for blk in (row, row_a, row_b, row_d):
        x = call[blk]
        for n0 in range(0, Fc, Fc // 2):
            n = slice(n0, n0 + Fc // 2)
            ga_o[blk, :, n] = nt(x, w_dn_v[col, n, :])
    cot_out = local(call, cot_h)

    def hidden_other(blk):
        def one(k, carry):
            for n0 in range(0, Fc, Fc // 2):
                n = slice(n0, n0 + Fc // 2)
                gh[col, blk, k, :, n] = nn(xall[blk], w_gu_v[other, k, :, n]).astype(BF)
            return carry

        lax.fori_loop(0, 2, one, 0)
        return links.send(gh.at[col, blk], hid_r.at[blk], to_col)

    loaded("gu")
    hid_sent = [hidden_other(row), hidden_other(row_a)]
    second_in()
    hid_sent.append(hidden_other(row_b))
    third_in()
    hid_sent.append(hidden_other(row_d))
    n2_out = local(xall, n2_h)

    gh_in = {}
    for name, blk in (("d", row_d), ("a", row_a), ("b", row_b), ("o", row)):

        def one(k, carry, blk=blk):
            for n0 in range(0, Fc, Fc // 2):
                n = slice(n0, n0 + Fc // 2)
                hid_o[k, :, n] = nn(xall[blk], w_gu_v[col, k, :, n])
            return carry

        lax.fori_loop(0, 2, one, 0)
        which = {"o": 0, "a": 1, "b": 2, "d": 3}[name]
        theirs = {"o": 0, "a": 2, "b": 1, "d": 3}[name]
        hid_sent[theirs].wait_recv()
        ga_sent[theirs].wait_recv()
        links.sent(hid_sent[which], ga_sent[which])

        def activate(r0, blk=blk):
            at = pl.ds(r0, 16)
            for n0 in range(0, Fc, Fc // 2):
                n = slice(n0, n0 + Fc // 2)
                gate = hid_o[0, at, n] + hid_r[blk, 0, at, n].astype(F32)
                up = hid_o[1, at, n] + hid_r[blk, 1, at, n].astype(F32)
                ga = ga_o[blk, at, n] + ga_r[blk, at, n].astype(F32)
                s = jax.nn.sigmoid(gate)
                silu = gate * s
                act[col, blk, at, n] = (silu * up).astype(BF)
                gh[col, blk, 0, at, n] = (ga * up * s * (1.0 + gate * (1.0 - s))).astype(BF)
                gh[col, blk, 1, at, n] = (ga * silu).astype(BF)

        rows_loop(B, 16, activate)
        gh_in[name] = (
            links.send(gh.at[col, blk], gh.at[col, blk], to_col),
            links.send(act.at[col, blk], act.at[col, blk], to_col),
        )
    for pair in gh_in.values():
        for c in pair:
            c.wait_recv()
    n2_out.wait()
    all_sent()

    def gu_partial(blk, put):
        for n0 in range(0, Dl, Dl // 4):
            n = slice(n0, n0 + Dl // 4)
            total = None
            for c in range(2):
                for k in range(2):
                    part = nt(gh[c, blk, k], w_gu_v[c, k, n, :])
                    total = part if total is None else total + part
            put(n0, total)

    sent = row_sum(rs_s, rs_r, gu_partial)

    def back_two(r0):
        at = pl.ds(r0, 16)
        g = row_total(rs_r, at)
        gres[at, :] = g
        ss_s[2, at, :] = lanes(jnp.sum(g * g2[...] * resid[at, :], axis=1, keepdims=True))

    rows_loop(B, 16, back_two)
    links.sent(*sent)
    col_total(2)

    def inner_of(place, at):
        return (ss_s[place, at, :] + ss_r[place, at, :])[:, :1]

    def branch(i, gain):
        at = pl.ds(pl.multiple_of(i * 16, 16), 16)
        g = gres[at, :]
        x = resid[at, :]
        s = scale_of(1, at)
        y = cot[at, :].astype(F32) + s * g2[...] * g - x * (s * s * s) * inner_of(2, at) / width
        gres[at, :] = y
        xall[row, at, :] = y.astype(BF)
        return gain + jnp.sum(g * x * s, axis=0, keepdims=True)

    gain_two = lax.fori_loop(0, B // 16, branch, jnp.zeros((1, Dl), F32))
    relay, second_in, third_in, all_sent = gather(xall)

    def down_partial(blk, put):
        for n0 in range(0, Dl, Dl // 2):
            n = slice(n0, n0 + Dl // 2)
            put(n0, nn(act[0, blk], w_dn_v[0, :, n]) + nn(act[1, blk], w_dn_v[1, :, n]))

    def gated_other(blk):
        gg_s[blk] = nt(xall[blk], w_out_v[other]).astype(BF)
        c = links.send(gg_s.at[blk], gg_r.at[blk], to_col)
        gg_o[blk] = nt(xall[blk], w_out_v[col])
        return c

    sent = [gated_other(row)]
    relay()
    sent.append(gated_other(row_a))
    second_in()
    sent.append(gated_other(row_b))
    third_in()
    sent.append(gated_other(row_d))
    gb_out = local(xall, gb_h)

    for blk, c in zip((row, row_b, row_a, row_d), sent):
        c.wait_recv()
        base = blk * B

        def conv_grad(r0, blk=blk, base=base):
            at = pl.ds(r0, 32)
            to = pl.ds(pl.multiple_of(base + r0, 32), 32)
            g = gg_o[blk, at, :] + gg_r[blk, at, :].astype(F32)
            gext[to, :] = g * proj_o[1, to, :]
            gp[col, blk, 1, at, :] = (g * cout[to, :]).astype(BF)

        rows_loop(B, 32, conv_grad)

    ahead = links.slot()

    @pl.when(dp > 0)
    def _():
        links.copy(gext.at[pl.ds(0, 8), :], halo_a, {"dp": lax.rem(dp + n_dp - 1, n_dp)}, ahead).start()

    @pl.when(dp < n_dp - 1)
    def _():
        links.copy(gext.at[pl.ds(0, 8), :], halo_a, {"dp": lax.rem(dp + n_dp - 1, n_dp)}, ahead).wait_recv()
        gext[T : T + 8, :] = halo_a[...]

    @pl.when(dp == n_dp - 1)
    def _():
        gext[T : T + 8, :] = jnp.zeros((8, Uc), F32)

    terms = [jnp.zeros((1, Uc), F32) for _ in range(3)]
    for i in range(T // CH):
        at = pl.ds(i * CH, CH)
        more = pl.ds(i * CH, CH + 8)
        x = mext[more, :]
        g = gext[more, :]
        m1, m2 = mask_of(mask1, more), mask_of(mask2, more)
        now = g[:CH]
        terms[0] = terms[0] + jnp.sum(now * x[8 : 8 + CH], axis=0, keepdims=True)
        terms[1] = terms[1] + jnp.sum(m1[:CH] * now * x[7 : 7 + CH], axis=0, keepdims=True)
        terms[2] = terms[2] + jnp.sum(m2[:CH] * now * x[6 : 6 + CH], axis=0, keepdims=True)
        y = cw[0:1, :] * now
        y = y + cw[1:2, :] * (m1 * g)[1 : 1 + CH]
        y = y + cw[2:3, :] * (m2 * g)[2 : 2 + CH]
        blk, to = i * CH // B, slice(i * CH % B, i * CH % B + CH)
        gp[col, blk, 0, to, :] = (y * proj_o[2, at, :]).astype(BF)
        gp[col, blk, 2, to, :] = (y * proj_o[0, at, :]).astype(BF)
    red_s[...] = jnp.zeros_like(red_s)
    for k in range(3):
        red_s[8 + k : 9 + k, :Uc] = terms[k]
    gp_in = links.send(gp.at[col], gp.at[col], to_col)
    gp_in.wait_recv()

    def in_partial(blk, put):
        for n0 in range(0, Dl, Dl // 4):
            n = slice(n0, n0 + Dl // 4)
            total = None
            for c in range(2):
                for k in range(3):
                    part = nt(gp[c, blk, k], w_in_v[c, k, n, :])
                    total = part if total is None else total + part
            put(n0, total)

    gb_out.wait()
    sent_in = row_sum(rs_s, rs_r, in_partial)

    def back_one(r0):
        at = pl.ds(r0, 16)
        g = row_total(rs_r, at)
        d_tok[at, :] = g
        ss_s[3, at, :] = lanes(
            jnp.sum(g * g1[...] * tok[at, :].astype(F32), axis=1, keepdims=True)
        )

    rows_loop(B, 16, back_one)
    col_total(3)

    def token_grad(i, gain):
        at = pl.ds(pl.multiple_of(i * 16, 16), 16)
        g = d_tok[at, :]
        x = tok[at, :].astype(F32)
        s = scale_of(0, at)
        y = gres[at, :] + s * g1[...] * g - x * (s * s * s) * inner_of(3, at) / width
        d_tok[at, :] = y
        return gain + jnp.sum(g * x * s, axis=0, keepdims=True)

    gain_one = lax.fori_loop(0, B // 16, token_grad, jnp.zeros((1, Dl), F32))

    red_s[0:1, :] = gain_one
    red_s[1:2, :] = gain_two
    c0 = links.send(red_s.at[pl.ds(0, 8), :], red_r.at[0], to_a)
    sent_down = row_sum(rt_s, rt_r, down_partial)

    def block_rows(r0):
        at = pl.ds(r0, 16)
        block_out[at, :] = (resid[at, :] + row_total(rt_r, at)).astype(BF)

    rows_loop(B, 16, block_rows)
    c0.wait_recv()
    links.sent(c0)
    red_s[0:8, :] = red_s[0:8, :] + red_r[0]
    c1 = links.send(red_s.at[pl.ds(0, 8), :], red_r.at[1], to_b)
    c1.wait_recv()
    red_z[dp] = red_s[...]
    red_z[dp, 0:8, :] = red_s[0:8, :] + red_r[1]
    arrived = []
    for k in range(1, n_dp):
        arrived.append(links.send(red_z.at[dp], red_z.at[dp], {"dp": lax.rem(dp + k, n_dp)}))
    outs = [local(gat, gat_h), local(act, act_h), local(gh, gh_h), local(gp, gp_h)]
    for c in arrived:
        c.wait_recv()
    total = red_z[0]
    for k in range(1, n_dp):
        total = total + red_z[k]
    d_gain[...] = total[0:8]
    d_conv[...] = total[8:16, :Uc]

    @pl.when(dp < n_dp - 1)
    def _():
        links.copy(mext.at[pl.ds(T, 8), :], halo_b, {"dp": lax.rem(dp + 1, n_dp)}, behind).wait_send()

    @pl.when(dp > 0)
    def _():
        links.copy(gext.at[pl.ds(0, 8), :], halo_a, {"dp": lax.rem(dp + n_dp - 1, n_dp)}, ahead).wait_send()

    for c in [cot_out, *outs]:
        c.wait()
    links.close()


def run_block(n_dp, width, tok, g1, w_in, cw, w_out, g2, w_gu, w_dn, cot, mask1, mask2):
    B, Dl = tok.shape
    R = 4
    T = R * B
    Uc = w_out.shape[0] // 2
    Fc = w_dn.shape[0] // 2
    vm = lambda shape, kind=BF: pltpu.VMEM(shape, kind)
    any_spec, vmem_spec = pl.BlockSpec(memory_space=pl.ANY), pl.BlockSpec(memory_space=pltpu.VMEM)
    shape = jax.ShapeDtypeStruct
    rows = shape((R, B, Dl), BF)
    return pl.pallas_call(
        functools.partial(block_kernel, n_dp, width),
        out_shape=(
            shape((B, Dl), BF),
            shape((B, Dl), F32),
            shape((8, Dl), F32),
            shape((8, Uc), F32),
            rows, rows, rows, rows,
            shape((2, R, B, Uc), BF),
            shape((2, R, B, Fc), BF),
            shape((2, R, 2, B, Fc), BF),
            shape((2, R, 3, B, Uc), BF),
        ),
        in_specs=[
            vmem_spec, vmem_spec, any_spec, vmem_spec, any_spec, vmem_spec,
            any_spec, any_spec, vmem_spec, vmem_spec, vmem_spec,
        ],
        out_specs=[vmem_spec] * 4 + [any_spec] * 8,
        scratch_shapes=[
            vm((2, 3, Dl, Uc)), vm((2, Uc, Dl)), vm((2, 2, Dl, Fc)), vm((2, Fc, Dl)),
            vm((R, B, Dl)), vm((R, B, Dl)),
            vm((2, R, B, Uc)), vm((2, R, B, Fc)), vm((2, R, 2, B, Fc)), vm((2, R, 3, B, Uc)),
            vm((3, T, Uc), F32), vm((R, 3, B, Uc)), vm((T + 8, Uc), F32), vm((8, Uc), F32),
            vm((T, Uc), F32), vm((T + 8, Uc), F32), vm((8, Uc), F32),
            vm((R, B, Uc)), vm((R, B, Uc)), vm((R, B, Uc), F32),
            vm((2, B, Fc), F32), vm((R, 2, B, Fc)), vm((R, B, Fc), F32), vm((R, B, Fc)),
            vm((3, B, Dl)), vm((3, B, Dl)), vm((3, B, Dl)), vm((3, B, Dl)),
            vm((B, Dl), F32), vm((B, Dl), F32),
            vm((B, Dl), F32), vm((B, Dl), F32),
            vm((4, B, 128), F32), vm((4, B, 128), F32),
            vm((16, Dl), F32), vm((2, 8, Dl), F32), vm((n_dp, 16, Dl), F32),
            pltpu.SemaphoreType.DMA((96,)), pltpu.SemaphoreType.DMA((96,)),
            pltpu.SemaphoreType.DMA((40,)),
        ],
        compiler_params=pltpu.CompilerParams(
            collective_id=0, has_side_effects=True, vmem_limit_bytes=VMEM_LIMIT
        ),
        name="block",
    )(tok, g1, w_in, cw, w_out, g2, w_gu, w_dn, cot, mask1, mask2)


def sequence_offsets(lengths, index):
    ends = jnp.cumsum(lengths)
    starts = ends - lengths
    reached = starts[None, :] <= index[:, None]
    return index - jnp.max(jnp.where(reached, starts[None, :], 0), axis=1)


def on_device(
    tokens, gain_one, in_weight, conv_weight, out_weight, gain_two, gate_up_weight, down_weight,
    cotangent, lengths,
):
    n_dp = lax.axis_size("dp")
    B, Dl = tokens.shape
    T = B * lax.axis_size("row")
    width = Dl * lax.axis_size("col")
    index = lax.axis_index("dp") * T + jnp.arange(T + 16, dtype=jnp.int32)
    offset = sequence_offsets(lengths, index)
    masks = [
        jnp.broadcast_to((offset >= lag).astype(F32)[:, None], (T + 16, 128)) for lag in (1, 2)
    ]
    conv = jnp.pad(conv_weight.astype(F32), ((0, 5), (0, 0)))
    block_out, d_tok, d_gain, d_conv, n1, n2, cot, gb, gat, act, gh, gp = run_block(
        n_dp,
        float(width),
        tokens,
        gain_one.astype(F32)[None, :],
        jnp.transpose(in_weight, (1, 0, 2)),
        conv,
        out_weight,
        gain_two.astype(F32)[None, :],
        jnp.transpose(gate_up_weight, (1, 0, 2)),
        down_weight,
        cotangent,
        *masks,
    )

    def reduced(grad, dim):
        return lax.psum_scatter(grad.astype(BF), "dp", scatter_dimension=dim, tiled=True).astype(F32)

    dot = functools.partial(jnp.einsum, preferred_element_type=F32)
    r_down = reduced(dot("crtf,rti->cfi", act, cot).reshape(-1, Dl), 0)
    r_gu = reduced(dot("rti,crktf->ikcf", n2, gh).reshape(Dl, 2, -1), 2)
    r_out = reduced(dot("crtu,rti->cui", gat, gb).reshape(-1, Dl), 0)
    r_in = reduced(dot("rti,crktu->ikcu", n1, gp).reshape(Dl, 3, -1), 2)
    part = d_conv.shape[1] * 1 // n_dp
    mine = lax.dynamic_slice(d_conv, (0, lax.axis_index("dp") * part), (3, part))
    return (
        block_out,
        d_tok,
        d_gain[0],
        r_in.reshape(Dl, 3, 1, 1, -1),
        mine.reshape(3, 1, 1, part),
        r_out.reshape(1, 1, -1, Dl),
        d_gain[1],
        r_gu.reshape(Dl, 2, 1, 1, -1),
        r_down.reshape(1, 1, -1, Dl),
    )


def solution(mesh):
    placed = (
        P(("dp", "row"), "col"),
        P("col"),
        P("col", None, "row"),
        P(None, ("row", "col")),
        P("row", "col"),
        P("col"),
        P("col", None, "row"),
        P("row", "col"),
        P(("dp", "row"), "col"),
        P(),
    )
    return jax.shard_map(
        on_device,
        mesh=mesh,
        in_specs=placed,
        out_specs=(
            P(("dp", "row"), "col"),
            P(("dp", "row"), "col"),
            P("col"),
            P("col", None, "row", "dp", None),
            P(None, ("row", "col"), "dp", None),
            P("row", "dp", None, "col"),
            P("col"),
            P("col", None, "row", "dp", None),
            P("row", "dp", None, "col"),
        ),
        check_vma=False,
    )
```

```python
import functools

import jax
import jax.numpy as jnp
from jax import lax
from jax.experimental import pallas as pl
from jax.experimental.pallas import tpu as pltpu
from jax.sharding import PartitionSpec as P

MESH = pl.DeviceIdType.MESH
BF = jnp.bfloat16
F32 = jnp.float32
EPS = 1e-05
VMEM_LIMIT = 63 * 2**20


def nn(a, b):
    return lax.dot_general(a, b, (((1,), (0,)), ((), ())), preferred_element_type=F32)


def nt(a, b):
    return lax.dot_general(a, b, (((1,), (1,)), ((), ())), preferred_element_type=F32)


class Links:
    def __init__(self, send_sems, recv_sems):
        self.send_sems, self.recv_sems = send_sems, recv_sems
        self.count = 0
        self.open = []

    def slot(self):
        self.count += 1
        return self.count - 1

    def copy(self, src, dst, to, slot=None):
        if slot is None:
            slot = self.slot()
        return pltpu.make_async_remote_copy(
            src_ref=src,
            dst_ref=dst,
            send_sem=self.send_sems.at[slot],
            recv_sem=self.recv_sems.at[slot],
            device_id=to,
            device_id_type=MESH,
        )

    def send(self, src, dst, to):
        c = self.copy(src, dst, to)
        c.start()
        self.open.append(c)
        return c

    def sent(self, *copies):
        for c in copies:
            c.wait_send()
            self.open = [o for o in self.open if o is not c]

    def close(self):
        for c in self.open:
            c.wait_send()
        self.open = []


def rows_loop(count, step, body):
    def one(i, carry):
        body(pl.multiple_of(i * step, step))
        return carry

    lax.fori_loop(0, count // step, one, 0)


def block_kernel(n_dp, width, split_in, *refs):
    (
        tok, g1, w_in, cw, w_out, g2, w_gu, w_dn, cot, mask1, mask2,
        block_out, d_tok, d_gain, d_conv, d_out, n1z, n2z, cotz, actz, ghz, gpz,
        w_in_v, w_out_v, w_gu_v, w_dn_v,
        xall, call, gat, act, gh, gp,
        proj_o, proj_r, mext, halo_b, cout, gext, halo_a, gg_s, gg_r, gg_o,
        hid_o, hid_r, ga_o, ga_r,
        rs_s, rs_r, rt_s, rt_r, acc_b, acc_o,
        resid, gres, ss_s, ss_r, red_s, red_r, red_z, po_s, po_r,
        send_sems, recv_sems, local_sems,
    ) = refs
    R, B, Dl = xall.shape
    Uc = w_out_v.shape[1]
    Fc = w_dn_v.shape[1]
    T = R * B
    dp, row, col = lax.axis_index("dp"), lax.axis_index("row"), lax.axis_index("col")
    other = 1 - col
    low = row + 1 - 2 * lax.rem(row, 2)
    high = row + 2 - 4 * lax.rem(row // 2, 2)
    row_a = low * other + high * col
    row_b = high * other + low * col
    row_d = low + high - row
    to_a, to_b, to_col = {"row": row_a}, {"row": row_b}, {"col": other}
    links = Links(send_sems, recv_sems)
    half = n_dp // 2
    holder = dp // half
    peers = [lax.rem(dp + k, n_dp) for k in range(n_dp)]
    sources = [lax.rem(dp + n_dp - k, n_dp) for k in range(n_dp)]

    loads = {"in": [], "out": [], "gu": [], "dn": []}
    n_local = 0

    def local(src, dst):
        nonlocal n_local
        c = pltpu.make_async_copy(src, dst, local_sems.at[n_local])
        n_local += 1
        c.start()
        return c

    for c in range(2):
        for k in range(3):
            loads["in"].append(local(w_in.at[k, :, pl.ds(c * Uc, Uc)], w_in_v.at[c, k]))
    for c in range(2):
        loads["dn"].append(local(w_dn.at[pl.ds(c * Fc, Fc), :], w_dn_v.at[c]))
        loads["out"].append(local(w_out.at[pl.ds(c * Uc, Uc), :], w_out_v.at[c]))
    for c in range(2):
        for k in range(2):
            loads["gu"].append(local(w_gu.at[k, :, pl.ds(c * Fc, Fc)], w_gu_v.at[c, k]))

    def loaded(name):
        for c in loads[name]:
            c.wait()

    barrier = pltpu.get_barrier_semaphore()
    for to in (to_col, {"row": low}, {"row": high}):
        pl.semaphore_signal(barrier, inc=1, device_id=to, device_id_type=MESH)
    for k in range(1, n_dp):
        pl.semaphore_signal(
            barrier, inc=1, device_id={"dp": lax.rem(dp + k, n_dp)}, device_id_type=MESH
        )

    def col_total(place):
        c = links.send(ss_s.at[place], ss_r.at[place], to_col)
        c.wait_recv()

    def gather(buf):
        first = links.send(buf.at[row], buf.at[row], to_a)
        second = links.send(buf.at[row], buf.at[row], to_b)
        state = {}

        def relay():
            first.wait_recv()
            state["third"] = links.send(buf.at[row_a], buf.at[row_a], to_b)

        def second_in():
            second.wait_recv()

        def third_in():
            state["third"].wait_recv()

        def all_sent():
            links.sent(first, second, state["third"])

        return relay, second_in, third_in, all_sent

    class Line:
        def __init__(self, first, dst):
            self.first, self.dst = first, dst
            self.up = [links.slot() for _ in range(n_dp + 1)]
            self.down = [links.slot() for _ in range(n_dp + 1)]

        def up_copy(self, hop):
            at = self.dst.at[lax.rem(dp + n_dp - (hop - 1), n_dp), row]
            src = self.first if hop == 1 else at
            return links.copy(src, at, {"dp": peers[1]}, self.up[hop])

        def down_copy(self, hop):
            at = self.dst.at[lax.rem(dp + hop - 1, n_dp), row]
            src = self.first if hop == 1 else at
            return links.copy(src, at, {"dp": sources[1]}, self.down[hop])

        def arrived(self, hop):
            @pl.when(dp >= hop)
            def _():
                self.up_copy(hop).wait_recv()

            @pl.when(dp + hop < n_dp)
            def _():
                self.down_copy(hop).wait_recv()

        def start(self, hop):
            if hop > 1:
                self.arrived(hop - 1)

            @pl.when((dp + 1 < n_dp) & (dp >= hop - 1))
            def _():
                self.up_copy(hop).start()

            @pl.when((dp >= 1) & (dp + hop - 1 < n_dp))
            def _():
                self.down_copy(hop).start()

        def sent(self, hop):
            @pl.when((dp + 1 < n_dp) & (dp >= hop - 1))
            def _():
                self.up_copy(hop).wait_send()

            @pl.when((dp >= 1) & (dp + hop - 1 < n_dp))
            def _():
                self.down_copy(hop).wait_send()

        def rest(self):
            for hop in range(3, n_dp):
                self.start(hop)
            self.arrived(n_dp - 1)

        def plane(self):
            at = lambda z, r: self.dst.at[z, r]
            self.to_a = [links.send(at(z, row), at(z, row), to_a) for z in peers[1:]]
            self.to_b = [links.send(at(z, row), at(z, row), to_b) for z in peers[1:]]

        def relay(self):
            self.on = []
            for z, c in zip(peers[1:], self.to_a):
                c.wait_recv()
                self.on.append(links.send(self.dst.at[z, row_a], self.dst.at[z, row_a], to_b))

        def finish(self):
            for c in (*self.to_b, *self.on):
                c.wait_recv()

    class Units:
        def __init__(self, src, dst):
            self.src, self.dst = src, dst
            self.size = dst.shape[-1]
            self.slots = [links.slot() for _ in range(n_dp)]

        def chunk(self, z):
            at = pl.ds(pl.multiple_of(lax.rem(z, half) * self.size, self.size), self.size)
            return self.src.at[(z // half, *([slice(None)] * (len(self.src.shape) - 2)), at)]

        def across(self, k):
            return links.copy(self.chunk(peers[k]), self.dst.at[dp], {"dp": peers[k]}, self.slots[k])

        def start(self):
            for k in range(1, n_dp):

                @pl.when(peers[k] // half == col)
                def _(k=k):
                    self.across(k).start()

        def keep(self):
            return local(self.chunk(dp), self.dst.at[dp])

        def hand_on(self):
            self.handed = [links.slot() for _ in range(n_dp)]
            for k in range(1, n_dp):

                @pl.when(holder == col)
                def _(k=k):
                    self.across(k).wait_recv()
                    self.hand(k).start()

        def hand(self, k):
            at = self.dst.at[sources[k]]
            return links.copy(at, at, to_col, self.handed[k])

        def finish(self):
            for k in range(1, n_dp):

                @pl.when(holder != col)
                def _(k=k):
                    self.hand(k).wait_recv()

        def close(self):
            for k in range(1, n_dp):

                @pl.when(peers[k] // half == col)
                def _(k=k):
                    self.across(k).wait_send()

                @pl.when(holder == col)
                def _(k=k):
                    self.hand(k).wait_send()

    def row_sum(sends, recvs, partial, filler=None):
        def to_bf(slot):
            def put(n0, value):
                sends[slot, :, n0 : n0 + value.shape[1]] = value.astype(BF)

            return put

        def to_f32(acc):
            def put(n0, value):
                acc[:, n0 : n0 + value.shape[1]] = value

            return put

        partial(row_d, to_bf(0))
        c0 = links.send(sends.at[0], recvs.at[0], to_a)
        partial(row_a, to_bf(1))
        c1 = links.send(sends.at[1], recvs.at[1], to_a)
        partial(row_b, to_f32(acc_b))
        c0.wait_recv()

        def combine(r0):
            at = pl.ds(r0, 16)
            sends[2, at, :] = (acc_b[at, :] + recvs[0, at, :].astype(F32)).astype(BF)

        rows_loop(B, 16, combine)
        c2 = links.send(sends.at[2], recvs.at[2], to_b)
        partial(row, to_f32(acc_o))
        if filler is not None:
            filler()
        c1.wait_recv()
        c2.wait_recv()
        return c0, c1, c2

    def row_total(recvs, at):
        return acc_o[at, :] + recvs[1, at, :].astype(F32) + recvs[2, at, :].astype(F32)

    def lanes(x):
        return jnp.broadcast_to(x, (x.shape[0], 128))

    def squares(r0):
        at = pl.ds(r0, 16)
        x = tok[at, :].astype(F32)
        ss_s[0, at, :] = lanes(jnp.sum(x * x, axis=1, keepdims=True))

    rows_loop(B, 16, squares)
    pl.semaphore_wait(barrier, 3 + n_dp - 1)
    cot_line = Line(cot, cotz)
    n1_line = Line(xall.at[row], n1z)
    n2_line = Line(xall.at[row], n2z)
    cot_line.start(1)
    col_total(0)

    def scale_of(place, at):
        return lax.rsqrt((ss_s[place, at, :] + ss_r[place, at, :]) / width + EPS)[:, :1]

    def normed_one(r0):
        at = pl.ds(r0, 16)
        x = tok[at, :].astype(F32)
        xall[row, at, :] = (x * scale_of(0, at) * g1[...]).astype(BF)

    rows_loop(B, 16, normed_one)
    relay, second_in, third_in, all_sent = gather(xall)
    n1_line.start(1)

    def project(blk):
        x = xall[blk]
        for k in range(3):
            gp[col, blk, k] = nn(x, w_in_v[other, k]).astype(BF)
        c = links.send(gp.at[col, blk], proj_r.at[blk], to_col)
        for k in range(3):
            proj_o[k, pl.ds(pl.multiple_of(blk * B, B), B), :] = nn(x, w_in_v[col, k])
        return c

    loaded("in")
    sent = [project(row)]
    relay()
    sent.append(project(row_a))
    second_in()
    sent.append(project(row_b))
    third_in()
    call[row] = cot[...]
    cot_relay, cot_second, cot_third, _ = gather(call)
    sent.append(project(row_d))
    n1_out = local(xall, n1z.at[dp])
    cot_line.start(2)
    n1_line.start(2)

    for blk, c in zip((row, row_b, row_a, row_d), sent):
        c.wait_recv()
        base = blk * B

        def add(r0, blk=blk, base=base):
            at = pl.ds(r0, 32)
            to = pl.ds(pl.multiple_of(base + r0, 32), 32)
            g = [proj_o[k, to, :] + proj_r[blk, k, at, :].astype(F32) for k in range(3)]
            for k in range(3):
                proj_o[k, to, :] = g[k]
            mext[pl.ds(pl.multiple_of(base + r0 + 8, 8), 32), :] = g[0] * g[2]

        rows_loop(B, 32, add)
    links.sent(*sent)

    behind = links.slot()

    @pl.when(dp < n_dp - 1)
    def _():
        links.copy(mext.at[pl.ds(T, 8), :], halo_b, {"dp": lax.rem(dp + 1, n_dp)}, behind).start()

    @pl.when(dp > 0)
    def _():
        links.copy(mext.at[pl.ds(T, 8), :], halo_b, {"dp": lax.rem(dp + 1, n_dp)}, behind).wait_recv()
        mext[0:8, :] = halo_b[...]

    @pl.when(dp == 0)
    def _():
        mext[0:8, :] = jnp.zeros((8, Uc), F32)

    CH = B // 2

    def mask_of(mask, at):
        return jnp.concatenate([mask[at, :]] * (Uc // 128), axis=1)

    for i in range(T // CH):
        at = pl.ds(i * CH, CH)
        x = mext[pl.ds(i * CH, CH + 8), :]
        y = cw[0:1, :] * x[8 : 8 + CH]
        y = y + cw[1:2, :] * mask_of(mask1, at) * x[7 : 7 + CH]
        y = y + cw[2:3, :] * mask_of(mask2, at) * x[6 : 6 + CH]
        cout[at, :] = y
        gat[col, i * CH // B, i * CH % B : i * CH % B + CH, :] = (proj_o[1, at, :] * y).astype(BF)
    gated_in = links.send(gat.at[col], gat.at[col], to_col)
    cot_line.rest()
    n1_line.rest()
    gated_in.wait_recv()

    loaded("out")
    n1_out.wait()
    n1_line.sent(1)
    all_sent()

    def out_partial(blk, put):
        for n0 in range(0, Dl, Dl // 2):
            n = slice(n0, n0 + Dl // 2)
            put(n0, nn(gat[0, blk], w_out_v[0, :, n]) + nn(gat[1, blk], w_out_v[1, :, n]))

    sent = row_sum(rs_s, rs_r, out_partial, filler=cot_relay)

    def residual(r0):
        at = pl.ds(r0, 16)
        x = tok[at, :].astype(F32) + row_total(rs_r, at)
        resid[at, :] = x
        ss_s[1, at, :] = lanes(jnp.sum(x * x, axis=1, keepdims=True))

    rows_loop(B, 16, residual)
    links.sent(*sent)
    col_total(1)

    def normed_two(r0):
        at = pl.ds(r0, 16)
        xall[row, at, :] = (resid[at, :] * scale_of(1, at) * g2[...]).astype(BF)

    rows_loop(B, 16, normed_two)
    relay, second_in, third_in, all_sent = gather(xall)
    n2_line.start(1)

    cot_second()
    cot_third()
    loaded("dn")
    ga_sent = []
    for blk in (row, row_a, row_b, row_d):
        x = call[blk]
        for n0 in range(0, Fc, Fc // 2):
            n = slice(n0, n0 + Fc // 2)
            act[col, blk, :, n] = nt(x, w_dn_v[other, n, :]).astype(BF)
        ga_sent.append(links.send(act.at[col, blk], ga_r.at[blk], to_col))
    relay()
    for blk in (row, row_a, row_b, row_d):
        x = call[blk]
        for n0 in range(0, Fc, Fc // 2):
            n = slice(n0, n0 + Fc // 2)
            ga_o[blk, :, n] = nt(x, w_dn_v[col, n, :])
    cot_out = local(call, cotz.at[dp])

    def hidden_other(blk):
        def one(k, carry):
            for n0 in range(0, Fc, Fc // 2):
                n = slice(n0, n0 + Fc // 2)
                gh[col, blk, k, :, n] = nn(xall[blk], w_gu_v[other, k, :, n]).astype(BF)
            return carry

        lax.fori_loop(0, 2, one, 0)
        return links.send(gh.at[col, blk], hid_r.at[blk], to_col)

    loaded("gu")
    hid_sent = [hidden_other(row), hidden_other(row_a)]
    second_in()
    hid_sent.append(hidden_other(row_b))
    third_in()
    hid_sent.append(hidden_other(row_d))
    n2_out = local(xall, n2z.at[dp])
    cot_line.plane()
    n2_line.start(2)

    gh_in = {}
    for name, blk in (("d", row_d), ("a", row_a), ("b", row_b), ("o", row)):

        def one(k, carry, blk=blk):
            for n0 in range(0, Fc, Fc // 2):
                n = slice(n0, n0 + Fc // 2)
                hid_o[k, :, n] = nn(xall[blk], w_gu_v[col, k, :, n])
            return carry

        lax.fori_loop(0, 2, one, 0)
        which = {"o": 0, "a": 1, "b": 2, "d": 3}[name]
        theirs = {"o": 0, "a": 2, "b": 1, "d": 3}[name]
        hid_sent[theirs].wait_recv()
        ga_sent[theirs].wait_recv()
        links.sent(hid_sent[which], ga_sent[which])

        def activate(r0, blk=blk):
            at = pl.ds(r0, 16)
            for n0 in range(0, Fc, Fc // 2):
                n = slice(n0, n0 + Fc // 2)
                gate = hid_o[0, at, n] + hid_r[blk, 0, at, n].astype(F32)
                up = hid_o[1, at, n] + hid_r[blk, 1, at, n].astype(F32)
                ga = ga_o[blk, at, n] + ga_r[blk, at, n].astype(F32)
                s = jax.nn.sigmoid(gate)
                silu = gate * s
                act[col, blk, at, n] = (silu * up).astype(BF)
                gh[col, blk, 0, at, n] = (ga * up * s * (1.0 + gate * (1.0 - s))).astype(BF)
                gh[col, blk, 1, at, n] = (ga * silu).astype(BF)

        rows_loop(B, 16, activate)
        gh_in[name] = (
            links.send(gh.at[col, blk], gh.at[col, blk], to_col),
            links.send(act.at[col, blk], act.at[col, blk], to_col),
        )
    act_units, gh_units = Units(act, actz), Units(gh, ghz)
    act_units.start()
    gh_units.start()
    for pair in gh_in.values():
        for c in pair:
            c.wait_recv()
    kept = [act_units.keep(), gh_units.keep()]
    n2_out.wait()
    n2_line.sent(1)
    n2_line.rest()
    cot_line.relay()
    all_sent()

    def gu_partial(blk, put):
        for n0 in range(0, Dl, Dl // 4):
            n = slice(n0, n0 + Dl // 4)
            total = None
            for c in range(2):
                for k in range(2):
                    part = nt(gh[c, blk, k], w_gu_v[c, k, n, :])
                    total = part if total is None else total + part
            put(n0, total)

    sent = row_sum(rs_s, rs_r, gu_partial)

    def back_two(r0):
        at = pl.ds(r0, 16)
        g = row_total(rs_r, at)
        gres[at, :] = g
        ss_s[2, at, :] = lanes(jnp.sum(g * g2[...] * resid[at, :], axis=1, keepdims=True))

    rows_loop(B, 16, back_two)
    links.sent(*sent)
    col_total(2)

    def inner_of(place, at):
        return (ss_s[place, at, :] + ss_r[place, at, :])[:, :1]

    def branch(i, gain):
        at = pl.ds(pl.multiple_of(i * 16, 16), 16)
        g = gres[at, :]
        x = resid[at, :]
        s = scale_of(1, at)
        y = cot[at, :].astype(F32) + s * g2[...] * g - x * (s * s * s) * inner_of(2, at) / width
        gres[at, :] = y
        xall[row, at, :] = y.astype(BF)
        return gain + jnp.sum(g * x * s, axis=0, keepdims=True)

    gain_two = lax.fori_loop(0, B // 16, branch, jnp.zeros((1, Dl), F32))
    relay, second_in, third_in, all_sent = gather(xall)

    def down_partial(blk, put):
        for n0 in range(0, Dl, Dl // 2):
            n = slice(n0, n0 + Dl // 2)
            put(n0, nn(act[0, blk], w_dn_v[0, :, n]) + nn(act[1, blk], w_dn_v[1, :, n]))

    def gated_other(blk):
        gg_s[blk] = nt(xall[blk], w_out_v[other]).astype(BF)
        c = links.send(gg_s.at[blk], gg_r.at[blk], to_col)
        gg_o[blk] = nt(xall[blk], w_out_v[col])
        return c

    sent = [gated_other(row)]
    relay()
    sent.append(gated_other(row_a))
    second_in()
    sent.append(gated_other(row_b))
    third_in()
    sent.append(gated_other(row_d))
    n2_line.plane()

    for blk, c in zip((row, row_b, row_a, row_d), sent):
        c.wait_recv()
        base = blk * B

        def conv_grad(r0, blk=blk, base=base):
            at = pl.ds(r0, 32)
            to = pl.ds(pl.multiple_of(base + r0, 32), 32)
            g = gg_o[blk, at, :] + gg_r[blk, at, :].astype(F32)
            gext[to, :] = g * proj_o[1, to, :]
            gp[col, blk, 1, at, :] = (g * cout[to, :]).astype(BF)

        rows_loop(B, 32, conv_grad)

    ahead = links.slot()

    @pl.when(dp > 0)
    def _():
        links.copy(gext.at[pl.ds(0, 8), :], halo_a, {"dp": lax.rem(dp + n_dp - 1, n_dp)}, ahead).start()

    @pl.when(dp < n_dp - 1)
    def _():
        links.copy(gext.at[pl.ds(0, 8), :], halo_a, {"dp": lax.rem(dp + n_dp - 1, n_dp)}, ahead).wait_recv()
        gext[T : T + 8, :] = halo_a[...]

    @pl.when(dp == n_dp - 1)
    def _():
        gext[T : T + 8, :] = jnp.zeros((8, Uc), F32)

    terms = [jnp.zeros((1, Uc), F32) for _ in range(3)]
    for i in range(T // CH):
        at = pl.ds(i * CH, CH)
        more = pl.ds(i * CH, CH + 8)
        x = mext[more, :]
        g = gext[more, :]
        m1, m2 = mask_of(mask1, more), mask_of(mask2, more)
        now = g[:CH]
        terms[0] = terms[0] + jnp.sum(now * x[8 : 8 + CH], axis=0, keepdims=True)
        terms[1] = terms[1] + jnp.sum(m1[:CH] * now * x[7 : 7 + CH], axis=0, keepdims=True)
        terms[2] = terms[2] + jnp.sum(m2[:CH] * now * x[6 : 6 + CH], axis=0, keepdims=True)
        y = cw[0:1, :] * now
        y = y + cw[1:2, :] * (m1 * g)[1 : 1 + CH]
        y = y + cw[2:3, :] * (m2 * g)[2 : 2 + CH]
        blk, to = i * CH // B, slice(i * CH % B, i * CH % B + CH)
        gp[col, blk, 0, to, :] = (y * proj_o[2, at, :]).astype(BF)
        gp[col, blk, 2, to, :] = (y * proj_o[0, at, :]).astype(BF)
    red_s[...] = jnp.zeros_like(red_s)
    for k in range(3):
        red_s[8 + k : 9 + k, :Uc] = terms[k]
    gp_in = links.send(gp.at[col], gp.at[col], to_col)
    if split_in:
        gp_units = Units(gp, gpz)
        gp_units.start()

    po_all = []
    for z in range(n_dp):
        rows = po_s.shape[1]
        at = pl.ds(z % half * rows, rows)
        g = lax.dot_general(
            gat[z // half, :, :, at].reshape(T, rows), xall[...].reshape(T, Dl),
            (((0,), (0,)), ((), ())), preferred_element_type=F32,
        )
        po_s[z] = g.astype(BF)
    for k in range(1, n_dp):
        po_all.append(links.send(po_s.at[peers[k]], po_r.at[dp], {"dp": peers[k]}))
    gp_in.wait_recv()
    if split_in:
        kept.append(gp_units.keep())
    else:
        kept.append(local(gp, gpz))
    n2_line.relay()

    def in_partial(blk, put):
        for n0 in range(0, Dl, Dl // 4):
            n = slice(n0, n0 + Dl // 4)
            total = None
            for c in range(2):
                for k in range(3):
                    part = nt(gp[c, blk, k], w_in_v[c, k, n, :])
                    total = part if total is None else total + part
            put(n0, total)

    sent_in = row_sum(rs_s, rs_r, in_partial)

    def back_one(r0):
        at = pl.ds(r0, 16)
        g = row_total(rs_r, at)
        d_tok[at, :] = g
        ss_s[3, at, :] = lanes(
            jnp.sum(g * g1[...] * tok[at, :].astype(F32), axis=1, keepdims=True)
        )

    rows_loop(B, 16, back_one)
    col_total(3)

    def token_grad(i, gain):
        at = pl.ds(pl.multiple_of(i * 16, 16), 16)
        g = d_tok[at, :]
        x = tok[at, :].astype(F32)
        s = scale_of(0, at)
        y = gres[at, :] + s * g1[...] * g - x * (s * s * s) * inner_of(3, at) / width
        d_tok[at, :] = y
        return gain + jnp.sum(g * x * s, axis=0, keepdims=True)

    gain_one = lax.fori_loop(0, B // 16, token_grad, jnp.zeros((1, Dl), F32))

    red_s[0:1, :] = gain_one
    red_s[1:2, :] = gain_two
    c0 = links.send(red_s.at[pl.ds(0, 8), :], red_r.at[0], to_a)
    n1_line.plane()
    act_units.hand_on()
    gh_units.hand_on()
    sent_down = row_sum(rt_s, rt_r, down_partial)

    def block_rows(r0):
        at = pl.ds(r0, 16)
        block_out[at, :] = (resid[at, :] + row_total(rt_r, at)).astype(BF)

    rows_loop(B, 16, block_rows)
    c0.wait_recv()
    links.sent(c0)
    red_s[0:8, :] = red_s[0:8, :] + red_r[0]
    c1 = links.send(red_s.at[pl.ds(0, 8), :], red_r.at[1], to_b)
    c1.wait_recv()
    red_z[dp] = red_s[...]
    red_z[dp, 0:8, :] = red_s[0:8, :] + red_r[1]
    arrived = []
    for k in range(1, n_dp):
        arrived.append(links.send(red_z.at[dp], red_z.at[dp], {"dp": lax.rem(dp + k, n_dp)}))
    for c in arrived:
        c.wait_recv()
    total = red_z[0]
    for k in range(1, n_dp):
        total = total + red_z[k]
    d_gain[...] = total[0:8]
    d_conv[...] = total[8:16, :Uc]

    @pl.when(dp < n_dp - 1)
    def _():
        links.copy(mext.at[pl.ds(T, 8), :], halo_b, {"dp": lax.rem(dp + 1, n_dp)}, behind).wait_send()

    @pl.when(dp > 0)
    def _():
        links.copy(gext.at[pl.ds(0, 8), :], halo_a, {"dp": lax.rem(dp + n_dp - 1, n_dp)}, ahead).wait_send()

    n1_line.relay()
    for c in po_all:
        c.wait_recv()
    out_total = po_s[dp].astype(F32)
    for k in range(1, n_dp):
        out_total = out_total + po_r[peers[k]].astype(F32)
    d_out[...] = out_total
    units = [act_units, gh_units]
    if split_in:
        gp_units.hand_on()
        units.append(gp_units)
    for line in (cot_line, n1_line, n2_line):
        line.finish()
    for unit in units:
        unit.finish()
        unit.close()
    for hop in range(1, n_dp):
        cot_line.sent(hop)
        if hop > 1:
            n1_line.sent(hop)
            n2_line.sent(hop)
    for c in [cot_out, *kept]:
        c.wait()
    links.close()


def run_block(n_dp, width, split_in, tok, g1, w_in, cw, w_out, g2, w_gu, w_dn, cot, mask1, mask2):
    B, Dl = tok.shape
    R = 4
    T = R * B
    Uc = w_out.shape[0] // 2
    Fc = w_dn.shape[0] // 2
    vm = lambda shape, kind=BF: pltpu.VMEM(shape, kind)
    any_spec, vmem_spec = pl.BlockSpec(memory_space=pl.ANY), pl.BlockSpec(memory_space=pltpu.VMEM)
    shape = jax.ShapeDtypeStruct
    rows = shape((n_dp, R, B, Dl), BF)
    return pl.pallas_call(
        functools.partial(block_kernel, n_dp, width, split_in),
        out_shape=(
            shape((B, Dl), BF),
            shape((B, Dl), F32),
            shape((8, Dl), F32),
            shape((8, Uc), F32),
            shape((2 * Uc // n_dp, Dl), F32),
            rows,
            rows,
            rows,
            shape((n_dp, R, B, 2 * Fc // n_dp), BF),
            shape((n_dp, R, 2, B, 2 * Fc // n_dp), BF),
            shape((n_dp, R, 3, B, 2 * Uc // n_dp) if split_in else (2, R, 3, B, Uc), BF),
        ),
        in_specs=[
            vmem_spec, vmem_spec, any_spec, vmem_spec, any_spec, vmem_spec,
            any_spec, any_spec, vmem_spec, vmem_spec, vmem_spec,
        ],
        out_specs=[vmem_spec] * 5 + [any_spec] * 6,
        scratch_shapes=[
            vm((2, 3, Dl, Uc)), vm((2, Uc, Dl)), vm((2, 2, Dl, Fc)), vm((2, Fc, Dl)),
            vm((R, B, Dl)), vm((R, B, Dl)),
            vm((2, R, B, Uc)), vm((2, R, B, Fc)), vm((2, R, 2, B, Fc)), vm((2, R, 3, B, Uc)),
            vm((3, T, Uc), F32), vm((R, 3, B, Uc)), vm((T + 8, Uc), F32), vm((8, Uc), F32),
            vm((T, Uc), F32), vm((T + 8, Uc), F32), vm((8, Uc), F32),
            vm((R, B, Uc)), vm((R, B, Uc)), vm((R, B, Uc), F32),
            vm((2, B, Fc), F32), vm((R, 2, B, Fc)), vm((R, B, Fc), F32), vm((R, B, Fc)),
            vm((3, B, Dl)), vm((3, B, Dl)), vm((3, B, Dl)), vm((3, B, Dl)),
            vm((B, Dl), F32), vm((B, Dl), F32),
            vm((B, Dl), F32), vm((B, Dl), F32),
            vm((4, B, 128), F32), vm((4, B, 128), F32),
            vm((16, Dl), F32), vm((2, 8, Dl), F32), vm((n_dp, 16, Dl), F32),
            vm((n_dp, 2 * Uc // n_dp, Dl)), vm((n_dp, 2 * Uc // n_dp, Dl)),
            pltpu.SemaphoreType.DMA((80 + 40 * n_dp,)), pltpu.SemaphoreType.DMA((80 + 40 * n_dp,)),
            pltpu.SemaphoreType.DMA((40,)),
        ],
        compiler_params=pltpu.CompilerParams(
            collective_id=0, has_side_effects=True, vmem_limit_bytes=VMEM_LIMIT
        ),
        name="block",
    )(tok, g1, w_in, cw, w_out, g2, w_gu, w_dn, cot, mask1, mask2)


def sequence_offsets(lengths, index):
    ends = jnp.cumsum(lengths)
    starts = ends - lengths
    reached = starts[None, :] <= index[:, None]
    return index - jnp.max(jnp.where(reached, starts[None, :], 0), axis=1)


def on_device(
    tokens, gain_one, in_weight, conv_weight, out_weight, gain_two, gate_up_weight, down_weight,
    cotangent, lengths,
):
    n_dp = lax.axis_size("dp")
    B, Dl = tokens.shape
    T = B * lax.axis_size("row")
    width = Dl * lax.axis_size("col")
    index = lax.axis_index("dp") * T + jnp.arange(T + 16, dtype=jnp.int32)
    offset = sequence_offsets(lengths, index)
    masks = [
        jnp.broadcast_to((offset >= lag).astype(F32)[:, None], (T + 16, 128)) for lag in (1, 2)
    ]
    conv = jnp.pad(conv_weight.astype(F32), ((0, 5), (0, 0)))
    chunk = in_weight.shape[2] // n_dp
    split_in = chunk % 128 == 0
    block_out, d_tok, d_gain, d_conv, d_out, n1, n2, cot, act, gh, gp = run_block(
        n_dp,
        float(width),
        split_in,
        tokens,
        gain_one.astype(F32)[None, :],
        jnp.transpose(in_weight, (1, 0, 2)),
        conv,
        out_weight,
        gain_two.astype(F32)[None, :],
        jnp.transpose(gate_up_weight, (1, 0, 2)),
        down_weight,
        cotangent,
        *masks,
    )

    dot = functools.partial(jnp.einsum, preferred_element_type=F32)
    d_down = dot("zrtf,zrti->fi", act, cot)
    d_gu = dot("zrti,zrktf->ikf", n2, gh)
    if split_in:
        d_in = dot("zrti,zrktu->iku", n1, gp)
    else:
        mine = lax.dynamic_index_in_dim(n1, lax.axis_index("dp"), 0, keepdims=False)
        d_in = lax.psum_scatter(
            dot("rti,crktu->ikcu", mine, gp).reshape(Dl, 3, -1).astype(BF),
            "dp",
            scatter_dimension=2,
            tiled=True,
        ).astype(F32)
    part = d_conv.shape[1] * 1 // n_dp
    mine = lax.dynamic_slice(d_conv, (0, lax.axis_index("dp") * part), (3, part))
    return (
        block_out,
        d_tok,
        d_gain[0],
        d_in.reshape(Dl, 3, 1, 1, -1),
        mine.reshape(3, 1, 1, part),
        d_out.reshape(1, 1, -1, Dl),
        d_gain[1],
        d_gu.reshape(Dl, 2, 1, 1, -1),
        d_down.reshape(1, 1, -1, Dl),
    )


def solution(mesh):
    placed = (
        P(("dp", "row"), "col"),
        P("col"),
        P("col", None, "row"),
        P(None, ("row", "col")),
        P("row", "col"),
        P("col"),
        P("col", None, "row"),
        P("row", "col"),
        P(("dp", "row"), "col"),
        P(),
    )
    return jax.shard_map(
        on_device,
        mesh=mesh,
        in_specs=placed,
        out_specs=(
            P(("dp", "row"), "col"),
            P(("dp", "row"), "col"),
            P("col"),
            P("col", None, "row", "dp", None),
            P(None, ("row", "col"), "dp", None),
            P("row", "dp", None, "col"),
            P("col"),
            P("col", None, "row", "dp", None),
            P("row", "dp", None, "col"),
        ),
        check_vma=False,
    )
```

```python
import functools

import jax
import jax.numpy as jnp
from jax import lax
from jax.experimental import pallas as pl
from jax.experimental.pallas import tpu as pltpu
from jax.sharding import PartitionSpec as P

MESH = pl.DeviceIdType.MESH
BF = jnp.bfloat16
F32 = jnp.float32
EPS = 1e-05
VMEM_LIMIT = 63 * 2**20


def nn(a, b):
    return lax.dot_general(a, b, (((1,), (0,)), ((), ())), preferred_element_type=F32)


def nt(a, b):
    return lax.dot_general(a, b, (((1,), (1,)), ((), ())), preferred_element_type=F32)


class Links:
    def __init__(self, send_sems, recv_sems):
        self.send_sems, self.recv_sems = send_sems, recv_sems
        self.count = 0
        self.open = []

    def slot(self):
        self.count += 1
        return self.count - 1

    def copy(self, src, dst, to, slot=None):
        if slot is None:
            slot = self.slot()
        return pltpu.make_async_remote_copy(
            src_ref=src,
            dst_ref=dst,
            send_sem=self.send_sems.at[slot],
            recv_sem=self.recv_sems.at[slot],
            device_id=to,
            device_id_type=MESH,
        )

    def send(self, src, dst, to):
        c = self.copy(src, dst, to)
        c.start()
        self.open.append(c)
        return c

    def sent(self, *copies):
        for c in copies:
            c.wait_send()
            self.open = [o for o in self.open if o is not c]

    def close(self):
        for c in self.open:
            c.wait_send()
        self.open = []


def rows_loop(count, step, body):
    def one(i, carry):
        body(pl.multiple_of(i * step, step))
        return carry

    lax.fori_loop(0, count // step, one, 0)


def block_kernel(n_dp, width, split_in, *refs):
    (
        tok, g1, w_in, cw, w_out, g2, w_gu, w_dn, cot, mask1, mask2,
        block_out, d_tok, d_gain, d_conv, d_out, n1z, n2z, cotz, actz, ghz, gpz,
        w_in_v, w_out_v, w_gu_v, w_dn_v,
        xall, call, gat, act, gh, gp,
        proj_o, proj_r, mext, halo_b, cout, gext, halo_a, gg_s, gg_r, gg_o,
        hid_o, hid_r, ga_o, ga_r,
        rs_s, rs_r, rt_s, rt_r, acc_b, acc_o, down_o,
        resid, gres, ss_s, ss_r, red_s, red_r, red_z, po_s, po_r,
        send_sems, recv_sems, local_sems,
    ) = refs
    R, B, Dl = xall.shape
    Uc = w_out_v.shape[1]
    Fc = w_dn_v.shape[1]
    T = R * B
    dp, row, col = lax.axis_index("dp"), lax.axis_index("row"), lax.axis_index("col")
    other = 1 - col
    low = row + 1 - 2 * lax.rem(row, 2)
    high = row + 2 - 4 * lax.rem(row // 2, 2)
    row_a = low * other + high * col
    row_b = high * other + low * col
    row_d = low + high - row
    to_a, to_b, to_col = {"row": row_a}, {"row": row_b}, {"col": other}
    links = Links(send_sems, recv_sems)
    half = n_dp // 2
    holder = dp // half
    peers = [lax.rem(dp + k, n_dp) for k in range(n_dp)]
    sources = [lax.rem(dp + n_dp - k, n_dp) for k in range(n_dp)]

    loads = {"in": [], "out": [], "gu": [], "dn": []}
    n_local = 0

    def local(src, dst):
        nonlocal n_local
        c = pltpu.make_async_copy(src, dst, local_sems.at[n_local])
        n_local += 1
        c.start()
        return c

    for c in range(2):
        for k in range(3):
            loads["in"].append(local(w_in.at[k, :, pl.ds(c * Uc, Uc)], w_in_v.at[c, k]))
    for c in range(2):
        loads["dn"].append(local(w_dn.at[pl.ds(c * Fc, Fc), :], w_dn_v.at[c]))
        loads["out"].append(local(w_out.at[pl.ds(c * Uc, Uc), :], w_out_v.at[c]))
    for c in range(2):
        for k in range(2):
            loads["gu"].append(local(w_gu.at[k, :, pl.ds(c * Fc, Fc)], w_gu_v.at[c, k]))

    def loaded(name):
        for c in loads[name]:
            c.wait()

    barrier = pltpu.get_barrier_semaphore()
    for to in (to_col, {"row": low}, {"row": high}):
        pl.semaphore_signal(barrier, inc=1, device_id=to, device_id_type=MESH)
    for k in range(1, n_dp):
        pl.semaphore_signal(
            barrier, inc=1, device_id={"dp": lax.rem(dp + k, n_dp)}, device_id_type=MESH
        )

    def col_total(place):
        c = links.send(ss_s.at[place], ss_r.at[place], to_col)
        c.wait_recv()

    def gather(buf):
        first = links.send(buf.at[row], buf.at[row], to_a)
        second = links.send(buf.at[row], buf.at[row], to_b)
        state = {}

        def relay():
            first.wait_recv()
            state["third"] = links.send(buf.at[row_a], buf.at[row_a], to_b)

        def second_in():
            second.wait_recv()

        def third_in():
            state["third"].wait_recv()

        def all_sent():
            links.sent(first, second, state["third"])

        return relay, second_in, third_in, all_sent

    class Line:
        def __init__(self, first, dst):
            self.first, self.dst = first, dst
            self.up = [links.slot() for _ in range(n_dp + 1)]
            self.down = [links.slot() for _ in range(n_dp + 1)]
            self.sent_to, self.last = {}, []

        def up_copy(self, hop):
            at = self.dst.at[lax.rem(dp + n_dp - (hop - 1), n_dp), row]
            src = self.first if hop == 1 else at
            return links.copy(src, at, {"dp": peers[1]}, self.up[hop])

        def down_copy(self, hop):
            at = self.dst.at[lax.rem(dp + hop - 1, n_dp), row]
            src = self.first if hop == 1 else at
            return links.copy(src, at, {"dp": sources[1]}, self.down[hop])

        def arrived(self, hop):
            @pl.when(dp >= hop)
            def _():
                self.up_copy(hop).wait_recv()

            @pl.when(dp + hop < n_dp)
            def _():
                self.down_copy(hop).wait_recv()

        def start(self, hop):
            if hop > 1:
                self.arrived(hop - 1)

            @pl.when((dp + 1 < n_dp) & (dp >= hop - 1))
            def _():
                self.up_copy(hop).start()

            @pl.when((dp >= 1) & (dp + hop - 1 < n_dp))
            def _():
                self.down_copy(hop).start()

        def sent(self, hop):
            @pl.when((dp + 1 < n_dp) & (dp >= hop - 1))
            def _():
                self.up_copy(hop).wait_send()

            @pl.when((dp >= 1) & (dp + hop - 1 < n_dp))
            def _():
                self.down_copy(hop).wait_send()

        def plane(self, *ks):
            if not self.sent_to:
                for hop in range(4, n_dp):
                    self.start(hop)
                self.arrived(n_dp - 1)
            for k in ks:
                at = self.dst.at[peers[k], row]
                self.sent_to[k] = (links.send(at, at, to_a), links.send(at, at, to_b))

        def relay(self, *ks):
            for k in ks:
                first, second = self.sent_to[k]
                first.wait_recv()
                at = self.dst.at[peers[k], row_a]
                self.last.append(second)
                self.last.append(links.send(at, at, to_b))

        def finish(self):
            for c in self.last:
                c.wait_recv()

    class Units:
        def __init__(self, src, dst):
            self.src, self.dst = src, dst
            self.size = dst.shape[-1]
            self.slots = [[links.slot() for _ in range(n_dp)] for _ in range(R)]
            self.handed = [links.slot() for _ in range(n_dp)]

        def chunk(self, z, blk):
            at = pl.ds(pl.multiple_of(lax.rem(z, half) * self.size, self.size), self.size)
            return self.src.at[(z // half, blk, *([slice(None)] * (len(self.src.shape) - 3)), at)]

        def across(self, k, i, blk):
            to = self.dst.at[dp, blk]
            return links.copy(self.chunk(peers[k], blk), to, {"dp": peers[k]}, self.slots[i][k])

        def start(self, i, blk):
            for k in range(1, n_dp):

                @pl.when(peers[k] // half == col)
                def _(k=k):
                    self.across(k, i, blk).start()

        def keep(self):
            return local(self.chunk(dp, slice(None)), self.dst.at[dp])

        def hand_on(self):
            for k in range(1, n_dp):

                @pl.when(holder == col)
                def _(k=k):
                    for i in range(R):
                        self.across(k, i, 0).wait_recv()
                    self.hand(k).start()

        def hand(self, k):
            at = self.dst.at[sources[k]]
            return links.copy(at, at, to_col, self.handed[k])

        def finish(self):
            for k in range(1, n_dp):

                @pl.when(holder != col)
                def _(k=k):
                    self.hand(k).wait_recv()

        def close(self):
            for k in range(1, n_dp):

                @pl.when(peers[k] // half == col)
                def _(k=k):
                    for i in range(R):
                        self.across(k, i, 0).wait_send()

                @pl.when(holder == col)
                def _(k=k):
                    self.hand(k).wait_send()

    def row_sum(sends, recvs, partial, filler=None):
        def to_bf(slot):
            def put(n0, value):
                sends[slot, :, n0 : n0 + value.shape[1]] = value.astype(BF)

            return put

        def to_f32(acc):
            def put(n0, value):
                acc[:, n0 : n0 + value.shape[1]] = value

            return put

        partial(row_d, to_bf(0))
        c0 = links.send(sends.at[0], recvs.at[0], to_a)
        partial(row_a, to_bf(1))
        c1 = links.send(sends.at[1], recvs.at[1], to_a)
        partial(row_b, to_f32(acc_b))
        c0.wait_recv()

        def combine(r0):
            at = pl.ds(r0, 16)
            sends[2, at, :] = (acc_b[at, :] + recvs[0, at, :].astype(F32)).astype(BF)

        rows_loop(B, 16, combine)
        c2 = links.send(sends.at[2], recvs.at[2], to_b)
        partial(row, to_f32(acc_o))
        if filler is not None:
            filler()
        c1.wait_recv()
        c2.wait_recv()
        return c0, c1, c2

    def row_total(recvs, at):
        return acc_o[at, :] + recvs[1, at, :].astype(F32) + recvs[2, at, :].astype(F32)

    def lanes(x):
        return jnp.broadcast_to(x, (x.shape[0], 128))

    def squares(r0):
        at = pl.ds(r0, 16)
        x = tok[at, :].astype(F32)
        ss_s[0, at, :] = lanes(jnp.sum(x * x, axis=1, keepdims=True))

    rows_loop(B, 16, squares)
    pl.semaphore_wait(barrier, 3 + n_dp - 1)
    cot_line = Line(cot, cotz)
    n1_line = Line(xall.at[row], n1z)
    n2_line = Line(xall.at[row], n2z)
    cot_line.start(1)
    col_total(0)

    def scale_of(place, at):
        return lax.rsqrt((ss_s[place, at, :] + ss_r[place, at, :]) / width + EPS)[:, :1]

    def normed_one(r0):
        at = pl.ds(r0, 16)
        x = tok[at, :].astype(F32)
        xall[row, at, :] = (x * scale_of(0, at) * g1[...]).astype(BF)

    rows_loop(B, 16, normed_one)
    relay, second_in, third_in, all_sent = gather(xall)
    n1_line.start(1)

    def project(blk):
        x = xall[blk]
        for k in range(3):
            gp[col, blk, k] = nn(x, w_in_v[other, k]).astype(BF)
        c = links.send(gp.at[col, blk], proj_r.at[blk], to_col)
        for k in range(3):
            proj_o[k, pl.ds(pl.multiple_of(blk * B, B), B), :] = nn(x, w_in_v[col, k])
        return c

    loaded("in")
    sent = [project(row)]
    relay()
    sent.append(project(row_a))
    cot_line.start(2)
    second_in()
    sent.append(project(row_b))
    third_in()
    call[row] = cot[...]
    cot_relay, cot_second, cot_third, _ = gather(call)
    sent.append(project(row_d))
    n1_out = local(xall, n1z.at[dp])
    n1_line.start(2)

    for blk, c in zip((row, row_b, row_a, row_d), sent):
        c.wait_recv()
        base = blk * B

        def add(r0, blk=blk, base=base):
            at = pl.ds(r0, 32)
            to = pl.ds(pl.multiple_of(base + r0, 32), 32)
            g = [proj_o[k, to, :] + proj_r[blk, k, at, :].astype(F32) for k in range(3)]
            for k in range(3):
                proj_o[k, to, :] = g[k]
            mext[pl.ds(pl.multiple_of(base + r0 + 8, 8), 32), :] = g[0] * g[2]

        rows_loop(B, 32, add)
    links.sent(*sent)

    behind = links.slot()

    @pl.when(dp < n_dp - 1)
    def _():
        links.copy(mext.at[pl.ds(T, 8), :], halo_b, {"dp": lax.rem(dp + 1, n_dp)}, behind).start()

    @pl.when(dp > 0)
    def _():
        links.copy(mext.at[pl.ds(T, 8), :], halo_b, {"dp": lax.rem(dp + 1, n_dp)}, behind).wait_recv()
        mext[0:8, :] = halo_b[...]

    @pl.when(dp == 0)
    def _():
        mext[0:8, :] = jnp.zeros((8, Uc), F32)

    cot_line.start(3)
    CH = B // 2

    def mask_of(mask, at):
        return jnp.concatenate([mask[at, :]] * (Uc // 128), axis=1)

    for i in range(T // CH):
        at = pl.ds(i * CH, CH)
        x = mext[pl.ds(i * CH, CH + 8), :]
        y = cw[0:1, :] * x[8 : 8 + CH]
        y = y + cw[1:2, :] * mask_of(mask1, at) * x[7 : 7 + CH]
        y = y + cw[2:3, :] * mask_of(mask2, at) * x[6 : 6 + CH]
        cout[at, :] = y
        gat[col, i * CH // B, i * CH % B : i * CH % B + CH, :] = (proj_o[1, at, :] * y).astype(BF)
    gated_in = links.send(gat.at[col], gat.at[col], to_col)
    gated_in.wait_recv()

    loaded("out")
    n1_out.wait()
    n1_line.sent(1)
    all_sent()

    def out_partial(blk, put):
        for n0 in range(0, Dl, Dl // 2):
            n = slice(n0, n0 + Dl // 2)
            put(n0, nn(gat[0, blk], w_out_v[0, :, n]) + nn(gat[1, blk], w_out_v[1, :, n]))

    def fill():
        cot_relay()
        n1_line.start(3)

    sent = row_sum(rs_s, rs_r, out_partial, filler=fill)

    def residual(r0):
        at = pl.ds(r0, 16)
        x = tok[at, :].astype(F32) + row_total(rs_r, at)
        resid[at, :] = x
        ss_s[1, at, :] = lanes(jnp.sum(x * x, axis=1, keepdims=True))

    rows_loop(B, 16, residual)
    links.sent(*sent)
    col_total(1)

    def normed_two(r0):
        at = pl.ds(r0, 16)
        xall[row, at, :] = (resid[at, :] * scale_of(1, at) * g2[...]).astype(BF)

    rows_loop(B, 16, normed_two)
    relay, second_in, third_in, all_sent = gather(xall)
    n2_line.start(1)

    cot_second()
    cot_third()
    loaded("dn")
    ga_sent = []
    for blk in (row, row_a, row_b, row_d):
        x = call[blk]
        for n0 in range(0, Fc, Fc // 2):
            n = slice(n0, n0 + Fc // 2)
            act[col, blk, :, n] = nt(x, w_dn_v[other, n, :]).astype(BF)
        ga_sent.append(links.send(act.at[col, blk], ga_r.at[blk], to_col))
    relay()
    for blk in (row, row_a, row_b, row_d):
        x = call[blk]
        for n0 in range(0, Fc, Fc // 2):
            n = slice(n0, n0 + Fc // 2)
            ga_o[blk, :, n] = nt(x, w_dn_v[col, n, :])
    cot_out = local(call, cotz.at[dp])
    n2_line.start(2)

    def hidden_other(blk):
        def one(k, carry):
            for n0 in range(0, Fc, Fc // 2):
                n = slice(n0, n0 + Fc // 2)
                gh[col, blk, k, :, n] = nn(xall[blk], w_gu_v[other, k, :, n]).astype(BF)
            return carry

        lax.fori_loop(0, 2, one, 0)
        return links.send(gh.at[col, blk], hid_r.at[blk], to_col)

    loaded("gu")
    hid_sent = [hidden_other(row), hidden_other(row_a)]
    second_in()
    hid_sent.append(hidden_other(row_b))
    third_in()
    hid_sent.append(hidden_other(row_d))
    n2_out = local(xall, n2z.at[dp])
    cot_line.plane(1, 2)
    n2_line.start(3)
    act_units, gh_units = Units(act, actz), Units(gh, ghz)

    gh_in = {}
    for i, (name, blk) in enumerate((("d", row_d), ("a", row_a), ("b", row_b), ("o", row))):

        def one(k, carry, blk=blk):
            for n0 in range(0, Fc, Fc // 2):
                n = slice(n0, n0 + Fc // 2)
                hid_o[k, :, n] = nn(xall[blk], w_gu_v[col, k, :, n])
            return carry

        lax.fori_loop(0, 2, one, 0)
        which = {"o": 0, "a": 1, "b": 2, "d": 3}[name]
        theirs = {"o": 0, "a": 2, "b": 1, "d": 3}[name]
        hid_sent[theirs].wait_recv()
        ga_sent[theirs].wait_recv()
        links.sent(hid_sent[which], ga_sent[which])

        def activate(r0, blk=blk):
            at = pl.ds(r0, 16)
            for n0 in range(0, Fc, Fc // 2):
                n = slice(n0, n0 + Fc // 2)
                gate = hid_o[0, at, n] + hid_r[blk, 0, at, n].astype(F32)
                up = hid_o[1, at, n] + hid_r[blk, 1, at, n].astype(F32)
                ga = ga_o[blk, at, n] + ga_r[blk, at, n].astype(F32)
                s = jax.nn.sigmoid(gate)
                silu = gate * s
                act[col, blk, at, n] = (silu * up).astype(BF)
                gh[col, blk, 0, at, n] = (ga * up * s * (1.0 + gate * (1.0 - s))).astype(BF)
                gh[col, blk, 1, at, n] = (ga * silu).astype(BF)

        rows_loop(B, 16, activate)
        gh_in[name] = (
            links.send(gh.at[col, blk], gh.at[col, blk], to_col),
            links.send(act.at[col, blk], act.at[col, blk], to_col),
        )
        act_units.start(i, blk)
        gh_units.start(i, blk)
    cot_line.relay(1, 2)
    for pair in gh_in.values():
        for c in pair:
            c.wait_recv()
    kept = [act_units.keep(), gh_units.keep()]
    n2_out.wait()
    n2_line.sent(1)
    all_sent()

    def gu_partial(blk, put):
        for n0 in range(0, Dl, Dl // 4):
            n = slice(n0, n0 + Dl // 4)
            total = None
            for c in range(2):
                for k in range(2):
                    part = nt(gh[c, blk, k], w_gu_v[c, k, n, :])
                    total = part if total is None else total + part
            put(n0, total)

    sent = row_sum(rs_s, rs_r, gu_partial)

    def back_two(r0):
        at = pl.ds(r0, 16)
        g = row_total(rs_r, at)
        gres[at, :] = g
        ss_s[2, at, :] = lanes(jnp.sum(g * g2[...] * resid[at, :], axis=1, keepdims=True))

    rows_loop(B, 16, back_two)
    links.sent(*sent)
    col_total(2)

    def inner_of(place, at):
        return (ss_s[place, at, :] + ss_r[place, at, :])[:, :1]

    def branch(i, gain):
        at = pl.ds(pl.multiple_of(i * 16, 16), 16)
        g = gres[at, :]
        x = resid[at, :]
        s = scale_of(1, at)
        y = cot[at, :].astype(F32) + s * g2[...] * g - x * (s * s * s) * inner_of(2, at) / width
        gres[at, :] = y
        xall[row, at, :] = y.astype(BF)
        return gain + jnp.sum(g * x * s, axis=0, keepdims=True)

    gain_two = lax.fori_loop(0, B // 16, branch, jnp.zeros((1, Dl), F32))
    relay, second_in, third_in, all_sent = gather(xall)

    def down_partial(blk, put):
        for n0 in range(0, Dl, Dl // 2):
            n = slice(n0, n0 + Dl // 2)
            put(n0, nn(act[0, blk], w_dn_v[0, :, n]) + nn(act[1, blk], w_dn_v[1, :, n]))

    def put_to(ref):
        def put(n0, value):
            ref[:, n0 : n0 + value.shape[1]] = value.astype(ref.dtype)

        return put

    down_partial(row_d, put_to(rt_s.at[0]))
    down_partial(row_a, put_to(rt_s.at[1]))

    def gated_other(blk):
        gg_s[blk] = nt(xall[blk], w_out_v[other]).astype(BF)
        c = links.send(gg_s.at[blk], gg_r.at[blk], to_col)
        gg_o[blk] = nt(xall[blk], w_out_v[col])
        return c

    sent = [gated_other(row)]
    relay()
    down_partial(row_b, put_to(acc_b))
    down_partial(row, put_to(down_o))
    sent.append(gated_other(row_a))
    second_in()
    sent.append(gated_other(row_b))
    third_in()
    sent.append(gated_other(row_d))
    down_sent = [
        links.send(rt_s.at[0], rt_r.at[0], to_a),
        links.send(rt_s.at[1], rt_r.at[1], to_a),
    ]

    for blk, c in zip((row, row_b, row_a, row_d), sent):
        c.wait_recv()
        base = blk * B

        def conv_grad(r0, blk=blk, base=base):
            at = pl.ds(r0, 32)
            to = pl.ds(pl.multiple_of(base + r0, 32), 32)
            g = gg_o[blk, at, :] + gg_r[blk, at, :].astype(F32)
            gext[to, :] = g * proj_o[1, to, :]
            gp[col, blk, 1, at, :] = (g * cout[to, :]).astype(BF)

        rows_loop(B, 32, conv_grad)

    ahead = links.slot()

    @pl.when(dp > 0)
    def _():
        links.copy(gext.at[pl.ds(0, 8), :], halo_a, {"dp": lax.rem(dp + n_dp - 1, n_dp)}, ahead).start()

    @pl.when(dp < n_dp - 1)
    def _():
        links.copy(gext.at[pl.ds(0, 8), :], halo_a, {"dp": lax.rem(dp + n_dp - 1, n_dp)}, ahead).wait_recv()
        gext[T : T + 8, :] = halo_a[...]

    @pl.when(dp == n_dp - 1)
    def _():
        gext[T : T + 8, :] = jnp.zeros((8, Uc), F32)

    terms = [jnp.zeros((1, Uc), F32) for _ in range(3)]
    for i in range(T // CH):
        at = pl.ds(i * CH, CH)
        more = pl.ds(i * CH, CH + 8)
        x = mext[more, :]
        g = gext[more, :]
        m1, m2 = mask_of(mask1, more), mask_of(mask2, more)
        now = g[:CH]
        terms[0] = terms[0] + jnp.sum(now * x[8 : 8 + CH], axis=0, keepdims=True)
        terms[1] = terms[1] + jnp.sum(m1[:CH] * now * x[7 : 7 + CH], axis=0, keepdims=True)
        terms[2] = terms[2] + jnp.sum(m2[:CH] * now * x[6 : 6 + CH], axis=0, keepdims=True)
        y = cw[0:1, :] * now
        y = y + cw[1:2, :] * (m1 * g)[1 : 1 + CH]
        y = y + cw[2:3, :] * (m2 * g)[2 : 2 + CH]
        blk, to = i * CH // B, slice(i * CH % B, i * CH % B + CH)
        gp[col, blk, 0, to, :] = (y * proj_o[2, at, :]).astype(BF)
        gp[col, blk, 2, to, :] = (y * proj_o[0, at, :]).astype(BF)
    red_s[...] = jnp.zeros_like(red_s)
    for k in range(3):
        red_s[2 + k : 3 + k, :Uc] = terms[k]
    gp_in = links.send(gp.at[col], gp.at[col], to_col)
    if split_in:
        gp_units = Units(gp, gpz)
        for i in range(R):
            gp_units.start(i, i)
    down_sent[0].wait_recv()

    def down_combine(r0):
        at = pl.ds(r0, 16)
        rt_s[2, at, :] = (acc_b[at, :] + rt_r[0, at, :].astype(F32)).astype(BF)

    rows_loop(B, 16, down_combine)
    down_sent.append(links.send(rt_s.at[2], rt_r.at[2], to_b))

    po_all = []
    for z in range(n_dp):
        rows = po_s.shape[1]
        at = pl.ds(z % half * rows, rows)
        g = lax.dot_general(
            gat[z // half, :, :, at].reshape(T, rows), xall[...].reshape(T, Dl),
            (((0,), (0,)), ((), ())), preferred_element_type=F32,
        )
        po_s[z] = g.astype(BF)
    for k in range(1, n_dp):
        po_all.append(links.send(po_s.at[peers[k]], po_r.at[dp], {"dp": peers[k]}))
    gp_in.wait_recv()
    if split_in:
        kept.append(gp_units.keep())
    else:
        kept.append(local(gp, gpz))

    def in_partial(blk, put):
        for n0 in range(0, Dl, Dl // 4):
            n = slice(n0, n0 + Dl // 4)
            total = None
            for c in range(2):
                for k in range(3):
                    part = nt(gp[c, blk, k], w_in_v[c, k, n, :])
                    total = part if total is None else total + part
            put(n0, total)

    sent_in = row_sum(rs_s, rs_r, in_partial)
    n2_line.plane(*range(1, n_dp))

    def back_one(r0):
        at = pl.ds(r0, 16)
        g = row_total(rs_r, at)
        d_tok[at, :] = g
        ss_s[3, at, :] = lanes(
            jnp.sum(g * g1[...] * tok[at, :].astype(F32), axis=1, keepdims=True)
        )

    rows_loop(B, 16, back_one)
    col_total(3)

    def token_grad(i, gain):
        at = pl.ds(pl.multiple_of(i * 16, 16), 16)
        g = d_tok[at, :]
        x = tok[at, :].astype(F32)
        s = scale_of(0, at)
        y = gres[at, :] + s * g1[...] * g - x * (s * s * s) * inner_of(3, at) / width
        d_tok[at, :] = y
        return gain + jnp.sum(g * x * s, axis=0, keepdims=True)

    gain_one = lax.fori_loop(0, B // 16, token_grad, jnp.zeros((1, Dl), F32))

    red_s[0:1, :] = gain_one
    red_s[1:2, :] = gain_two
    c0 = links.send(red_s, red_r.at[0], to_a)
    for c in down_sent[1:]:
        c.wait_recv()

    def block_rows(r0):
        at = pl.ds(r0, 16)
        total = down_o[at, :] + rt_r[1, at, :].astype(F32) + rt_r[2, at, :].astype(F32)
        block_out[at, :] = (resid[at, :] + total).astype(BF)

    rows_loop(B, 16, block_rows)
    c0.wait_recv()
    links.sent(c0)
    red_s[0:2, :] = red_s[0:2, :] + red_r[0, 0:2, :]
    c1 = links.send(red_s, red_r.at[1], to_b)
    c1.wait_recv()
    red_z[dp] = red_s[...]
    red_z[dp, 0:2, :] = red_s[0:2, :] + red_r[1, 0:2, :]
    arrived = []
    for k in range(1, n_dp):
        arrived.append(links.send(red_z.at[dp], red_z.at[dp], {"dp": lax.rem(dp + k, n_dp)}))
    for c in arrived:
        c.wait_recv()
    total = red_z[0]
    for k in range(1, n_dp):
        total = total + red_z[k]
    d_gain[...] = total
    d_conv[...] = total[:, :Uc]

    @pl.when(dp < n_dp - 1)
    def _():
        links.copy(mext.at[pl.ds(T, 8), :], halo_b, {"dp": lax.rem(dp + 1, n_dp)}, behind).wait_send()

    @pl.when(dp > 0)
    def _():
        links.copy(gext.at[pl.ds(0, 8), :], halo_a, {"dp": lax.rem(dp + n_dp - 1, n_dp)}, ahead).wait_send()

    n1_line.plane(*range(1, n_dp))
    cot_line.plane(*range(3, n_dp))
    n2_line.relay(*range(1, n_dp))
    act_units.hand_on()
    gh_units.hand_on()
    n1_line.relay(*range(1, n_dp))
    cot_line.relay(*range(3, n_dp))
    for c in po_all:
        c.wait_recv()
    out_total = po_s[dp].astype(F32)
    for k in range(1, n_dp):
        out_total = out_total + po_r[peers[k]].astype(F32)
    d_out[...] = out_total
    units = [act_units, gh_units]
    if split_in:
        gp_units.hand_on()
        units.append(gp_units)
    for line in (cot_line, n1_line, n2_line):
        line.finish()
    for unit in units:
        unit.finish()
        unit.close()
    for hop in range(1, n_dp):
        cot_line.sent(hop)
        if hop > 1:
            n1_line.sent(hop)
            n2_line.sent(hop)
    for c in [cot_out, *kept]:
        c.wait()
    assert links.count <= send_sems.shape[0]
    links.close()


def run_block(n_dp, width, split_in, tok, g1, w_in, cw, w_out, g2, w_gu, w_dn, cot, mask1, mask2):
    B, Dl = tok.shape
    R = 4
    T = R * B
    Uc = w_out.shape[0] // 2
    Fc = w_dn.shape[0] // 2
    vm = lambda shape, kind=BF: pltpu.VMEM(shape, kind)
    any_spec, vmem_spec = pl.BlockSpec(memory_space=pl.ANY), pl.BlockSpec(memory_space=pltpu.VMEM)
    shape = jax.ShapeDtypeStruct
    rows = shape((n_dp, R, B, Dl), BF)
    return pl.pallas_call(
        functools.partial(block_kernel, n_dp, width, split_in),
        out_shape=(
            shape((B, Dl), BF),
            shape((B, Dl), F32),
            shape((8, Dl), F32),
            shape((8, Uc), F32),
            shape((2 * Uc // n_dp, Dl), F32),
            rows,
            rows,
            rows,
            shape((n_dp, R, B, 2 * Fc // n_dp), BF),
            shape((n_dp, R, 2, B, 2 * Fc // n_dp), BF),
            shape((n_dp, R, 3, B, 2 * Uc // n_dp) if split_in else (2, R, 3, B, Uc), BF),
        ),
        in_specs=[
            vmem_spec, vmem_spec, any_spec, vmem_spec, any_spec, vmem_spec,
            any_spec, any_spec, vmem_spec, vmem_spec, vmem_spec,
        ],
        out_specs=[vmem_spec] * 5 + [any_spec] * 6,
        scratch_shapes=[
            vm((2, 3, Dl, Uc)), vm((2, Uc, Dl)), vm((2, 2, Dl, Fc)), vm((2, Fc, Dl)),
            vm((R, B, Dl)), vm((R, B, Dl)),
            vm((2, R, B, Uc)), vm((2, R, B, Fc)), vm((2, R, 2, B, Fc)), vm((2, R, 3, B, Uc)),
            vm((3, T, Uc), F32), vm((R, 3, B, Uc)), vm((T + 8, Uc), F32), vm((8, Uc), F32),
            vm((T, Uc), F32), vm((T + 8, Uc), F32), vm((8, Uc), F32),
            vm((R, B, Uc)), vm((R, B, Uc)), vm((R, B, Uc), F32),
            vm((2, B, Fc), F32), vm((R, 2, B, Fc)), vm((R, B, Fc), F32), vm((R, B, Fc)),
            vm((3, B, Dl)), vm((3, B, Dl)), vm((3, B, Dl)), vm((3, B, Dl)),
            vm((B, Dl), F32), vm((B, Dl), F32), vm((B, Dl), F32),
            vm((B, Dl), F32), vm((B, Dl), F32),
            vm((4, B, 128), F32), vm((4, B, 128), F32),
            vm((8, Dl), F32), vm((2, 8, Dl), F32), vm((n_dp, 8, Dl), F32),
            vm((n_dp, 2 * Uc // n_dp, Dl)), vm((n_dp, 2 * Uc // n_dp, Dl)),
            pltpu.SemaphoreType.DMA((80 + 48 * n_dp,)), pltpu.SemaphoreType.DMA((80 + 48 * n_dp,)),
            pltpu.SemaphoreType.DMA((40,)),
        ],
        compiler_params=pltpu.CompilerParams(
            collective_id=0, has_side_effects=True, vmem_limit_bytes=VMEM_LIMIT
        ),
        name="block",
    )(tok, g1, w_in, cw, w_out, g2, w_gu, w_dn, cot, mask1, mask2)


def sequence_offsets(lengths, index):
    ends = jnp.cumsum(lengths)
    starts = ends - lengths
    reached = starts[None, :] <= index[:, None]
    return index - jnp.max(jnp.where(reached, starts[None, :], 0), axis=1)


def on_device(
    tokens, gain_one, in_weight, conv_weight, out_weight, gain_two, gate_up_weight, down_weight,
    cotangent, lengths,
):
    n_dp = lax.axis_size("dp")
    B, Dl = tokens.shape
    T = B * lax.axis_size("row")
    width = Dl * lax.axis_size("col")
    index = lax.axis_index("dp") * T + jnp.arange(T + 16, dtype=jnp.int32)
    offset = sequence_offsets(lengths, index)
    masks = [
        jnp.broadcast_to((offset >= lag).astype(F32)[:, None], (T + 16, 128)) for lag in (1, 2)
    ]
    conv = jnp.pad(conv_weight.astype(F32), ((0, 5), (0, 0)))
    chunk = in_weight.shape[2] // n_dp
    split_in = chunk % 128 == 0
    block_out, d_tok, d_gain, d_conv, d_out, n1, n2, cot, act, gh, gp = run_block(
        n_dp,
        float(width),
        split_in,
        tokens,
        gain_one.astype(F32)[None, :],
        jnp.transpose(in_weight, (1, 0, 2)),
        conv,
        out_weight,
        gain_two.astype(F32)[None, :],
        jnp.transpose(gate_up_weight, (1, 0, 2)),
        down_weight,
        cotangent,
        *masks,
    )

    dot = functools.partial(jnp.einsum, preferred_element_type=F32)
    d_down = dot("zrtf,zrti->fi", act, cot)
    d_gu = dot("zrti,zrktf->ikf", n2, gh)
    if split_in:
        d_in = dot("zrti,zrktu->iku", n1, gp)
    else:
        mine = lax.dynamic_index_in_dim(n1, lax.axis_index("dp"), 0, keepdims=False)
        d_in = lax.psum_scatter(
            dot("rti,crktu->ikcu", mine, gp).reshape(Dl, 3, -1).astype(BF),
            "dp",
            scatter_dimension=2,
            tiled=True,
        ).astype(F32)
    part = d_conv.shape[1] * 1 // n_dp
    mine = lax.dynamic_slice(d_conv, (2, lax.axis_index("dp") * part), (3, part))
    return (
        block_out,
        d_tok,
        d_gain[0],
        d_in.reshape(Dl, 3, 1, 1, -1),
        mine.reshape(3, 1, 1, part),
        d_out.reshape(1, 1, -1, Dl),
        d_gain[1],
        d_gu.reshape(Dl, 2, 1, 1, -1),
        d_down.reshape(1, 1, -1, Dl),
    )


def solution(mesh):
    placed = (
        P(("dp", "row"), "col"),
        P("col"),
        P("col", None, "row"),
        P(None, ("row", "col")),
        P("row", "col"),
        P("col"),
        P("col", None, "row"),
        P("row", "col"),
        P(("dp", "row"), "col"),
        P(),
    )
    return jax.shard_map(
        on_device,
        mesh=mesh,
        in_specs=placed,
        out_specs=(
            P(("dp", "row"), "col"),
            P(("dp", "row"), "col"),
            P("col"),
            P("col", None, "row", "dp", None),
            P(None, ("row", "col"), "dp", None),
            P("row", "dp", None, "col"),
            P("col"),
            P("col", None, "row", "dp", None),
            P("row", "dp", None, "col"),
        ),
        check_vma=False,
    )
```

```python
import functools

import jax
import jax.numpy as jnp
from jax import lax
from jax.experimental import pallas as pl
from jax.experimental.pallas import tpu as pltpu
from jax.sharding import PartitionSpec as P

MESH = pl.DeviceIdType.MESH
BF = jnp.bfloat16
F32 = jnp.float32
EPS = 1e-05
VMEM_LIMIT = 63 * 2**20


def nn(a, b):
    return lax.dot_general(a, b, (((1,), (0,)), ((), ())), preferred_element_type=F32)


def nt(a, b):
    return lax.dot_general(a, b, (((1,), (1,)), ((), ())), preferred_element_type=F32)


class Links:
    def __init__(self, send_sems, recv_sems):
        self.send_sems, self.recv_sems = send_sems, recv_sems
        self.count = 0
        self.open = []

    def slot(self):
        self.count += 1
        return self.count - 1

    def copy(self, src, dst, to, slot=None):
        if slot is None:
            slot = self.slot()
        return pltpu.make_async_remote_copy(
            src_ref=src,
            dst_ref=dst,
            send_sem=self.send_sems.at[slot],
            recv_sem=self.recv_sems.at[slot],
            device_id=to,
            device_id_type=MESH,
        )

    def send(self, src, dst, to):
        c = self.copy(src, dst, to)
        c.start()
        self.open.append(c)
        return c

    def sent(self, *copies):
        for c in copies:
            c.wait_send()
            self.open = [o for o in self.open if o is not c]

    def close(self):
        for c in self.open:
            c.wait_send()
        self.open = []


def rows_loop(count, step, body):
    def one(i, carry):
        body(pl.multiple_of(i * step, step))
        return carry

    lax.fori_loop(0, count // step, one, 0)


def block_kernel(n_dp, width, split_in, *refs):
    (
        tok, g1, w_in, cw, w_out, g2, w_gu, w_dn, cot, mask1, mask2,
        block_out, d_tok, d_gain, d_conv, d_out, n1z, n2z, cotz, actz, ghz, gpz,
        w_in_v, w_out_v, w_gu_v, w_dn_v,
        xall, call, gat, act, gh, gp,
        proj_o, proj_r, mext, halo_b, cout, gext, halo_a, gg_s, gg_r, gg_o,
        hid_o, hid_r, ga_o, ga_r,
        rs_s, rs_r, rt_s, rt_r, acc_b, acc_o, down_o,
        resid, gres, ss_s, ss_r, red_s, red_r, red_z, po_s, po_r,
        send_sems, recv_sems, local_sems,
    ) = refs
    R, B, Dl = xall.shape
    Uc = w_out_v.shape[1]
    Fc = w_dn_v.shape[1]
    T = R * B
    dp, row, col = lax.axis_index("dp"), lax.axis_index("row"), lax.axis_index("col")
    other = 1 - col
    low = row + 1 - 2 * lax.rem(row, 2)
    high = row + 2 - 4 * lax.rem(row // 2, 2)
    row_a = low * other + high * col
    row_b = high * other + low * col
    row_d = low + high - row
    to_a, to_b, to_col = {"row": row_a}, {"row": row_b}, {"col": other}
    links = Links(send_sems, recv_sems)
    half = n_dp // 2
    holder = dp // half
    peers = [lax.rem(dp + k, n_dp) for k in range(n_dp)]
    sources = [lax.rem(dp + n_dp - k, n_dp) for k in range(n_dp)]

    loads = {"in": [], "out": [], "gu": [], "dn": []}
    n_local = 0

    def local(src, dst):
        nonlocal n_local
        c = pltpu.make_async_copy(src, dst, local_sems.at[n_local])
        n_local += 1
        c.start()
        return c

    for c in range(2):
        for k in range(3):
            loads["in"].append(local(w_in.at[k, :, pl.ds(c * Uc, Uc)], w_in_v.at[c, k]))
    for c in range(2):
        loads["dn"].append(local(w_dn.at[pl.ds(c * Fc, Fc), :], w_dn_v.at[c]))
        loads["out"].append(local(w_out.at[pl.ds(c * Uc, Uc), :], w_out_v.at[c]))
    for c in range(2):
        for k in range(2):
            loads["gu"].append(local(w_gu.at[k, :, pl.ds(c * Fc, Fc)], w_gu_v.at[c, k]))

    def loaded(name):
        for c in loads[name]:
            c.wait()

    barrier = pltpu.get_barrier_semaphore()
    for to in (to_col, {"row": low}, {"row": high}):
        pl.semaphore_signal(barrier, inc=1, device_id=to, device_id_type=MESH)
    for k in range(1, n_dp):
        pl.semaphore_signal(
            barrier, inc=1, device_id={"dp": lax.rem(dp + k, n_dp)}, device_id_type=MESH
        )

    def col_total(place):
        c = links.send(ss_s.at[place], ss_r.at[place], to_col)
        c.wait_recv()

    def gather(buf):
        first = links.send(buf.at[row], buf.at[row], to_a)
        second = links.send(buf.at[row], buf.at[row], to_b)
        state = {}

        def relay():
            first.wait_recv()
            state["third"] = links.send(buf.at[row_a], buf.at[row_a], to_b)

        def second_in():
            second.wait_recv()

        def third_in():
            state["third"].wait_recv()

        def all_sent():
            links.sent(first, second, state["third"])

        return relay, second_in, third_in, all_sent

    class Line:
        def __init__(self, first, dst, whole=False):
            self.first, self.dst, self.whole = first, dst, whole
            self.up = [links.slot() for _ in range(n_dp + 1)]
            self.down = [links.slot() for _ in range(n_dp + 1)]
            self.sent_to, self.last = {}, []

        def at(self, z):
            return self.dst.at[z] if self.whole else self.dst.at[z, row]

        def up_copy(self, hop):
            at = self.at(lax.rem(dp + n_dp - (hop - 1), n_dp))
            src = self.first if hop == 1 else at
            return links.copy(src, at, {"dp": peers[1]}, self.up[hop])

        def down_copy(self, hop):
            at = self.at(lax.rem(dp + hop - 1, n_dp))
            src = self.first if hop == 1 else at
            return links.copy(src, at, {"dp": sources[1]}, self.down[hop])

        def arrived(self, hop):
            @pl.when(dp >= hop)
            def _():
                self.up_copy(hop).wait_recv()

            @pl.when(dp + hop < n_dp)
            def _():
                self.down_copy(hop).wait_recv()

        def start(self, hop):
            if hop > 1:
                self.arrived(hop - 1)

            @pl.when((dp + 1 < n_dp) & (dp >= hop - 1))
            def _():
                self.up_copy(hop).start()

            @pl.when((dp >= 1) & (dp + hop - 1 < n_dp))
            def _():
                self.down_copy(hop).start()

        def sent(self, hop):
            @pl.when((dp + 1 < n_dp) & (dp >= hop - 1))
            def _():
                self.up_copy(hop).wait_send()

            @pl.when((dp >= 1) & (dp + hop - 1 < n_dp))
            def _():
                self.down_copy(hop).wait_send()

        def rest(self):
            for hop in range(4, n_dp):
                self.start(hop)
            self.arrived(n_dp - 1)

        def plane(self, *ks):
            if not self.sent_to:
                self.rest()
            for k in ks:
                at = self.dst.at[peers[k], row]
                self.sent_to[k] = (links.send(at, at, to_a), links.send(at, at, to_b))

        def relay(self, *ks):
            for k in ks:
                first, second = self.sent_to[k]
                first.wait_recv()
                at = self.dst.at[peers[k], row_a]
                self.last.append(second)
                self.last.append(links.send(at, at, to_b))

        def finish(self):
            for c in self.last:
                c.wait_recv()

    class Units:
        def __init__(self, src, dst):
            self.src, self.dst = src, dst
            self.size = dst.shape[-1]
            self.slots = [[links.slot() for _ in range(n_dp)] for _ in range(R)]
            self.handed = [links.slot() for _ in range(n_dp)]

        def chunk(self, z, blk):
            at = pl.ds(pl.multiple_of(lax.rem(z, half) * self.size, self.size), self.size)
            return self.src.at[(z // half, blk, *([slice(None)] * (len(self.src.shape) - 3)), at)]

        def across(self, k, i, blk):
            to = self.dst.at[dp, blk]
            return links.copy(self.chunk(peers[k], blk), to, {"dp": peers[k]}, self.slots[i][k])

        def start(self, i, blk):
            for k in range(1, n_dp):

                @pl.when(peers[k] // half == col)
                def _(k=k):
                    self.across(k, i, blk).start()

        def keep(self):
            return local(self.chunk(dp, slice(None)), self.dst.at[dp])

        def hand_on(self):
            for k in range(1, n_dp):

                @pl.when(holder == col)
                def _(k=k):
                    for i in range(R):
                        self.across(k, i, 0).wait_recv()
                    self.hand(k).start()

        def hand(self, k):
            at = self.dst.at[sources[k]]
            return links.copy(at, at, to_col, self.handed[k])

        def finish(self):
            for k in range(1, n_dp):

                @pl.when(holder != col)
                def _(k=k):
                    self.hand(k).wait_recv()

        def close(self):
            for k in range(1, n_dp):

                @pl.when(peers[k] // half == col)
                def _(k=k):
                    for i in range(R):
                        self.across(k, i, 0).wait_send()

                @pl.when(holder == col)
                def _(k=k):
                    self.hand(k).wait_send()

    def row_sum(sends, recvs, partial, filler=None):
        def to_bf(slot):
            def put(n0, value):
                sends[slot, :, n0 : n0 + value.shape[1]] = value.astype(BF)

            return put

        def to_f32(acc):
            def put(n0, value):
                acc[:, n0 : n0 + value.shape[1]] = value

            return put

        partial(row_d, to_bf(0))
        c0 = links.send(sends.at[0], recvs.at[0], to_a)
        partial(row_a, to_bf(1))
        c1 = links.send(sends.at[1], recvs.at[1], to_a)
        partial(row_b, to_f32(acc_b))
        c0.wait_recv()

        def combine(r0):
            at = pl.ds(r0, 16)
            sends[2, at, :] = (acc_b[at, :] + recvs[0, at, :].astype(F32)).astype(BF)

        rows_loop(B, 16, combine)
        c2 = links.send(sends.at[2], recvs.at[2], to_b)
        partial(row, to_f32(acc_o))
        if filler is not None:
            filler()
        c1.wait_recv()
        c2.wait_recv()
        return c0, c1, c2

    def row_total(recvs, at):
        return acc_o[at, :] + recvs[1, at, :].astype(F32) + recvs[2, at, :].astype(F32)

    def lanes(x):
        return jnp.broadcast_to(x, (x.shape[0], 128))

    def squares(r0):
        at = pl.ds(r0, 16)
        x = tok[at, :].astype(F32)
        ss_s[0, at, :] = lanes(jnp.sum(x * x, axis=1, keepdims=True))

    rows_loop(B, 16, squares)
    pl.semaphore_wait(barrier, 3 + n_dp - 1)
    cot_line = Line(call, cotz, whole=True)
    n1_line = Line(xall.at[row], n1z)
    n2_line = Line(xall.at[row], n2z)
    col_total(0)

    def scale_of(place, at):
        return lax.rsqrt((ss_s[place, at, :] + ss_r[place, at, :]) / width + EPS)[:, :1]

    def normed_one(r0):
        at = pl.ds(r0, 16)
        x = tok[at, :].astype(F32)
        xall[row, at, :] = (x * scale_of(0, at) * g1[...]).astype(BF)

    rows_loop(B, 16, normed_one)
    relay, second_in, third_in, all_sent = gather(xall)
    n1_line.start(1)

    def project(blk):
        x = xall[blk]
        for k in range(3):
            gp[col, blk, k] = nn(x, w_in_v[other, k]).astype(BF)
        c = links.send(gp.at[col, blk], proj_r.at[blk], to_col)
        for k in range(3):
            proj_o[k, pl.ds(pl.multiple_of(blk * B, B), B), :] = nn(x, w_in_v[col, k])
        return c

    loaded("in")
    sent = [project(row)]
    relay()
    sent.append(project(row_a))
    second_in()
    sent.append(project(row_b))
    third_in()
    call[row] = cot[...]
    cot_relay, cot_second, cot_third, cot_all_sent = gather(call)
    sent.append(project(row_d))
    n1_out = local(xall, n1z.at[dp])
    n1_line.start(2)

    for blk, c in zip((row, row_b, row_a, row_d), sent):
        c.wait_recv()
        base = blk * B

        def add(r0, blk=blk, base=base):
            at = pl.ds(r0, 32)
            to = pl.ds(pl.multiple_of(base + r0, 32), 32)
            g = [proj_o[k, to, :] + proj_r[blk, k, at, :].astype(F32) for k in range(3)]
            for k in range(3):
                proj_o[k, to, :] = g[k]
            mext[pl.ds(pl.multiple_of(base + r0 + 8, 8), 32), :] = g[0] * g[2]

        rows_loop(B, 32, add)
    links.sent(*sent)

    behind = links.slot()

    @pl.when(dp < n_dp - 1)
    def _():
        links.copy(mext.at[pl.ds(T, 8), :], halo_b, {"dp": lax.rem(dp + 1, n_dp)}, behind).start()

    @pl.when(dp > 0)
    def _():
        links.copy(mext.at[pl.ds(T, 8), :], halo_b, {"dp": lax.rem(dp + 1, n_dp)}, behind).wait_recv()
        mext[0:8, :] = halo_b[...]

    @pl.when(dp == 0)
    def _():
        mext[0:8, :] = jnp.zeros((8, Uc), F32)

    cot_relay()
    n1_line.start(3)
    CH = B // 2

    def mask_of(mask, at):
        return jnp.concatenate([mask[at, :]] * (Uc // 128), axis=1)

    for i in range(T // CH):
        at = pl.ds(i * CH, CH)
        x = mext[pl.ds(i * CH, CH + 8), :]
        y = cw[0:1, :] * x[8 : 8 + CH]
        y = y + cw[1:2, :] * mask_of(mask1, at) * x[7 : 7 + CH]
        y = y + cw[2:3, :] * mask_of(mask2, at) * x[6 : 6 + CH]
        cout[at, :] = y
        gat[col, i * CH // B, i * CH % B : i * CH % B + CH, :] = (proj_o[1, at, :] * y).astype(BF)
    gated_in = links.send(gat.at[col], gat.at[col], to_col)
    gated_in.wait_recv()

    loaded("out")
    n1_out.wait()
    n1_line.sent(1)
    all_sent()

    def out_partial(blk, put):
        for n0 in range(0, Dl, Dl // 2):
            n = slice(n0, n0 + Dl // 2)
            put(n0, nn(gat[0, blk], w_out_v[0, :, n]) + nn(gat[1, blk], w_out_v[1, :, n]))

    sent = row_sum(rs_s, rs_r, out_partial)

    def residual(r0):
        at = pl.ds(r0, 16)
        x = tok[at, :].astype(F32) + row_total(rs_r, at)
        resid[at, :] = x
        ss_s[1, at, :] = lanes(jnp.sum(x * x, axis=1, keepdims=True))

    cot_second()
    cot_third()
    cot_line.start(1)
    rows_loop(B, 16, residual)
    links.sent(*sent)
    col_total(1)

    def normed_two(r0):
        at = pl.ds(r0, 16)
        xall[row, at, :] = (resid[at, :] * scale_of(1, at) * g2[...]).astype(BF)

    rows_loop(B, 16, normed_two)
    relay, second_in, third_in, all_sent = gather(xall)
    n2_line.start(1)

    loaded("dn")
    ga_sent = []
    for blk in (row, row_a, row_b, row_d):
        x = call[blk]
        for n0 in range(0, Fc, Fc // 2):
            n = slice(n0, n0 + Fc // 2)
            act[col, blk, :, n] = nt(x, w_dn_v[other, n, :]).astype(BF)
        ga_sent.append(links.send(act.at[col, blk], ga_r.at[blk], to_col))
    relay()
    for blk in (row, row_a, row_b, row_d):
        x = call[blk]
        for n0 in range(0, Fc, Fc // 2):
            n = slice(n0, n0 + Fc // 2)
            ga_o[blk, :, n] = nt(x, w_dn_v[col, n, :])
    cot_out = local(call, cotz.at[dp])

    def hidden_other(blk):
        def one(k, carry):
            for n0 in range(0, Fc, Fc // 2):
                n = slice(n0, n0 + Fc // 2)
                gh[col, blk, k, :, n] = nn(xall[blk], w_gu_v[other, k, :, n]).astype(BF)
            return carry

        lax.fori_loop(0, 2, one, 0)
        return links.send(gh.at[col, blk], hid_r.at[blk], to_col)

    loaded("gu")
    hid_sent = [hidden_other(row), hidden_other(row_a)]
    second_in()
    hid_sent.append(hidden_other(row_b))
    third_in()
    hid_sent.append(hidden_other(row_d))
    n2_out = local(xall, n2z.at[dp])
    n1_line.plane(1, 2)
    n2_line.start(2)

    gh_in = {}
    for name, blk in (("d", row_d), ("a", row_a), ("b", row_b), ("o", row)):

        def one(k, carry, blk=blk):
            for n0 in range(0, Fc, Fc // 2):
                n = slice(n0, n0 + Fc // 2)
                hid_o[k, :, n] = nn(xall[blk], w_gu_v[col, k, :, n])
            return carry

        lax.fori_loop(0, 2, one, 0)
        which = {"o": 0, "a": 1, "b": 2, "d": 3}[name]
        theirs = {"o": 0, "a": 2, "b": 1, "d": 3}[name]
        hid_sent[theirs].wait_recv()
        ga_sent[theirs].wait_recv()
        links.sent(hid_sent[which], ga_sent[which])

        def activate(r0, blk=blk):
            at = pl.ds(r0, 16)
            for n0 in range(0, Fc, Fc // 2):
                n = slice(n0, n0 + Fc // 2)
                gate = hid_o[0, at, n] + hid_r[blk, 0, at, n].astype(F32)
                up = hid_o[1, at, n] + hid_r[blk, 1, at, n].astype(F32)
                ga = ga_o[blk, at, n] + ga_r[blk, at, n].astype(F32)
                s = jax.nn.sigmoid(gate)
                silu = gate * s
                act[col, blk, at, n] = (silu * up).astype(BF)
                gh[col, blk, 0, at, n] = (ga * up * s * (1.0 + gate * (1.0 - s))).astype(BF)
                gh[col, blk, 1, at, n] = (ga * silu).astype(BF)

        rows_loop(B, 16, activate)
        gh_in[name] = (
            links.send(gh.at[col, blk], gh.at[col, blk], to_col),
            links.send(act.at[col, blk], act.at[col, blk], to_col),
        )
    n1_line.relay(1, 2)
    n2_line.start(3)
    cot_line.start(2)
    for pair in gh_in.values():
        for c in pair:
            c.wait_recv()
    size = actz.shape[-1]
    mine = pl.ds(pl.multiple_of(lax.rem(dp, half) * size, size), size)
    kept_units = [
        local(act.at[holder, :, :, mine], actz.at[dp]),
        local(gh.at[holder, :, :, :, mine], ghz.at[dp]),
    ]
    kept = []
    n2_out.wait()
    n2_line.sent(1)
    all_sent()

    def gu_partial(blk, put):
        for n0 in range(0, Dl, Dl // 4):
            n = slice(n0, n0 + Dl // 4)
            total = None
            for c in range(2):
                for k in range(2):
                    part = nt(gh[c, blk, k], w_gu_v[c, k, n, :])
                    total = part if total is None else total + part
            put(n0, total)

    sent = row_sum(rs_s, rs_r, gu_partial)

    def back_two(r0):
        at = pl.ds(r0, 16)
        g = row_total(rs_r, at)
        gres[at, :] = g
        ss_s[2, at, :] = lanes(jnp.sum(g * g2[...] * resid[at, :], axis=1, keepdims=True))

    rows_loop(B, 16, back_two)
    links.sent(*sent)
    col_total(2)

    def inner_of(place, at):
        return (ss_s[place, at, :] + ss_r[place, at, :])[:, :1]

    def branch(i, gain):
        at = pl.ds(pl.multiple_of(i * 16, 16), 16)
        g = gres[at, :]
        x = resid[at, :]
        s = scale_of(1, at)
        y = cot[at, :].astype(F32) + s * g2[...] * g - x * (s * s * s) * inner_of(2, at) / width
        gres[at, :] = y
        xall[row, at, :] = y.astype(BF)
        return gain + jnp.sum(g * x * s, axis=0, keepdims=True)

    gain_two = lax.fori_loop(0, B // 16, branch, jnp.zeros((1, Dl), F32))
    relay, second_in, third_in, all_sent = gather(xall)

    def down_partial(blk, put):
        for n0 in range(0, Dl, Dl // 2):
            n = slice(n0, n0 + Dl // 2)
            put(n0, nn(act[0, blk], w_dn_v[0, :, n]) + nn(act[1, blk], w_dn_v[1, :, n]))

    def put_to(ref):
        def put(n0, value):
            ref[:, n0 : n0 + value.shape[1]] = value.astype(ref.dtype)

        return put

    down_partial(row_d, put_to(rt_s.at[0]))
    down_partial(row_a, put_to(rt_s.at[1]))

    def gated_other(blk):
        gg_s[blk] = nt(xall[blk], w_out_v[other]).astype(BF)
        c = links.send(gg_s.at[blk], gg_r.at[blk], to_col)
        gg_o[blk] = nt(xall[blk], w_out_v[col])
        return c

    sent = [gated_other(row)]
    relay()
    down_partial(row_b, put_to(acc_b))
    down_partial(row, put_to(down_o))
    sent.append(gated_other(row_a))
    second_in()
    sent.append(gated_other(row_b))
    third_in()
    sent.append(gated_other(row_d))
    down_sent = [
        links.send(rt_s.at[0], rt_r.at[0], to_a),
        links.send(rt_s.at[1], rt_r.at[1], to_a),
    ]

    for blk, c in zip((row, row_b, row_a, row_d), sent):
        c.wait_recv()
        base = blk * B

        def conv_grad(r0, blk=blk, base=base):
            at = pl.ds(r0, 32)
            to = pl.ds(pl.multiple_of(base + r0, 32), 32)
            g = gg_o[blk, at, :] + gg_r[blk, at, :].astype(F32)
            gext[to, :] = g * proj_o[1, to, :]
            gp[col, blk, 1, at, :] = (g * cout[to, :]).astype(BF)

        rows_loop(B, 32, conv_grad)

    ahead = links.slot()

    @pl.when(dp > 0)
    def _():
        links.copy(gext.at[pl.ds(0, 8), :], halo_a, {"dp": lax.rem(dp + n_dp - 1, n_dp)}, ahead).start()

    @pl.when(dp < n_dp - 1)
    def _():
        links.copy(gext.at[pl.ds(0, 8), :], halo_a, {"dp": lax.rem(dp + n_dp - 1, n_dp)}, ahead).wait_recv()
        gext[T : T + 8, :] = halo_a[...]

    @pl.when(dp == n_dp - 1)
    def _():
        gext[T : T + 8, :] = jnp.zeros((8, Uc), F32)

    terms = [jnp.zeros((1, Uc), F32) for _ in range(3)]
    for i in range(T // CH):
        at = pl.ds(i * CH, CH)
        more = pl.ds(i * CH, CH + 8)
        x = mext[more, :]
        g = gext[more, :]
        m1, m2 = mask_of(mask1, more), mask_of(mask2, more)
        now = g[:CH]
        terms[0] = terms[0] + jnp.sum(now * x[8 : 8 + CH], axis=0, keepdims=True)
        terms[1] = terms[1] + jnp.sum(m1[:CH] * now * x[7 : 7 + CH], axis=0, keepdims=True)
        terms[2] = terms[2] + jnp.sum(m2[:CH] * now * x[6 : 6 + CH], axis=0, keepdims=True)
        y = cw[0:1, :] * now
        y = y + cw[1:2, :] * (m1 * g)[1 : 1 + CH]
        y = y + cw[2:3, :] * (m2 * g)[2 : 2 + CH]
        blk, to = i * CH // B, slice(i * CH % B, i * CH % B + CH)
        gp[col, blk, 0, to, :] = (y * proj_o[2, at, :]).astype(BF)
        gp[col, blk, 2, to, :] = (y * proj_o[0, at, :]).astype(BF)
    red_s[...] = jnp.zeros_like(red_s)
    for k in range(3):
        red_s[2 + k : 3 + k, :Uc] = terms[k]
    gp_in = links.send(gp.at[col], gp.at[col], to_col)
    if split_in:
        gp_units = Units(gp, gpz)
        for i in range(R):
            gp_units.start(i, i)
    cot_line.start(3)
    down_sent[0].wait_recv()

    def down_combine(r0):
        at = pl.ds(r0, 16)
        rt_s[2, at, :] = (acc_b[at, :] + rt_r[0, at, :].astype(F32)).astype(BF)

    rows_loop(B, 16, down_combine)
    down_sent.append(links.send(rt_s.at[2], rt_r.at[2], to_b))

    po_all = []
    for z in range(n_dp):
        rows = po_s.shape[1]
        at = pl.ds(z % half * rows, rows)
        g = lax.dot_general(
            gat[z // half, :, :, at].reshape(T, rows), xall[...].reshape(T, Dl),
            (((0,), (0,)), ((), ())), preferred_element_type=F32,
        )
        po_s[z] = g.astype(BF)
    for k in range(1, n_dp):
        po_all.append(links.send(po_s.at[peers[k]], po_r.at[dp], {"dp": peers[k]}))
    gp_in.wait_recv()
    if split_in:
        kept.append(gp_units.keep())
    else:
        kept.append(local(gp, gpz))

    def in_partial(blk, put):
        for n0 in range(0, Dl, Dl // 4):
            n = slice(n0, n0 + Dl // 4)
            total = None
            for c in range(2):
                for k in range(3):
                    part = nt(gp[c, blk, k], w_in_v[c, k, n, :])
                    total = part if total is None else total + part
            put(n0, total)

    sent_in = row_sum(rs_s, rs_r, in_partial)
    n2_line.plane(*range(1, n_dp))
    n1_line.plane(*range(3, n_dp))

    def back_one(r0):
        at = pl.ds(r0, 16)
        g = row_total(rs_r, at)
        d_tok[at, :] = g
        ss_s[3, at, :] = lanes(
            jnp.sum(g * g1[...] * tok[at, :].astype(F32), axis=1, keepdims=True)
        )

    rows_loop(B, 16, back_one)
    col_total(3)

    def token_grad(i, gain):
        at = pl.ds(pl.multiple_of(i * 16, 16), 16)
        g = d_tok[at, :]
        x = tok[at, :].astype(F32)
        s = scale_of(0, at)
        y = gres[at, :] + s * g1[...] * g - x * (s * s * s) * inner_of(3, at) / width
        d_tok[at, :] = y
        return gain + jnp.sum(g * x * s, axis=0, keepdims=True)

    gain_one = lax.fori_loop(0, B // 16, token_grad, jnp.zeros((1, Dl), F32))

    red_s[0:1, :] = gain_one
    red_s[1:2, :] = gain_two
    c0 = links.send(red_s, red_r.at[0], to_a)
    for c in down_sent[1:]:
        c.wait_recv()

    def block_rows(r0):
        at = pl.ds(r0, 16)
        total = down_o[at, :] + rt_r[1, at, :].astype(F32) + rt_r[2, at, :].astype(F32)
        block_out[at, :] = (resid[at, :] + total).astype(BF)

    rows_loop(B, 16, block_rows)
    c0.wait_recv()
    links.sent(c0)
    red_s[0:2, :] = red_s[0:2, :] + red_r[0, 0:2, :]
    c1 = links.send(red_s, red_r.at[1], to_b)
    c1.wait_recv()
    red_z[dp] = red_s[...]
    red_z[dp, 0:2, :] = red_s[0:2, :] + red_r[1, 0:2, :]
    arrived = []
    for k in range(1, n_dp):
        arrived.append(links.send(red_z.at[dp], red_z.at[dp], {"dp": lax.rem(dp + k, n_dp)}))
    for c in arrived:
        c.wait_recv()
    total = red_z[0]
    for k in range(1, n_dp):
        total = total + red_z[k]
    d_gain[...] = total
    d_conv[...] = total[:, :Uc]

    @pl.when(dp < n_dp - 1)
    def _():
        links.copy(mext.at[pl.ds(T, 8), :], halo_b, {"dp": lax.rem(dp + 1, n_dp)}, behind).wait_send()

    @pl.when(dp > 0)
    def _():
        links.copy(gext.at[pl.ds(0, 8), :], halo_a, {"dp": lax.rem(dp + n_dp - 1, n_dp)}, ahead).wait_send()

    n2_line.relay(*range(1, n_dp))
    n1_line.relay(*range(3, n_dp))
    cot_line.rest()
    n2_line.finish()
    for c in [cot_out, *kept_units]:
        c.wait()
    for pair in gh_in.values():
        links.sent(*pair)
    cot_line.sent(1)
    cot_all_sent()
    all_sent()

    slots = Fc // size

    def place(k, r, rank):
        q = (k - 1) * 2 + r
        lanes_at = slice(q % slots * size, q % slots * size + size)
        return (q // slots, *([slice(None)] * (rank - 2)), lanes_at)

    def again(k):
        z = peers[k]
        loads = [local(n2z.at[z], xall), local(cotz.at[z], call)]
        for c in loads:
            c.wait()
        copies = []
        for core, keep in ((other, False), (col, True)):
            x = xall[pl.ds(core * 2, 2)].reshape(2 * B, Dl)
            for j in range(2):
                h = nn(x, w_gu_v[holder, j, :, mine])
                for r in range(2):
                    if keep:
                        hid_o[j, :, r * size : r * size + size] = h[r * B : r * B + B]
                    else:
                        q, _, _, n = place(k, r, 4)
                        gh[0, q, j, :, n] = h[r * B : r * B + B].astype(BF)
            y = call[pl.ds(core * 2, 2)].reshape(2 * B, Dl)
            g = nt(y, w_dn_v[holder, mine, :])
            for r in range(2):
                if keep:
                    ga_o[r, :, :size] = g[r * B : r * B + B]
                else:
                    q, _, n = place(k, r, 3)
                    act[0, q, :, n] = g[r * B : r * B + B].astype(BF)
            if not keep:
                for r in range(2):
                    h_at, g_at = place(k, r, 4), place(k, r, 3)
                    copies.append(links.send(gh.at[0].at[h_at], hid_r.at[h_at], to_col))
                    copies.append(links.send(act.at[0].at[g_at], ga_r.at[g_at], to_col))
        for c in copies:
            c.wait_recv()
        done = []
        for r in range(2):
            q, _, n = place(k, r, 3)

            def finish(r0, r=r, q=q, n=n):
                at = pl.ds(r0, 16)
                own = slice(r * size, r * size + size)
                gate = hid_o[0, at, own] + hid_r[q, 0, at, n].astype(F32)
                up = hid_o[1, at, own] + hid_r[q, 1, at, n].astype(F32)
                ga = ga_o[r, at, :size] + ga_r[q, at, n].astype(F32)
                s = jax.nn.sigmoid(gate)
                silu = gate * s
                act[1, q, at, n] = (silu * up).astype(BF)
                gh[1, q, 0, at, n] = (ga * up * s * (1.0 + gate * (1.0 - s))).astype(BF)
                gh[1, q, 1, at, n] = (ga * silu).astype(BF)

            rows_loop(B, 16, finish)
            blk = col * 2 + r
            h_src, a_src = gh.at[1].at[place(k, r, 4)], act.at[1].at[place(k, r, 3)]
            done.append(links.send(h_src, ghz.at[z, blk], to_col))
            done.append(links.send(a_src, actz.at[z, blk], to_col))
            kept.append(local(h_src, ghz.at[z, blk]))
            kept.append(local(a_src, actz.at[z, blk]))
        return done

    again_in = []
    for k in range(1, n_dp):
        again_in += again(k)
    for c in again_in:
        c.wait_recv()
    for c in po_all:
        c.wait_recv()
    out_total = po_s[dp].astype(F32)
    for k in range(1, n_dp):
        out_total = out_total + po_r[peers[k]].astype(F32)
    d_out[...] = out_total
    n1_line.finish()
    if split_in:
        gp_units.hand_on()
        gp_units.finish()
        gp_units.close()
    for hop in range(1, n_dp):
        if hop > 1:
            cot_line.sent(hop)
            n1_line.sent(hop)
            n2_line.sent(hop)
    for c in kept:
        c.wait()
    assert links.count <= send_sems.shape[0]
    links.close()


def run_block(n_dp, width, split_in, tok, g1, w_in, cw, w_out, g2, w_gu, w_dn, cot, mask1, mask2):
    B, Dl = tok.shape
    R = 4
    T = R * B
    Uc = w_out.shape[0] // 2
    Fc = w_dn.shape[0] // 2
    vm = lambda shape, kind=BF: pltpu.VMEM(shape, kind)
    any_spec, vmem_spec = pl.BlockSpec(memory_space=pl.ANY), pl.BlockSpec(memory_space=pltpu.VMEM)
    shape = jax.ShapeDtypeStruct
    rows = shape((n_dp, R, B, Dl), BF)
    return pl.pallas_call(
        functools.partial(block_kernel, n_dp, width, split_in),
        out_shape=(
            shape((B, Dl), BF),
            shape((B, Dl), F32),
            shape((8, Dl), F32),
            shape((8, Uc), F32),
            shape((2 * Uc // n_dp, Dl), F32),
            rows,
            rows,
            rows,
            shape((n_dp, R, B, 2 * Fc // n_dp), BF),
            shape((n_dp, R, 2, B, 2 * Fc // n_dp), BF),
            shape((n_dp, R, 3, B, 2 * Uc // n_dp) if split_in else (2, R, 3, B, Uc), BF),
        ),
        in_specs=[
            vmem_spec, vmem_spec, any_spec, vmem_spec, any_spec, vmem_spec,
            any_spec, any_spec, vmem_spec, vmem_spec, vmem_spec,
        ],
        out_specs=[vmem_spec] * 5 + [any_spec] * 6,
        scratch_shapes=[
            vm((2, 3, Dl, Uc)), vm((2, Uc, Dl)), vm((2, 2, Dl, Fc)), vm((2, Fc, Dl)),
            vm((R, B, Dl)), vm((R, B, Dl)),
            vm((2, R, B, Uc)), vm((2, R, B, Fc)), vm((2, R, 2, B, Fc)), vm((2, R, 3, B, Uc)),
            vm((3, T, Uc), F32), vm((R, 3, B, Uc)), vm((T + 8, Uc), F32), vm((8, Uc), F32),
            vm((T, Uc), F32), vm((T + 8, Uc), F32), vm((8, Uc), F32),
            vm((R, B, Uc)), vm((R, B, Uc)), vm((R, B, Uc), F32),
            vm((2, B, Fc), F32), vm((R, 2, B, Fc)), vm((R, B, Fc), F32), vm((R, B, Fc)),
            vm((3, B, Dl)), vm((3, B, Dl)), vm((3, B, Dl)), vm((3, B, Dl)),
            vm((B, Dl), F32), vm((B, Dl), F32), vm((B, Dl), F32),
            vm((B, Dl), F32), vm((B, Dl), F32),
            vm((4, B, 128), F32), vm((4, B, 128), F32),
            vm((8, Dl), F32), vm((2, 8, Dl), F32), vm((n_dp, 8, Dl), F32),
            vm((n_dp, 2 * Uc // n_dp, Dl)), vm((n_dp, 2 * Uc // n_dp, Dl)),
            pltpu.SemaphoreType.DMA((80 + 48 * n_dp,)), pltpu.SemaphoreType.DMA((80 + 48 * n_dp,)),
            pltpu.SemaphoreType.DMA((32 + 6 * n_dp,)),
        ],
        compiler_params=pltpu.CompilerParams(
            collective_id=0, has_side_effects=True, vmem_limit_bytes=VMEM_LIMIT
        ),
        name="block",
    )(tok, g1, w_in, cw, w_out, g2, w_gu, w_dn, cot, mask1, mask2)


def sequence_offsets(lengths, index):
    ends = jnp.cumsum(lengths)
    starts = ends - lengths
    reached = starts[None, :] <= index[:, None]
    return index - jnp.max(jnp.where(reached, starts[None, :], 0), axis=1)


def on_device(
    tokens, gain_one, in_weight, conv_weight, out_weight, gain_two, gate_up_weight, down_weight,
    cotangent, lengths,
):
    n_dp = lax.axis_size("dp")
    B, Dl = tokens.shape
    T = B * lax.axis_size("row")
    width = Dl * lax.axis_size("col")
    index = lax.axis_index("dp") * T + jnp.arange(T + 16, dtype=jnp.int32)
    offset = sequence_offsets(lengths, index)
    masks = [
        jnp.broadcast_to((offset >= lag).astype(F32)[:, None], (T + 16, 128)) for lag in (1, 2)
    ]
    conv = jnp.pad(conv_weight.astype(F32), ((0, 5), (0, 0)))
    chunk = in_weight.shape[2] // n_dp
    split_in = chunk % 128 == 0
    block_out, d_tok, d_gain, d_conv, d_out, n1, n2, cot, act, gh, gp = run_block(
        n_dp,
        float(width),
        split_in,
        tokens,
        gain_one.astype(F32)[None, :],
        jnp.transpose(in_weight, (1, 0, 2)),
        conv,
        out_weight,
        gain_two.astype(F32)[None, :],
        jnp.transpose(gate_up_weight, (1, 0, 2)),
        down_weight,
        cotangent,
        *masks,
    )

    dot = functools.partial(jnp.einsum, preferred_element_type=F32)
    d_down = dot("zrtf,zrti->fi", act, cot)
    d_gu = dot("zrti,zrktf->ikf", n2, gh)
    if split_in:
        d_in = dot("zrti,zrktu->iku", n1, gp)
    else:
        mine = lax.dynamic_index_in_dim(n1, lax.axis_index("dp"), 0, keepdims=False)
        d_in = lax.psum_scatter(
            dot("rti,crktu->ikcu", mine, gp).reshape(Dl, 3, -1).astype(BF),
            "dp",
            scatter_dimension=2,
            tiled=True,
        ).astype(F32)
    part = d_conv.shape[1] * 1 // n_dp
    mine = lax.dynamic_slice(d_conv, (2, lax.axis_index("dp") * part), (3, part))
    return (
        block_out,
        d_tok,
        d_gain[0],
        d_in.reshape(Dl, 3, 1, 1, -1),
        mine.reshape(3, 1, 1, part),
        d_out.reshape(1, 1, -1, Dl),
        d_gain[1],
        d_gu.reshape(Dl, 2, 1, 1, -1),
        d_down.reshape(1, 1, -1, Dl),
    )


def solution(mesh):
    placed = (
        P(("dp", "row"), "col"),
        P("col"),
        P("col", None, "row"),
        P(None, ("row", "col")),
        P("row", "col"),
        P("col"),
        P("col", None, "row"),
        P("row", "col"),
        P(("dp", "row"), "col"),
        P(),
    )
    return jax.shard_map(
        on_device,
        mesh=mesh,
        in_specs=placed,
        out_specs=(
            P(("dp", "row"), "col"),
            P(("dp", "row"), "col"),
            P("col"),
            P("col", None, "row", "dp", None),
            P(None, ("row", "col"), "dp", None),
            P("row", "dp", None, "col"),
            P("col"),
            P("col", None, "row", "dp", None),
            P("row", "dp", None, "col"),
        ),
        check_vma=False,
    )
```

```python
import functools

import jax
import jax.numpy as jnp
from jax import lax
from jax.experimental import pallas as pl
from jax.experimental.pallas import tpu as pltpu
from jax.sharding import PartitionSpec as P

MESH = pl.DeviceIdType.MESH
BF = jnp.bfloat16
F32 = jnp.float32
EPS = 1e-05
VMEM_LIMIT = 63 * 2**20


def nn(a, b):
    return lax.dot_general(a, b, (((1,), (0,)), ((), ())), preferred_element_type=F32)


def nt(a, b):
    return lax.dot_general(a, b, (((1,), (1,)), ((), ())), preferred_element_type=F32)


class Links:
    def __init__(self, send_sems, recv_sems):
        self.send_sems, self.recv_sems = send_sems, recv_sems
        self.count = 0
        self.open = []

    def slot(self):
        self.count += 1
        return self.count - 1

    def copy(self, src, dst, to, slot=None):
        if slot is None:
            slot = self.slot()
        return pltpu.make_async_remote_copy(
            src_ref=src,
            dst_ref=dst,
            send_sem=self.send_sems.at[slot],
            recv_sem=self.recv_sems.at[slot],
            device_id=to,
            device_id_type=MESH,
        )

    def send(self, src, dst, to):
        c = self.copy(src, dst, to)
        c.start()
        self.open.append(c)
        return c

    def sent(self, *copies):
        for c in copies:
            c.wait_send()
            self.open = [o for o in self.open if o is not c]

    def close(self):
        for c in self.open:
            c.wait_send()
        self.open = []


def rows_loop(count, step, body):
    def one(i, carry):
        body(pl.multiple_of(i * step, step))
        return carry

    lax.fori_loop(0, count // step, one, 0)


def block_kernel(n_dp, width, split_in, *refs):
    (
        tok, g1, w_in, cw, w_out, g2, w_gu, w_dn, cot, mask1, mask2,
        block_out, d_tok, d_gain, d_conv, d_out, n1z, n2z, cotz, actz, ghz, gpz,
        w_in_v, w_out_v, w_gu_v, w_dn_v,
        xall, call, gat, act, gh, gp,
        proj_o, proj_r, mext, halo_b, cout, gext, halo_a, gg_s, gg_r, gg_o,
        hid_o, hid_r, ga_o, ga_r,
        rs_s, rs_r, rt_s, rt_r, acc_b, acc_o, down_o,
        resid, gres, ss_s, ss_r, red_s, red_r, red_z, po_s, po_r,
        send_sems, recv_sems, local_sems,
    ) = refs
    R, B, Dl = xall.shape
    Uc = w_out_v.shape[1]
    Fc = w_dn_v.shape[1]
    T = R * B
    dp, row, col = lax.axis_index("dp"), lax.axis_index("row"), lax.axis_index("col")
    other = 1 - col
    low = row + 1 - 2 * lax.rem(row, 2)
    high = row + 2 - 4 * lax.rem(row // 2, 2)
    row_a = low * other + high * col
    row_b = high * other + low * col
    row_d = low + high - row
    to_a, to_b, to_col = {"row": row_a}, {"row": row_b}, {"col": other}
    links = Links(send_sems, recv_sems)
    half = n_dp // 2
    holder = dp // half
    peers = [lax.rem(dp + k, n_dp) for k in range(n_dp)]
    sources = [lax.rem(dp + n_dp - k, n_dp) for k in range(n_dp)]

    loads = {"in": [], "out": [], "gu": [], "dn": []}
    n_local = 0

    def local(src, dst):
        nonlocal n_local
        c = pltpu.make_async_copy(src, dst, local_sems.at[n_local])
        n_local += 1
        c.start()
        return c

    for c in range(2):
        for k in range(3):
            loads["in"].append(local(w_in.at[k, :, pl.ds(c * Uc, Uc)], w_in_v.at[c, k]))
    for c in range(2):
        loads["dn"].append(local(w_dn.at[pl.ds(c * Fc, Fc), :], w_dn_v.at[c]))
        loads["out"].append(local(w_out.at[pl.ds(c * Uc, Uc), :], w_out_v.at[c]))
    for c in range(2):
        for k in range(2):
            loads["gu"].append(local(w_gu.at[k, :, pl.ds(c * Fc, Fc)], w_gu_v.at[c, k]))

    def loaded(name):
        for c in loads[name]:
            c.wait()

    barrier = pltpu.get_barrier_semaphore()
    for to in (to_col, {"row": low}, {"row": high}):
        pl.semaphore_signal(barrier, inc=1, device_id=to, device_id_type=MESH)
    for k in range(1, n_dp):
        pl.semaphore_signal(
            barrier, inc=1, device_id={"dp": lax.rem(dp + k, n_dp)}, device_id_type=MESH
        )

    def col_total(place):
        c = links.send(ss_s.at[place], ss_r.at[place], to_col)
        c.wait_recv()

    def gather(buf):
        first = links.send(buf.at[row], buf.at[row], to_a)
        second = links.send(buf.at[row], buf.at[row], to_b)
        state = {}

        def relay():
            first.wait_recv()
            state["third"] = links.send(buf.at[row_a], buf.at[row_a], to_b)

        def second_in():
            second.wait_recv()

        def third_in():
            state["third"].wait_recv()

        def all_sent():
            links.sent(first, second, state["third"])

        return relay, second_in, third_in, all_sent

    class Line:
        def __init__(self, first, dst, block=None):
            self.first, self.dst, self.block = first, dst, row if block is None else block
            self.up = [links.slot() for _ in range(n_dp + 1)]
            self.down = [links.slot() for _ in range(n_dp + 1)]
            self.sent_to, self.last = {}, {}

        def at(self, z):
            return self.dst.at[z, self.block]

        def up_copy(self, hop):
            at = self.at(lax.rem(dp + n_dp - (hop - 1), n_dp))
            src = self.first if hop == 1 else at
            return links.copy(src, at, {"dp": peers[1]}, self.up[hop])

        def down_copy(self, hop):
            at = self.at(lax.rem(dp + hop - 1, n_dp))
            src = self.first if hop == 1 else at
            return links.copy(src, at, {"dp": sources[1]}, self.down[hop])

        def arrived(self, hop):
            @pl.when(dp >= hop)
            def _():
                self.up_copy(hop).wait_recv()

            @pl.when(dp + hop < n_dp)
            def _():
                self.down_copy(hop).wait_recv()

        def start(self, hop):
            if hop > 1:
                self.arrived(hop - 1)

            @pl.when((dp + 1 < n_dp) & (dp >= hop - 1))
            def _():
                self.up_copy(hop).start()

            @pl.when((dp >= 1) & (dp + hop - 1 < n_dp))
            def _():
                self.down_copy(hop).start()

        def sent(self, hop):
            @pl.when((dp + 1 < n_dp) & (dp >= hop - 1))
            def _():
                self.up_copy(hop).wait_send()

            @pl.when((dp >= 1) & (dp + hop - 1 < n_dp))
            def _():
                self.down_copy(hop).wait_send()

        def rest(self):
            for hop in range(4, n_dp):
                self.start(hop)
            self.arrived(n_dp - 1)

        def plane(self, *ks):
            if not self.sent_to:
                self.rest()
            for k in ks:
                at = self.dst.at[peers[k], row]
                self.sent_to[k] = (links.send(at, at, to_a), links.send(at, at, to_b))

        def relay(self, *ks):
            for k in ks:
                first, second = self.sent_to[k]
                first.wait_recv()
                at = self.dst.at[peers[k], row_a]
                self.last[k] = (second, links.send(at, at, to_b))

        def finish(self, *ks):
            for k in ks:
                for c in self.last[k]:
                    c.wait_recv()

    class Units:
        def __init__(self, src, dst):
            self.src, self.dst = src, dst
            self.size = dst.shape[-1]
            self.slots = [[links.slot() for _ in range(n_dp)] for _ in range(R)]
            self.handed = [links.slot() for _ in range(n_dp)]

        def chunk(self, z, blk):
            at = pl.ds(pl.multiple_of(lax.rem(z, half) * self.size, self.size), self.size)
            return self.src.at[(z // half, blk, *([slice(None)] * (len(self.src.shape) - 3)), at)]

        def across(self, k, i, blk):
            to = self.dst.at[dp, blk]
            return links.copy(self.chunk(peers[k], blk), to, {"dp": peers[k]}, self.slots[i][k])

        def start(self, i, blk):
            for k in range(1, n_dp):

                @pl.when(peers[k] // half == col)
                def _(k=k):
                    self.across(k, i, blk).start()

        def keep(self):
            return local(self.chunk(dp, slice(None)), self.dst.at[dp])

        def hand_on(self):
            for k in range(1, n_dp):

                @pl.when(holder == col)
                def _(k=k):
                    for i in range(R):
                        self.across(k, i, 0).wait_recv()
                    self.hand(k).start()

        def hand(self, k):
            at = self.dst.at[sources[k]]
            return links.copy(at, at, to_col, self.handed[k])

        def finish(self):
            for k in range(1, n_dp):

                @pl.when(holder != col)
                def _(k=k):
                    self.hand(k).wait_recv()

        def close(self):
            for k in range(1, n_dp):

                @pl.when(peers[k] // half == col)
                def _(k=k):
                    for i in range(R):
                        self.across(k, i, 0).wait_send()

                @pl.when(holder == col)
                def _(k=k):
                    self.hand(k).wait_send()

    def row_sum(sends, recvs, partial, filler=None):
        def to_bf(slot):
            def put(n0, value):
                sends[slot, :, n0 : n0 + value.shape[1]] = value.astype(BF)

            return put

        def to_f32(acc):
            def put(n0, value):
                acc[:, n0 : n0 + value.shape[1]] = value

            return put

        partial(row_d, to_bf(0))
        c0 = links.send(sends.at[0], recvs.at[0], to_a)
        partial(row_a, to_bf(1))
        c1 = links.send(sends.at[1], recvs.at[1], to_a)
        partial(row_b, to_f32(acc_b))
        c0.wait_recv()

        def combine(r0):
            at = pl.ds(r0, 16)
            sends[2, at, :] = (acc_b[at, :] + recvs[0, at, :].astype(F32)).astype(BF)

        rows_loop(B, 16, combine)
        c2 = links.send(sends.at[2], recvs.at[2], to_b)
        partial(row, to_f32(acc_o))
        if filler is not None:
            filler()
        c1.wait_recv()
        c2.wait_recv()
        return c0, c1, c2

    def row_total(recvs, at):
        return acc_o[at, :] + recvs[1, at, :].astype(F32) + recvs[2, at, :].astype(F32)

    def lanes(x):
        return jnp.broadcast_to(x, (x.shape[0], 128))

    def squares(r0):
        at = pl.ds(r0, 16)
        x = tok[at, :].astype(F32)
        ss_s[0, at, :] = lanes(jnp.sum(x * x, axis=1, keepdims=True))

    rows_loop(B, 16, squares)
    pl.semaphore_wait(barrier, 3 + n_dp - 1)
    cot_lines = [
        Line(cot, cotz),
        Line(call.at[row_a], cotz, row_a),
        Line(call.at[row_b], cotz, row_b),
        Line(call.at[row_d], cotz, row_d),
    ]
    n1_line = Line(xall.at[row], n1z)
    n2_line = Line(xall.at[row], n2z)
    cot_lines[0].start(1)
    col_total(0)

    def scale_of(place, at):
        return lax.rsqrt((ss_s[place, at, :] + ss_r[place, at, :]) / width + EPS)[:, :1]

    def normed_one(r0):
        at = pl.ds(r0, 16)
        x = tok[at, :].astype(F32)
        xall[row, at, :] = (x * scale_of(0, at) * g1[...]).astype(BF)

    rows_loop(B, 16, normed_one)
    relay, second_in, third_in, all_sent = gather(xall)
    n1_line.start(1)

    def project(blk):
        x = xall[blk]
        for k in range(3):
            gp[col, blk, k] = nn(x, w_in_v[other, k]).astype(BF)
        c = links.send(gp.at[col, blk], proj_r.at[blk], to_col)
        for k in range(3):
            proj_o[k, pl.ds(pl.multiple_of(blk * B, B), B), :] = nn(x, w_in_v[col, k])
        return c

    loaded("in")
    sent = [project(row)]
    relay()
    sent.append(project(row_a))
    cot_lines[0].start(2)
    second_in()
    sent.append(project(row_b))
    third_in()
    call[row] = cot[...]
    cot_relay, cot_second, cot_third, cot_all_sent = gather(call)
    sent.append(project(row_d))
    n1_out = local(xall, n1z.at[dp])
    n1_line.start(2)

    for blk, c in zip((row, row_b, row_a, row_d), sent):
        c.wait_recv()
        base = blk * B

        def add(r0, blk=blk, base=base):
            at = pl.ds(r0, 32)
            to = pl.ds(pl.multiple_of(base + r0, 32), 32)
            g = [proj_o[k, to, :] + proj_r[blk, k, at, :].astype(F32) for k in range(3)]
            for k in range(3):
                proj_o[k, to, :] = g[k]
            mext[pl.ds(pl.multiple_of(base + r0 + 8, 8), 32), :] = g[0] * g[2]

        rows_loop(B, 32, add)
    links.sent(*sent)

    behind = links.slot()

    @pl.when(dp < n_dp - 1)
    def _():
        links.copy(mext.at[pl.ds(T, 8), :], halo_b, {"dp": lax.rem(dp + 1, n_dp)}, behind).start()

    @pl.when(dp > 0)
    def _():
        links.copy(mext.at[pl.ds(T, 8), :], halo_b, {"dp": lax.rem(dp + 1, n_dp)}, behind).wait_recv()
        mext[0:8, :] = halo_b[...]

    @pl.when(dp == 0)
    def _():
        mext[0:8, :] = jnp.zeros((8, Uc), F32)

    cot_relay()
    cot_lines[1].start(1)
    n1_line.start(3)
    cot_lines[0].start(3)
    CH = B // 2

    def mask_of(mask, at):
        return jnp.concatenate([mask[at, :]] * (Uc // 128), axis=1)

    for i in range(T // CH):
        at = pl.ds(i * CH, CH)
        x = mext[pl.ds(i * CH, CH + 8), :]
        y = cw[0:1, :] * x[8 : 8 + CH]
        y = y + cw[1:2, :] * mask_of(mask1, at) * x[7 : 7 + CH]
        y = y + cw[2:3, :] * mask_of(mask2, at) * x[6 : 6 + CH]
        cout[at, :] = y
        gat[col, i * CH // B, i * CH % B : i * CH % B + CH, :] = (proj_o[1, at, :] * y).astype(BF)
    gated_in = links.send(gat.at[col], gat.at[col], to_col)
    cot_second()
    cot_lines[2].start(1)
    gated_in.wait_recv()

    loaded("out")
    n1_out.wait()
    n1_line.sent(1)
    all_sent()

    def out_partial(blk, put):
        for n0 in range(0, Dl, Dl // 2):
            n = slice(n0, n0 + Dl // 2)
            put(n0, nn(gat[0, blk], w_out_v[0, :, n]) + nn(gat[1, blk], w_out_v[1, :, n]))

    sent = row_sum(rs_s, rs_r, out_partial)

    def residual(r0):
        at = pl.ds(r0, 16)
        x = tok[at, :].astype(F32) + row_total(rs_r, at)
        resid[at, :] = x
        ss_s[1, at, :] = lanes(jnp.sum(x * x, axis=1, keepdims=True))

    cot_third()
    cot_lines[3].start(1)
    cot_lines[1].start(2)
    rows_loop(B, 16, residual)
    links.sent(*sent)
    col_total(1)

    def normed_two(r0):
        at = pl.ds(r0, 16)
        xall[row, at, :] = (resid[at, :] * scale_of(1, at) * g2[...]).astype(BF)

    rows_loop(B, 16, normed_two)
    relay, second_in, third_in, all_sent = gather(xall)
    n2_line.start(1)

    loaded("dn")
    ga_sent = []
    for blk in (row, row_a, row_b, row_d):
        x = call[blk]
        for n0 in range(0, Fc, Fc // 2):
            n = slice(n0, n0 + Fc // 2)
            act[col, blk, :, n] = nt(x, w_dn_v[other, n, :]).astype(BF)
        ga_sent.append(links.send(act.at[col, blk], ga_r.at[blk], to_col))
    relay()
    for blk in (row, row_a, row_b, row_d):
        x = call[blk]
        for n0 in range(0, Fc, Fc // 2):
            n = slice(n0, n0 + Fc // 2)
            ga_o[blk, :, n] = nt(x, w_dn_v[col, n, :])
    cot_out = local(call, cotz.at[dp])
    n2_line.start(2)
    cot_lines[2].start(2)
    cot_lines[1].start(3)

    def hidden_other(blk):
        def one(k, carry):
            for n0 in range(0, Fc, Fc // 2):
                n = slice(n0, n0 + Fc // 2)
                gh[col, blk, k, :, n] = nn(xall[blk], w_gu_v[other, k, :, n]).astype(BF)
            return carry

        lax.fori_loop(0, 2, one, 0)
        return links.send(gh.at[col, blk], hid_r.at[blk], to_col)

    loaded("gu")
    hid_sent = [hidden_other(row), hidden_other(row_a)]
    second_in()
    hid_sent.append(hidden_other(row_b))
    third_in()
    hid_sent.append(hidden_other(row_d))
    n2_out = local(xall, n2z.at[dp])
    n1_line.plane(1, 2)
    n2_line.start(3)
    cot_lines[3].start(2)
    cot_lines[2].start(3)

    gh_in = {}
    for name, blk in (("d", row_d), ("a", row_a), ("b", row_b), ("o", row)):

        def one(k, carry, blk=blk):
            for n0 in range(0, Fc, Fc // 2):
                n = slice(n0, n0 + Fc // 2)
                hid_o[k, :, n] = nn(xall[blk], w_gu_v[col, k, :, n])
            return carry

        lax.fori_loop(0, 2, one, 0)
        which = {"o": 0, "a": 1, "b": 2, "d": 3}[name]
        theirs = {"o": 0, "a": 2, "b": 1, "d": 3}[name]
        hid_sent[theirs].wait_recv()
        ga_sent[theirs].wait_recv()
        links.sent(hid_sent[which], ga_sent[which])

        def activate(r0, blk=blk):
            at = pl.ds(r0, 16)
            for n0 in range(0, Fc, Fc // 2):
                n = slice(n0, n0 + Fc // 2)
                gate = hid_o[0, at, n] + hid_r[blk, 0, at, n].astype(F32)
                up = hid_o[1, at, n] + hid_r[blk, 1, at, n].astype(F32)
                ga = ga_o[blk, at, n] + ga_r[blk, at, n].astype(F32)
                s = jax.nn.sigmoid(gate)
                silu = gate * s
                act[col, blk, at, n] = (silu * up).astype(BF)
                gh[col, blk, 0, at, n] = (ga * up * s * (1.0 + gate * (1.0 - s))).astype(BF)
                gh[col, blk, 1, at, n] = (ga * silu).astype(BF)

        rows_loop(B, 16, activate)
        gh_in[name] = (
            links.send(gh.at[col, blk], gh.at[col, blk], to_col),
            links.send(act.at[col, blk], act.at[col, blk], to_col),
        )
    n1_line.relay(1, 2)
    cot_lines[3].start(3)
    for pair in gh_in.values():
        for c in pair:
            c.wait_recv()
    size = actz.shape[-1]
    mine = pl.ds(pl.multiple_of(lax.rem(dp, half) * size, size), size)
    kept_units = [
        local(act.at[holder, :, :, mine], actz.at[dp]),
        local(gh.at[holder, :, :, :, mine], ghz.at[dp]),
    ]
    kept = []
    n2_out.wait()
    n2_line.sent(1)
    all_sent()

    def gu_partial(blk, put):
        for n0 in range(0, Dl, Dl // 4):
            n = slice(n0, n0 + Dl // 4)
            total = None
            for c in range(2):
                for k in range(2):
                    part = nt(gh[c, blk, k], w_gu_v[c, k, n, :])
                    total = part if total is None else total + part
            put(n0, total)

    sent = row_sum(rs_s, rs_r, gu_partial)

    def back_two(r0):
        at = pl.ds(r0, 16)
        g = row_total(rs_r, at)
        gres[at, :] = g
        ss_s[2, at, :] = lanes(jnp.sum(g * g2[...] * resid[at, :], axis=1, keepdims=True))

    rows_loop(B, 16, back_two)
    links.sent(*sent)
    col_total(2)

    def inner_of(place, at):
        return (ss_s[place, at, :] + ss_r[place, at, :])[:, :1]

    def branch(i, gain):
        at = pl.ds(pl.multiple_of(i * 16, 16), 16)
        g = gres[at, :]
        x = resid[at, :]
        s = scale_of(1, at)
        y = cot[at, :].astype(F32) + s * g2[...] * g - x * (s * s * s) * inner_of(2, at) / width
        gres[at, :] = y
        xall[row, at, :] = y.astype(BF)
        return gain + jnp.sum(g * x * s, axis=0, keepdims=True)

    gain_two = lax.fori_loop(0, B // 16, branch, jnp.zeros((1, Dl), F32))
    relay, second_in, third_in, all_sent = gather(xall)

    def down_partial(blk, put):
        for n0 in range(0, Dl, Dl // 2):
            n = slice(n0, n0 + Dl // 2)
            put(n0, nn(act[0, blk], w_dn_v[0, :, n]) + nn(act[1, blk], w_dn_v[1, :, n]))

    def put_to(ref):
        def put(n0, value):
            ref[:, n0 : n0 + value.shape[1]] = value.astype(ref.dtype)

        return put

    down_partial(row_d, put_to(rt_s.at[0]))
    down_partial(row_a, put_to(rt_s.at[1]))

    def gated_other(blk):
        gg_s[blk] = nt(xall[blk], w_out_v[other]).astype(BF)
        c = links.send(gg_s.at[blk], gg_r.at[blk], to_col)
        gg_o[blk] = nt(xall[blk], w_out_v[col])
        return c

    sent = [gated_other(row)]
    relay()
    down_partial(row, put_to(down_o))
    sent.append(gated_other(row_a))
    second_in()
    sent.append(gated_other(row_b))
    third_in()
    sent.append(gated_other(row_d))
    n2_line.plane(1)

    for blk, c in zip((row, row_b, row_a, row_d), sent):
        c.wait_recv()
        base = blk * B

        def conv_grad(r0, blk=blk, base=base):
            at = pl.ds(r0, 32)
            to = pl.ds(pl.multiple_of(base + r0, 32), 32)
            g = gg_o[blk, at, :] + gg_r[blk, at, :].astype(F32)
            gext[to, :] = g * proj_o[1, to, :]
            gp[col, blk, 1, at, :] = (g * cout[to, :]).astype(BF)

        rows_loop(B, 32, conv_grad)

    ahead = links.slot()

    @pl.when(dp > 0)
    def _():
        links.copy(gext.at[pl.ds(0, 8), :], halo_a, {"dp": lax.rem(dp + n_dp - 1, n_dp)}, ahead).start()

    @pl.when(dp < n_dp - 1)
    def _():
        links.copy(gext.at[pl.ds(0, 8), :], halo_a, {"dp": lax.rem(dp + n_dp - 1, n_dp)}, ahead).wait_recv()
        gext[T : T + 8, :] = halo_a[...]

    @pl.when(dp == n_dp - 1)
    def _():
        gext[T : T + 8, :] = jnp.zeros((8, Uc), F32)

    terms = [jnp.zeros((1, Uc), F32) for _ in range(3)]
    for i in range(T // CH):
        at = pl.ds(i * CH, CH)
        more = pl.ds(i * CH, CH + 8)
        x = mext[more, :]
        g = gext[more, :]
        m1, m2 = mask_of(mask1, more), mask_of(mask2, more)
        now = g[:CH]
        terms[0] = terms[0] + jnp.sum(now * x[8 : 8 + CH], axis=0, keepdims=True)
        terms[1] = terms[1] + jnp.sum(m1[:CH] * now * x[7 : 7 + CH], axis=0, keepdims=True)
        terms[2] = terms[2] + jnp.sum(m2[:CH] * now * x[6 : 6 + CH], axis=0, keepdims=True)
        y = cw[0:1, :] * now
        y = y + cw[1:2, :] * (m1 * g)[1 : 1 + CH]
        y = y + cw[2:3, :] * (m2 * g)[2 : 2 + CH]
        blk, to = i * CH // B, slice(i * CH % B, i * CH % B + CH)
        gp[col, blk, 0, to, :] = (y * proj_o[2, at, :]).astype(BF)
        gp[col, blk, 2, to, :] = (y * proj_o[0, at, :]).astype(BF)
    red_s[...] = jnp.zeros_like(red_s)
    for k in range(3):
        red_s[2 + k : 3 + k, :Uc] = terms[k]
    gp_in = links.send(gp.at[col], gp.at[col], to_col)
    if split_in:
        gp_units = Units(gp, gpz)
        for i in range(R):
            gp_units.start(i, i)
    n2_line.relay(1)
    gp_in.wait_recv()
    if split_in:
        kept.append(gp_units.keep())
    else:
        kept.append(local(gp, gpz))

    def in_partial(blk, put):
        for n0 in range(0, Dl, Dl // 4):
            n = slice(n0, n0 + Dl // 4)
            total = None
            for c in range(2):
                for k in range(3):
                    part = nt(gp[c, blk, k], w_in_v[c, k, n, :])
                    total = part if total is None else total + part
            put(n0, total)

    po_all = []

    def out_weights():
        rows = po_s.shape[1]
        for z in range(n_dp):
            at = pl.ds(z % half * rows, rows)
            g = lax.dot_general(
                gat[z // half, :, :, at].reshape(T, rows), xall[...].reshape(T, Dl),
                (((0,), (0,)), ((), ())), preferred_element_type=F32,
            )
            po_s[z] = g.astype(BF)
        for k in range(1, n_dp):
            po_all.append(links.send(po_s.at[peers[k]], po_r.at[dp], {"dp": peers[k]}))

    sent_in = row_sum(rs_s, rs_r, in_partial, filler=out_weights)
    n2_line.plane(*range(2, min(3, n_dp)))
    down_sent = [
        links.send(rt_s.at[0], rt_r.at[0], to_a),
        links.send(rt_s.at[1], rt_r.at[1], to_a),
    ]
    down_partial(row_b, put_to(acc_b))

    def back_one(r0):
        at = pl.ds(r0, 16)
        g = row_total(rs_r, at)
        d_tok[at, :] = g
        ss_s[3, at, :] = lanes(
            jnp.sum(g * g1[...] * tok[at, :].astype(F32), axis=1, keepdims=True)
        )

    rows_loop(B, 16, back_one)
    col_total(3)

    def token_grad(i, gain):
        at = pl.ds(pl.multiple_of(i * 16, 16), 16)
        g = d_tok[at, :]
        x = tok[at, :].astype(F32)
        s = scale_of(0, at)
        y = gres[at, :] + s * g1[...] * g - x * (s * s * s) * inner_of(3, at) / width
        d_tok[at, :] = y
        return gain + jnp.sum(g * x * s, axis=0, keepdims=True)

    gain_one = lax.fori_loop(0, B // 16, token_grad, jnp.zeros((1, Dl), F32))

    red_s[0:1, :] = gain_one
    red_s[1:2, :] = gain_two
    c0 = links.send(red_s, red_r.at[0], to_a)
    n2_line.relay(*range(2, min(3, n_dp)))
    n2_line.plane(*range(3, n_dp))
    for line in cot_lines:
        line.rest()
    for c in [cot_out, *kept_units]:
        c.wait()
    for pair in gh_in.values():
        links.sent(*pair)
    for line in cot_lines[1:]:
        line.sent(1)
    cot_all_sent()
    all_sent()

    slots = Fc // size

    def place(k, r, rank):
        q = (k - 1) * 2 + r
        lanes_at = slice(q % slots * size, q % slots * size + size)
        return (q // slots, *([slice(None)] * (rank - 2)), lanes_at)

    def again(k):
        z = peers[k]
        loads = [local(n2z.at[z], xall), local(cotz.at[z], call)]
        for c in loads:
            c.wait()
        copies = []
        for core, keep in ((other, False), (col, True)):
            x = xall[pl.ds(core * 2, 2)].reshape(2 * B, Dl)
            for j in range(2):
                h = nn(x, w_gu_v[holder, j, :, mine])
                for r in range(2):
                    if keep:
                        hid_o[j, :, r * size : r * size + size] = h[r * B : r * B + B]
                    else:
                        q, _, _, n = place(k, r, 4)
                        gh[0, q, j, :, n] = h[r * B : r * B + B].astype(BF)
            y = call[pl.ds(core * 2, 2)].reshape(2 * B, Dl)
            g = nt(y, w_dn_v[holder, mine, :])
            for r in range(2):
                if keep:
                    ga_o[r, :, :size] = g[r * B : r * B + B]
                else:
                    q, _, n = place(k, r, 3)
                    act[0, q, :, n] = g[r * B : r * B + B].astype(BF)
            if not keep:
                for r in range(2):
                    h_at, g_at = place(k, r, 4), place(k, r, 3)
                    copies.append(links.send(gh.at[0].at[h_at], hid_r.at[h_at], to_col))
                    copies.append(links.send(act.at[0].at[g_at], ga_r.at[g_at], to_col))
        for c in copies:
            c.wait_recv()
        done = []
        for r in range(2):
            q, _, n = place(k, r, 3)

            def finish(r0, r=r, q=q, n=n):
                at = pl.ds(r0, 16)
                own = slice(r * size, r * size + size)
                gate = hid_o[0, at, own] + hid_r[q, 0, at, n].astype(F32)
                up = hid_o[1, at, own] + hid_r[q, 1, at, n].astype(F32)
                ga = ga_o[r, at, :size] + ga_r[q, at, n].astype(F32)
                s = jax.nn.sigmoid(gate)
                silu = gate * s
                act[1, q, at, n] = (silu * up).astype(BF)
                gh[1, q, 0, at, n] = (ga * up * s * (1.0 + gate * (1.0 - s))).astype(BF)
                gh[1, q, 1, at, n] = (ga * silu).astype(BF)

            rows_loop(B, 16, finish)
            blk = col * 2 + r
            h_src, a_src = gh.at[1].at[place(k, r, 4)], act.at[1].at[place(k, r, 3)]
            done.append(links.send(h_src, ghz.at[z, blk], to_col))
            done.append(links.send(a_src, actz.at[z, blk], to_col))
            kept.append(local(h_src, ghz.at[z, blk]))
            kept.append(local(a_src, actz.at[z, blk]))
        return done

    n2_line.finish(1)
    again_in = again(1)

    down_sent[0].wait_recv()

    def down_combine(r0):
        at = pl.ds(r0, 16)
        rt_s[2, at, :] = (acc_b[at, :] + rt_r[0, at, :].astype(F32)).astype(BF)

    rows_loop(B, 16, down_combine)
    down_sent.append(links.send(rt_s.at[2], rt_r.at[2], to_b))
    c0.wait_recv()
    links.sent(c0)
    red_s[0:2, :] = red_s[0:2, :] + red_r[0, 0:2, :]
    c1 = links.send(red_s, red_r.at[1], to_b)
    n2_line.relay(*range(3, n_dp))
    n1_line.plane(*range(3, n_dp))
    n2_line.finish(2)
    again_in += again(2)
    c1.wait_recv()
    red_z[dp] = red_s[...]
    red_z[dp, 0:2, :] = red_s[0:2, :] + red_r[1, 0:2, :]
    arrived = []
    for k in range(1, n_dp):
        arrived.append(links.send(red_z.at[dp], red_z.at[dp], {"dp": lax.rem(dp + k, n_dp)}))
    for k in range(3, n_dp):
        n2_line.finish(k)
        again_in += again(k)
    n1_line.relay(*range(3, n_dp))
    for c in down_sent[1:]:
        c.wait_recv()

    def block_rows(r0):
        at = pl.ds(r0, 16)
        total = down_o[at, :] + rt_r[1, at, :].astype(F32) + rt_r[2, at, :].astype(F32)
        block_out[at, :] = (resid[at, :] + total).astype(BF)

    rows_loop(B, 16, block_rows)
    for c in arrived:
        c.wait_recv()
    total = red_z[0]
    for k in range(1, n_dp):
        total = total + red_z[k]
    d_gain[...] = total
    d_conv[...] = total[:, :Uc]

    @pl.when(dp < n_dp - 1)
    def _():
        links.copy(mext.at[pl.ds(T, 8), :], halo_b, {"dp": lax.rem(dp + 1, n_dp)}, behind).wait_send()

    @pl.when(dp > 0)
    def _():
        links.copy(gext.at[pl.ds(0, 8), :], halo_a, {"dp": lax.rem(dp + n_dp - 1, n_dp)}, ahead).wait_send()

    for c in again_in:
        c.wait_recv()
    for c in po_all:
        c.wait_recv()
    out_total = po_s[dp].astype(F32)
    for k in range(1, n_dp):
        out_total = out_total + po_r[peers[k]].astype(F32)
    d_out[...] = out_total
    n1_line.finish(*range(1, n_dp))
    if split_in:
        gp_units.hand_on()
        gp_units.finish()
        gp_units.close()
    cot_lines[0].sent(1)
    for hop in range(2, n_dp):
        for line in (*cot_lines, n1_line, n2_line):
            line.sent(hop)
    for c in kept:
        c.wait()
    assert links.count <= send_sems.shape[0]
    links.close()


def run_block(n_dp, width, split_in, tok, g1, w_in, cw, w_out, g2, w_gu, w_dn, cot, mask1, mask2):
    B, Dl = tok.shape
    R = 4
    T = R * B
    Uc = w_out.shape[0] // 2
    Fc = w_dn.shape[0] // 2
    vm = lambda shape, kind=BF: pltpu.VMEM(shape, kind)
    any_spec, vmem_spec = pl.BlockSpec(memory_space=pl.ANY), pl.BlockSpec(memory_space=pltpu.VMEM)
    shape = jax.ShapeDtypeStruct
    rows = shape((n_dp, R, B, Dl), BF)
    return pl.pallas_call(
        functools.partial(block_kernel, n_dp, width, split_in),
        out_shape=(
            shape((B, Dl), BF),
            shape((B, Dl), F32),
            shape((8, Dl), F32),
            shape((8, Uc), F32),
            shape((2 * Uc // n_dp, Dl), F32),
            rows,
            rows,
            rows,
            shape((n_dp, R, B, 2 * Fc // n_dp), BF),
            shape((n_dp, R, 2, B, 2 * Fc // n_dp), BF),
            shape((n_dp, R, 3, B, 2 * Uc // n_dp) if split_in else (2, R, 3, B, Uc), BF),
        ),
        in_specs=[
            vmem_spec, vmem_spec, any_spec, vmem_spec, any_spec, vmem_spec,
            any_spec, any_spec, vmem_spec, vmem_spec, vmem_spec,
        ],
        out_specs=[vmem_spec] * 5 + [any_spec] * 6,
        scratch_shapes=[
            vm((2, 3, Dl, Uc)), vm((2, Uc, Dl)), vm((2, 2, Dl, Fc)), vm((2, Fc, Dl)),
            vm((R, B, Dl)), vm((R, B, Dl)),
            vm((2, R, B, Uc)), vm((2, R, B, Fc)), vm((2, R, 2, B, Fc)), vm((2, R, 3, B, Uc)),
            vm((3, T, Uc), F32), vm((R, 3, B, Uc)), vm((T + 8, Uc), F32), vm((8, Uc), F32),
            vm((T, Uc), F32), vm((T + 8, Uc), F32), vm((8, Uc), F32),
            vm((R, B, Uc)), vm((R, B, Uc)), vm((R, B, Uc), F32),
            vm((2, B, Fc), F32), vm((R, 2, B, Fc)), vm((R, B, Fc), F32), vm((R, B, Fc)),
            vm((3, B, Dl)), vm((3, B, Dl)), vm((3, B, Dl)), vm((3, B, Dl)),
            vm((B, Dl), F32), vm((B, Dl), F32), vm((B, Dl), F32),
            vm((B, Dl), F32), vm((B, Dl), F32),
            vm((4, B, 128), F32), vm((4, B, 128), F32),
            vm((8, Dl), F32), vm((2, 8, Dl), F32), vm((n_dp, 8, Dl), F32),
            vm((n_dp, 2 * Uc // n_dp, Dl)), vm((n_dp, 2 * Uc // n_dp, Dl)),
            pltpu.SemaphoreType.DMA((96 + 48 * n_dp,)), pltpu.SemaphoreType.DMA((96 + 48 * n_dp,)),
            pltpu.SemaphoreType.DMA((32 + 6 * n_dp,)),
        ],
        compiler_params=pltpu.CompilerParams(
            collective_id=0, has_side_effects=True, vmem_limit_bytes=VMEM_LIMIT
        ),
        name="block",
    )(tok, g1, w_in, cw, w_out, g2, w_gu, w_dn, cot, mask1, mask2)


def sequence_offsets(lengths, index):
    ends = jnp.cumsum(lengths)
    starts = ends - lengths
    reached = starts[None, :] <= index[:, None]
    return index - jnp.max(jnp.where(reached, starts[None, :], 0), axis=1)


def on_device(
    tokens, gain_one, in_weight, conv_weight, out_weight, gain_two, gate_up_weight, down_weight,
    cotangent, lengths,
):
    n_dp = lax.axis_size("dp")
    B, Dl = tokens.shape
    T = B * lax.axis_size("row")
    width = Dl * lax.axis_size("col")
    index = lax.axis_index("dp") * T + jnp.arange(T + 16, dtype=jnp.int32)
    offset = sequence_offsets(lengths, index)
    masks = [
        jnp.broadcast_to((offset >= lag).astype(F32)[:, None], (T + 16, 128)) for lag in (1, 2)
    ]
    conv = jnp.pad(conv_weight.astype(F32), ((0, 5), (0, 0)))
    chunk = in_weight.shape[2] // n_dp
    split_in = chunk % 128 == 0
    block_out, d_tok, d_gain, d_conv, d_out, n1, n2, cot, act, gh, gp = run_block(
        n_dp,
        float(width),
        split_in,
        tokens,
        gain_one.astype(F32)[None, :],
        jnp.transpose(in_weight, (1, 0, 2)),
        conv,
        out_weight,
        gain_two.astype(F32)[None, :],
        jnp.transpose(gate_up_weight, (1, 0, 2)),
        down_weight,
        cotangent,
        *masks,
    )

    dot = functools.partial(jnp.einsum, preferred_element_type=F32)
    d_down = dot("zrtf,zrti->fi", act, cot)
    d_gu = dot("zrti,zrktf->ikf", n2, gh)
    if split_in:
        d_in = dot("zrti,zrktu->iku", n1, gp)
    else:
        mine = lax.dynamic_index_in_dim(n1, lax.axis_index("dp"), 0, keepdims=False)
        d_in = lax.psum_scatter(
            dot("rti,crktu->ikcu", mine, gp).reshape(Dl, 3, -1).astype(BF),
            "dp",
            scatter_dimension=2,
            tiled=True,
        ).astype(F32)
    part = d_conv.shape[1] * 1 // n_dp
    mine = lax.dynamic_slice(d_conv, (2, lax.axis_index("dp") * part), (3, part))
    return (
        block_out,
        d_tok,
        d_gain[0],
        d_in.reshape(Dl, 3, 1, 1, -1),
        mine.reshape(3, 1, 1, part),
        d_out.reshape(1, 1, -1, Dl),
        d_gain[1],
        d_gu.reshape(Dl, 2, 1, 1, -1),
        d_down.reshape(1, 1, -1, Dl),
    )


def solution(mesh):
    placed = (
        P(("dp", "row"), "col"),
        P("col"),
        P("col", None, "row"),
        P(None, ("row", "col")),
        P("row", "col"),
        P("col"),
        P("col", None, "row"),
        P("row", "col"),
        P(("dp", "row"), "col"),
        P(),
    )
    return jax.shard_map(
        on_device,
        mesh=mesh,
        in_specs=placed,
        out_specs=(
            P(("dp", "row"), "col"),
            P(("dp", "row"), "col"),
            P("col"),
            P("col", None, "row", "dp", None),
            P(None, ("row", "col"), "dp", None),
            P("row", "dp", None, "col"),
            P("col"),
            P("col", None, "row", "dp", None),
            P("row", "dp", None, "col"),
        ),
        check_vma=False,
    )
```

```python
import functools

import jax
import jax.numpy as jnp
from jax import lax
from jax.experimental import pallas as pl
from jax.experimental.pallas import tpu as pltpu
from jax.sharding import PartitionSpec as P

MESH = pl.DeviceIdType.MESH
BF = jnp.bfloat16
F32 = jnp.float32
EPS = 1e-05
VMEM_LIMIT = 63 * 2**20


def nn(a, b):
    return lax.dot_general(a, b, (((1,), (0,)), ((), ())), preferred_element_type=F32)


def nt(a, b):
    return lax.dot_general(a, b, (((1,), (1,)), ((), ())), preferred_element_type=F32)


class Links:
    def __init__(self, send_sems, recv_sems):
        self.send_sems, self.recv_sems = send_sems, recv_sems
        self.count = 0
        self.open = []

    def slot(self):
        self.count += 1
        return self.count - 1

    def copy(self, src, dst, to, slot=None):
        if slot is None:
            slot = self.slot()
        return pltpu.make_async_remote_copy(
            src_ref=src,
            dst_ref=dst,
            send_sem=self.send_sems.at[slot],
            recv_sem=self.recv_sems.at[slot],
            device_id=to,
            device_id_type=MESH,
        )

    def send(self, src, dst, to):
        c = self.copy(src, dst, to)
        c.start()
        self.open.append(c)
        return c

    def sent(self, *copies):
        for c in copies:
            c.wait_send()
            self.open = [o for o in self.open if o is not c]

    def close(self):
        for c in self.open:
            c.wait_send()
        self.open = []


def rows_loop(count, step, body):
    def one(i, carry):
        body(pl.multiple_of(i * step, step))
        return carry

    lax.fori_loop(0, count // step, one, 0)


def block_kernel(n_dp, width, split_in, *refs):
    (
        tok, g1_in, w_in, cw_in, w_out, g2_in, w_gu, w_dn, cot, lengths,
        block_out, d_tok, d_gain, d_conv, d_out, n1_h, n2z, cotz, actz, ghz, d_in, in_up, in_dn,
        w_in_v, w_out_v, w_gu_v, w_dn_v,
        xall, call, gat, act, gh, gp,
        proj_o, proj_r, mext, halo_b, cout, gext, halo_a, gg_s, gg_r, gg_o,
        hid_o, hid_r, ga_o, ga_r,
        rs_s, rs_r, rt_s, rt_r, acc_b, acc_o, down_o,
        resid, gres, ss_s, ss_r, red_s, red_r, red_z, po_r,
        g1, g2, cw, reach, in_add,
        send_sems, recv_sems, local_sems,
    ) = refs
    R, B, Dl = xall.shape
    Uc = w_out_v.shape[1]
    Fc = w_dn_v.shape[1]
    T = R * B
    dp, row, col = lax.axis_index("dp"), lax.axis_index("row"), lax.axis_index("col")
    other = 1 - col
    low = row + 1 - 2 * lax.rem(row, 2)
    high = row + 2 - 4 * lax.rem(row // 2, 2)
    row_a = low * other + high * col
    row_b = high * other + low * col
    row_d = low + high - row
    to_a, to_b, to_col = {"row": row_a}, {"row": row_b}, {"col": other}
    links = Links(send_sems, recv_sems)
    half = n_dp // 2
    holder = dp // half
    peers = [lax.rem(dp + k, n_dp) for k in range(n_dp)]
    sources = [lax.rem(dp + n_dp - k, n_dp) for k in range(n_dp)]

    loads = {"in": [], "out": [], "gu": [], "dn": []}
    n_local = 0

    def local(src, dst):
        nonlocal n_local
        c = pltpu.make_async_copy(src, dst, local_sems.at[n_local])
        n_local += 1
        c.start()
        return c

    for c in range(2):
        for k in range(3):
            loads["in"].append(local(w_in.at[k, :, pl.ds(c * Uc, Uc)], w_in_v.at[c, k]))
    for c in range(2):
        loads["dn"].append(local(w_dn.at[pl.ds(c * Fc, Fc), :], w_dn_v.at[c]))
        loads["out"].append(local(w_out.at[pl.ds(c * Uc, Uc), :], w_out_v.at[c]))
    for c in range(2):
        for k in range(2):
            loads["gu"].append(local(w_gu.at[k, :, pl.ds(c * Fc, Fc)], w_gu_v.at[c, k]))

    def loaded(name):
        for c in loads[name]:
            c.wait()

    barrier = pltpu.get_barrier_semaphore()
    for to in (to_col, {"row": low}, {"row": high}):
        pl.semaphore_signal(barrier, inc=1, device_id=to, device_id_type=MESH)
    for k in range(1, n_dp):
        pl.semaphore_signal(
            barrier, inc=1, device_id={"dp": lax.rem(dp + k, n_dp)}, device_id_type=MESH
        )

    def col_total(place):
        c = links.send(ss_s.at[place], ss_r.at[place], to_col)
        c.wait_recv()

    def gather(buf):
        first = links.send(buf.at[row], buf.at[row], to_a)
        second = links.send(buf.at[row], buf.at[row], to_b)
        state = {}

        def relay():
            first.wait_recv()
            state["third"] = links.send(buf.at[row_a], buf.at[row_a], to_b)

        def second_in():
            second.wait_recv()

        def third_in():
            state["third"].wait_recv()

        def all_sent():
            links.sent(first, second, state["third"])

        return relay, second_in, third_in, all_sent

    class Line:
        def __init__(self, first, dst, block=None):
            self.first, self.dst, self.block = first, dst, row if block is None else block
            self.up = [links.slot() for _ in range(n_dp + 1)]
            self.down = [links.slot() for _ in range(n_dp + 1)]
            self.sent_to, self.last = {}, {}

        def at(self, z):
            return self.dst.at[z, self.block]

        def up_copy(self, hop):
            at = self.at(lax.rem(dp + n_dp - (hop - 1), n_dp))
            src = self.first if hop == 1 else at
            return links.copy(src, at, {"dp": peers[1]}, self.up[hop])

        def down_copy(self, hop):
            at = self.at(lax.rem(dp + hop - 1, n_dp))
            src = self.first if hop == 1 else at
            return links.copy(src, at, {"dp": sources[1]}, self.down[hop])

        def arrived(self, hop):
            @pl.when(dp >= hop)
            def _():
                self.up_copy(hop).wait_recv()

            @pl.when(dp + hop < n_dp)
            def _():
                self.down_copy(hop).wait_recv()

        def start(self, hop):
            if hop > 1:
                self.arrived(hop - 1)

            @pl.when((dp + 1 < n_dp) & (dp >= hop - 1))
            def _():
                self.up_copy(hop).start()

            @pl.when((dp >= 1) & (dp + hop - 1 < n_dp))
            def _():
                self.down_copy(hop).start()

        def sent(self, hop):
            @pl.when((dp + 1 < n_dp) & (dp >= hop - 1))
            def _():
                self.up_copy(hop).wait_send()

            @pl.when((dp >= 1) & (dp + hop - 1 < n_dp))
            def _():
                self.down_copy(hop).wait_send()

        def rest(self):
            for hop in range(4, n_dp):
                self.start(hop)
            self.arrived(n_dp - 1)

        def plane(self, *ks):
            if not self.sent_to:
                self.rest()
            for k in ks:
                at = self.dst.at[peers[k], row]
                self.sent_to[k] = (links.send(at, at, to_a), links.send(at, at, to_b))

        def relay(self, *ks):
            for k in ks:
                first, second = self.sent_to[k]
                first.wait_recv()
                at = self.dst.at[peers[k], row_a]
                self.last[k] = (second, links.send(at, at, to_b))

        def finish(self, *ks):
            for k in ks:
                for c in self.last[k]:
                    c.wait_recv()

    def row_sum(sends, recvs, partial, filler=None):
        def to_bf(slot):
            def put(n0, value):
                sends[slot, :, n0 : n0 + value.shape[1]] = value.astype(BF)

            return put

        def to_f32(acc):
            def put(n0, value):
                acc[:, n0 : n0 + value.shape[1]] = value

            return put

        partial(row_d, to_bf(0))
        c0 = links.send(sends.at[0], recvs.at[0], to_a)
        partial(row_a, to_bf(1))
        c1 = links.send(sends.at[1], recvs.at[1], to_a)
        partial(row_b, to_f32(acc_b))
        c0.wait_recv()

        def combine(r0):
            at = pl.ds(r0, 16)
            sends[2, at, :] = (acc_b[at, :] + recvs[0, at, :].astype(F32)).astype(BF)

        rows_loop(B, 16, combine)
        c2 = links.send(sends.at[2], recvs.at[2], to_b)
        partial(row, to_f32(acc_o))
        if filler is not None:
            filler()
        c1.wait_recv()
        c2.wait_recv()
        return c0, c1, c2

    def row_total(recvs, at):
        return acc_o[at, :] + recvs[1, at, :].astype(F32) + recvs[2, at, :].astype(F32)

    def lanes(x):
        return jnp.broadcast_to(x, (x.shape[0], 128))

    g1[...] = g1_in[...].astype(F32)
    g2[...] = g2_in[...].astype(F32)
    cw[...] = cw_in[...].astype(F32)
    starts = [jnp.int32(0)]
    for i in range(lengths.shape[0] - 1):
        starts.append(starts[-1] + lengths[i])

    def masks(r0):
        t = dp * T + r0 + lax.broadcasted_iota(jnp.int32, (16, 128), 0)
        count = jnp.full((16, 128), 2.0, F32)
        for start in starts:
            away = t - start
            count = jnp.where((away >= 0) & (away < 2), away.astype(F32), count)
        reach[pl.ds(r0, 16), :] = count

    rows_loop(T + 16, 16, masks)

    def squares(r0):
        at = pl.ds(r0, 16)
        x = tok[at, :].astype(F32)
        ss_s[0, at, :] = lanes(jnp.sum(x * x, axis=1, keepdims=True))

    rows_loop(B, 16, squares)
    pl.semaphore_wait(barrier, 3 + n_dp - 1)
    cot_line = Line(cot, cotz)
    n2_line = Line(xall.at[row], n2z)
    cot_line.start(1)
    col_total(0)

    def scale_of(place, at):
        return lax.rsqrt((ss_s[place, at, :] + ss_r[place, at, :]) / width + EPS)[:, :1]

    def normed_one(r0):
        at = pl.ds(r0, 16)
        x = tok[at, :].astype(F32)
        xall[row, at, :] = (x * scale_of(0, at) * g1[...]).astype(BF)

    rows_loop(B, 16, normed_one)
    relay, second_in, third_in, all_sent = gather(xall)

    def project(blk):
        x = xall[blk]
        for k in range(3):
            gp[col, blk, k] = nn(x, w_in_v[other, k]).astype(BF)
        c = links.send(gp.at[col, blk], proj_r.at[blk], to_col)
        for k in range(3):
            proj_o[k, pl.ds(pl.multiple_of(blk * B, B), B), :] = nn(x, w_in_v[col, k])
        return c

    loaded("in")
    sent = [project(row)]
    relay()
    sent.append(project(row_a))
    cot_line.start(2)
    second_in()
    sent.append(project(row_b))
    third_in()
    call[row] = cot[...]
    cot_relay, cot_second, cot_third, cot_all_sent = gather(call)
    sent.append(project(row_d))
    n1_out = local(xall, n1_h)

    for blk, c in zip((row, row_b, row_a, row_d), sent):
        c.wait_recv()
        base = blk * B

        def add(r0, blk=blk, base=base):
            at = pl.ds(r0, 32)
            to = pl.ds(pl.multiple_of(base + r0, 32), 32)
            g = [proj_o[k, to, :] + proj_r[blk, k, at, :].astype(F32) for k in range(3)]
            for k in range(3):
                proj_o[k, to, :] = g[k]
            mext[pl.ds(pl.multiple_of(base + r0 + 8, 8), 32), :] = g[0] * g[2]

        rows_loop(B, 32, add)
    links.sent(*sent)

    behind = links.slot()

    @pl.when(dp < n_dp - 1)
    def _():
        links.copy(mext.at[pl.ds(T, 8), :], halo_b, {"dp": lax.rem(dp + 1, n_dp)}, behind).start()

    @pl.when(dp > 0)
    def _():
        links.copy(mext.at[pl.ds(T, 8), :], halo_b, {"dp": lax.rem(dp + 1, n_dp)}, behind).wait_recv()
        mext[0:8, :] = halo_b[...]

    @pl.when(dp == 0)
    def _():
        mext[0:8, :] = jnp.zeros((8, Uc), F32)

    cot_relay()
    cot_line.start(3)
    CH = B // 2

    def masks_of(at):
        count = jnp.concatenate([reach[at, :]] * (Uc // 128), axis=1)
        return jnp.minimum(count, 1.0), jnp.maximum(count - 1.0, 0.0)

    for i in range(T // CH):
        at = pl.ds(i * CH, CH)
        x = mext[pl.ds(i * CH, CH + 8), :]
        m1, m2 = masks_of(at)
        y = cw[0:1, :] * x[8 : 8 + CH]
        y = y + cw[1:2, :] * m1 * x[7 : 7 + CH]
        y = y + cw[2:3, :] * m2 * x[6 : 6 + CH]
        cout[at, :] = y
        gat[col, i * CH // B, i * CH % B : i * CH % B + CH, :] = (proj_o[1, at, :] * y).astype(BF)
    gated_in = links.send(gat.at[col], gat.at[col], to_col)
    cot_second()
    gated_in.wait_recv()

    loaded("out")
    n1_out.wait()
    all_sent()

    def out_partial(blk, put):
        for n0 in range(0, Dl, Dl // 2):
            n = slice(n0, n0 + Dl // 2)
            put(n0, nn(gat[0, blk], w_out_v[0, :, n]) + nn(gat[1, blk], w_out_v[1, :, n]))

    sent = row_sum(rs_s, rs_r, out_partial)

    def residual(r0):
        at = pl.ds(r0, 16)
        x = tok[at, :].astype(F32) + row_total(rs_r, at)
        resid[at, :] = x
        ss_s[1, at, :] = lanes(jnp.sum(x * x, axis=1, keepdims=True))

    cot_third()
    rows_loop(B, 16, residual)
    links.sent(*sent)
    col_total(1)

    def normed_two(r0):
        at = pl.ds(r0, 16)
        xall[row, at, :] = (resid[at, :] * scale_of(1, at) * g2[...]).astype(BF)

    rows_loop(B, 16, normed_two)
    relay, second_in, third_in, all_sent = gather(xall)
    n2_line.start(1)

    loaded("dn")
    ga_sent = []
    for blk in (row, row_a, row_b, row_d):
        x = call[blk]
        for n0 in range(0, Fc, Fc // 2):
            n = slice(n0, n0 + Fc // 2)
            act[col, blk, :, n] = nt(x, w_dn_v[other, n, :]).astype(BF)
        ga_sent.append(links.send(act.at[col, blk], ga_r.at[blk], to_col))
    relay()
    for blk in (row, row_a, row_b, row_d):
        x = call[blk]
        for n0 in range(0, Fc, Fc // 2):
            n = slice(n0, n0 + Fc // 2)
            ga_o[blk, :, n] = nt(x, w_dn_v[col, n, :])
    cot_out = local(call, cotz.at[dp])
    n2_line.start(2)

    def hidden_other(blk):
        def one(k, carry):
            for n0 in range(0, Fc, Fc // 2):
                n = slice(n0, n0 + Fc // 2)
                gh[col, blk, k, :, n] = nn(xall[blk], w_gu_v[other, k, :, n]).astype(BF)
            return carry

        lax.fori_loop(0, 2, one, 0)
        return links.send(gh.at[col, blk], hid_r.at[blk], to_col)

    loaded("gu")
    hid_sent = [hidden_other(row), hidden_other(row_a)]
    second_in()
    hid_sent.append(hidden_other(row_b))
    third_in()
    hid_sent.append(hidden_other(row_d))
    n2_out = local(xall, n2z.at[dp])
    cot_line.plane(1, 2)
    n2_line.start(3)

    gh_in = {}
    for name, blk in (("d", row_d), ("a", row_a), ("b", row_b), ("o", row)):

        def one(k, carry, blk=blk):
            for n0 in range(0, Fc, Fc // 2):
                n = slice(n0, n0 + Fc // 2)
                hid_o[k, :, n] = nn(xall[blk], w_gu_v[col, k, :, n])
            return carry

        lax.fori_loop(0, 2, one, 0)
        which = {"o": 0, "a": 1, "b": 2, "d": 3}[name]
        theirs = {"o": 0, "a": 2, "b": 1, "d": 3}[name]
        hid_sent[theirs].wait_recv()
        ga_sent[theirs].wait_recv()
        links.sent(hid_sent[which], ga_sent[which])

        def activate(r0, blk=blk):
            at = pl.ds(r0, 16)
            for n0 in range(0, Fc, Fc // 2):
                n = slice(n0, n0 + Fc // 2)
                gate = hid_o[0, at, n] + hid_r[blk, 0, at, n].astype(F32)
                up = hid_o[1, at, n] + hid_r[blk, 1, at, n].astype(F32)
                ga = ga_o[blk, at, n] + ga_r[blk, at, n].astype(F32)
                s = jax.nn.sigmoid(gate)
                silu = gate * s
                act[col, blk, at, n] = (silu * up).astype(BF)
                gh[col, blk, 0, at, n] = (ga * up * s * (1.0 + gate * (1.0 - s))).astype(BF)
                gh[col, blk, 1, at, n] = (ga * silu).astype(BF)

        rows_loop(B, 16, activate)
        gh_in[name] = (
            links.send(gh.at[col, blk], gh.at[col, blk], to_col),
            links.send(act.at[col, blk], act.at[col, blk], to_col),
        )
    cot_line.relay(1, 2)
    for pair in gh_in.values():
        for c in pair:
            c.wait_recv()
    size = actz.shape[-1]
    mine = pl.ds(pl.multiple_of(lax.rem(dp, half) * size, size), size)
    kept_units = [
        local(act.at[holder, :, :, mine], actz.at[dp]),
        local(gh.at[holder, :, :, :, mine], ghz.at[dp]),
    ]
    kept = []
    n2_out.wait()
    n2_line.sent(1)
    all_sent()

    def gu_partial(blk, put):
        for n0 in range(0, Dl, Dl // 4):
            n = slice(n0, n0 + Dl // 4)
            total = None
            for c in range(2):
                for k in range(2):
                    part = nt(gh[c, blk, k], w_gu_v[c, k, n, :])
                    total = part if total is None else total + part
            put(n0, total)

    sent = row_sum(rs_s, rs_r, gu_partial)

    def back_two(r0):
        at = pl.ds(r0, 16)
        g = row_total(rs_r, at)
        gres[at, :] = g
        ss_s[2, at, :] = lanes(jnp.sum(g * g2[...] * resid[at, :], axis=1, keepdims=True))

    rows_loop(B, 16, back_two)
    links.sent(*sent)
    col_total(2)

    def inner_of(place, at):
        return (ss_s[place, at, :] + ss_r[place, at, :])[:, :1]

    def branch(i, gain):
        at = pl.ds(pl.multiple_of(i * 16, 16), 16)
        g = gres[at, :]
        x = resid[at, :]
        s = scale_of(1, at)
        y = cot[at, :].astype(F32) + s * g2[...] * g - x * (s * s * s) * inner_of(2, at) / width
        gres[at, :] = y
        xall[row, at, :] = y.astype(BF)
        return gain + jnp.sum(g * x * s, axis=0, keepdims=True)

    cot_out.wait()
    cot_all_sent()
    n1_back = local(n1_h, call)
    gain_two = lax.fori_loop(0, B // 16, branch, jnp.zeros((1, Dl), F32))
    relay, second_in, third_in, all_sent = gather(xall)

    def down_partial(blk, put):
        for n0 in range(0, Dl, Dl // 2):
            n = slice(n0, n0 + Dl // 2)
            put(n0, nn(act[0, blk], w_dn_v[0, :, n]) + nn(act[1, blk], w_dn_v[1, :, n]))

    def put_to(ref):
        def put(n0, value):
            ref[:, n0 : n0 + value.shape[1]] = value.astype(ref.dtype)

        return put

    down_partial(row_d, put_to(rt_s.at[0]))
    down_partial(row_a, put_to(rt_s.at[1]))

    def gated_other(blk):
        gg_s[blk] = nt(xall[blk], w_out_v[other]).astype(BF)
        c = links.send(gg_s.at[blk], gg_r.at[blk], to_col)
        gg_o[blk] = nt(xall[blk], w_out_v[col])
        return c

    sent = [gated_other(row)]
    relay()
    down_partial(row, put_to(down_o))
    sent.append(gated_other(row_a))
    second_in()
    sent.append(gated_other(row_b))
    third_in()
    sent.append(gated_other(row_d))
    n2_line.plane(1)

    for blk, c in zip((row, row_b, row_a, row_d), sent):
        c.wait_recv()
        base = blk * B

        def conv_grad(r0, blk=blk, base=base):
            at = pl.ds(r0, 32)
            to = pl.ds(pl.multiple_of(base + r0, 32), 32)
            g = gg_o[blk, at, :] + gg_r[blk, at, :].astype(F32)
            gext[to, :] = g * proj_o[1, to, :]
            gp[col, blk, 1, at, :] = (g * cout[to, :]).astype(BF)

        rows_loop(B, 32, conv_grad)

    ahead = links.slot()

    @pl.when(dp > 0)
    def _():
        links.copy(gext.at[pl.ds(0, 8), :], halo_a, {"dp": lax.rem(dp + n_dp - 1, n_dp)}, ahead).start()

    @pl.when(dp < n_dp - 1)
    def _():
        links.copy(gext.at[pl.ds(0, 8), :], halo_a, {"dp": lax.rem(dp + n_dp - 1, n_dp)}, ahead).wait_recv()
        gext[T : T + 8, :] = halo_a[...]

    @pl.when(dp == n_dp - 1)
    def _():
        gext[T : T + 8, :] = jnp.zeros((8, Uc), F32)

    terms = [jnp.zeros((1, Uc), F32) for _ in range(3)]
    for i in range(T // CH):
        at = pl.ds(i * CH, CH)
        more = pl.ds(i * CH, CH + 8)
        x = mext[more, :]
        g = gext[more, :]
        m1, m2 = masks_of(more)
        now = g[:CH]
        terms[0] = terms[0] + jnp.sum(now * x[8 : 8 + CH], axis=0, keepdims=True)
        terms[1] = terms[1] + jnp.sum(m1[:CH] * now * x[7 : 7 + CH], axis=0, keepdims=True)
        terms[2] = terms[2] + jnp.sum(m2[:CH] * now * x[6 : 6 + CH], axis=0, keepdims=True)
        y = cw[0:1, :] * now
        y = y + cw[1:2, :] * (m1 * g)[1 : 1 + CH]
        y = y + cw[2:3, :] * (m2 * g)[2 : 2 + CH]
        blk, to = i * CH // B, slice(i * CH % B, i * CH % B + CH)
        gp[col, blk, 0, to, :] = (y * proj_o[2, at, :]).astype(BF)
        gp[col, blk, 2, to, :] = (y * proj_o[0, at, :]).astype(BF)
    red_s[...] = jnp.zeros_like(red_s)
    for k in range(3):
        red_s[2 + k : 3 + k, :Uc] = terms[k]
    gp_in = links.send(gp.at[col], gp.at[col], to_col)
    n2_line.relay(1)
    gp_in.wait_recv()
    if not split_in:
        kept.append(local(gp, d_in))

    def in_partial(blk, put):
        for n0 in range(0, Dl, Dl // 4):
            n = slice(n0, n0 + Dl // 4)
            total = None
            for c in range(2):
                for k in range(3):
                    part = nt(gp[c, blk, k], w_in_v[c, k, n, :])
                    total = part if total is None else total + part
            put(n0, total)

    po_all = []

    rows = po_r.shape[1]

    def out_chunk(z):
        return (z // half, pl.ds(pl.multiple_of(lax.rem(z, half) * rows, rows), rows), slice(None))

    def out_weights():
        for z in range(n_dp):
            at = pl.ds(z % half * rows, rows)
            g = lax.dot_general(
                gat[z // half, :, :, at].reshape(T, rows), xall[...].reshape(T, Dl),
                (((0,), (0,)), ((), ())), preferred_element_type=F32,
            )
            w_out_v[z // half, at, :] = g.astype(BF)
        for k in range(1, n_dp):
            po_all.append(links.send(w_out_v.at[out_chunk(peers[k])], po_r.at[dp], {"dp": peers[k]}))

    up_slots = [links.slot() for _ in range(n_dp)]
    down_slots = [links.slot() for _ in range(n_dp)]
    unit = 2 * Uc // n_dp

    def in_chunk(z):
        at = pl.ds(pl.multiple_of(lax.rem(z, half) * unit, unit), unit)
        return (z // half, slice(None), slice(None), at)

    def go_up(z):
        return links.copy(w_in_v.at[in_chunk(z)], in_up.at[z], {"dp": peers[1]}, up_slots[z])

    def go_down(z):
        return links.copy(w_in_v.at[in_chunk(z)], in_dn.at[z], {"dp": sources[1]}, down_slots[z])

    def in_weights():
        n1_back.wait()
        x = call[...].reshape(T, Dl)
        for c in range(2):
            for k in range(3):
                g = gp[c, :, k].reshape(T, Uc)
                for m0 in range(0, Dl, Dl // 2):
                    m = slice(m0, m0 + Dl // 2)
                    w_in_v[c, k, m, :] = lax.dot_general(
                        x[:, m], g, (((0,), (0,)), ((), ())), preferred_element_type=F32
                    ).astype(BF)
        for z in range(n_dp - 1, 0, -1):

            @pl.when(dp == 0)
            def _(z=z):
                go_up(z).start()

        for z in range(n_dp - 1):

            @pl.when(dp == n_dp - 1)
            def _(z=z):
                go_down(z).start()

    def take(src, z):
        at = in_chunk(z)
        for k in range(3):
            c = pltpu.make_async_copy(src.at[k], in_add, local_sems.at[local_sems.shape[0] - 1])
            c.start()
            c.wait()
            here = (at[0], k, slice(None), at[3])
            w_in_v[here] = (w_in_v[here].astype(F32) + in_add[...].astype(F32)).astype(BF)

    def in_step(i):
        z = n_dp - 1 - i

        @pl.when((dp > 0) & (dp < z))
        def _():
            go_up(z).wait_recv()
            take(in_up.at[z], z)
            go_up(z).start()

        @pl.when((dp < n_dp - 1) & (dp > i))
        def _():
            go_down(i).wait_recv()
            take(in_dn.at[i], i)
            go_down(i).start()

    def in_end():
        @pl.when(dp > 0)
        def _():
            for z in range(1, n_dp):

                @pl.when(dp == z)
                def _(z=z):
                    go_up(z).wait_recv()

            take(in_up.at[dp], dp)

        @pl.when(dp < n_dp - 1)
        def _():
            for z in range(n_dp - 1):

                @pl.when(dp == z)
                def _(z=z):
                    go_down(z).wait_recv()

            take(in_dn.at[dp], dp)

        out = local(w_in_v.at[in_chunk(dp)], d_in)
        for z in range(1, n_dp):

            @pl.when(dp < z)
            def _(z=z):
                go_up(z).wait_send()

        for z in range(n_dp - 1):

            @pl.when(dp > z)
            def _(z=z):
                go_down(z).wait_send()

        out.wait()

    def weights_wait():
        if split_in:
            in_weights()
        else:
            n1_back.wait()
        out_weights()

    sent_in = row_sum(rs_s, rs_r, in_partial, filler=weights_wait)
    n2_line.plane(*range(2, min(3, n_dp)))
    down_sent = [
        links.send(rt_s.at[0], rt_r.at[0], to_a),
        links.send(rt_s.at[1], rt_r.at[1], to_a),
    ]
    down_partial(row_b, put_to(acc_b))

    def back_one(r0):
        at = pl.ds(r0, 16)
        g = row_total(rs_r, at)
        d_tok[at, :] = g
        ss_s[3, at, :] = lanes(
            jnp.sum(g * g1[...] * tok[at, :].astype(F32), axis=1, keepdims=True)
        )

    rows_loop(B, 16, back_one)
    col_total(3)

    def token_grad(i, gain):
        at = pl.ds(pl.multiple_of(i * 16, 16), 16)
        g = d_tok[at, :]
        x = tok[at, :].astype(F32)
        s = scale_of(0, at)
        y = gres[at, :] + s * g1[...] * g - x * (s * s * s) * inner_of(3, at) / width
        d_tok[at, :] = y
        return gain + jnp.sum(g * x * s, axis=0, keepdims=True)

    gain_one = lax.fori_loop(0, B // 16, token_grad, jnp.zeros((1, Dl), F32))

    red_s[0:1, :] = gain_one
    red_s[1:2, :] = gain_two
    c0 = links.send(red_s, red_r.at[0], to_a)
    n2_line.relay(*range(2, min(3, n_dp)))
    n2_line.plane(*range(3, n_dp))
    cot_line.plane(*range(3, n_dp))
    for c in kept_units:
        c.wait()
    for pair in gh_in.values():
        links.sent(*pair)
    all_sent()

    slots = Fc // size

    def place(k, r, rank):
        q = (k - 1) * 2 + r
        lanes_at = slice(q % slots * size, q % slots * size + size)
        return (q // slots, *([slice(None)] * (rank - 2)), lanes_at)

    def again(k):
        z = peers[k]
        loads = [local(n2z.at[z], xall), local(cotz.at[z], call)]
        for c in loads:
            c.wait()
        copies = []
        for core, keep in ((other, False), (col, True)):
            x = xall[pl.ds(core * 2, 2)].reshape(2 * B, Dl)
            for j in range(2):
                h = nn(x, w_gu_v[holder, j, :, mine])
                for r in range(2):
                    if keep:
                        hid_o[j, :, r * size : r * size + size] = h[r * B : r * B + B]
                    else:
                        q, _, _, n = place(k, r, 4)
                        gh[0, q, j, :, n] = h[r * B : r * B + B].astype(BF)
            y = call[pl.ds(core * 2, 2)].reshape(2 * B, Dl)
            g = nt(y, w_dn_v[holder, mine, :])
            for r in range(2):
                if keep:
                    ga_o[r, :, :size] = g[r * B : r * B + B]
                else:
                    q, _, n = place(k, r, 3)
                    act[0, q, :, n] = g[r * B : r * B + B].astype(BF)
            if not keep:
                for r in range(2):
                    h_at, g_at = place(k, r, 4), place(k, r, 3)
                    copies.append(links.send(gh.at[0].at[h_at], hid_r.at[h_at], to_col))
                    copies.append(links.send(act.at[0].at[g_at], ga_r.at[g_at], to_col))
        for c in copies:
            c.wait_recv()
        done = []
        for r in range(2):
            q, _, n = place(k, r, 3)

            def finish(r0, r=r, q=q, n=n):
                at = pl.ds(r0, 16)
                own = slice(r * size, r * size + size)
                gate = hid_o[0, at, own] + hid_r[q, 0, at, n].astype(F32)
                up = hid_o[1, at, own] + hid_r[q, 1, at, n].astype(F32)
                ga = ga_o[r, at, :size] + ga_r[q, at, n].astype(F32)
                s = jax.nn.sigmoid(gate)
                silu = gate * s
                act[1, q, at, n] = (silu * up).astype(BF)
                gh[1, q, 0, at, n] = (ga * up * s * (1.0 + gate * (1.0 - s))).astype(BF)
                gh[1, q, 1, at, n] = (ga * silu).astype(BF)

            rows_loop(B, 16, finish)
            blk = col * 2 + r
            h_src, a_src = gh.at[1].at[place(k, r, 4)], act.at[1].at[place(k, r, 3)]
            done.append(links.send(h_src, ghz.at[z, blk], to_col))
            done.append(links.send(a_src, actz.at[z, blk], to_col))
            kept.append(local(h_src, ghz.at[z, blk]))
            kept.append(local(a_src, actz.at[z, blk]))
        return done

    n2_line.finish(1)
    cot_line.finish(1, 2)
    again_in = again(1)
    if split_in:
        in_step(0)

    down_sent[0].wait_recv()

    def down_combine(r0):
        at = pl.ds(r0, 16)
        rt_s[2, at, :] = (acc_b[at, :] + rt_r[0, at, :].astype(F32)).astype(BF)

    rows_loop(B, 16, down_combine)
    down_sent.append(links.send(rt_s.at[2], rt_r.at[2], to_b))
    c0.wait_recv()
    links.sent(c0)
    red_s[0:2, :] = red_s[0:2, :] + red_r[0, 0:2, :]
    c1 = links.send(red_s, red_r.at[1], to_b)
    n2_line.relay(*range(3, n_dp))
    cot_line.relay(*range(3, n_dp))
    n2_line.finish(2)
    again_in += again(2)
    if split_in:
        for i in range(1, n_dp - 2):
            in_step(i)
    c1.wait_recv()
    red_z[dp] = red_s[...]
    red_z[dp, 0:2, :] = red_s[0:2, :] + red_r[1, 0:2, :]
    arrived = []
    for k in range(1, n_dp):
        arrived.append(links.send(red_z.at[dp], red_z.at[dp], {"dp": lax.rem(dp + k, n_dp)}))
    for k in range(3, n_dp):
        n2_line.finish(k)
        cot_line.finish(k)
        again_in += again(k)
    for c in down_sent[1:]:
        c.wait_recv()

    def block_rows(r0):
        at = pl.ds(r0, 16)
        total = down_o[at, :] + rt_r[1, at, :].astype(F32) + rt_r[2, at, :].astype(F32)
        block_out[at, :] = (resid[at, :] + total).astype(BF)

    rows_loop(B, 16, block_rows)
    for c in arrived:
        c.wait_recv()
    total = red_z[0]
    for k in range(1, n_dp):
        total = total + red_z[k]
    d_gain[...] = total
    d_conv[...] = total[:, :Uc]

    @pl.when(dp < n_dp - 1)
    def _():
        links.copy(mext.at[pl.ds(T, 8), :], halo_b, {"dp": lax.rem(dp + 1, n_dp)}, behind).wait_send()

    @pl.when(dp > 0)
    def _():
        links.copy(gext.at[pl.ds(0, 8), :], halo_a, {"dp": lax.rem(dp + n_dp - 1, n_dp)}, ahead).wait_send()

    for c in again_in:
        c.wait_recv()
    for c in po_all:
        c.wait_recv()
    out_total = w_out_v[out_chunk(dp)].astype(F32)
    for k in range(1, n_dp):
        out_total = out_total + po_r[peers[k]].astype(F32)
    d_out[...] = out_total
    if split_in:
        in_end()
    cot_line.sent(1)
    for hop in range(2, n_dp):
        for line in (cot_line, n2_line):
            line.sent(hop)
    for c in kept:
        c.wait()
    assert links.count <= send_sems.shape[0]
    links.close()


def run_block(n_dp, width, split_in, tok, g1, w_in, cw, w_out, g2, w_gu, w_dn, cot, lengths):
    B, Dl = tok.shape
    R = 4
    T = R * B
    Uc = w_out.shape[0] // 2
    Fc = w_dn.shape[0] // 2
    vm = lambda shape, kind=BF: pltpu.VMEM(shape, kind)
    any_spec, vmem_spec = pl.BlockSpec(memory_space=pl.ANY), pl.BlockSpec(memory_space=pltpu.VMEM)
    shape = jax.ShapeDtypeStruct
    rows = shape((n_dp, R, B, Dl), BF)
    return pl.pallas_call(
        functools.partial(block_kernel, n_dp, width, split_in),
        out_shape=(
            shape((B, Dl), BF),
            shape((B, Dl), F32),
            shape((8, Dl), F32),
            shape((8, Uc), F32),
            shape((2 * Uc // n_dp, Dl), F32),
            shape((R, B, Dl), BF),
            rows,
            rows,
            shape((n_dp, R, B, 2 * Fc // n_dp), BF),
            shape((n_dp, R, 2, B, 2 * Fc // n_dp), BF),
            shape((3, Dl, 2 * Uc // n_dp) if split_in else (2, R, 3, B, Uc), BF),
            shape((n_dp, 3, Dl, 2 * Uc // n_dp), BF),
            shape((n_dp, 3, Dl, 2 * Uc // n_dp), BF),
        ),
        in_specs=[
            vmem_spec, vmem_spec, any_spec, vmem_spec, any_spec, vmem_spec,
            any_spec, any_spec, vmem_spec, pl.BlockSpec(memory_space=pltpu.SMEM),
        ],
        out_specs=[vmem_spec] * 5 + [any_spec] * 8,
        scratch_shapes=[
            vm((2, 3, Dl, Uc)), vm((2, Uc, Dl)), vm((2, 2, Dl, Fc)), vm((2, Fc, Dl)),
            vm((R, B, Dl)), vm((R, B, Dl)),
            vm((2, R, B, Uc)), vm((2, R, B, Fc)), vm((2, R, 2, B, Fc)), vm((2, R, 3, B, Uc)),
            vm((3, T, Uc), F32), vm((R, 3, B, Uc)), vm((T + 8, Uc), F32), vm((8, Uc), F32),
            vm((T, Uc), F32), vm((T + 8, Uc), F32), vm((8, Uc), F32),
            vm((R, B, Uc)), vm((R, B, Uc)), vm((R, B, Uc), F32),
            vm((2, B, Fc), F32), vm((R, 2, B, Fc)), vm((R, B, Fc), F32), vm((R, B, Fc)),
            vm((3, B, Dl)), vm((3, B, Dl)), vm((3, B, Dl)), vm((3, B, Dl)),
            vm((B, Dl), F32), vm((B, Dl), F32), vm((B, Dl), F32),
            vm((B, Dl), F32), vm((B, Dl), F32),
            vm((4, B, 128), F32), vm((4, B, 128), F32),
            vm((8, Dl), F32), vm((2, 8, Dl), F32), vm((n_dp, 8, Dl), F32),
            vm((n_dp, 2 * Uc // n_dp, Dl)),
            vm((1, Dl), F32), vm((1, Dl), F32), vm((3, Uc), F32),
            vm((T + 16, 128), F32), vm((Dl, 2 * Uc // n_dp)),
            pltpu.SemaphoreType.DMA((96 + 48 * n_dp,)), pltpu.SemaphoreType.DMA((96 + 48 * n_dp,)),
            pltpu.SemaphoreType.DMA((32 + 6 * n_dp,)),
        ],
        compiler_params=pltpu.CompilerParams(
            collective_id=0, has_side_effects=True, vmem_limit_bytes=VMEM_LIMIT
        ),
        name="block",
    )(tok, g1, w_in, cw, w_out, g2, w_gu, w_dn, cot, lengths)


def weights_kernel(n2, cot, act, gh, gu_out, dn_out, gu_acc):
    _, R, B, Dl = n2.shape
    T, size = R * B, act.shape[-1]
    step, tile = pl.program_id(0), 256

    def tn(a, b):
        return lax.dot_general(a, b, (((0,), (0,)), ((), ())), preferred_element_type=F32)

    @pl.when(step == 0)
    def _():
        gu_acc[...] = jnp.zeros_like(gu_acc)
        dn_out[...] = jnp.zeros_like(dn_out)

    g = jnp.concatenate([gh[0, :, k].reshape(T, size) for k in range(2)], axis=1)
    for m in range(0, Dl, tile):
        at = slice(m, m + tile)
        gu_acc[at, :] += tn(n2[0, :, :, at].reshape(T, tile), g)
    c = cot[0].reshape(T, Dl)
    for m in range(0, size, min(tile, size)):
        at = slice(m, m + min(tile, size))
        dn_out[at, :] += tn(act[0, :, :, at].reshape(T, min(tile, size)), c)

    @pl.when(step == pl.num_programs(0) - 1)
    def _():
        parts = 2 * size // 128
        for p in range(parts):
            gu_out[pl.ds(p, Dl, stride=parts), :] = gu_acc[:, p * 128 : p * 128 + 128]


def run_weights(n2, cot, act, gh):
    n_dp, R, B, Dl = n2.shape
    size = act.shape[-1]
    whole = lambda *shape: pl.BlockSpec(shape, lambda z: (0,) * len(shape))
    one = lambda a: pl.BlockSpec((1, *a.shape[1:]), lambda z: (z,) + (0,) * (len(a.shape) - 1))
    out = ((Dl * 2 * size // 128, 128), (size, Dl))
    return pl.pallas_call(
        weights_kernel,
        grid=(n_dp,),
        out_shape=[jax.ShapeDtypeStruct(o, F32) for o in out],
        in_specs=[one(n2), one(cot), one(act), one(gh)],
        out_specs=[whole(*o) for o in out],
        scratch_shapes=[pltpu.VMEM((Dl, 2 * size), F32)],
        compiler_params=pltpu.CompilerParams(vmem_limit_bytes=VMEM_LIMIT),
        name="weights",
    )(n2, cot, act, gh)


def on_device(
    tokens, gain_one, in_weight, conv_weight, out_weight, gain_two, gate_up_weight, down_weight,
    cotangent, lengths,
):
    n_dp = lax.axis_size("dp")
    B, Dl = tokens.shape
    width = Dl * lax.axis_size("col")
    chunk = in_weight.shape[2] // n_dp
    split_in = chunk % 128 == 0
    block_out, d_tok, d_gain, d_conv, d_out, n1, n2, cot, act, gh, d_in, _, _ = run_block(
        n_dp,
        float(width),
        split_in,
        tokens,
        gain_one[None, :],
        jnp.transpose(in_weight, (1, 0, 2)),
        conv_weight,
        out_weight,
        gain_two[None, :],
        jnp.transpose(gate_up_weight, (1, 0, 2)),
        down_weight,
        cotangent,
        lengths,
    )
    d_gu, d_down = run_weights(n2, cot, act, gh)
    if split_in:
        d_in = jnp.transpose(d_in, (1, 0, 2)).astype(F32)
    else:
        d_in = lax.psum_scatter(
            jnp.einsum("rti,crktu->ikcu", n1, d_in, preferred_element_type=F32)
            .reshape(Dl, 3, -1)
            .astype(BF),
            "dp",
            scatter_dimension=2,
            tiled=True,
        ).astype(F32)
    part = d_conv.shape[1] * 1 // n_dp
    mine = lax.dynamic_slice(d_conv, (2, lax.axis_index("dp") * part), (3, part))
    return (
        block_out,
        d_tok,
        d_gain[0],
        d_in.reshape(Dl, 3, 1, 1, -1),
        mine.reshape(3, 1, 1, part),
        d_out.reshape(1, 1, -1, Dl),
        d_gain[1],
        d_gu.reshape(Dl, 2, 1, 1, -1),
        d_down.reshape(1, 1, -1, Dl),
    )


def solution(mesh):
    placed = (
        P(("dp", "row"), "col"),
        P("col"),
        P("col", None, "row"),
        P(None, ("row", "col")),
        P("row", "col"),
        P("col"),
        P("col", None, "row"),
        P("row", "col"),
        P(("dp", "row"), "col"),
        P(),
    )
    return jax.shard_map(
        on_device,
        mesh=mesh,
        in_specs=placed,
        out_specs=(
            P(("dp", "row"), "col"),
            P(("dp", "row"), "col"),
            P("col"),
            P("col", None, "row", "dp", None),
            P(None, ("row", "col"), "dp", None),
            P("row", "dp", None, "col"),
            P("col"),
            P("col", None, "row", "dp", None),
            P("row", "dp", None, "col"),
        ),
        check_vma=False,
    )
```

```python
import functools

import jax
import jax.numpy as jnp
from jax import lax
from jax.experimental import pallas as pl
from jax.experimental.pallas import tpu as pltpu
from jax.sharding import PartitionSpec as P

MESH = pl.DeviceIdType.MESH
BF = jnp.bfloat16
F32 = jnp.float32
EPS = 1e-05
VMEM_LIMIT = 63 * 2**20


def nn(a, b):
    return lax.dot_general(a, b, (((1,), (0,)), ((), ())), preferred_element_type=F32)


def nt(a, b):
    return lax.dot_general(a, b, (((1,), (1,)), ((), ())), preferred_element_type=F32)


class Links:
    def __init__(self, send_sems, recv_sems):
        self.send_sems, self.recv_sems = send_sems, recv_sems
        self.count = 0
        self.open = []

    def slot(self):
        self.count += 1
        return self.count - 1

    def copy(self, src, dst, to, slot=None):
        if slot is None:
            slot = self.slot()
        return pltpu.make_async_remote_copy(
            src_ref=src,
            dst_ref=dst,
            send_sem=self.send_sems.at[slot],
            recv_sem=self.recv_sems.at[slot],
            device_id=to,
            device_id_type=MESH,
        )

    def send(self, src, dst, to):
        c = self.copy(src, dst, to)
        c.start()
        self.open.append(c)
        return c

    def sent(self, *copies):
        for c in copies:
            c.wait_send()
            self.open = [o for o in self.open if o is not c]

    def close(self):
        for c in self.open:
            c.wait_send()
        self.open = []


def rows_loop(count, step, body):
    def one(i, carry):
        body(pl.multiple_of(i * step, step))
        return carry

    lax.fori_loop(0, count // step, one, 0)


def block_kernel(n_dp, width, split_in, *refs):
    (
        tok, g1_in, w_in, cw_in, w_out, g2_in, w_gu, w_dn, cot, lengths,
        block_out, d_tok, d_gain, d_conv, d_out, n1_h, n2z, cotz, actz, ghz, d_in, in_up, in_dn,
        w_in_v, w_out_v, w_gu_v, w_dn_v,
        xall, call, gat, act, gh, gp,
        proj_o, proj_r, mext, halo_b, cout, gext, halo_a, gg_s, gg_r, gg_o,
        hid_o, hid_r, ga_o, ga_r,
        rs_s, rs_r, rt_s, rt_r, acc_b, acc_o, down_o,
        resid, gres, ss_s, ss_r, red_s, red_r, red_z, po_r,
        g1, g2, cw, reach, in_add,
        send_sems, recv_sems, local_sems,
    ) = refs
    R, B, Dl = xall.shape
    Uc = w_out_v.shape[1]
    Fc = w_dn_v.shape[1]
    T = R * B
    dp, row, col = lax.axis_index("dp"), lax.axis_index("row"), lax.axis_index("col")
    other = 1 - col
    low = row + 1 - 2 * lax.rem(row, 2)
    high = row + 2 - 4 * lax.rem(row // 2, 2)
    row_a = low * other + high * col
    row_b = high * other + low * col
    row_d = low + high - row
    to_a, to_b, to_col = {"row": row_a}, {"row": row_b}, {"col": other}
    links = Links(send_sems, recv_sems)
    half = n_dp // 2
    holder = dp // half
    peers = [lax.rem(dp + k, n_dp) for k in range(n_dp)]
    sources = [lax.rem(dp + n_dp - k, n_dp) for k in range(n_dp)]

    loads = {"in": [], "out": [], "gu": [], "dn": []}
    n_local = 0

    def local(src, dst):
        nonlocal n_local
        c = pltpu.make_async_copy(src, dst, local_sems.at[n_local])
        n_local += 1
        c.start()
        return c

    for c in range(2):
        for k in range(3):
            loads["in"].append(local(w_in.at[k, :, pl.ds(c * Uc, Uc)], w_in_v.at[c, k]))
    for c in range(2):
        loads["dn"].append(local(w_dn.at[pl.ds(c * Fc, Fc), :], w_dn_v.at[c]))
        loads["out"].append(local(w_out.at[pl.ds(c * Uc, Uc), :], w_out_v.at[c]))
    for c in range(2):
        for k in range(2):
            loads["gu"].append(local(w_gu.at[k, :, pl.ds(c * Fc, Fc)], w_gu_v.at[c, k]))

    def loaded(name):
        for c in loads[name]:
            c.wait()

    barrier = pltpu.get_barrier_semaphore()
    for to in (to_col, {"row": low}, {"row": high}):
        pl.semaphore_signal(barrier, inc=1, device_id=to, device_id_type=MESH)
    for k in range(1, n_dp):
        pl.semaphore_signal(
            barrier, inc=1, device_id={"dp": lax.rem(dp + k, n_dp)}, device_id_type=MESH
        )

    def col_total(place):
        c = links.send(ss_s.at[place], ss_r.at[place], to_col)
        c.wait_recv()

    def gather(buf):
        first = links.send(buf.at[row], buf.at[row], to_a)
        second = links.send(buf.at[row], buf.at[row], to_b)
        state = {}

        def relay():
            first.wait_recv()
            state["third"] = links.send(buf.at[row_a], buf.at[row_a], to_b)

        def second_in():
            second.wait_recv()

        def third_in():
            state["third"].wait_recv()

        def all_sent():
            links.sent(first, second, state["third"])

        return relay, second_in, third_in, all_sent

    class Line:
        def __init__(self, first, dst, block=None):
            self.first, self.dst, self.block = first, dst, row if block is None else block
            self.up = [links.slot() for _ in range(n_dp + 1)]
            self.down = [links.slot() for _ in range(n_dp + 1)]
            self.sent_to, self.last = {}, {}

        def at(self, z):
            return self.dst.at[z, self.block]

        def up_copy(self, hop):
            at = self.at(lax.rem(dp + n_dp - (hop - 1), n_dp))
            src = self.first if hop == 1 else at
            return links.copy(src, at, {"dp": peers[1]}, self.up[hop])

        def down_copy(self, hop):
            at = self.at(lax.rem(dp + hop - 1, n_dp))
            src = self.first if hop == 1 else at
            return links.copy(src, at, {"dp": sources[1]}, self.down[hop])

        def arrived(self, hop):
            @pl.when(dp >= hop)
            def _():
                self.up_copy(hop).wait_recv()

            @pl.when(dp + hop < n_dp)
            def _():
                self.down_copy(hop).wait_recv()

        def start(self, hop):
            if hop > 1:
                self.arrived(hop - 1)

            @pl.when((dp + 1 < n_dp) & (dp >= hop - 1))
            def _():
                self.up_copy(hop).start()

            @pl.when((dp >= 1) & (dp + hop - 1 < n_dp))
            def _():
                self.down_copy(hop).start()

        def sent(self, hop):
            @pl.when((dp + 1 < n_dp) & (dp >= hop - 1))
            def _():
                self.up_copy(hop).wait_send()

            @pl.when((dp >= 1) & (dp + hop - 1 < n_dp))
            def _():
                self.down_copy(hop).wait_send()

        def rest(self):
            for hop in range(4, n_dp):
                self.start(hop)
            self.arrived(n_dp - 1)

        def plane(self, *ks):
            if not self.sent_to:
                self.rest()
            for k in ks:
                at = self.dst.at[peers[k], row]
                self.sent_to[k] = (links.send(at, at, to_a), links.send(at, at, to_b))

        def relay(self, *ks):
            for k in ks:
                first, second = self.sent_to[k]
                first.wait_recv()
                at = self.dst.at[peers[k], row_a]
                self.last[k] = (second, links.send(at, at, to_b))

        def finish(self, *ks):
            for k in ks:
                for c in self.last[k]:
                    c.wait_recv()

    def put_to(ref):
        def put(n0, value):
            ref[:, n0 : n0 + value.shape[1]] = value.astype(ref.dtype)

        return put

    def both(first, second):
        def put(n0, value):
            first(n0, value[:B])
            second(n0, value[B:])

        return put

    def two(buf, blk, other_blk):
        return jnp.concatenate([buf[blk], buf[other_blk]], axis=0)

    def row_sum(sends, recvs, partial, filler=None):
        partial(row_d, row_a, both(put_to(sends.at[0]), put_to(sends.at[1])))
        c0 = links.send(sends.at[0], recvs.at[0], to_a)
        c1 = links.send(sends.at[1], recvs.at[1], to_a)
        partial(row_b, row, both(put_to(acc_b), put_to(acc_o)))
        c0.wait_recv()

        def combine(r0):
            at = pl.ds(r0, 32)
            sends[2, at, :] = (acc_b[at, :] + recvs[0, at, :].astype(F32)).astype(BF)

        rows_loop(B, 32, combine)
        c2 = links.send(sends.at[2], recvs.at[2], to_b)
        if filler is not None:
            filler()
        c1.wait_recv()
        c2.wait_recv()
        return c0, c1, c2

    def row_total(recvs, at):
        return acc_o[at, :] + recvs[1, at, :].astype(F32) + recvs[2, at, :].astype(F32)

    def lanes(x):
        return jnp.broadcast_to(x, (x.shape[0], 128))

    g1[...] = g1_in[...].astype(F32)
    g2[...] = g2_in[...].astype(F32)
    cw[...] = cw_in[...].astype(F32)
    starts = [jnp.int32(0)]
    for i in range(lengths.shape[0] - 1):
        starts.append(starts[-1] + lengths[i])

    def masks(r0):
        t = dp * T + r0 + lax.broadcasted_iota(jnp.int32, (16, 128), 0)
        count = jnp.full((16, 128), 2.0, F32)
        for start in starts:
            away = t - start
            count = jnp.where((away >= 0) & (away < 2), away.astype(F32), count)
        reach[pl.ds(r0, 16), :] = count

    rows_loop(T + 16, 16, masks)

    def squares(r0):
        at = pl.ds(r0, 32)
        x = tok[at, :].astype(F32)
        ss_s[0, at, :] = lanes(jnp.sum(x * x, axis=1, keepdims=True))

    rows_loop(B, 32, squares)
    pl.semaphore_wait(barrier, 3 + n_dp - 1)
    cot_line = Line(cot, cotz)
    n2_line = Line(xall.at[row], n2z)
    cot_line.start(1)
    col_total(0)

    def scale_of(place, at):
        return lax.rsqrt((ss_s[place, at, :] + ss_r[place, at, :]) / width + EPS)[:, :1]

    def normed_one(r0):
        at = pl.ds(r0, 32)
        x = tok[at, :].astype(F32)
        xall[row, at, :] = (x * scale_of(0, at) * g1[...]).astype(BF)

    rows_loop(B, 32, normed_one)
    relay, second_in, third_in, all_sent = gather(xall)

    def project(blk, other_blk):
        x = two(xall, blk, other_blk)
        for k in range(3):
            y = nn(x, w_in_v[other, k]).astype(BF)
            gp[col, blk, k] = y[:B]
            gp[col, other_blk, k] = y[B:]
        copies = [links.send(gp.at[col, b], proj_r.at[b], to_col) for b in (blk, other_blk)]
        for k in range(3):
            y = nn(x, w_in_v[col, k])
            proj_o[k, pl.ds(pl.multiple_of(blk * B, B), B), :] = y[:B]
            proj_o[k, pl.ds(pl.multiple_of(other_blk * B, B), B), :] = y[B:]
        return copies

    loaded("in")
    relay()
    sent = project(row, row_a)
    cot_line.start(2)
    second_in()
    third_in()
    call[row] = cot[...]
    cot_relay, cot_second, cot_third, cot_all_sent = gather(call)
    sent += project(row_b, row_d)
    n1_out = local(xall, n1_h)

    for blk, c in zip((row, row_b, row_a, row_d), sent):
        c.wait_recv()
        base = blk * B

        def add(r0, blk=blk, base=base):
            at = pl.ds(r0, 32)
            to = pl.ds(pl.multiple_of(base + r0, 32), 32)
            g = [proj_o[k, to, :] + proj_r[blk, k, at, :].astype(F32) for k in range(3)]
            for k in range(3):
                proj_o[k, to, :] = g[k]
            mext[pl.ds(pl.multiple_of(base + r0 + 8, 8), 32), :] = g[0] * g[2]

        rows_loop(B, 32, add)
    links.sent(*sent)

    behind = links.slot()

    @pl.when(dp < n_dp - 1)
    def _():
        links.copy(mext.at[pl.ds(T, 8), :], halo_b, {"dp": lax.rem(dp + 1, n_dp)}, behind).start()

    @pl.when(dp > 0)
    def _():
        links.copy(mext.at[pl.ds(T, 8), :], halo_b, {"dp": lax.rem(dp + 1, n_dp)}, behind).wait_recv()
        mext[0:8, :] = halo_b[...]

    @pl.when(dp == 0)
    def _():
        mext[0:8, :] = jnp.zeros((8, Uc), F32)

    cot_relay()
    cot_line.start(3)
    CH = B // 2

    def masks_of(at):
        count = jnp.concatenate([reach[at, :]] * (Uc // 128), axis=1)
        return jnp.minimum(count, 1.0), jnp.maximum(count - 1.0, 0.0)

    for i in range(T // CH):
        at = pl.ds(i * CH, CH)
        x = mext[pl.ds(i * CH, CH + 8), :]
        m1, m2 = masks_of(at)
        y = cw[0:1, :] * x[8 : 8 + CH]
        y = y + cw[1:2, :] * m1 * x[7 : 7 + CH]
        y = y + cw[2:3, :] * m2 * x[6 : 6 + CH]
        cout[at, :] = y
        gat[col, i * CH // B, i * CH % B : i * CH % B + CH, :] = (proj_o[1, at, :] * y).astype(BF)
    gated_in = links.send(gat.at[col], gat.at[col], to_col)
    cot_second()
    gated_in.wait_recv()

    loaded("out")
    n1_out.wait()
    all_sent()

    def out_partial(blk, other_blk, put):
        x = [two(gat.at[c], blk, other_blk) for c in range(2)]
        for n0 in range(0, Dl, Dl // 4):
            n = slice(n0, n0 + Dl // 4)
            put(n0, nn(x[0], w_out_v[0, :, n]) + nn(x[1], w_out_v[1, :, n]))

    sent = row_sum(rs_s, rs_r, out_partial)

    def residual(r0):
        at = pl.ds(r0, 32)
        x = tok[at, :].astype(F32) + row_total(rs_r, at)
        resid[at, :] = x
        ss_s[1, at, :] = lanes(jnp.sum(x * x, axis=1, keepdims=True))

    cot_third()
    rows_loop(B, 32, residual)
    links.sent(*sent)
    col_total(1)

    def normed_two(r0):
        at = pl.ds(r0, 32)
        xall[row, at, :] = (resid[at, :] * scale_of(1, at) * g2[...]).astype(BF)

    rows_loop(B, 32, normed_two)
    relay, second_in, third_in, all_sent = gather(xall)
    n2_line.start(1)

    loaded("dn")
    ga_step = min(Fc, 256)

    def ga_other(i, carry):
        n = pl.ds(pl.multiple_of(i * ga_step, ga_step), ga_step)
        y = nt(call[...].reshape(T, Dl), w_dn_v[other, n, :]).astype(BF)
        act[col, :, :, n] = y.reshape(R, B, ga_step)
        return carry

    def ga_own(i, carry):
        n = pl.ds(pl.multiple_of(i * ga_step, ga_step), ga_step)
        ga_o[:, :, n] = nt(call[...].reshape(T, Dl), w_dn_v[col, n, :]).reshape(R, B, ga_step)
        return carry

    lax.fori_loop(0, Fc // ga_step, ga_other, 0)
    ga_sent = links.send(act.at[col], ga_r, to_col)
    relay()
    lax.fori_loop(0, Fc // ga_step, ga_own, 0)
    cot_out = local(call, cotz.at[dp])
    n2_line.start(2)

    def hidden_other(blk, other_blk):
        def one(k, carry):
            x = two(xall, blk, other_blk)
            for n0 in range(0, Fc, Fc // 2):
                n = slice(n0, n0 + Fc // 2)
                y = nn(x, w_gu_v[other, k, :, n]).astype(BF)
                gh[col, blk, k, :, n] = y[:B]
                gh[col, other_blk, k, :, n] = y[B:]
            return carry

        lax.fori_loop(0, 2, one, 0)
        return [links.send(gh.at[col, b], hid_r.at[b], to_col) for b in (blk, other_blk)]

    loaded("gu")
    hid_sent = hidden_other(row, row_a)
    second_in()
    third_in()
    hid_sent += hidden_other(row_b, row_d)
    n2_out = local(xall, n2z.at[dp])
    cot_line.plane(1, 2)
    n2_line.start(3)

    gh_in = {}
    ga_sent.wait_recv()
    links.sent(ga_sent)
    H = Fc // 2
    for blks, mine_at, theirs_at in (((row_d, row_a), (3, 1), (3, 2)), ((row_b, row), (2, 0), (1, 0))):
        for h in range(2):

            def one(k, carry, h=h, blks=blks):
                y = nn(two(xall, *blks), w_gu_v[col, k, :, h * H : h * H + H])
                hid_o[k, :, :H] = y[:B]
                hid_o[k, :, H:] = y[B:]
                return carry

            lax.fori_loop(0, 2, one, 0)
            for i, blk in enumerate(blks):
                if h == 0:
                    hid_sent[theirs_at[i]].wait_recv()
                    links.sent(hid_sent[mine_at[i]])

                def activate(r0, blk=blk, i=i, h=h):
                    at = pl.ds(r0, 32)
                    n = slice(h * H, h * H + H)
                    own = slice(i * H, i * H + H)
                    gate = hid_o[0, at, own] + hid_r[blk, 0, at, n].astype(F32)
                    up = hid_o[1, at, own] + hid_r[blk, 1, at, n].astype(F32)
                    ga = ga_o[blk, at, n] + ga_r[blk, at, n].astype(F32)
                    s = jax.nn.sigmoid(gate)
                    silu = gate * s
                    act[col, blk, at, n] = (silu * up).astype(BF)
                    gh[col, blk, 0, at, n] = (ga * up * s * (1.0 + gate * (1.0 - s))).astype(BF)
                    gh[col, blk, 1, at, n] = (ga * silu).astype(BF)

                rows_loop(B, 32, activate)
                if h == 1:
                    gh_in[mine_at[i]] = (
                        links.send(gh.at[col, blk], gh.at[col, blk], to_col),
                        links.send(act.at[col, blk], act.at[col, blk], to_col),
                    )
    cot_line.relay(1, 2)
    for pair in gh_in.values():
        for c in pair:
            c.wait_recv()
    size = actz.shape[-1]
    mine = pl.ds(pl.multiple_of(lax.rem(dp, half) * size, size), size)
    kept_units = [
        local(act.at[holder, :, :, mine], actz.at[dp]),
        local(gh.at[holder, :, :, :, mine], ghz.at[dp]),
    ]
    kept = []
    n2_out.wait()
    n2_line.sent(1)
    all_sent()

    def gu_partial(blk, other_blk, put):
        for n0 in range(0, Dl, Dl // 4):
            n = slice(n0, n0 + Dl // 4)
            total = None
            for c in range(2):
                for k in range(2):
                    part = nt(two(gh.at[c, :, k], blk, other_blk), w_gu_v[c, k, n, :])
                    total = part if total is None else total + part
            put(n0, total)

    sent = row_sum(rs_s, rs_r, gu_partial)

    def back_two(r0):
        at = pl.ds(r0, 32)
        g = row_total(rs_r, at)
        gres[at, :] = g
        ss_s[2, at, :] = lanes(jnp.sum(g * g2[...] * resid[at, :], axis=1, keepdims=True))

    rows_loop(B, 32, back_two)
    links.sent(*sent)
    col_total(2)

    def inner_of(place, at):
        return (ss_s[place, at, :] + ss_r[place, at, :])[:, :1]

    def branch(i, gain):
        at = pl.ds(pl.multiple_of(i * 32, 32), 32)
        g = gres[at, :]
        x = resid[at, :]
        s = scale_of(1, at)
        y = cot[at, :].astype(F32) + s * g2[...] * g - x * (s * s * s) * inner_of(2, at) / width
        gres[at, :] = y
        xall[row, at, :] = y.astype(BF)
        return gain + jnp.sum(g * x * s, axis=0, keepdims=True)

    cot_out.wait()
    cot_all_sent()
    n1_back = local(n1_h, call)
    gain_two = lax.fori_loop(0, B // 32, branch, jnp.zeros((1, Dl), F32))
    relay, second_in, third_in, all_sent = gather(xall)

    def down_partial(blk, other_blk, put):
        x = [two(act.at[c], blk, other_blk) for c in range(2)]
        for n0 in range(0, Dl, Dl // 4):
            n = slice(n0, n0 + Dl // 4)
            put(n0, nn(x[0], w_dn_v[0, :, n]) + nn(x[1], w_dn_v[1, :, n]))

    down_partial(row_d, row_a, both(put_to(rt_s.at[0]), put_to(rt_s.at[1])))

    def gated_other(blk, other_blk):
        x = two(xall, blk, other_blk)
        y = nt(x, w_out_v[other]).astype(BF)
        gg_s[blk] = y[:B]
        gg_s[other_blk] = y[B:]
        copies = [links.send(gg_s.at[b], gg_r.at[b], to_col) for b in (blk, other_blk)]
        y = nt(x, w_out_v[col])
        gg_o[blk] = y[:B]
        gg_o[other_blk] = y[B:]
        return copies

    relay()
    sent = gated_other(row, row_a)
    down_partial(row_b, row, both(put_to(rt_s.at[2]), put_to(down_o)))
    second_in()
    third_in()
    sent += gated_other(row_b, row_d)
    n2_line.plane(1)

    for blk, c in zip((row, row_b, row_a, row_d), sent):
        c.wait_recv()
        base = blk * B

        def conv_grad(r0, blk=blk, base=base):
            at = pl.ds(r0, 32)
            to = pl.ds(pl.multiple_of(base + r0, 32), 32)
            g = gg_o[blk, at, :] + gg_r[blk, at, :].astype(F32)
            gext[to, :] = g * proj_o[1, to, :]
            gp[col, blk, 1, at, :] = (g * cout[to, :]).astype(BF)

        rows_loop(B, 32, conv_grad)

    ahead = links.slot()

    @pl.when(dp > 0)
    def _():
        links.copy(gext.at[pl.ds(0, 8), :], halo_a, {"dp": lax.rem(dp + n_dp - 1, n_dp)}, ahead).start()

    @pl.when(dp < n_dp - 1)
    def _():
        links.copy(gext.at[pl.ds(0, 8), :], halo_a, {"dp": lax.rem(dp + n_dp - 1, n_dp)}, ahead).wait_recv()
        gext[T : T + 8, :] = halo_a[...]

    @pl.when(dp == n_dp - 1)
    def _():
        gext[T : T + 8, :] = jnp.zeros((8, Uc), F32)

    terms = [jnp.zeros((1, Uc), F32) for _ in range(3)]
    for i in range(T // CH):
        at = pl.ds(i * CH, CH)
        more = pl.ds(i * CH, CH + 8)
        x = mext[more, :]
        g = gext[more, :]
        m1, m2 = masks_of(more)
        now = g[:CH]
        terms[0] = terms[0] + jnp.sum(now * x[8 : 8 + CH], axis=0, keepdims=True)
        terms[1] = terms[1] + jnp.sum(m1[:CH] * now * x[7 : 7 + CH], axis=0, keepdims=True)
        terms[2] = terms[2] + jnp.sum(m2[:CH] * now * x[6 : 6 + CH], axis=0, keepdims=True)
        y = cw[0:1, :] * now
        y = y + cw[1:2, :] * (m1 * g)[1 : 1 + CH]
        y = y + cw[2:3, :] * (m2 * g)[2 : 2 + CH]
        blk, to = i * CH // B, slice(i * CH % B, i * CH % B + CH)
        gp[col, blk, 0, to, :] = (y * proj_o[2, at, :]).astype(BF)
        gp[col, blk, 2, to, :] = (y * proj_o[0, at, :]).astype(BF)
    red_s[...] = jnp.zeros_like(red_s)
    for k in range(3):
        red_s[2 + k : 3 + k, :Uc] = terms[k]
    gp_in = links.send(gp.at[col], gp.at[col], to_col)
    n2_line.relay(1)
    gp_in.wait_recv()
    if not split_in:
        kept.append(local(gp, d_in))

    def in_partial(blk, other_blk, put):
        for n0 in range(0, Dl, Dl // 4):
            n = slice(n0, n0 + Dl // 4)
            total = None
            for c in range(2):
                for k in range(3):
                    part = nt(two(gp.at[c, :, k], blk, other_blk), w_in_v[c, k, n, :])
                    total = part if total is None else total + part
            put(n0, total)

    po_all = []

    rows = po_r.shape[1]

    def out_chunk(z):
        return (z // half, pl.ds(pl.multiple_of(lax.rem(z, half) * rows, rows), rows), slice(None))

    def out_weights():
        for z in range(n_dp):
            at = pl.ds(z % half * rows, rows)
            g = lax.dot_general(
                gat[z // half, :, :, at].reshape(T, rows), xall[...].reshape(T, Dl),
                (((0,), (0,)), ((), ())), preferred_element_type=F32,
            )
            w_out_v[z // half, at, :] = g.astype(BF)
        for k in range(1, n_dp):
            po_all.append(links.send(w_out_v.at[out_chunk(peers[k])], po_r.at[dp], {"dp": peers[k]}))

    up_slots = [links.slot() for _ in range(n_dp)]
    down_slots = [links.slot() for _ in range(n_dp)]
    unit = 2 * Uc // n_dp

    def in_chunk(z):
        at = pl.ds(pl.multiple_of(lax.rem(z, half) * unit, unit), unit)
        return (z // half, slice(None), slice(None), at)

    def go_up(z):
        return links.copy(w_in_v.at[in_chunk(z)], in_up.at[z], {"dp": peers[1]}, up_slots[z])

    def go_down(z):
        return links.copy(w_in_v.at[in_chunk(z)], in_dn.at[z], {"dp": sources[1]}, down_slots[z])

    def in_weights():
        n1_back.wait()
        x = call[...].reshape(T, Dl)
        units = [(c, k) for c in range(2) for k in range(3)]
        g = jnp.concatenate([gp[c, :, k].reshape(T, Uc) for c, k in units], axis=1)
        for m0 in range(0, Dl, Dl // 4):
            m = slice(m0, m0 + Dl // 4)
            y = lax.dot_general(x[:, m], g, (((0,), (0,)), ((), ())), preferred_element_type=F32)
            for u, (c, k) in enumerate(units):
                w_in_v[c, k, m, :] = y[:, u * Uc : u * Uc + Uc].astype(BF)
        for z in range(n_dp - 1, 0, -1):

            @pl.when(dp == 0)
            def _(z=z):
                go_up(z).start()

        for z in range(n_dp - 1):

            @pl.when(dp == n_dp - 1)
            def _(z=z):
                go_down(z).start()

    def take(src, z):
        c = pltpu.make_async_copy(src, in_add, local_sems.at[local_sems.shape[0] - 1])
        c.start()
        c.wait()
        at = in_chunk(z)
        for k in range(3):
            here = (at[0], k, slice(None), at[3])
            w_in_v[here] = (w_in_v[here].astype(F32) + in_add[k].astype(F32)).astype(BF)

    def in_step(i):
        z = n_dp - 1 - i

        @pl.when((dp > 0) & (dp < z))
        def _():
            go_up(z).wait_recv()
            take(in_up.at[z], z)
            go_up(z).start()

        @pl.when((dp < n_dp - 1) & (dp > i))
        def _():
            go_down(i).wait_recv()
            take(in_dn.at[i], i)
            go_down(i).start()

    def in_end():
        @pl.when(dp > 0)
        def _():
            for z in range(1, n_dp):

                @pl.when(dp == z)
                def _(z=z):
                    go_up(z).wait_recv()

            take(in_up.at[dp], dp)

        @pl.when(dp < n_dp - 1)
        def _():
            for z in range(n_dp - 1):

                @pl.when(dp == z)
                def _(z=z):
                    go_down(z).wait_recv()

            take(in_dn.at[dp], dp)

        out = local(w_in_v.at[in_chunk(dp)], d_in)
        for z in range(1, n_dp):

            @pl.when(dp < z)
            def _(z=z):
                go_up(z).wait_send()

        for z in range(n_dp - 1):

            @pl.when(dp > z)
            def _(z=z):
                go_down(z).wait_send()

        out.wait()

    def weights_wait():
        if split_in:
            in_weights()
        else:
            n1_back.wait()
        out_weights()

    sent_in = row_sum(rs_s, rs_r, in_partial, filler=weights_wait)
    n2_line.plane(*range(2, min(3, n_dp)))
    down_sent = [
        links.send(rt_s.at[0], rt_r.at[0], to_a),
        links.send(rt_s.at[1], rt_r.at[1], to_a),
    ]

    def back_one(r0):
        at = pl.ds(r0, 32)
        g = row_total(rs_r, at)
        acc_o[at, :] = g
        ss_s[3, at, :] = lanes(
            jnp.sum(g * g1[...] * tok[at, :].astype(F32), axis=1, keepdims=True)
        )

    rows_loop(B, 32, back_one)
    col_total(3)

    def token_grad(i, gain):
        at = pl.ds(pl.multiple_of(i * 32, 32), 32)
        g = acc_o[at, :]
        x = tok[at, :].astype(F32)
        s = scale_of(0, at)
        y = gres[at, :] + s * g1[...] * g - x * (s * s * s) * inner_of(3, at) / width
        gres[at, :] = y
        return gain + jnp.sum(g * x * s, axis=0, keepdims=True)

    gain_one = lax.fori_loop(0, B // 32, token_grad, jnp.zeros((1, Dl), F32))

    kept.append(local(gres, d_tok))

    red_s[0:1, :] = gain_one
    red_s[1:2, :] = gain_two
    c0 = links.send(red_s, red_r.at[0], to_a)
    n2_line.relay(*range(2, min(3, n_dp)))
    n2_line.plane(*range(3, n_dp))
    cot_line.plane(*range(3, n_dp))
    for c in kept_units:
        c.wait()
    for pair in gh_in.values():
        links.sent(*pair)
    all_sent()

    slots = Fc // size

    def place(k, r, rank):
        q = (k - 1) * 2 + r
        lanes_at = slice(q % slots * size, q % slots * size + size)
        return (q // slots, *([slice(None)] * (rank - 2)), lanes_at)

    def again(k):
        z = peers[k]
        loads = [local(n2z.at[z], xall), local(cotz.at[z], call)]
        for c in loads:
            c.wait()
        copies = []
        for core, keep in ((other, False), (col, True)):
            x = xall[pl.ds(core * 2, 2)].reshape(2 * B, Dl)
            for j in range(2):
                h = nn(x, w_gu_v[holder, j, :, mine])
                for r in range(2):
                    if keep:
                        hid_o[j, :, r * size : r * size + size] = h[r * B : r * B + B]
                    else:
                        q, _, _, n = place(k, r, 4)
                        gh[0, q, j, :, n] = h[r * B : r * B + B].astype(BF)
            y = call[pl.ds(core * 2, 2)].reshape(2 * B, Dl)
            g = nt(y, w_dn_v[holder, mine, :])
            for r in range(2):
                if keep:
                    ga_o[r, :, :size] = g[r * B : r * B + B]
                else:
                    q, _, n = place(k, r, 3)
                    act[0, q, :, n] = g[r * B : r * B + B].astype(BF)
            if not keep:
                for r in range(2):
                    h_at, g_at = place(k, r, 4), place(k, r, 3)
                    copies.append(links.send(gh.at[0].at[h_at], hid_r.at[h_at], to_col))
                    copies.append(links.send(act.at[0].at[g_at], ga_r.at[g_at], to_col))
        for c in copies:
            c.wait_recv()
        done = []
        for r in range(2):
            q, _, n = place(k, r, 3)

            def finish(r0, r=r, q=q, n=n):
                at = pl.ds(r0, 32)
                own = slice(r * size, r * size + size)
                gate = hid_o[0, at, own] + hid_r[q, 0, at, n].astype(F32)
                up = hid_o[1, at, own] + hid_r[q, 1, at, n].astype(F32)
                ga = ga_o[r, at, :size] + ga_r[q, at, n].astype(F32)
                s = jax.nn.sigmoid(gate)
                silu = gate * s
                act[1, q, at, n] = (silu * up).astype(BF)
                gh[1, q, 0, at, n] = (ga * up * s * (1.0 + gate * (1.0 - s))).astype(BF)
                gh[1, q, 1, at, n] = (ga * silu).astype(BF)

            rows_loop(B, 32, finish)
            blk = col * 2 + r
            h_src, a_src = gh.at[1].at[place(k, r, 4)], act.at[1].at[place(k, r, 3)]
            done.append(links.send(h_src, ghz.at[z, blk], to_col))
            done.append(links.send(a_src, actz.at[z, blk], to_col))
            kept.append(local(h_src, ghz.at[z, blk]))
            kept.append(local(a_src, actz.at[z, blk]))
        return done

    n2_line.finish(1)
    cot_line.finish(1, 2)
    again_in = again(1)
    if split_in:
        in_step(0)

    down_sent[0].wait_recv()

    def down_combine(r0):
        at = pl.ds(r0, 16)
        rt_s[2, at, :] = (rt_s[2, at, :].astype(F32) + rt_r[0, at, :].astype(F32)).astype(BF)

    rows_loop(B, 16, down_combine)
    down_sent.append(links.send(rt_s.at[2], rt_r.at[2], to_b))
    c0.wait_recv()
    links.sent(c0)
    red_s[0:2, :] = red_s[0:2, :] + red_r[0, 0:2, :]
    c1 = links.send(red_s, red_r.at[1], to_b)
    n2_line.relay(*range(3, n_dp))
    cot_line.relay(*range(3, n_dp))
    n2_line.finish(2)
    again_in += again(2)
    if split_in:
        for i in range(1, n_dp - 2):
            in_step(i)
    c1.wait_recv()
    red_z[dp] = red_s[...]
    red_z[dp, 0:2, :] = red_s[0:2, :] + red_r[1, 0:2, :]
    arrived = []
    for k in range(1, n_dp):
        arrived.append(links.send(red_z.at[dp], red_z.at[dp], {"dp": lax.rem(dp + k, n_dp)}))
    for k in range(3, n_dp):
        n2_line.finish(k)
        cot_line.finish(k)
        again_in += again(k)
    for c in down_sent[1:]:
        c.wait_recv()

    def block_rows(r0):
        at = pl.ds(r0, 16)
        total = down_o[at, :] + rt_r[1, at, :].astype(F32) + rt_r[2, at, :].astype(F32)
        block_out[at, :] = (resid[at, :] + total).astype(BF)

    rows_loop(B, 16, block_rows)
    for c in arrived:
        c.wait_recv()
    total = red_z[0]
    for k in range(1, n_dp):
        total = total + red_z[k]
    d_gain[...] = total
    d_conv[...] = total[:, :Uc]

    @pl.when(dp < n_dp - 1)
    def _():
        links.copy(mext.at[pl.ds(T, 8), :], halo_b, {"dp": lax.rem(dp + 1, n_dp)}, behind).wait_send()

    @pl.when(dp > 0)
    def _():
        links.copy(gext.at[pl.ds(0, 8), :], halo_a, {"dp": lax.rem(dp + n_dp - 1, n_dp)}, ahead).wait_send()

    for c in again_in:
        c.wait_recv()
    for c in po_all:
        c.wait_recv()
    out_total = w_out_v[out_chunk(dp)].astype(F32)
    for k in range(1, n_dp):
        out_total = out_total + po_r[peers[k]].astype(F32)
    acc_b[:rows, :] = out_total
    kept.append(local(acc_b.at[pl.ds(0, rows), :], d_out))
    if split_in:
        in_end()
    cot_line.sent(1)
    for hop in range(2, n_dp):
        for line in (cot_line, n2_line):
            line.sent(hop)
    for c in kept:
        c.wait()
    assert links.count <= send_sems.shape[0]
    links.close()


def run_block(n_dp, width, split_in, tok, g1, w_in, cw, w_out, g2, w_gu, w_dn, cot, lengths):
    B, Dl = tok.shape
    R = 4
    T = R * B
    Uc = w_out.shape[0] // 2
    Fc = w_dn.shape[0] // 2
    vm = lambda shape, kind=BF: pltpu.VMEM(shape, kind)
    any_spec, vmem_spec = pl.BlockSpec(memory_space=pl.ANY), pl.BlockSpec(memory_space=pltpu.VMEM)
    shape = jax.ShapeDtypeStruct
    rows = shape((n_dp, R, B, Dl), BF)
    return pl.pallas_call(
        functools.partial(block_kernel, n_dp, width, split_in),
        out_shape=(
            shape((B, Dl), BF),
            shape((B, Dl), F32),
            shape((8, Dl), F32),
            shape((8, Uc), F32),
            shape((2 * Uc // n_dp, Dl), F32),
            shape((R, B, Dl), BF),
            rows,
            rows,
            shape((n_dp, R, B, 2 * Fc // n_dp), BF),
            shape((n_dp, R, 2, B, 2 * Fc // n_dp), BF),
            shape((3, Dl, 2 * Uc // n_dp) if split_in else (2, R, 3, B, Uc), BF),
            shape((n_dp, 3, Dl, 2 * Uc // n_dp), BF),
            shape((n_dp, 3, Dl, 2 * Uc // n_dp), BF),
        ),
        in_specs=[
            vmem_spec, vmem_spec, any_spec, vmem_spec, any_spec, vmem_spec,
            any_spec, any_spec, vmem_spec, pl.BlockSpec(memory_space=pltpu.SMEM),
        ],
        out_specs=[vmem_spec, any_spec, vmem_spec, vmem_spec] + [any_spec] * 9,
        scratch_shapes=[
            vm((2, 3, Dl, Uc)), vm((2, Uc, Dl)), vm((2, 2, Dl, Fc)), vm((2, Fc, Dl)),
            vm((R, B, Dl)), vm((R, B, Dl)),
            vm((2, R, B, Uc)), vm((2, R, B, Fc)), vm((2, R, 2, B, Fc)), vm((2, R, 3, B, Uc)),
            vm((3, T, Uc), F32), vm((R, 3, B, Uc)), vm((T + 8, Uc), F32), vm((8, Uc), F32),
            vm((T, Uc), F32), vm((T + 8, Uc), F32), vm((8, Uc), F32),
            vm((R, B, Uc)), vm((R, B, Uc)), vm((R, B, Uc), F32),
            vm((2, B, Fc), F32), vm((R, 2, B, Fc)), vm((R, B, Fc), F32), vm((R, B, Fc)),
            vm((3, B, Dl)), vm((3, B, Dl)), vm((3, B, Dl)), vm((3, B, Dl)),
            vm((B, Dl), F32), vm((B, Dl), F32), vm((B, Dl), F32),
            vm((B, Dl), F32), vm((B, Dl), F32),
            vm((4, B, 128), F32), vm((4, B, 128), F32),
            vm((8, Dl), F32), vm((2, 8, Dl), F32), vm((n_dp, 8, Dl), F32),
            vm((n_dp, 2 * Uc // n_dp, Dl)),
            vm((1, Dl), F32), vm((1, Dl), F32), vm((3, Uc), F32),
            vm((T + 16, 128), F32), vm((3, Dl, 2 * Uc // n_dp)),
            pltpu.SemaphoreType.DMA((96 + 48 * n_dp,)), pltpu.SemaphoreType.DMA((96 + 48 * n_dp,)),
            pltpu.SemaphoreType.DMA((32 + 6 * n_dp,)),
        ],
        compiler_params=pltpu.CompilerParams(
            collective_id=0, has_side_effects=True, vmem_limit_bytes=VMEM_LIMIT
        ),
        name="block",
    )(tok, g1, w_in, cw, w_out, g2, w_gu, w_dn, cot, lengths)


def weights_kernel(n2, cot, act, gh, gu_out, dn_out, gu_acc):
    _, R, B, Dl = n2.shape
    T, size = R * B, act.shape[-1]
    step, tile = pl.program_id(0), 256

    def tn(a, b):
        return lax.dot_general(a, b, (((0,), (0,)), ((), ())), preferred_element_type=F32)

    @pl.when(step == 0)
    def _():
        gu_acc[...] = jnp.zeros_like(gu_acc)
        dn_out[...] = jnp.zeros_like(dn_out)

    g = jnp.concatenate([gh[0, :, k].reshape(T, size) for k in range(2)], axis=1)
    for m in range(0, Dl, tile):
        at = slice(m, m + tile)
        gu_acc[at, :] += tn(n2[0, :, :, at].reshape(T, tile), g)
    c = cot[0].reshape(T, Dl)
    for m in range(0, size, min(tile, size)):
        at = slice(m, m + min(tile, size))
        dn_out[at, :] += tn(act[0, :, :, at].reshape(T, min(tile, size)), c)

    @pl.when(step == pl.num_programs(0) - 1)
    def _():
        parts = 2 * size // 128
        for p in range(parts):
            gu_out[pl.ds(p, Dl, stride=parts), :] = gu_acc[:, p * 128 : p * 128 + 128]


def run_weights(n2, cot, act, gh):
    n_dp, R, B, Dl = n2.shape
    size = act.shape[-1]
    whole = lambda *shape: pl.BlockSpec(shape, lambda z: (0,) * len(shape))
    one = lambda a: pl.BlockSpec((1, *a.shape[1:]), lambda z: (z,) + (0,) * (len(a.shape) - 1))
    out = ((Dl * 2 * size // 128, 128), (size, Dl))
    return pl.pallas_call(
        weights_kernel,
        grid=(n_dp,),
        out_shape=[jax.ShapeDtypeStruct(o, F32) for o in out],
        in_specs=[one(n2), one(cot), one(act), one(gh)],
        out_specs=[whole(*o) for o in out],
        scratch_shapes=[pltpu.VMEM((Dl, 2 * size), F32)],
        compiler_params=pltpu.CompilerParams(vmem_limit_bytes=VMEM_LIMIT),
        name="weights",
    )(n2, cot, act, gh)


def on_device(
    tokens, gain_one, in_weight, conv_weight, out_weight, gain_two, gate_up_weight, down_weight,
    cotangent, lengths,
):
    n_dp = lax.axis_size("dp")
    B, Dl = tokens.shape
    width = Dl * lax.axis_size("col")
    chunk = in_weight.shape[2] // n_dp
    split_in = chunk % 128 == 0
    block_out, d_tok, d_gain, d_conv, d_out, n1, n2, cot, act, gh, d_in, _, _ = run_block(
        n_dp,
        float(width),
        split_in,
        tokens,
        gain_one[None, :],
        jnp.transpose(in_weight, (1, 0, 2)),
        conv_weight,
        out_weight,
        gain_two[None, :],
        jnp.transpose(gate_up_weight, (1, 0, 2)),
        down_weight,
        cotangent,
        lengths,
    )
    d_gu, d_down = run_weights(n2, cot, act, gh)
    if split_in:
        d_in = jnp.transpose(d_in, (1, 0, 2)).astype(F32)
    else:
        d_in = lax.psum_scatter(
            jnp.einsum("rti,crktu->ikcu", n1, d_in, preferred_element_type=F32)
            .reshape(Dl, 3, -1)
            .astype(BF),
            "dp",
            scatter_dimension=2,
            tiled=True,
        ).astype(F32)
    part = d_conv.shape[1] * 1 // n_dp
    mine = lax.dynamic_slice(d_conv, (2, lax.axis_index("dp") * part), (3, part))
    return (
        block_out,
        d_tok,
        d_gain[0],
        d_in.reshape(Dl, 3, 1, 1, -1),
        mine.reshape(3, 1, 1, part),
        d_out.reshape(1, 1, -1, Dl),
        d_gain[1],
        d_gu.reshape(Dl, 2, 1, 1, -1),
        d_down.reshape(1, 1, -1, Dl),
    )


def solution(mesh):
    placed = (
        P(("dp", "row"), "col"),
        P("col"),
        P("col", None, "row"),
        P(None, ("row", "col")),
        P("row", "col"),
        P("col"),
        P("col", None, "row"),
        P("row", "col"),
        P(("dp", "row"), "col"),
        P(),
    )
    return jax.shard_map(
        on_device,
        mesh=mesh,
        in_specs=placed,
        out_specs=(
            P(("dp", "row"), "col"),
            P(("dp", "row"), "col"),
            P("col"),
            P("col", None, "row", "dp", None),
            P(None, ("row", "col"), "dp", None),
            P("row", "dp", None, "col"),
            P("col"),
            P("col", None, "row", "dp", None),
            P("row", "dp", None, "col"),
        ),
        check_vma=False,
    )
```

```python
import functools

import jax
import jax.numpy as jnp
from jax import lax
from jax.experimental import pallas as pl
from jax.experimental.pallas import tpu as pltpu
from jax.sharding import PartitionSpec as P

MESH = pl.DeviceIdType.MESH
BF = jnp.bfloat16
F32 = jnp.float32
EPS = 1e-05
VMEM_LIMIT = 63 * 2**20


def nn(a, b):
    return lax.dot_general(a, b, (((1,), (0,)), ((), ())), preferred_element_type=F32)


def nt(a, b):
    return lax.dot_general(a, b, (((1,), (1,)), ((), ())), preferred_element_type=F32)


class Links:
    def __init__(self, send_sems, recv_sems):
        self.send_sems, self.recv_sems = send_sems, recv_sems
        self.count = 0
        self.open = []

    def slot(self):
        self.count += 1
        return self.count - 1

    def copy(self, src, dst, to, slot=None):
        if slot is None:
            slot = self.slot()
        return pltpu.make_async_remote_copy(
            src_ref=src,
            dst_ref=dst,
            send_sem=self.send_sems.at[slot],
            recv_sem=self.recv_sems.at[slot],
            device_id=to,
            device_id_type=MESH,
        )

    def send(self, src, dst, to):
        c = self.copy(src, dst, to)
        c.start()
        self.open.append(c)
        return c

    def sent(self, *copies):
        for c in copies:
            c.wait_send()
            self.open = [o for o in self.open if o is not c]

    def close(self):
        for c in self.open:
            c.wait_send()
        self.open = []


def rows_loop(count, step, body):
    def one(i, carry):
        body(pl.multiple_of(i * step, step))
        return carry

    lax.fori_loop(0, count // step, one, 0)


def block_kernel(n_dp, width, split_in, *refs):
    (
        tok, g1_in, w_in, cw_in, w_out, g2_in, w_gu, w_dn, cot, lengths,
        block_out, d_tok, d_gain, d_conv, d_out, n1_h, n2z, cotz, actz, ghz, d_in, in_up, in_dn,
        w_in_v, w_out_v, w_gu_v, w_dn_v,
        xall, call, gat, act, gh, gp,
        proj_o, proj_r, mext, halo_b, cout, gext, halo_a, gg_s, gg_r, gg_o,
        hid_o, hid_r, ga_o, ga_r,
        rs_s, rs_r, rt_s, rt_r, acc_b, acc_o, down_o,
        resid, gres, ss_s, ss_r, red_s, red_r, red_z, po_r,
        g1, g2, cw, reach, in_add,
        send_sems, recv_sems, local_sems,
    ) = refs
    R, B, Dl = xall.shape
    Uc = w_out_v.shape[1]
    Fc = w_dn_v.shape[1]
    T = R * B
    dp, row, col = lax.axis_index("dp"), lax.axis_index("row"), lax.axis_index("col")
    other = 1 - col
    low = row + 1 - 2 * lax.rem(row, 2)
    high = row + 2 - 4 * lax.rem(row // 2, 2)
    row_a = low * other + high * col
    row_b = high * other + low * col
    row_d = low + high - row
    to_a, to_b, to_col = {"row": row_a}, {"row": row_b}, {"col": other}
    links = Links(send_sems, recv_sems)
    half = n_dp // 2
    holder = dp // half
    peers = [lax.rem(dp + k, n_dp) for k in range(n_dp)]
    sources = [lax.rem(dp + n_dp - k, n_dp) for k in range(n_dp)]

    loads = {"in": [], "out": [], "gu": [], "dn": []}
    n_local = 0

    def local(src, dst):
        nonlocal n_local
        c = pltpu.make_async_copy(src, dst, local_sems.at[n_local])
        n_local += 1
        c.start()
        return c

    for c in range(2):
        for k in range(3):
            loads["in"].append(local(w_in.at[k, :, pl.ds(c * Uc, Uc)], w_in_v.at[c, k]))
    for c in range(2):
        loads["dn"].append(local(w_dn.at[pl.ds(c * Fc, Fc), :], w_dn_v.at[c]))
        loads["out"].append(local(w_out.at[pl.ds(c * Uc, Uc), :], w_out_v.at[c]))
    for c in range(2):
        for k in range(2):
            loads["gu"].append(local(w_gu.at[k, :, pl.ds(c * Fc, Fc)], w_gu_v.at[c, k]))

    def loaded(name):
        for c in loads[name]:
            c.wait()

    barrier = pltpu.get_barrier_semaphore()
    for to in (to_col, {"row": low}, {"row": high}):
        pl.semaphore_signal(barrier, inc=1, device_id=to, device_id_type=MESH)
    for k in range(1, n_dp):
        pl.semaphore_signal(
            barrier, inc=1, device_id={"dp": lax.rem(dp + k, n_dp)}, device_id_type=MESH
        )

    def col_total(place):
        c = links.send(ss_s.at[place], ss_r.at[place], to_col)
        c.wait_recv()

    def gather(buf):
        first = links.send(buf.at[row], buf.at[row], to_a)
        second = links.send(buf.at[row], buf.at[row], to_b)
        state = {}

        def relay():
            first.wait_recv()
            state["third"] = links.send(buf.at[row_a], buf.at[row_a], to_b)

        def second_in():
            second.wait_recv()

        def third_in():
            state["third"].wait_recv()

        def all_sent():
            links.sent(first, second, state["third"])

        return relay, second_in, third_in, all_sent

    class Line:
        def __init__(self, first, dst, block=None):
            self.first, self.dst, self.block = first, dst, row if block is None else block
            self.up = [links.slot() for _ in range(n_dp + 1)]
            self.down = [links.slot() for _ in range(n_dp + 1)]
            self.sent_to, self.last = {}, {}

        def at(self, z):
            return self.dst.at[z, self.block]

        def up_copy(self, hop):
            at = self.at(lax.rem(dp + n_dp - (hop - 1), n_dp))
            src = self.first if hop == 1 else at
            return links.copy(src, at, {"dp": peers[1]}, self.up[hop])

        def down_copy(self, hop):
            at = self.at(lax.rem(dp + hop - 1, n_dp))
            src = self.first if hop == 1 else at
            return links.copy(src, at, {"dp": sources[1]}, self.down[hop])

        def arrived(self, hop):
            @pl.when(dp >= hop)
            def _():
                self.up_copy(hop).wait_recv()

            @pl.when(dp + hop < n_dp)
            def _():
                self.down_copy(hop).wait_recv()

        def start(self, hop):
            if hop > 1:
                self.arrived(hop - 1)

            @pl.when((dp + 1 < n_dp) & (dp >= hop - 1))
            def _():
                self.up_copy(hop).start()

            @pl.when((dp >= 1) & (dp + hop - 1 < n_dp))
            def _():
                self.down_copy(hop).start()

        def sent(self, hop):
            @pl.when((dp + 1 < n_dp) & (dp >= hop - 1))
            def _():
                self.up_copy(hop).wait_send()

            @pl.when((dp >= 1) & (dp + hop - 1 < n_dp))
            def _():
                self.down_copy(hop).wait_send()

        def rest(self):
            for hop in range(4, n_dp):
                self.start(hop)
            self.arrived(n_dp - 1)

        def plane(self, *ks):
            if not self.sent_to:
                self.rest()
            for k in ks:
                at = self.dst.at[peers[k], row]
                self.sent_to[k] = (links.send(at, at, to_a), links.send(at, at, to_b))

        def relay(self, *ks):
            for k in ks:
                first, second = self.sent_to[k]
                first.wait_recv()
                at = self.dst.at[peers[k], row_a]
                self.last[k] = (second, links.send(at, at, to_b))

        def finish(self, *ks):
            for k in ks:
                for c in self.last[k]:
                    c.wait_recv()

    def put_to(ref):
        def put(n0, value):
            ref[:, n0 : n0 + value.shape[1]] = value.astype(ref.dtype)

        return put

    def both(first, second):
        def put(n0, value):
            first(n0, value[:B])
            second(n0, value[B:])

        return put

    def two(buf, blk, other_blk):
        return jnp.concatenate([buf[blk], buf[other_blk]], axis=0)

    def row_sum(sends, recvs, partial, filler=None):
        partial(row_d, row_a, both(put_to(sends.at[0]), put_to(sends.at[1])))
        c0 = links.send(sends.at[0], recvs.at[0], to_a)
        c1 = links.send(sends.at[1], recvs.at[1], to_a)
        partial(row_b, row, both(put_to(acc_b), put_to(acc_o)))
        c0.wait_recv()

        def combine(r0):
            at = pl.ds(r0, 32)
            sends[2, at, :] = (acc_b[at, :] + recvs[0, at, :].astype(F32)).astype(BF)

        rows_loop(B, 32, combine)
        c2 = links.send(sends.at[2], recvs.at[2], to_b)
        if filler is not None:
            filler()
        c1.wait_recv()
        c2.wait_recv()
        return c0, c1, c2

    def row_total(recvs, at):
        return acc_o[at, :] + recvs[1, at, :].astype(F32) + recvs[2, at, :].astype(F32)

    def lanes(x):
        return jnp.broadcast_to(x, (x.shape[0], 128))

    g1[...] = g1_in[...].astype(F32)
    g2[...] = g2_in[...].astype(F32)
    cw[...] = cw_in[...].astype(F32)
    starts = [jnp.int32(0)]
    for i in range(lengths.shape[0] - 1):
        starts.append(starts[-1] + lengths[i])

    def masks(r0):
        t = dp * T + r0 + lax.broadcasted_iota(jnp.int32, (16, 128), 0)
        count = jnp.full((16, 128), 2.0, F32)
        for start in starts:
            away = t - start
            count = jnp.where((away >= 0) & (away < 2), away.astype(F32), count)
        reach[pl.ds(r0, 16), :] = count

    rows_loop(T + 16, 16, masks)

    def squares(r0):
        at = pl.ds(r0, 32)
        x = tok[at, :].astype(F32)
        ss_s[0, at, :] = lanes(jnp.sum(x * x, axis=1, keepdims=True))

    rows_loop(B, 32, squares)
    pl.semaphore_wait(barrier, 3 + n_dp - 1)
    cot_line = Line(cot, cotz)
    n2_line = Line(xall.at[row], n2z)
    cot_line.start(1)
    col_total(0)

    def scale_of(place, at):
        return lax.rsqrt((ss_s[place, at, :] + ss_r[place, at, :]) / width + EPS)[:, :1]

    def normed_one(r0):
        at = pl.ds(r0, 32)
        x = tok[at, :].astype(F32)
        xall[row, at, :] = (x * scale_of(0, at) * g1[...]).astype(BF)

    rows_loop(B, 32, normed_one)
    relay, second_in, third_in, all_sent = gather(xall)

    def project(blk, other_blk):
        x = two(xall, blk, other_blk)
        for k in range(3):
            y = nn(x, w_in_v[other, k]).astype(BF)
            gp[col, blk, k] = y[:B]
            gp[col, other_blk, k] = y[B:]
        copies = [links.send(gp.at[col, b], proj_r.at[b], to_col) for b in (blk, other_blk)]
        for k in range(3):
            y = nn(x, w_in_v[col, k])
            proj_o[k, pl.ds(pl.multiple_of(blk * B, B), B), :] = y[:B]
            proj_o[k, pl.ds(pl.multiple_of(other_blk * B, B), B), :] = y[B:]
        return copies

    loaded("in")
    relay()
    sent = project(row, row_a)
    cot_line.start(2)
    second_in()
    third_in()
    call[row] = cot[...]
    cot_relay, cot_second, cot_third, cot_all_sent = gather(call)
    sent += project(row_b, row_d)
    n1_out = local(xall, n1_h)

    for blk, c in zip((row, row_b, row_a, row_d), sent):
        c.wait_recv()
        base = blk * B

        def add(r0, blk=blk, base=base):
            at = pl.ds(r0, 32)
            to = pl.ds(pl.multiple_of(base + r0, 32), 32)
            g = [proj_o[k, to, :] + proj_r[blk, k, at, :].astype(F32) for k in range(3)]
            for k in range(3):
                proj_o[k, to, :] = g[k]
            mext[pl.ds(pl.multiple_of(base + r0 + 8, 8), 32), :] = g[0] * g[2]

        rows_loop(B, 32, add)
    links.sent(*sent)

    behind = links.slot()

    @pl.when(dp < n_dp - 1)
    def _():
        links.copy(mext.at[pl.ds(T, 8), :], halo_b, {"dp": lax.rem(dp + 1, n_dp)}, behind).start()

    @pl.when(dp > 0)
    def _():
        links.copy(mext.at[pl.ds(T, 8), :], halo_b, {"dp": lax.rem(dp + 1, n_dp)}, behind).wait_recv()
        mext[0:8, :] = halo_b[...]

    @pl.when(dp == 0)
    def _():
        mext[0:8, :] = jnp.zeros((8, Uc), F32)

    cot_relay()
    cot_line.start(3)
    CH = B // 2

    def masks_of(at):
        count = jnp.concatenate([reach[at, :]] * (Uc // 128), axis=1)
        return jnp.minimum(count, 1.0), jnp.maximum(count - 1.0, 0.0)

    for i in range(T // CH):
        at = pl.ds(i * CH, CH)
        x = mext[pl.ds(i * CH, CH + 8), :]
        m1, m2 = masks_of(at)
        y = cw[0:1, :] * x[8 : 8 + CH]
        y = y + cw[1:2, :] * m1 * x[7 : 7 + CH]
        y = y + cw[2:3, :] * m2 * x[6 : 6 + CH]
        cout[at, :] = y
        gat[col, i * CH // B, i * CH % B : i * CH % B + CH, :] = (proj_o[1, at, :] * y).astype(BF)
    gated_in = links.send(gat.at[col], gat.at[col], to_col)
    cot_second()
    gated_in.wait_recv()

    loaded("out")
    n1_out.wait()
    all_sent()

    def out_partial(blk, other_blk, put):
        x = [two(gat.at[c], blk, other_blk) for c in range(2)]
        for n0 in range(0, Dl, Dl // 4):
            n = slice(n0, n0 + Dl // 4)
            put(n0, nn(x[0], w_out_v[0, :, n]) + nn(x[1], w_out_v[1, :, n]))

    sent = row_sum(rs_s, rs_r, out_partial)

    def residual(r0):
        at = pl.ds(r0, 32)
        x = tok[at, :].astype(F32) + row_total(rs_r, at)
        resid[at, :] = x
        ss_s[1, at, :] = lanes(jnp.sum(x * x, axis=1, keepdims=True))

    cot_third()
    rows_loop(B, 32, residual)
    links.sent(*sent)
    col_total(1)

    def normed_two(r0):
        at = pl.ds(r0, 32)
        xall[row, at, :] = (resid[at, :] * scale_of(1, at) * g2[...]).astype(BF)

    rows_loop(B, 32, normed_two)
    relay, second_in, third_in, all_sent = gather(xall)
    n2_line.start(1)

    loaded("dn")
    ga_step = min(Fc, 256)

    def ga_other(i, carry):
        n = pl.ds(pl.multiple_of(i * ga_step, ga_step), ga_step)
        y = nt(call[...].reshape(T, Dl), w_dn_v[other, n, :]).astype(BF)
        act[col, :, :, n] = y.reshape(R, B, ga_step)
        return carry

    def ga_own(i, carry):
        n = pl.ds(pl.multiple_of(i * ga_step, ga_step), ga_step)
        ga_o[:, :, n] = nt(call[...].reshape(T, Dl), w_dn_v[col, n, :]).reshape(R, B, ga_step)
        return carry

    lax.fori_loop(0, Fc // ga_step, ga_other, 0)
    ga_sent = links.send(act.at[col], ga_r, to_col)
    relay()
    lax.fori_loop(0, Fc // ga_step, ga_own, 0)
    cot_out = local(call, cotz.at[dp])
    n2_line.start(2)

    def hidden_other(blk, other_blk):
        def one(k, carry):
            x = two(xall, blk, other_blk)
            for n0 in range(0, Fc, Fc // 2):
                n = slice(n0, n0 + Fc // 2)
                y = nn(x, w_gu_v[other, k, :, n]).astype(BF)
                gh[col, blk, k, :, n] = y[:B]
                gh[col, other_blk, k, :, n] = y[B:]
            return carry

        lax.fori_loop(0, 2, one, 0)
        return [links.send(gh.at[col, b], hid_r.at[b], to_col) for b in (blk, other_blk)]

    loaded("gu")
    hid_sent = hidden_other(row, row_a)
    second_in()
    third_in()
    hid_sent += hidden_other(row_b, row_d)
    n2_out = local(xall, n2z.at[dp])
    cot_line.plane(1, 2)

    gh_in = {}
    ga_sent.wait_recv()
    links.sent(ga_sent)
    H = Fc // 2
    for blks, mine_at, theirs_at in (((row_d, row_a), (3, 1), (3, 2)), ((row_b, row), (2, 0), (1, 0))):
        for h in range(2):

            def one(k, carry, h=h, blks=blks):
                y = nn(two(xall, *blks), w_gu_v[col, k, :, h * H : h * H + H])
                hid_o[k, :, :H] = y[:B]
                hid_o[k, :, H:] = y[B:]
                return carry

            lax.fori_loop(0, 2, one, 0)
            for i, blk in enumerate(blks):
                if h == 0:
                    hid_sent[theirs_at[i]].wait_recv()
                    links.sent(hid_sent[mine_at[i]])

                def activate(r0, blk=blk, i=i, h=h):
                    at = pl.ds(r0, 32)
                    n = slice(h * H, h * H + H)
                    own = slice(i * H, i * H + H)
                    gate = hid_o[0, at, own] + hid_r[blk, 0, at, n].astype(F32)
                    up = hid_o[1, at, own] + hid_r[blk, 1, at, n].astype(F32)
                    ga = ga_o[blk, at, n] + ga_r[blk, at, n].astype(F32)
                    s = jax.nn.sigmoid(gate)
                    silu = gate * s
                    act[col, blk, at, n] = (silu * up).astype(BF)
                    gh[col, blk, 0, at, n] = (ga * up * s * (1.0 + gate * (1.0 - s))).astype(BF)
                    gh[col, blk, 1, at, n] = (ga * silu).astype(BF)

                rows_loop(B, 32, activate)
                if h == 1:
                    gh_in[mine_at[i]] = (
                        links.send(gh.at[col, blk], gh.at[col, blk], to_col),
                        links.send(act.at[col, blk], act.at[col, blk], to_col),
                    )
    cot_line.relay(1, 2)
    for pair in gh_in.values():
        for c in pair:
            c.wait_recv()
    size = actz.shape[-1]
    mine = pl.ds(pl.multiple_of(lax.rem(dp, half) * size, size), size)
    kept_units = [
        local(act.at[holder, :, :, mine], actz.at[dp]),
        local(gh.at[holder, :, :, :, mine], ghz.at[dp]),
    ]
    kept = []
    n2_out.wait()
    n2_line.start(3)
    n2_line.sent(1)
    all_sent()

    def gu_partial(blk, other_blk, put):
        for n0 in range(0, Dl, Dl // 4):
            n = slice(n0, n0 + Dl // 4)
            total = None
            for c in range(2):
                for k in range(2):
                    part = nt(two(gh.at[c, :, k], blk, other_blk), w_gu_v[c, k, n, :])
                    total = part if total is None else total + part
            put(n0, total)

    sent = row_sum(rs_s, rs_r, gu_partial)

    def back_two(r0):
        at = pl.ds(r0, 32)
        g = row_total(rs_r, at)
        gres[at, :] = g
        ss_s[2, at, :] = lanes(jnp.sum(g * g2[...] * resid[at, :], axis=1, keepdims=True))

    rows_loop(B, 32, back_two)
    links.sent(*sent)
    col_total(2)

    def inner_of(place, at):
        return (ss_s[place, at, :] + ss_r[place, at, :])[:, :1]

    def branch(i, gain):
        at = pl.ds(pl.multiple_of(i * 32, 32), 32)
        g = gres[at, :]
        x = resid[at, :]
        s = scale_of(1, at)
        y = cot[at, :].astype(F32) + s * g2[...] * g - x * (s * s * s) * inner_of(2, at) / width
        gres[at, :] = y
        xall[row, at, :] = y.astype(BF)
        return gain + jnp.sum(g * x * s, axis=0, keepdims=True)

    cot_out.wait()
    cot_all_sent()
    n1_back = local(n1_h, call)
    gain_two = lax.fori_loop(0, B // 32, branch, jnp.zeros((1, Dl), F32))
    relay, second_in, third_in, all_sent = gather(xall)

    def down_partial(blk, other_blk, put):
        x = [two(act.at[c], blk, other_blk) for c in range(2)]
        for n0 in range(0, Dl, Dl // 4):
            n = slice(n0, n0 + Dl // 4)
            put(n0, nn(x[0], w_dn_v[0, :, n]) + nn(x[1], w_dn_v[1, :, n]))

    down_partial(row_d, row_a, both(put_to(rt_s.at[0]), put_to(rt_s.at[1])))

    def gated_other(blk, other_blk):
        x = two(xall, blk, other_blk)
        y = nt(x, w_out_v[other]).astype(BF)
        gg_s[blk] = y[:B]
        gg_s[other_blk] = y[B:]
        copies = [links.send(gg_s.at[b], gg_r.at[b], to_col) for b in (blk, other_blk)]
        y = nt(x, w_out_v[col])
        gg_o[blk] = y[:B]
        gg_o[other_blk] = y[B:]
        return copies

    relay()
    sent = gated_other(row, row_a)
    down_partial(row_b, row, both(put_to(rt_s.at[2]), put_to(down_o)))
    second_in()
    third_in()
    sent += gated_other(row_b, row_d)
    n2_line.plane(1)

    for blk, c in zip((row, row_b, row_a, row_d), sent):
        c.wait_recv()
        base = blk * B

        def conv_grad(r0, blk=blk, base=base):
            at = pl.ds(r0, 32)
            to = pl.ds(pl.multiple_of(base + r0, 32), 32)
            g = gg_o[blk, at, :] + gg_r[blk, at, :].astype(F32)
            gext[to, :] = g * proj_o[1, to, :]
            gp[col, blk, 1, at, :] = (g * cout[to, :]).astype(BF)

        rows_loop(B, 32, conv_grad)

    ahead = links.slot()

    @pl.when(dp > 0)
    def _():
        links.copy(gext.at[pl.ds(0, 8), :], halo_a, {"dp": lax.rem(dp + n_dp - 1, n_dp)}, ahead).start()

    @pl.when(dp < n_dp - 1)
    def _():
        links.copy(gext.at[pl.ds(0, 8), :], halo_a, {"dp": lax.rem(dp + n_dp - 1, n_dp)}, ahead).wait_recv()
        gext[T : T + 8, :] = halo_a[...]

    @pl.when(dp == n_dp - 1)
    def _():
        gext[T : T + 8, :] = jnp.zeros((8, Uc), F32)

    terms = [jnp.zeros((1, Uc), F32) for _ in range(3)]
    for i in range(T // CH):
        at = pl.ds(i * CH, CH)
        more = pl.ds(i * CH, CH + 8)
        x = mext[more, :]
        g = gext[more, :]
        m1, m2 = masks_of(more)
        now = g[:CH]
        terms[0] = terms[0] + jnp.sum(now * x[8 : 8 + CH], axis=0, keepdims=True)
        terms[1] = terms[1] + jnp.sum(m1[:CH] * now * x[7 : 7 + CH], axis=0, keepdims=True)
        terms[2] = terms[2] + jnp.sum(m2[:CH] * now * x[6 : 6 + CH], axis=0, keepdims=True)
        y = cw[0:1, :] * now
        y = y + cw[1:2, :] * (m1 * g)[1 : 1 + CH]
        y = y + cw[2:3, :] * (m2 * g)[2 : 2 + CH]
        blk, to = i * CH // B, slice(i * CH % B, i * CH % B + CH)
        gp[col, blk, 0, to, :] = (y * proj_o[2, at, :]).astype(BF)
        gp[col, blk, 2, to, :] = (y * proj_o[0, at, :]).astype(BF)
    red_s[...] = jnp.zeros_like(red_s)
    for k in range(3):
        red_s[2 + k : 3 + k, :Uc] = terms[k]
    gp_in = links.send(gp.at[col], gp.at[col], to_col)
    n2_line.relay(1)
    gp_in.wait_recv()
    if not split_in:
        kept.append(local(gp, d_in))

    def in_partial(blk, other_blk, put):
        for n0 in range(0, Dl, Dl // 4):
            n = slice(n0, n0 + Dl // 4)
            total = None
            for c in range(2):
                for k in range(3):
                    part = nt(two(gp.at[c, :, k], blk, other_blk), w_in_v[c, k, n, :])
                    total = part if total is None else total + part
            put(n0, total)

    po_all = []

    rows = po_r.shape[1]

    def out_chunk(z):
        return (z // half, pl.ds(pl.multiple_of(lax.rem(z, half) * rows, rows), rows), slice(None))

    def out_weights():
        for z in range(n_dp):
            at = pl.ds(z % half * rows, rows)
            g = lax.dot_general(
                gat[z // half, :, :, at].reshape(T, rows), xall[...].reshape(T, Dl),
                (((0,), (0,)), ((), ())), preferred_element_type=F32,
            )
            w_out_v[z // half, at, :] = g.astype(BF)
        for k in range(1, n_dp):
            po_all.append(links.send(w_out_v.at[out_chunk(peers[k])], po_r.at[dp], {"dp": peers[k]}))

    up_slots = [links.slot() for _ in range(n_dp)][0]
    down_slots = [links.slot() for _ in range(n_dp)][0]
    unit = 2 * Uc // n_dp

    def in_chunk(z):
        at = pl.ds(pl.multiple_of(lax.rem(z, half) * unit, unit), unit)
        return (z // half, slice(None), slice(None), at)

    def go_up(z):
        return links.copy(w_in_v.at[in_chunk(z)], in_up.at[z], {"dp": peers[1]}, up_slots + z)

    def go_down(z):
        return links.copy(w_in_v.at[in_chunk(z)], in_dn.at[z], {"dp": sources[1]}, down_slots + z)

    def in_weights():
        n1_back.wait()
        x = call[...].reshape(T, Dl)
        units = [(c, k) for c in range(2) for k in range(3)]
        g = jnp.concatenate([gp[c, :, k].reshape(T, Uc) for c, k in units], axis=1)
        for m0 in range(0, Dl, Dl // 4):
            m = slice(m0, m0 + Dl // 4)
            y = lax.dot_general(x[:, m], g, (((0,), (0,)), ((), ())), preferred_element_type=F32)
            for u, (c, k) in enumerate(units):
                w_in_v[c, k, m, :] = y[:, u * Uc : u * Uc + Uc].astype(BF)
        for z in range(n_dp - 1, 0, -1):

            @pl.when(dp == 0)
            def _(z=z):
                go_up(z).start()

        for z in range(n_dp - 1):

            @pl.when(dp == n_dp - 1)
            def _(z=z):
                go_down(z).start()

    def take(src, z):
        c = pltpu.make_async_copy(src, in_add, local_sems.at[local_sems.shape[0] - 1])
        c.start()
        c.wait()
        at = in_chunk(z)
        for k in range(3):
            here = (at[0], k, slice(None), at[3])
            w_in_v[here] = (w_in_v[here].astype(F32) + in_add[k].astype(F32)).astype(BF)

    def in_step(step):
        up = n_dp - 1 - step + dp

        @pl.when((dp > 0) & (dp <= step))
        def _():
            go_up(up).wait_recv()
            take(in_up.at[up], up)
            go_up(up).start()

        down = step - (n_dp - 1 - dp)

        @pl.when((dp < n_dp - 1) & (down >= 0))
        def _():
            go_down(down).wait_recv()
            take(in_dn.at[down], down)
            go_down(down).start()

    def in_end():
        @pl.when(dp > 0)
        def _():
            go_up(dp).wait_recv()
            take(in_up.at[dp], dp)

        @pl.when(dp < n_dp - 1)
        def _():
            go_down(dp).wait_recv()
            take(in_dn.at[dp], dp)

        out = local(w_in_v.at[in_chunk(dp)], d_in)
        for z in range(1, n_dp):

            @pl.when(dp < z)
            def _(z=z):
                go_up(z).wait_send()

        for z in range(n_dp - 1):

            @pl.when(dp > z)
            def _(z=z):
                go_down(z).wait_send()

        out.wait()

    def weights_wait():
        if split_in:
            in_weights()
        else:
            n1_back.wait()
        out_weights()

    sent_in = row_sum(rs_s, rs_r, in_partial, filler=weights_wait)
    n2_line.plane(*range(2, min(3, n_dp)))
    down_sent = [
        links.send(rt_s.at[0], rt_r.at[0], to_a),
        links.send(rt_s.at[1], rt_r.at[1], to_a),
    ]

    def back_one(r0):
        at = pl.ds(r0, 32)
        g = row_total(rs_r, at)
        acc_o[at, :] = g
        ss_s[3, at, :] = lanes(
            jnp.sum(g * g1[...] * tok[at, :].astype(F32), axis=1, keepdims=True)
        )

    rows_loop(B, 32, back_one)
    col_total(3)

    def token_grad(i, gain):
        at = pl.ds(pl.multiple_of(i * 32, 32), 32)
        g = acc_o[at, :]
        x = tok[at, :].astype(F32)
        s = scale_of(0, at)
        y = gres[at, :] + s * g1[...] * g - x * (s * s * s) * inner_of(3, at) / width
        gres[at, :] = y
        return gain + jnp.sum(g * x * s, axis=0, keepdims=True)

    gain_one = lax.fori_loop(0, B // 32, token_grad, jnp.zeros((1, Dl), F32))

    kept.append(local(gres, d_tok))

    red_s[0:1, :] = gain_one
    red_s[1:2, :] = gain_two
    c0 = links.send(red_s, red_r.at[0], to_a)
    n2_line.relay(*range(2, min(3, n_dp)))
    n2_line.plane(*range(3, n_dp))
    cot_line.plane(*range(3, n_dp))
    for c in kept_units:
        c.wait()
    for pair in gh_in.values():
        links.sent(*pair)
    all_sent()

    slots = Fc // size

    def place(k, r, rank):
        q = (k - 1) * 2 + r
        lanes_at = slice(q % slots * size, q % slots * size + size)
        return (q // slots, *([slice(None)] * (rank - 2)), lanes_at)

    def again(k):
        z = peers[k]
        loads = [local(n2z.at[z], xall), local(cotz.at[z], call)]
        for c in loads:
            c.wait()
        copies = []
        for core, keep in ((other, False), (col, True)):
            x = xall[pl.ds(core * 2, 2)].reshape(2 * B, Dl)
            for j in range(2):
                h = nn(x, w_gu_v[holder, j, :, mine])
                for r in range(2):
                    if keep:
                        hid_o[j, :, r * size : r * size + size] = h[r * B : r * B + B]
                    else:
                        q, _, _, n = place(k, r, 4)
                        gh[0, q, j, :, n] = h[r * B : r * B + B].astype(BF)
            y = call[pl.ds(core * 2, 2)].reshape(2 * B, Dl)
            g = nt(y, w_dn_v[holder, mine, :])
            for r in range(2):
                if keep:
                    ga_o[r, :, :size] = g[r * B : r * B + B]
                else:
                    q, _, n = place(k, r, 3)
                    act[0, q, :, n] = g[r * B : r * B + B].astype(BF)
            if not keep:
                for r in range(2):
                    h_at, g_at = place(k, r, 4), place(k, r, 3)
                    copies.append(links.send(gh.at[0].at[h_at], hid_r.at[h_at], to_col))
                    copies.append(links.send(act.at[0].at[g_at], ga_r.at[g_at], to_col))
        for c in copies:
            c.wait_recv()
        done = []
        for r in range(2):
            q, _, n = place(k, r, 3)

            def finish(r0, r=r, q=q, n=n):
                at = pl.ds(r0, 32)
                own = slice(r * size, r * size + size)
                gate = hid_o[0, at, own] + hid_r[q, 0, at, n].astype(F32)
                up = hid_o[1, at, own] + hid_r[q, 1, at, n].astype(F32)
                ga = ga_o[r, at, :size] + ga_r[q, at, n].astype(F32)
                s = jax.nn.sigmoid(gate)
                silu = gate * s
                act[1, q, at, n] = (silu * up).astype(BF)
                gh[1, q, 0, at, n] = (ga * up * s * (1.0 + gate * (1.0 - s))).astype(BF)
                gh[1, q, 1, at, n] = (ga * silu).astype(BF)

            rows_loop(B, 32, finish)
            blk = col * 2 + r
            h_src, a_src = gh.at[1].at[place(k, r, 4)], act.at[1].at[place(k, r, 3)]
            done.append(links.send(h_src, ghz.at[z, blk], to_col))
            done.append(links.send(a_src, actz.at[z, blk], to_col))
            kept.append(local(h_src, ghz.at[z, blk]))
            kept.append(local(a_src, actz.at[z, blk]))
        return done

    n2_line.finish(1)
    cot_line.finish(1, 2)
    again_in = again(1)
    if split_in:
        in_step(1)

    down_sent[0].wait_recv()

    def down_combine(r0):
        at = pl.ds(r0, 16)
        rt_s[2, at, :] = (rt_s[2, at, :].astype(F32) + rt_r[0, at, :].astype(F32)).astype(BF)

    rows_loop(B, 16, down_combine)
    down_sent.append(links.send(rt_s.at[2], rt_r.at[2], to_b))
    c0.wait_recv()
    links.sent(c0)
    red_s[0:2, :] = red_s[0:2, :] + red_r[0, 0:2, :]
    c1 = links.send(red_s, red_r.at[1], to_b)
    n2_line.relay(*range(3, n_dp))
    cot_line.relay(*range(3, n_dp))
    n2_line.finish(2)
    again_in += again(2)
    if split_in:
        for step in range(2, n_dp - 1):
            in_step(step)
    c1.wait_recv()
    red_z[dp] = red_s[...]
    red_z[dp, 0:2, :] = red_s[0:2, :] + red_r[1, 0:2, :]
    arrived = []
    for k in range(1, n_dp):
        arrived.append(links.send(red_z.at[dp], red_z.at[dp], {"dp": lax.rem(dp + k, n_dp)}))
    for k in range(3, n_dp):
        n2_line.finish(k)
        cot_line.finish(k)
        again_in += again(k)
    for c in down_sent[1:]:
        c.wait_recv()

    def block_rows(r0):
        at = pl.ds(r0, 16)
        total = down_o[at, :] + rt_r[1, at, :].astype(F32) + rt_r[2, at, :].astype(F32)
        block_out[at, :] = (resid[at, :] + total).astype(BF)

    rows_loop(B, 16, block_rows)
    for c in arrived:
        c.wait_recv()
    total = red_z[0]
    for k in range(1, n_dp):
        total = total + red_z[k]
    d_gain[...] = total
    d_conv[...] = total[:, :Uc]

    @pl.when(dp < n_dp - 1)
    def _():
        links.copy(mext.at[pl.ds(T, 8), :], halo_b, {"dp": lax.rem(dp + 1, n_dp)}, behind).wait_send()

    @pl.when(dp > 0)
    def _():
        links.copy(gext.at[pl.ds(0, 8), :], halo_a, {"dp": lax.rem(dp + n_dp - 1, n_dp)}, ahead).wait_send()

    for c in again_in:
        c.wait_recv()
    for c in po_all:
        c.wait_recv()
    out_total = w_out_v[out_chunk(dp)].astype(F32)
    for k in range(1, n_dp):
        out_total = out_total + po_r[peers[k]].astype(F32)
    acc_b[:rows, :] = out_total
    kept.append(local(acc_b.at[pl.ds(0, rows), :], d_out))
    if split_in:
        in_end()
    cot_line.sent(1)
    for hop in range(2, n_dp):
        for line in (cot_line, n2_line):
            line.sent(hop)
    for c in kept:
        c.wait()
    assert links.count <= send_sems.shape[0]
    links.close()


def run_block(n_dp, width, split_in, tok, g1, w_in, cw, w_out, g2, w_gu, w_dn, cot, lengths):
    B, Dl = tok.shape
    R = 4
    T = R * B
    Uc = w_out.shape[0] // 2
    Fc = w_dn.shape[0] // 2
    vm = lambda shape, kind=BF: pltpu.VMEM(shape, kind)
    any_spec, vmem_spec = pl.BlockSpec(memory_space=pl.ANY), pl.BlockSpec(memory_space=pltpu.VMEM)
    shape = jax.ShapeDtypeStruct
    rows = shape((n_dp, R, B, Dl), BF)
    return pl.pallas_call(
        functools.partial(block_kernel, n_dp, width, split_in),
        out_shape=(
            shape((B, Dl), BF),
            shape((B, Dl), F32),
            shape((8, Dl), F32),
            shape((8, Uc), F32),
            shape((2 * Uc // n_dp, Dl), F32),
            shape((R, B, Dl), BF),
            rows,
            rows,
            shape((n_dp, R, B, 2 * Fc // n_dp), BF),
            shape((n_dp, R, 2, B, 2 * Fc // n_dp), BF),
            shape((3, Dl, 2 * Uc // n_dp) if split_in else (2, R, 3, B, Uc), BF),
            shape((n_dp, 3, Dl, 2 * Uc // n_dp), BF),
            shape((n_dp, 3, Dl, 2 * Uc // n_dp), BF),
        ),
        in_specs=[
            vmem_spec, vmem_spec, any_spec, vmem_spec, any_spec, vmem_spec,
            any_spec, any_spec, vmem_spec, pl.BlockSpec(memory_space=pltpu.SMEM),
        ],
        out_specs=[vmem_spec, any_spec, vmem_spec, vmem_spec] + [any_spec] * 9,
        scratch_shapes=[
            vm((2, 3, Dl, Uc)), vm((2, Uc, Dl)), vm((2, 2, Dl, Fc)), vm((2, Fc, Dl)),
            vm((R, B, Dl)), vm((R, B, Dl)),
            vm((2, R, B, Uc)), vm((2, R, B, Fc)), vm((2, R, 2, B, Fc)), vm((2, R, 3, B, Uc)),
            vm((3, T, Uc), F32), vm((R, 3, B, Uc)), vm((T + 8, Uc), F32), vm((8, Uc), F32),
            vm((T, Uc), F32), vm((T + 8, Uc), F32), vm((8, Uc), F32),
            vm((R, B, Uc)), vm((R, B, Uc)), vm((R, B, Uc), F32),
            vm((2, B, Fc), F32), vm((R, 2, B, Fc)), vm((R, B, Fc), F32), vm((R, B, Fc)),
            vm((3, B, Dl)), vm((3, B, Dl)), vm((3, B, Dl)), vm((3, B, Dl)),
            vm((B, Dl), F32), vm((B, Dl), F32), vm((B, Dl), F32),
            vm((B, Dl), F32), vm((B, Dl), F32),
            vm((4, B, 128), F32), vm((4, B, 128), F32),
            vm((8, Dl), F32), vm((2, 8, Dl), F32), vm((n_dp, 8, Dl), F32),
            vm((n_dp, 2 * Uc // n_dp, Dl)),
            vm((1, Dl), F32), vm((1, Dl), F32), vm((3, Uc), F32),
            vm((T + 16, 128), F32), vm((3, Dl, 2 * Uc // n_dp)),
            pltpu.SemaphoreType.DMA((96 + 48 * n_dp,)), pltpu.SemaphoreType.DMA((96 + 48 * n_dp,)),
            pltpu.SemaphoreType.DMA((32 + 6 * n_dp,)),
        ],
        compiler_params=pltpu.CompilerParams(
            collective_id=0, has_side_effects=True, vmem_limit_bytes=VMEM_LIMIT
        ),
        name="block",
    )(tok, g1, w_in, cw, w_out, g2, w_gu, w_dn, cot, lengths)


def weights_kernel(n2, cot, act, gh, gu_out, dn_out, gu_acc):
    _, R, B, Dl = n2.shape
    T, size = R * B, act.shape[-1]
    step, tile = pl.program_id(0), 256

    def tn(a, b):
        return lax.dot_general(a, b, (((0,), (0,)), ((), ())), preferred_element_type=F32)

    @pl.when(step == 0)
    def _():
        gu_acc[...] = jnp.zeros_like(gu_acc)
        dn_out[...] = jnp.zeros_like(dn_out)

    g = jnp.concatenate([gh[0, :, k].reshape(T, size) for k in range(2)], axis=1)
    for m in range(0, Dl, tile):
        at = slice(m, m + tile)
        gu_acc[at, :] += tn(n2[0, :, :, at].reshape(T, tile), g)
    c = cot[0].reshape(T, Dl)
    for m in range(0, size, min(tile, size)):
        at = slice(m, m + min(tile, size))
        dn_out[at, :] += tn(act[0, :, :, at].reshape(T, min(tile, size)), c)

    @pl.when(step == pl.num_programs(0) - 1)
    def _():
        parts = 2 * size // 128
        for p in range(parts):
            gu_out[pl.ds(p, Dl, stride=parts), :] = gu_acc[:, p * 128 : p * 128 + 128]


def run_weights(n2, cot, act, gh):
    n_dp, R, B, Dl = n2.shape
    size = act.shape[-1]
    whole = lambda *shape: pl.BlockSpec(shape, lambda z: (0,) * len(shape))
    one = lambda a: pl.BlockSpec((1, *a.shape[1:]), lambda z: (z,) + (0,) * (len(a.shape) - 1))
    out = ((Dl * 2 * size // 128, 128), (size, Dl))
    return pl.pallas_call(
        weights_kernel,
        grid=(n_dp,),
        out_shape=[jax.ShapeDtypeStruct(o, F32) for o in out],
        in_specs=[one(n2), one(cot), one(act), one(gh)],
        out_specs=[whole(*o) for o in out],
        scratch_shapes=[pltpu.VMEM((Dl, 2 * size), F32)],
        compiler_params=pltpu.CompilerParams(vmem_limit_bytes=VMEM_LIMIT),
        name="weights",
    )(n2, cot, act, gh)


def on_device(
    tokens, gain_one, in_weight, conv_weight, out_weight, gain_two, gate_up_weight, down_weight,
    cotangent, lengths,
):
    n_dp = lax.axis_size("dp")
    B, Dl = tokens.shape
    width = Dl * lax.axis_size("col")
    chunk = in_weight.shape[2] // n_dp
    split_in = chunk % 128 == 0
    block_out, d_tok, d_gain, d_conv, d_out, n1, n2, cot, act, gh, d_in, _, _ = run_block(
        n_dp,
        float(width),
        split_in,
        tokens,
        gain_one[None, :],
        jnp.transpose(in_weight, (1, 0, 2)),
        conv_weight,
        out_weight,
        gain_two[None, :],
        jnp.transpose(gate_up_weight, (1, 0, 2)),
        down_weight,
        cotangent,
        lengths,
    )
    d_gu, d_down = run_weights(n2, cot, act, gh)
    if split_in:
        d_in = jnp.transpose(d_in, (1, 0, 2)).astype(F32)
    else:
        d_in = lax.psum_scatter(
            jnp.einsum("rti,crktu->ikcu", n1, d_in, preferred_element_type=F32)
            .reshape(Dl, 3, -1)
            .astype(BF),
            "dp",
            scatter_dimension=2,
            tiled=True,
        ).astype(F32)
    part = d_conv.shape[1] * 1 // n_dp
    mine = lax.dynamic_slice(d_conv, (2, lax.axis_index("dp") * part), (3, part))
    return (
        block_out,
        d_tok,
        d_gain[0],
        d_in.reshape(Dl, 3, 1, 1, -1),
        mine.reshape(3, 1, 1, part),
        d_out.reshape(1, 1, -1, Dl),
        d_gain[1],
        d_gu.reshape(Dl, 2, 1, 1, -1),
        d_down.reshape(1, 1, -1, Dl),
    )


def solution(mesh):
    placed = (
        P(("dp", "row"), "col"),
        P("col"),
        P("col", None, "row"),
        P(None, ("row", "col")),
        P("row", "col"),
        P("col"),
        P("col", None, "row"),
        P("row", "col"),
        P(("dp", "row"), "col"),
        P(),
    )
    return jax.shard_map(
        on_device,
        mesh=mesh,
        in_specs=placed,
        out_specs=(
            P(("dp", "row"), "col"),
            P(("dp", "row"), "col"),
            P("col"),
            P("col", None, "row", "dp", None),
            P(None, ("row", "col"), "dp", None),
            P("row", "dp", None, "col"),
            P("col"),
            P("col", None, "row", "dp", None),
            P("row", "dp", None, "col"),
        ),
        check_vma=False,
    )
```

```python
import functools

import jax
import jax.numpy as jnp
from jax import lax
from jax.experimental import pallas as pl
from jax.experimental.pallas import tpu as pltpu
from jax.sharding import PartitionSpec as P

MESH = pl.DeviceIdType.MESH
BF = jnp.bfloat16
F32 = jnp.float32
EPS = 1e-05
VMEM_LIMIT = 63 * 2**20


def nn(a, b):
    return lax.dot_general(a, b, (((1,), (0,)), ((), ())), preferred_element_type=F32)


def nt(a, b):
    return lax.dot_general(a, b, (((1,), (1,)), ((), ())), preferred_element_type=F32)


class Links:
    def __init__(self, send_sems, recv_sems):
        self.send_sems, self.recv_sems = send_sems, recv_sems
        self.count = 0
        self.open = []

    def slot(self):
        self.count += 1
        return self.count - 1

    def copy(self, src, dst, to, slot=None):
        if slot is None:
            slot = self.slot()
        return pltpu.make_async_remote_copy(
            src_ref=src,
            dst_ref=dst,
            send_sem=self.send_sems.at[slot],
            recv_sem=self.recv_sems.at[slot],
            device_id=to,
            device_id_type=MESH,
        )

    def send(self, src, dst, to):
        c = self.copy(src, dst, to)
        c.start()
        self.open.append(c)
        return c

    def sent(self, *copies):
        for c in copies:
            c.wait_send()
            self.open = [o for o in self.open if o is not c]

    def close(self):
        for c in self.open:
            c.wait_send()
        self.open = []


def rows_loop(count, step, body):
    def one(i, carry):
        body(pl.multiple_of(i * step, step))
        return carry

    lax.fori_loop(0, count // step, one, 0)


def block_kernel(n_dp, width, split_in, *refs):
    (
        tok, g1_in, w_in, cw_in, w_out, g2_in, w_gu, w_dn, cot, lengths,
        block_out, d_tok, d_gain, d_conv, d_out, n1_h, n2z, cotz, actz, ghz, d_in, in_up, in_dn,
        w_in_v, w_out_v, w_gu_v, w_dn_v,
        xall, call, gat, act, gh, gp,
        proj_o, proj_r, mext, halo_b, cout, gext, halo_a, gg_s, gg_r, gg_o,
        hid_o, hid_r, ga_o, ga_r,
        rs_s, rs_r, rt_s, rt_r, acc_b, acc_o, down_o,
        resid, gres, ss_s, ss_r, red_s, red_r, red_z, po_r,
        g1, g2, cw, reach, in_add,
        send_sems, recv_sems, local_sems,
    ) = refs
    R, B, Dl = xall.shape
    Uc = w_out_v.shape[1]
    Fc = w_dn_v.shape[1]
    T = R * B
    dp, row, col = lax.axis_index("dp"), lax.axis_index("row"), lax.axis_index("col")
    other = 1 - col
    low = row + 1 - 2 * lax.rem(row, 2)
    high = row + 2 - 4 * lax.rem(row // 2, 2)
    row_a = low * other + high * col
    row_b = high * other + low * col
    row_d = low + high - row
    to_a, to_b, to_col = {"row": row_a}, {"row": row_b}, {"col": other}
    links = Links(send_sems, recv_sems)
    half = n_dp // 2
    holder = dp // half
    peers = [lax.rem(dp + k, n_dp) for k in range(n_dp)]
    sources = [lax.rem(dp + n_dp - k, n_dp) for k in range(n_dp)]

    loads = {"in": [], "out": [], "gu": [], "dn": []}
    n_local = 0

    def local(src, dst):
        nonlocal n_local
        c = pltpu.make_async_copy(src, dst, local_sems.at[n_local])
        n_local += 1
        c.start()
        return c

    for c in range(2):
        for k in range(3):
            loads["in"].append(local(w_in.at[k, :, pl.ds(c * Uc, Uc)], w_in_v.at[c, k]))
    for c in range(2):
        loads["dn"].append(local(w_dn.at[pl.ds(c * Fc, Fc), :], w_dn_v.at[c]))
        loads["out"].append(local(w_out.at[pl.ds(c * Uc, Uc), :], w_out_v.at[c]))
    for c in range(2):
        for k in range(2):
            loads["gu"].append(local(w_gu.at[k, :, pl.ds(c * Fc, Fc)], w_gu_v.at[c, k]))

    def loaded(name):
        for c in loads[name]:
            c.wait()

    barrier = pltpu.get_barrier_semaphore()
    for to in (to_col, {"row": low}, {"row": high}):
        pl.semaphore_signal(barrier, inc=1, device_id=to, device_id_type=MESH)
    for k in range(1, n_dp):
        pl.semaphore_signal(
            barrier, inc=1, device_id={"dp": lax.rem(dp + k, n_dp)}, device_id_type=MESH
        )

    def col_total(place):
        c = links.send(ss_s.at[place], ss_r.at[place], to_col)
        c.wait_recv()

    def gather(buf):
        first = links.send(buf.at[row], buf.at[row], to_a)
        second = links.send(buf.at[row], buf.at[row], to_b)
        state = {}

        def relay():
            first.wait_recv()
            state["third"] = links.send(buf.at[row_a], buf.at[row_a], to_b)

        def second_in():
            second.wait_recv()

        def third_in():
            state["third"].wait_recv()

        def all_sent():
            links.sent(first, second, state["third"])

        return relay, second_in, third_in, all_sent

    class Line:
        def __init__(self, first, dst, block=None):
            self.first, self.dst, self.block = first, dst, row if block is None else block
            self.up = [links.slot() for _ in range(n_dp + 1)]
            self.down = [links.slot() for _ in range(n_dp + 1)]
            self.sent_to = {}

        def at(self, z):
            return self.dst.at[z, self.block]

        def up_copy(self, hop):
            at = self.at(lax.rem(dp + n_dp - (hop - 1), n_dp))
            src = self.first if hop == 1 else at
            return links.copy(src, at, {"dp": peers[1]}, self.up[hop])

        def down_copy(self, hop):
            at = self.at(lax.rem(dp + hop - 1, n_dp))
            src = self.first if hop == 1 else at
            return links.copy(src, at, {"dp": sources[1]}, self.down[hop])

        def arrived(self, hop):
            @pl.when(dp >= hop)
            def _():
                self.up_copy(hop).wait_recv()

            @pl.when(dp + hop < n_dp)
            def _():
                self.down_copy(hop).wait_recv()

        def start(self, hop):
            if hop > 1:
                self.arrived(hop - 1)

            @pl.when((dp + 1 < n_dp) & (dp >= hop - 1))
            def _():
                self.up_copy(hop).start()

            @pl.when((dp >= 1) & (dp + hop - 1 < n_dp))
            def _():
                self.down_copy(hop).start()

        def sent(self, hop):
            @pl.when((dp + 1 < n_dp) & (dp >= hop - 1))
            def _():
                self.up_copy(hop).wait_send()

            @pl.when((dp >= 1) & (dp + hop - 1 < n_dp))
            def _():
                self.down_copy(hop).wait_send()

        def rest(self):
            for hop in range(4, n_dp):
                self.start(hop)
            self.arrived(n_dp - 1)

        def plane(self, *ks):
            if not self.sent_to:
                self.rest()
            for k in ks:
                at = self.dst.at[peers[k], row]
                self.sent_to[k] = (links.send(at, at, to_a), links.send(at, at, to_b))

        def finish(self, *ks):
            for k in ks:
                for c in self.sent_to[k]:
                    c.wait_recv()

    def put_to(ref):
        def put(n0, value):
            ref[:, n0 : n0 + value.shape[1]] = value.astype(ref.dtype)

        return put

    def both(first, second):
        def put(n0, value):
            first(n0, value[:B])
            second(n0, value[B:])

        return put

    def two(buf, blk, other_blk):
        return jnp.concatenate([buf[blk], buf[other_blk]], axis=0)

    def row_sum(sends, recvs, partial, filler=None):
        partial(row_d, row_a, both(put_to(sends.at[0]), put_to(sends.at[1])))
        c0 = links.send(sends.at[0], recvs.at[0], to_a)
        c1 = links.send(sends.at[1], recvs.at[1], to_a)
        partial(row_b, row, both(put_to(acc_b), put_to(acc_o)))
        c0.wait_recv()

        def combine(r0):
            at = pl.ds(r0, 32)
            sends[2, at, :] = (acc_b[at, :] + recvs[0, at, :].astype(F32)).astype(BF)

        rows_loop(B, 32, combine)
        c2 = links.send(sends.at[2], recvs.at[2], to_b)
        if filler is not None:
            filler()
        c1.wait_recv()
        c2.wait_recv()
        return c0, c1, c2

    def row_total(recvs, at):
        return acc_o[at, :] + recvs[1, at, :].astype(F32) + recvs[2, at, :].astype(F32)

    def lanes(x):
        return jnp.broadcast_to(x, (x.shape[0], 128))

    g1[...] = g1_in[...].astype(F32)
    g2[...] = g2_in[...].astype(F32)
    cw[...] = cw_in[...].astype(F32)
    starts = [jnp.int32(0)]
    for i in range(lengths.shape[0] - 1):
        starts.append(starts[-1] + lengths[i])

    def masks(r0):
        t = dp * T + r0 + lax.broadcasted_iota(jnp.int32, (16, 128), 0)
        count = jnp.full((16, 128), 2.0, F32)
        for start in starts:
            away = t - start
            count = jnp.where((away >= 0) & (away < 2), away.astype(F32), count)
        reach[pl.ds(r0, 16), :] = count

    rows_loop(T + 16, 16, masks)

    def squares(r0):
        at = pl.ds(r0, 32)
        x = tok[at, :].astype(F32)
        ss_s[0, at, :] = lanes(jnp.sum(x * x, axis=1, keepdims=True))

    rows_loop(B, 32, squares)
    pl.semaphore_wait(barrier, 3 + n_dp - 1)
    cot_line = Line(cot, cotz)
    cot_far = Line(call.at[row_d], cotz, row_d)
    n2_line = Line(xall.at[row], n2z)
    n2_far = Line(xall.at[row_d], n2z, row_d)
    cot_line.start(1)
    col_total(0)

    def scale_of(place, at):
        return lax.rsqrt((ss_s[place, at, :] + ss_r[place, at, :]) / width + EPS)[:, :1]

    def normed_one(r0):
        at = pl.ds(r0, 32)
        x = tok[at, :].astype(F32)
        xall[row, at, :] = (x * scale_of(0, at) * g1[...]).astype(BF)

    rows_loop(B, 32, normed_one)
    relay, second_in, third_in, all_sent = gather(xall)

    def project(blk, other_blk):
        x = two(xall, blk, other_blk)
        for k in range(3):
            y = nn(x, w_in_v[other, k]).astype(BF)
            gp[col, blk, k] = y[:B]
            gp[col, other_blk, k] = y[B:]
        copies = [links.send(gp.at[col, b], proj_r.at[b], to_col) for b in (blk, other_blk)]
        for k in range(3):
            y = nn(x, w_in_v[col, k])
            proj_o[k, pl.ds(pl.multiple_of(blk * B, B), B), :] = y[:B]
            proj_o[k, pl.ds(pl.multiple_of(other_blk * B, B), B), :] = y[B:]
        return copies

    loaded("in")
    relay()
    sent = project(row, row_a)
    cot_line.start(2)
    second_in()
    third_in()
    call[row] = cot[...]
    cot_relay, cot_second, cot_third, cot_all_sent = gather(call)
    sent += project(row_b, row_d)
    n1_out = local(xall, n1_h)

    for blk, c in zip((row, row_b, row_a, row_d), sent):
        c.wait_recv()
        base = blk * B

        def add(r0, blk=blk, base=base):
            at = pl.ds(r0, 32)
            to = pl.ds(pl.multiple_of(base + r0, 32), 32)
            g = [proj_o[k, to, :] + proj_r[blk, k, at, :].astype(F32) for k in range(3)]
            for k in range(3):
                proj_o[k, to, :] = g[k]
            mext[pl.ds(pl.multiple_of(base + r0 + 8, 8), 32), :] = g[0] * g[2]

        rows_loop(B, 32, add)
    links.sent(*sent)

    behind = links.slot()

    @pl.when(dp < n_dp - 1)
    def _():
        links.copy(mext.at[pl.ds(T, 8), :], halo_b, {"dp": lax.rem(dp + 1, n_dp)}, behind).start()

    @pl.when(dp > 0)
    def _():
        links.copy(mext.at[pl.ds(T, 8), :], halo_b, {"dp": lax.rem(dp + 1, n_dp)}, behind).wait_recv()
        mext[0:8, :] = halo_b[...]

    @pl.when(dp == 0)
    def _():
        mext[0:8, :] = jnp.zeros((8, Uc), F32)

    cot_relay()
    cot_line.start(3)
    CH = B // 2

    def masks_of(at):
        count = jnp.concatenate([reach[at, :]] * (Uc // 128), axis=1)
        return jnp.minimum(count, 1.0), jnp.maximum(count - 1.0, 0.0)

    for i in range(T // CH):
        at = pl.ds(i * CH, CH)
        x = mext[pl.ds(i * CH, CH + 8), :]
        m1, m2 = masks_of(at)
        y = cw[0:1, :] * x[8 : 8 + CH]
        y = y + cw[1:2, :] * m1 * x[7 : 7 + CH]
        y = y + cw[2:3, :] * m2 * x[6 : 6 + CH]
        cout[at, :] = y
        gat[col, i * CH // B, i * CH % B : i * CH % B + CH, :] = (proj_o[1, at, :] * y).astype(BF)
    gated_in = links.send(gat.at[col], gat.at[col], to_col)
    cot_second()
    gated_in.wait_recv()

    loaded("out")
    n1_out.wait()
    all_sent()

    def out_partial(blk, other_blk, put):
        x = [two(gat.at[c], blk, other_blk) for c in range(2)]
        for n0 in range(0, Dl, Dl // 4):
            n = slice(n0, n0 + Dl // 4)
            put(n0, nn(x[0], w_out_v[0, :, n]) + nn(x[1], w_out_v[1, :, n]))

    sent = row_sum(rs_s, rs_r, out_partial)

    def residual(r0):
        at = pl.ds(r0, 32)
        x = tok[at, :].astype(F32) + row_total(rs_r, at)
        resid[at, :] = x
        ss_s[1, at, :] = lanes(jnp.sum(x * x, axis=1, keepdims=True))

    cot_third()
    cot_far.start(1)
    rows_loop(B, 32, residual)
    links.sent(*sent)
    col_total(1)

    def normed_two(r0):
        at = pl.ds(r0, 32)
        xall[row, at, :] = (resid[at, :] * scale_of(1, at) * g2[...]).astype(BF)

    rows_loop(B, 32, normed_two)
    relay, second_in, third_in, all_sent = gather(xall)
    n2_line.start(1)

    loaded("dn")
    ga_step = min(Fc, 256)

    def ga_other(i, carry):
        n = pl.ds(pl.multiple_of(i * ga_step, ga_step), ga_step)
        y = nt(call[...].reshape(T, Dl), w_dn_v[other, n, :]).astype(BF)
        act[col, :, :, n] = y.reshape(R, B, ga_step)
        return carry

    def ga_own(i, carry):
        n = pl.ds(pl.multiple_of(i * ga_step, ga_step), ga_step)
        ga_o[:, :, n] = nt(call[...].reshape(T, Dl), w_dn_v[col, n, :]).reshape(R, B, ga_step)
        return carry

    lax.fori_loop(0, Fc // ga_step, ga_other, 0)
    ga_sent = links.send(act.at[col], ga_r, to_col)
    relay()
    lax.fori_loop(0, Fc // ga_step, ga_own, 0)
    cot_out = local(call, cotz.at[dp])
    n2_line.start(2)
    cot_far.start(2)

    def hidden_other(blk, other_blk):
        def one(k, carry):
            x = two(xall, blk, other_blk)
            for n0 in range(0, Fc, Fc // 2):
                n = slice(n0, n0 + Fc // 2)
                y = nn(x, w_gu_v[other, k, :, n]).astype(BF)
                gh[col, blk, k, :, n] = y[:B]
                gh[col, other_blk, k, :, n] = y[B:]
            return carry

        lax.fori_loop(0, 2, one, 0)
        return [links.send(gh.at[col, b], hid_r.at[b], to_col) for b in (blk, other_blk)]

    loaded("gu")
    hid_sent = hidden_other(row, row_a)
    second_in()
    third_in()
    hid_sent += hidden_other(row_b, row_d)
    n2_out = local(xall, n2z.at[dp])
    cot_line.plane(*range(1, n_dp))
    n2_far.start(1)

    gh_in = {}
    ga_sent.wait_recv()
    links.sent(ga_sent)
    H = Fc // 2
    for blks, mine_at, theirs_at in (((row_d, row_a), (3, 1), (3, 2)), ((row_b, row), (2, 0), (1, 0))):
        for h in range(2):

            def one(k, carry, h=h, blks=blks):
                y = nn(two(xall, *blks), w_gu_v[col, k, :, h * H : h * H + H])
                hid_o[k, :, :H] = y[:B]
                hid_o[k, :, H:] = y[B:]
                return carry

            lax.fori_loop(0, 2, one, 0)
            for i, blk in enumerate(blks):
                if h == 0:
                    hid_sent[theirs_at[i]].wait_recv()
                    links.sent(hid_sent[mine_at[i]])

                def activate(r0, blk=blk, i=i, h=h):
                    at = pl.ds(r0, 32)
                    n = slice(h * H, h * H + H)
                    own = slice(i * H, i * H + H)
                    gate = hid_o[0, at, own] + hid_r[blk, 0, at, n].astype(F32)
                    up = hid_o[1, at, own] + hid_r[blk, 1, at, n].astype(F32)
                    ga = ga_o[blk, at, n] + ga_r[blk, at, n].astype(F32)
                    s = jax.nn.sigmoid(gate)
                    silu = gate * s
                    act[col, blk, at, n] = (silu * up).astype(BF)
                    gh[col, blk, 0, at, n] = (ga * up * s * (1.0 + gate * (1.0 - s))).astype(BF)
                    gh[col, blk, 1, at, n] = (ga * silu).astype(BF)

                rows_loop(B, 32, activate)
                if h == 1:
                    gh_in[mine_at[i]] = (
                        links.send(gh.at[col, blk], gh.at[col, blk], to_col),
                        links.send(act.at[col, blk], act.at[col, blk], to_col),
                    )
    cot_far.start(3)
    n2_far.start(2)
    for pair in gh_in.values():
        for c in pair:
            c.wait_recv()
    size = actz.shape[-1]
    mine = pl.ds(pl.multiple_of(lax.rem(dp, half) * size, size), size)
    kept_units = [
        local(act.at[holder, :, :, mine], actz.at[dp]),
        local(gh.at[holder, :, :, :, mine], ghz.at[dp]),
    ]
    kept = []
    n2_out.wait()
    n2_line.start(3)
    n2_line.sent(1)
    n2_far.sent(1)
    all_sent()

    def gu_partial(blk, other_blk, put):
        for n0 in range(0, Dl, Dl // 4):
            n = slice(n0, n0 + Dl // 4)
            total = None
            for c in range(2):
                for k in range(2):
                    part = nt(two(gh.at[c, :, k], blk, other_blk), w_gu_v[c, k, n, :])
                    total = part if total is None else total + part
            put(n0, total)

    sent = row_sum(rs_s, rs_r, gu_partial)

    def back_two(r0):
        at = pl.ds(r0, 32)
        g = row_total(rs_r, at)
        gres[at, :] = g
        ss_s[2, at, :] = lanes(jnp.sum(g * g2[...] * resid[at, :], axis=1, keepdims=True))

    rows_loop(B, 32, back_two)
    links.sent(*sent)
    col_total(2)

    def inner_of(place, at):
        return (ss_s[place, at, :] + ss_r[place, at, :])[:, :1]

    def branch(i, gain):
        at = pl.ds(pl.multiple_of(i * 32, 32), 32)
        g = gres[at, :]
        x = resid[at, :]
        s = scale_of(1, at)
        y = cot[at, :].astype(F32) + s * g2[...] * g - x * (s * s * s) * inner_of(2, at) / width
        gres[at, :] = y
        xall[row, at, :] = y.astype(BF)
        return gain + jnp.sum(g * x * s, axis=0, keepdims=True)

    n2_far.start(3)
    cot_out.wait()
    cot_all_sent()
    cot_far.sent(1)
    n1_back = local(n1_h, call)
    gain_two = lax.fori_loop(0, B // 32, branch, jnp.zeros((1, Dl), F32))
    relay, second_in, third_in, all_sent = gather(xall)

    def down_partial(blk, other_blk, put):
        x = [two(act.at[c], blk, other_blk) for c in range(2)]
        for n0 in range(0, Dl, Dl // 4):
            n = slice(n0, n0 + Dl // 4)
            put(n0, nn(x[0], w_dn_v[0, :, n]) + nn(x[1], w_dn_v[1, :, n]))

    down_partial(row_d, row_a, both(put_to(rt_s.at[0]), put_to(rt_s.at[1])))

    def gated_other(blk, other_blk):
        x = two(xall, blk, other_blk)
        y = nt(x, w_out_v[other]).astype(BF)
        gg_s[blk] = y[:B]
        gg_s[other_blk] = y[B:]
        copies = [links.send(gg_s.at[b], gg_r.at[b], to_col) for b in (blk, other_blk)]
        y = nt(x, w_out_v[col])
        gg_o[blk] = y[:B]
        gg_o[other_blk] = y[B:]
        return copies

    relay()
    sent = gated_other(row, row_a)
    down_partial(row_b, row, both(put_to(rt_s.at[2]), put_to(down_o)))
    second_in()
    third_in()
    sent += gated_other(row_b, row_d)
    n2_line.plane(1)

    for blk, c in zip((row, row_b, row_a, row_d), sent):
        c.wait_recv()
        base = blk * B

        def conv_grad(r0, blk=blk, base=base):
            at = pl.ds(r0, 32)
            to = pl.ds(pl.multiple_of(base + r0, 32), 32)
            g = gg_o[blk, at, :] + gg_r[blk, at, :].astype(F32)
            gext[to, :] = g * proj_o[1, to, :]
            gp[col, blk, 1, at, :] = (g * cout[to, :]).astype(BF)

        rows_loop(B, 32, conv_grad)

    ahead = links.slot()

    @pl.when(dp > 0)
    def _():
        links.copy(gext.at[pl.ds(0, 8), :], halo_a, {"dp": lax.rem(dp + n_dp - 1, n_dp)}, ahead).start()

    @pl.when(dp < n_dp - 1)
    def _():
        links.copy(gext.at[pl.ds(0, 8), :], halo_a, {"dp": lax.rem(dp + n_dp - 1, n_dp)}, ahead).wait_recv()
        gext[T : T + 8, :] = halo_a[...]

    @pl.when(dp == n_dp - 1)
    def _():
        gext[T : T + 8, :] = jnp.zeros((8, Uc), F32)

    terms = [jnp.zeros((1, Uc), F32) for _ in range(3)]
    for i in range(T // CH):
        at = pl.ds(i * CH, CH)
        more = pl.ds(i * CH, CH + 8)
        x = mext[more, :]
        g = gext[more, :]
        m1, m2 = masks_of(more)
        now = g[:CH]
        terms[0] = terms[0] + jnp.sum(now * x[8 : 8 + CH], axis=0, keepdims=True)
        terms[1] = terms[1] + jnp.sum(m1[:CH] * now * x[7 : 7 + CH], axis=0, keepdims=True)
        terms[2] = terms[2] + jnp.sum(m2[:CH] * now * x[6 : 6 + CH], axis=0, keepdims=True)
        y = cw[0:1, :] * now
        y = y + cw[1:2, :] * (m1 * g)[1 : 1 + CH]
        y = y + cw[2:3, :] * (m2 * g)[2 : 2 + CH]
        blk, to = i * CH // B, slice(i * CH % B, i * CH % B + CH)
        gp[col, blk, 0, to, :] = (y * proj_o[2, at, :]).astype(BF)
        gp[col, blk, 2, to, :] = (y * proj_o[0, at, :]).astype(BF)
    red_s[...] = jnp.zeros_like(red_s)
    for k in range(3):
        red_s[2 + k : 3 + k, :Uc] = terms[k]
    gp_in = links.send(gp.at[col], gp.at[col], to_col)
    gp_in.wait_recv()
    if not split_in:
        kept.append(local(gp, d_in))

    def in_partial(blk, other_blk, put):
        for n0 in range(0, Dl, Dl // 4):
            n = slice(n0, n0 + Dl // 4)
            total = None
            for c in range(2):
                for k in range(3):
                    part = nt(two(gp.at[c, :, k], blk, other_blk), w_in_v[c, k, n, :])
                    total = part if total is None else total + part
            put(n0, total)

    po_all = []

    rows = po_r.shape[1]

    def out_chunk(z):
        return (z // half, pl.ds(pl.multiple_of(lax.rem(z, half) * rows, rows), rows), slice(None))

    def out_weights():
        for z in range(n_dp):
            at = pl.ds(z % half * rows, rows)
            g = lax.dot_general(
                gat[z // half, :, :, at].reshape(T, rows), xall[...].reshape(T, Dl),
                (((0,), (0,)), ((), ())), preferred_element_type=F32,
            )
            w_out_v[z // half, at, :] = g.astype(BF)
        for k in range(1, n_dp):
            po_all.append(links.send(w_out_v.at[out_chunk(peers[k])], po_r.at[dp], {"dp": peers[k]}))

    up_slots = [links.slot() for _ in range(n_dp)][0]
    down_slots = [links.slot() for _ in range(n_dp)][0]
    unit = 2 * Uc // n_dp

    def in_chunk(z):
        at = pl.ds(pl.multiple_of(lax.rem(z, half) * unit, unit), unit)
        return (z // half, slice(None), slice(None), at)

    def go_up(z):
        return links.copy(w_in_v.at[in_chunk(z)], in_up.at[z], {"dp": peers[1]}, up_slots + z)

    def go_down(z):
        return links.copy(w_in_v.at[in_chunk(z)], in_dn.at[z], {"dp": sources[1]}, down_slots + z)

    def in_weights():
        n1_back.wait()
        x = call[...].reshape(T, Dl)
        units = [(c, k) for c in range(2) for k in range(3)]
        g = jnp.concatenate([gp[c, :, k].reshape(T, Uc) for c, k in units], axis=1)
        for m0 in range(0, Dl, Dl // 4):
            m = slice(m0, m0 + Dl // 4)
            y = lax.dot_general(x[:, m], g, (((0,), (0,)), ((), ())), preferred_element_type=F32)
            for u, (c, k) in enumerate(units):
                w_in_v[c, k, m, :] = y[:, u * Uc : u * Uc + Uc].astype(BF)
        for z in range(n_dp - 1, 0, -1):

            @pl.when(dp == 0)
            def _(z=z):
                go_up(z).start()

        for z in range(n_dp - 1):

            @pl.when(dp == n_dp - 1)
            def _(z=z):
                go_down(z).start()

    def take(src, z):
        c = pltpu.make_async_copy(src, in_add, local_sems.at[local_sems.shape[0] - 1])
        c.start()
        c.wait()
        at = in_chunk(z)
        for k in range(3):
            here = (at[0], k, slice(None), at[3])
            w_in_v[here] = (w_in_v[here].astype(F32) + in_add[k].astype(F32)).astype(BF)

    def in_step(step):
        up = n_dp - 1 - step + dp

        @pl.when((dp > 0) & (dp <= step))
        def _():
            go_up(up).wait_recv()
            take(in_up.at[up], up)
            go_up(up).start()

        down = step - (n_dp - 1 - dp)

        @pl.when((dp < n_dp - 1) & (down >= 0))
        def _():
            go_down(down).wait_recv()
            take(in_dn.at[down], down)
            go_down(down).start()

    def in_end():
        @pl.when(dp > 0)
        def _():
            go_up(dp).wait_recv()
            take(in_up.at[dp], dp)

        @pl.when(dp < n_dp - 1)
        def _():
            go_down(dp).wait_recv()
            take(in_dn.at[dp], dp)

        out = local(w_in_v.at[in_chunk(dp)], d_in)
        for z in range(1, n_dp):

            @pl.when(dp < z)
            def _(z=z):
                go_up(z).wait_send()

        for z in range(n_dp - 1):

            @pl.when(dp > z)
            def _(z=z):
                go_down(z).wait_send()

        out.wait()

    def weights_wait():
        if split_in:
            in_weights()
        else:
            n1_back.wait()
        out_weights()

    sent_in = row_sum(rs_s, rs_r, in_partial, filler=weights_wait)
    n2_line.plane(*range(2, n_dp))
    down_sent = [
        links.send(rt_s.at[0], rt_r.at[0], to_a),
        links.send(rt_s.at[1], rt_r.at[1], to_a),
    ]

    def back_one(r0):
        at = pl.ds(r0, 32)
        g = row_total(rs_r, at)
        acc_o[at, :] = g
        ss_s[3, at, :] = lanes(
            jnp.sum(g * g1[...] * tok[at, :].astype(F32), axis=1, keepdims=True)
        )

    rows_loop(B, 32, back_one)
    col_total(3)

    def token_grad(i, gain):
        at = pl.ds(pl.multiple_of(i * 32, 32), 32)
        g = acc_o[at, :]
        x = tok[at, :].astype(F32)
        s = scale_of(0, at)
        y = gres[at, :] + s * g1[...] * g - x * (s * s * s) * inner_of(3, at) / width
        gres[at, :] = y
        return gain + jnp.sum(g * x * s, axis=0, keepdims=True)

    gain_one = lax.fori_loop(0, B // 32, token_grad, jnp.zeros((1, Dl), F32))

    kept.append(local(gres, d_tok))

    red_s[0:1, :] = gain_one
    red_s[1:2, :] = gain_two
    c0 = links.send(red_s, red_r.at[0], to_a)
    cot_far.rest()
    n2_far.rest()
    for c in kept_units:
        c.wait()
    for pair in gh_in.values():
        links.sent(*pair)
    all_sent()

    slots = Fc // size

    def place(k, r, rank):
        q = (k - 1) * 2 + r
        lanes_at = slice(q % slots * size, q % slots * size + size)
        return (q // slots, *([slice(None)] * (rank - 2)), lanes_at)

    def again(k):
        z = peers[k]
        loads = [local(n2z.at[z], xall), local(cotz.at[z], call)]
        for c in loads:
            c.wait()
        copies = []
        for core, keep in ((other, False), (col, True)):
            x = xall[pl.ds(core * 2, 2)].reshape(2 * B, Dl)
            for j in range(2):
                h = nn(x, w_gu_v[holder, j, :, mine])
                for r in range(2):
                    if keep:
                        hid_o[j, :, r * size : r * size + size] = h[r * B : r * B + B]
                    else:
                        q, _, _, n = place(k, r, 4)
                        gh[0, q, j, :, n] = h[r * B : r * B + B].astype(BF)
            y = call[pl.ds(core * 2, 2)].reshape(2 * B, Dl)
            g = nt(y, w_dn_v[holder, mine, :])
            for r in range(2):
                if keep:
                    ga_o[r, :, :size] = g[r * B : r * B + B]
                else:
                    q, _, n = place(k, r, 3)
                    act[0, q, :, n] = g[r * B : r * B + B].astype(BF)
            if not keep:
                for r in range(2):
                    h_at, g_at = place(k, r, 4), place(k, r, 3)
                    copies.append(links.send(gh.at[0].at[h_at], hid_r.at[h_at], to_col))
                    copies.append(links.send(act.at[0].at[g_at], ga_r.at[g_at], to_col))
        for c in copies:
            c.wait_recv()
        done = []
        for r in range(2):
            q, _, n = place(k, r, 3)

            def finish(r0, r=r, q=q, n=n):
                at = pl.ds(r0, 32)
                own = slice(r * size, r * size + size)
                gate = hid_o[0, at, own] + hid_r[q, 0, at, n].astype(F32)
                up = hid_o[1, at, own] + hid_r[q, 1, at, n].astype(F32)
                ga = ga_o[r, at, :size] + ga_r[q, at, n].astype(F32)
                s = jax.nn.sigmoid(gate)
                silu = gate * s
                act[1, q, at, n] = (silu * up).astype(BF)
                gh[1, q, 0, at, n] = (ga * up * s * (1.0 + gate * (1.0 - s))).astype(BF)
                gh[1, q, 1, at, n] = (ga * silu).astype(BF)

            rows_loop(B, 32, finish)
            blk = col * 2 + r
            h_src, a_src = gh.at[1].at[place(k, r, 4)], act.at[1].at[place(k, r, 3)]
            done.append(links.send(h_src, ghz.at[z, blk], to_col))
            done.append(links.send(a_src, actz.at[z, blk], to_col))
            kept.append(local(h_src, ghz.at[z, blk]))
            kept.append(local(a_src, actz.at[z, blk]))
        return done

    n2_line.finish(1)
    cot_line.finish(*range(1, n_dp))
    again_in = again(1)
    if split_in:
        in_step(1)

    down_sent[0].wait_recv()

    def down_combine(r0):
        at = pl.ds(r0, 16)
        rt_s[2, at, :] = (rt_s[2, at, :].astype(F32) + rt_r[0, at, :].astype(F32)).astype(BF)

    rows_loop(B, 16, down_combine)
    down_sent.append(links.send(rt_s.at[2], rt_r.at[2], to_b))
    c0.wait_recv()
    links.sent(c0)
    red_s[0:2, :] = red_s[0:2, :] + red_r[0, 0:2, :]
    c1 = links.send(red_s, red_r.at[1], to_b)
    n2_line.finish(2)
    again_in += again(2)
    if split_in:
        for step in range(2, n_dp - 1):
            in_step(step)
    c1.wait_recv()
    red_z[dp] = red_s[...]
    red_z[dp, 0:2, :] = red_s[0:2, :] + red_r[1, 0:2, :]
    arrived = []
    for k in range(1, n_dp):
        arrived.append(links.send(red_z.at[dp], red_z.at[dp], {"dp": lax.rem(dp + k, n_dp)}))
    for k in range(3, n_dp):
        n2_line.finish(k)
        again_in += again(k)
    for c in down_sent[1:]:
        c.wait_recv()

    def block_rows(r0):
        at = pl.ds(r0, 16)
        total = down_o[at, :] + rt_r[1, at, :].astype(F32) + rt_r[2, at, :].astype(F32)
        block_out[at, :] = (resid[at, :] + total).astype(BF)

    rows_loop(B, 16, block_rows)
    for c in arrived:
        c.wait_recv()
    total = red_z[0]
    for k in range(1, n_dp):
        total = total + red_z[k]
    d_gain[...] = total
    d_conv[...] = total[:, :Uc]

    @pl.when(dp < n_dp - 1)
    def _():
        links.copy(mext.at[pl.ds(T, 8), :], halo_b, {"dp": lax.rem(dp + 1, n_dp)}, behind).wait_send()

    @pl.when(dp > 0)
    def _():
        links.copy(gext.at[pl.ds(0, 8), :], halo_a, {"dp": lax.rem(dp + n_dp - 1, n_dp)}, ahead).wait_send()

    for c in again_in:
        c.wait_recv()
    for c in po_all:
        c.wait_recv()
    out_total = w_out_v[out_chunk(dp)].astype(F32)
    for k in range(1, n_dp):
        out_total = out_total + po_r[peers[k]].astype(F32)
    acc_b[:rows, :] = out_total
    kept.append(local(acc_b.at[pl.ds(0, rows), :], d_out))
    if split_in:
        in_end()
    cot_line.sent(1)
    for hop in range(2, n_dp):
        for line in (cot_line, cot_far, n2_line, n2_far):
            line.sent(hop)
    for c in kept:
        c.wait()
    assert links.count <= send_sems.shape[0]
    links.close()


def run_block(n_dp, width, split_in, tok, g1, w_in, cw, w_out, g2, w_gu, w_dn, cot, lengths):
    B, Dl = tok.shape
    R = 4
    T = R * B
    Uc = w_out.shape[0] // 2
    Fc = w_dn.shape[0] // 2
    vm = lambda shape, kind=BF: pltpu.VMEM(shape, kind)
    any_spec, vmem_spec = pl.BlockSpec(memory_space=pl.ANY), pl.BlockSpec(memory_space=pltpu.VMEM)
    shape = jax.ShapeDtypeStruct
    rows = shape((n_dp, R, B, Dl), BF)
    return pl.pallas_call(
        functools.partial(block_kernel, n_dp, width, split_in),
        out_shape=(
            shape((B, Dl), BF),
            shape((B, Dl), F32),
            shape((8, Dl), F32),
            shape((8, Uc), F32),
            shape((2 * Uc // n_dp, Dl), F32),
            shape((R, B, Dl), BF),
            rows,
            rows,
            shape((n_dp, R, B, 2 * Fc // n_dp), BF),
            shape((n_dp, R, 2, B, 2 * Fc // n_dp), BF),
            shape((3, Dl, 2 * Uc // n_dp) if split_in else (2, R, 3, B, Uc), BF),
            shape((n_dp, 3, Dl, 2 * Uc // n_dp), BF),
            shape((n_dp, 3, Dl, 2 * Uc // n_dp), BF),
        ),
        in_specs=[
            vmem_spec, vmem_spec, any_spec, vmem_spec, any_spec, vmem_spec,
            any_spec, any_spec, vmem_spec, pl.BlockSpec(memory_space=pltpu.SMEM),
        ],
        out_specs=[vmem_spec, any_spec, vmem_spec, vmem_spec] + [any_spec] * 9,
        scratch_shapes=[
            vm((2, 3, Dl, Uc)), vm((2, Uc, Dl)), vm((2, 2, Dl, Fc)), vm((2, Fc, Dl)),
            vm((R, B, Dl)), vm((R, B, Dl)),
            vm((2, R, B, Uc)), vm((2, R, B, Fc)), vm((2, R, 2, B, Fc)), vm((2, R, 3, B, Uc)),
            vm((3, T, Uc), F32), vm((R, 3, B, Uc)), vm((T + 8, Uc), F32), vm((8, Uc), F32),
            vm((T, Uc), F32), vm((T + 8, Uc), F32), vm((8, Uc), F32),
            vm((R, B, Uc)), vm((R, B, Uc)), vm((R, B, Uc), F32),
            vm((2, B, Fc), F32), vm((R, 2, B, Fc)), vm((R, B, Fc), F32), vm((R, B, Fc)),
            vm((3, B, Dl)), vm((3, B, Dl)), vm((3, B, Dl)), vm((3, B, Dl)),
            vm((B, Dl), F32), vm((B, Dl), F32), vm((B, Dl), F32),
            vm((B, Dl), F32), vm((B, Dl), F32),
            vm((4, B, 128), F32), vm((4, B, 128), F32),
            vm((8, Dl), F32), vm((2, 8, Dl), F32), vm((n_dp, 8, Dl), F32),
            vm((n_dp, 2 * Uc // n_dp, Dl)),
            vm((1, Dl), F32), vm((1, Dl), F32), vm((3, Uc), F32),
            vm((T + 16, 128), F32), vm((3, Dl, 2 * Uc // n_dp)),
            pltpu.SemaphoreType.DMA((96 + 48 * n_dp,)), pltpu.SemaphoreType.DMA((96 + 48 * n_dp,)),
            pltpu.SemaphoreType.DMA((32 + 6 * n_dp,)),
        ],
        compiler_params=pltpu.CompilerParams(
            collective_id=0, has_side_effects=True, vmem_limit_bytes=VMEM_LIMIT
        ),
        name="block",
    )(tok, g1, w_in, cw, w_out, g2, w_gu, w_dn, cot, lengths)


def weights_kernel(n2, cot, act, gh, gu_out, dn_out, gu_acc):
    _, R, B, Dl = n2.shape
    T, size = R * B, act.shape[-1]
    step, tile = pl.program_id(0), 256

    def tn(a, b):
        return lax.dot_general(a, b, (((0,), (0,)), ((), ())), preferred_element_type=F32)

    @pl.when(step == 0)
    def _():
        gu_acc[...] = jnp.zeros_like(gu_acc)
        dn_out[...] = jnp.zeros_like(dn_out)

    g = jnp.concatenate([gh[0, :, k].reshape(T, size) for k in range(2)], axis=1)
    for m in range(0, Dl, tile):
        at = slice(m, m + tile)
        gu_acc[at, :] += tn(n2[0, :, :, at].reshape(T, tile), g)
    c = cot[0].reshape(T, Dl)
    for m in range(0, size, min(tile, size)):
        at = slice(m, m + min(tile, size))
        dn_out[at, :] += tn(act[0, :, :, at].reshape(T, min(tile, size)), c)

    @pl.when(step == pl.num_programs(0) - 1)
    def _():
        parts = 2 * size // 128
        for p in range(parts):
            gu_out[pl.ds(p, Dl, stride=parts), :] = gu_acc[:, p * 128 : p * 128 + 128]


def run_weights(n2, cot, act, gh):
    n_dp, R, B, Dl = n2.shape
    size = act.shape[-1]
    whole = lambda *shape: pl.BlockSpec(shape, lambda z: (0,) * len(shape))
    one = lambda a: pl.BlockSpec((1, *a.shape[1:]), lambda z: (z,) + (0,) * (len(a.shape) - 1))
    out = ((Dl * 2 * size // 128, 128), (size, Dl))
    return pl.pallas_call(
        weights_kernel,
        grid=(n_dp,),
        out_shape=[jax.ShapeDtypeStruct(o, F32) for o in out],
        in_specs=[one(n2), one(cot), one(act), one(gh)],
        out_specs=[whole(*o) for o in out],
        scratch_shapes=[pltpu.VMEM((Dl, 2 * size), F32)],
        compiler_params=pltpu.CompilerParams(vmem_limit_bytes=VMEM_LIMIT),
        name="weights",
    )(n2, cot, act, gh)


def on_device(
    tokens, gain_one, in_weight, conv_weight, out_weight, gain_two, gate_up_weight, down_weight,
    cotangent, lengths,
):
    n_dp = lax.axis_size("dp")
    B, Dl = tokens.shape
    width = Dl * lax.axis_size("col")
    chunk = in_weight.shape[2] // n_dp
    split_in = chunk % 128 == 0
    block_out, d_tok, d_gain, d_conv, d_out, n1, n2, cot, act, gh, d_in, _, _ = run_block(
        n_dp,
        float(width),
        split_in,
        tokens,
        gain_one[None, :],
        jnp.transpose(in_weight, (1, 0, 2)),
        conv_weight,
        out_weight,
        gain_two[None, :],
        jnp.transpose(gate_up_weight, (1, 0, 2)),
        down_weight,
        cotangent,
        lengths,
    )
    d_gu, d_down = run_weights(n2, cot, act, gh)
    if split_in:
        d_in = jnp.transpose(d_in, (1, 0, 2)).astype(F32)
    else:
        d_in = lax.psum_scatter(
            jnp.einsum("rti,crktu->ikcu", n1, d_in, preferred_element_type=F32)
            .reshape(Dl, 3, -1)
            .astype(BF),
            "dp",
            scatter_dimension=2,
            tiled=True,
        ).astype(F32)
    part = d_conv.shape[1] * 1 // n_dp
    mine = lax.dynamic_slice(d_conv, (2, lax.axis_index("dp") * part), (3, part))
    return (
        block_out,
        d_tok,
        d_gain[0],
        d_in.reshape(Dl, 3, 1, 1, -1),
        mine.reshape(3, 1, 1, part),
        d_out.reshape(1, 1, -1, Dl),
        d_gain[1],
        d_gu.reshape(Dl, 2, 1, 1, -1),
        d_down.reshape(1, 1, -1, Dl),
    )


def solution(mesh):
    placed = (
        P(("dp", "row"), "col"),
        P("col"),
        P("col", None, "row"),
        P(None, ("row", "col")),
        P("row", "col"),
        P("col"),
        P("col", None, "row"),
        P("row", "col"),
        P(("dp", "row"), "col"),
        P(),
    )
    return jax.shard_map(
        on_device,
        mesh=mesh,
        in_specs=placed,
        out_specs=(
            P(("dp", "row"), "col"),
            P(("dp", "row"), "col"),
            P("col"),
            P("col", None, "row", "dp", None),
            P(None, ("row", "col"), "dp", None),
            P("row", "dp", None, "col"),
            P("col"),
            P("col", None, "row", "dp", None),
            P("row", "dp", None, "col"),
        ),
        check_vma=False,
    )
```

```python
import functools

import jax
import jax.numpy as jnp
from jax import lax
from jax.experimental import pallas as pl
from jax.experimental.pallas import tpu as pltpu
from jax.sharding import PartitionSpec as P

MESH = pl.DeviceIdType.MESH
BF = jnp.bfloat16
F32 = jnp.float32
EPS = 1e-05
VMEM_LIMIT = 63 * 2**20


def nn(a, b):
    return lax.dot_general(a, b, (((1,), (0,)), ((), ())), preferred_element_type=F32)


def nt(a, b):
    return lax.dot_general(a, b, (((1,), (1,)), ((), ())), preferred_element_type=F32)


class Links:
    def __init__(self, send_sems, recv_sems):
        self.send_sems, self.recv_sems = send_sems, recv_sems
        self.count = 0
        self.open = []

    def slot(self):
        self.count += 1
        return self.count - 1

    def copy(self, src, dst, to, slot=None):
        if slot is None:
            slot = self.slot()
        return pltpu.make_async_remote_copy(
            src_ref=src,
            dst_ref=dst,
            send_sem=self.send_sems.at[slot],
            recv_sem=self.recv_sems.at[slot],
            device_id=to,
            device_id_type=MESH,
        )

    def send(self, src, dst, to):
        c = self.copy(src, dst, to)
        c.start()
        self.open.append(c)
        return c

    def sent(self, *copies):
        for c in copies:
            c.wait_send()
            self.open = [o for o in self.open if o is not c]

    def close(self):
        for c in self.open:
            c.wait_send()
        self.open = []


def rows_loop(count, step, body):
    def one(i, carry):
        body(pl.multiple_of(i * step, step))
        return carry

    lax.fori_loop(0, count // step, one, 0)


def block_kernel(n_dp, width, split_in, *refs):
    (
        tok, g1_in, w_in, cw_in, w_out, g2_in, w_gu, w_dn, cot, lengths,
        block_out, d_tok, d_gain, d_conv, d_out, n1_h, n2z, cotz, actz, ghz, d_in, in_up, in_dn,
        w_in_v, w_out_v, w_gu_v, w_dn_v,
        xall, call, gat, act, gh, gp,
        proj_o, proj_r, mext, halo_b, cout, gext, halo_a, gg_s, gg_r, gg_o,
        hid_o, hid_r, ga_o, ga_r,
        rs_s, rs_r, rt_s, rt_r, acc_b, acc_o, down_o,
        resid, gres, ss_s, ss_r, red_s, red_r, red_z, po_r,
        g1, g2, cw, reach, in_add,
        send_sems, recv_sems, local_sems,
    ) = refs
    R, B, Dl = xall.shape
    Uc = w_out_v.shape[1]
    Fc = w_dn_v.shape[1]
    T = R * B
    dp, row, col = lax.axis_index("dp"), lax.axis_index("row"), lax.axis_index("col")
    other = 1 - col
    low = row + 1 - 2 * lax.rem(row, 2)
    high = row + 2 - 4 * lax.rem(row // 2, 2)
    row_a = low * other + high * col
    row_b = high * other + low * col
    row_d = low + high - row
    to_a, to_b, to_col = {"row": row_a}, {"row": row_b}, {"col": other}
    links = Links(send_sems, recv_sems)
    half = n_dp // 2
    holder = dp // half
    peers = [lax.rem(dp + k, n_dp) for k in range(n_dp)]
    sources = [lax.rem(dp + n_dp - k, n_dp) for k in range(n_dp)]

    loads = {"in": [], "out": [], "gu": [], "dn": []}
    n_local = 0

    def local(src, dst):
        nonlocal n_local
        c = pltpu.make_async_copy(src, dst, local_sems.at[n_local])
        n_local += 1
        c.start()
        return c

    for c in range(2):
        for k in range(3):
            loads["in"].append(local(w_in.at[k, :, pl.ds(c * Uc, Uc)], w_in_v.at[c, k]))
    for c in range(2):
        loads["dn"].append(local(w_dn.at[pl.ds(c * Fc, Fc), :], w_dn_v.at[c]))
        loads["out"].append(local(w_out.at[pl.ds(c * Uc, Uc), :], w_out_v.at[c]))
    for c in range(2):
        for k in range(2):
            loads["gu"].append(local(w_gu.at[k, :, pl.ds(c * Fc, Fc)], w_gu_v.at[c, k]))

    def loaded(name):
        for c in loads[name]:
            c.wait()

    barrier = pltpu.get_barrier_semaphore()
    for to in (to_col, {"row": low}, {"row": high}):
        pl.semaphore_signal(barrier, inc=1, device_id=to, device_id_type=MESH)
    for k in range(1, n_dp):
        pl.semaphore_signal(
            barrier, inc=1, device_id={"dp": lax.rem(dp + k, n_dp)}, device_id_type=MESH
        )

    def col_total(place):
        c = links.send(ss_s.at[place], ss_r.at[place], to_col)
        c.wait_recv()

    def gather(buf):
        first = links.send(buf.at[row], buf.at[row], to_a)
        second = links.send(buf.at[row], buf.at[row], to_b)
        state = {}

        def relay():
            first.wait_recv()
            state["third"] = links.send(buf.at[row_a], buf.at[row_a], to_b)

        def second_in():
            second.wait_recv()

        def third_in():
            state["third"].wait_recv()

        def all_sent():
            links.sent(first, second, state["third"])

        return relay, second_in, third_in, all_sent

    class Line:
        def __init__(self, first, dst, block=None):
            self.first, self.dst, self.block = first, dst, row if block is None else block
            self.up = [links.slot() for _ in range(n_dp + 1)]
            self.down = [links.slot() for _ in range(n_dp + 1)]
            self.sent_to = {}

        def at(self, z):
            return self.dst.at[z, self.block]

        def up_copy(self, hop):
            at = self.at(lax.rem(dp + n_dp - (hop - 1), n_dp))
            src = self.first if hop == 1 else at
            return links.copy(src, at, {"dp": peers[1]}, self.up[hop])

        def down_copy(self, hop):
            at = self.at(lax.rem(dp + hop - 1, n_dp))
            src = self.first if hop == 1 else at
            return links.copy(src, at, {"dp": sources[1]}, self.down[hop])

        def arrived(self, hop):
            @pl.when(dp >= hop)
            def _():
                self.up_copy(hop).wait_recv()

            @pl.when(dp + hop < n_dp)
            def _():
                self.down_copy(hop).wait_recv()

        def start(self, hop):
            if hop > 1:
                self.arrived(hop - 1)

            @pl.when((dp + 1 < n_dp) & (dp >= hop - 1))
            def _():
                self.up_copy(hop).start()

            @pl.when((dp >= 1) & (dp + hop - 1 < n_dp))
            def _():
                self.down_copy(hop).start()

        def sent(self, hop):
            @pl.when((dp + 1 < n_dp) & (dp >= hop - 1))
            def _():
                self.up_copy(hop).wait_send()

            @pl.when((dp >= 1) & (dp + hop - 1 < n_dp))
            def _():
                self.down_copy(hop).wait_send()

        def rest(self):
            for hop in range(4, n_dp):
                self.start(hop)
            self.arrived(n_dp - 1)

        def plane(self, *ks):
            if not self.sent_to:
                self.rest()
            for k in ks:
                at = self.dst.at[peers[k], row]
                self.sent_to[k] = (links.send(at, at, to_a), links.send(at, at, to_b))

        def finish(self, *ks):
            for k in ks:
                for c in self.sent_to[k]:
                    c.wait_recv()

    def put_to(ref):
        def put(n0, value):
            ref[:, n0 : n0 + value.shape[1]] = value.astype(ref.dtype)

        return put

    def both(first, second):
        def put(n0, value):
            first(n0, value[:B])
            second(n0, value[B:])

        return put

    def two(buf, blk, other_blk):
        return jnp.concatenate([buf[blk], buf[other_blk]], axis=0)

    def row_sum(sends, recvs, partial, filler=None):
        partial(row_d, row_a, both(put_to(sends.at[0]), put_to(sends.at[1])))
        c0 = links.send(sends.at[0], recvs.at[0], to_a)
        c1 = links.send(sends.at[1], recvs.at[1], to_a)
        partial(row_b, row, both(put_to(acc_b), put_to(acc_o)))
        c0.wait_recv()

        def combine(r0):
            at = pl.ds(r0, 32)
            sends[2, at, :] = (acc_b[at, :] + recvs[0, at, :].astype(F32)).astype(BF)

        rows_loop(B, 32, combine)
        c2 = links.send(sends.at[2], recvs.at[2], to_b)
        if filler is not None:
            filler()
        c1.wait_recv()
        c2.wait_recv()
        return c0, c1, c2

    def row_total(recvs, at):
        return acc_o[at, :] + recvs[1, at, :].astype(F32) + recvs[2, at, :].astype(F32)

    def lanes(x):
        return jnp.broadcast_to(x, (x.shape[0], 128))

    g1[...] = g1_in[...].astype(F32)
    g2[...] = g2_in[...].astype(F32)
    cw[...] = cw_in[...].astype(F32)
    starts = [jnp.int32(0)]
    for i in range(lengths.shape[0] - 1):
        starts.append(starts[-1] + lengths[i])

    def masks(r0):
        t = dp * T + r0 + lax.broadcasted_iota(jnp.int32, (16, 128), 0)
        count = jnp.full((16, 128), 2.0, F32)
        for start in starts:
            away = t - start
            count = jnp.where((away >= 0) & (away < 2), away.astype(F32), count)
        reach[pl.ds(r0, 16), :] = count

    rows_loop(T + 16, 16, masks)

    def squares(r0):
        at = pl.ds(r0, 32)
        x = tok[at, :].astype(F32)
        ss_s[0, at, :] = lanes(jnp.sum(x * x, axis=1, keepdims=True))

    rows_loop(B, 32, squares)
    pl.semaphore_wait(barrier, 3 + n_dp - 1)
    cot_line = Line(cot, cotz)
    cot_far = Line(call.at[row_d], cotz, row_d)
    n2_line = Line(xall.at[row], n2z)
    n2_far = Line(xall.at[row_d], n2z, row_d)
    cot_line.start(1)
    col_total(0)

    def scale_of(place, at):
        return lax.rsqrt((ss_s[place, at, :] + ss_r[place, at, :]) / width + EPS)[:, :1]

    def normed_one(r0):
        at = pl.ds(r0, 32)
        x = tok[at, :].astype(F32)
        xall[row, at, :] = (x * scale_of(0, at) * g1[...]).astype(BF)

    rows_loop(B, 32, normed_one)
    relay, second_in, third_in, all_sent = gather(xall)

    def project(blk, other_blk):
        x = two(xall, blk, other_blk)
        for k in range(3):
            y = nn(x, w_in_v[other, k]).astype(BF)
            gp[col, blk, k] = y[:B]
            gp[col, other_blk, k] = y[B:]
        copies = [links.send(gp.at[col, b], proj_r.at[b], to_col) for b in (blk, other_blk)]
        for k in range(3):
            y = nn(x, w_in_v[col, k])
            proj_o[k, pl.ds(pl.multiple_of(blk * B, B), B), :] = y[:B]
            proj_o[k, pl.ds(pl.multiple_of(other_blk * B, B), B), :] = y[B:]
        return copies

    loaded("in")
    relay()
    sent = project(row, row_a)
    cot_line.start(2)
    second_in()
    third_in()
    call[row] = cot[...]
    cot_relay, cot_second, cot_third, cot_all_sent = gather(call)
    sent += project(row_b, row_d)
    n1_out = local(xall, n1_h)

    for blk, c in zip((row, row_b, row_a, row_d), sent):
        c.wait_recv()
        base = blk * B

        def add(r0, blk=blk, base=base):
            at = pl.ds(r0, 32)
            to = pl.ds(pl.multiple_of(base + r0, 32), 32)
            g = [proj_o[k, to, :] + proj_r[blk, k, at, :].astype(F32) for k in range(3)]
            for k in range(3):
                proj_o[k, to, :] = g[k]
            mext[pl.ds(pl.multiple_of(base + r0 + 8, 8), 32), :] = g[0] * g[2]

        rows_loop(B, 32, add)
    links.sent(*sent)

    behind = links.slot()

    @pl.when(dp < n_dp - 1)
    def _():
        links.copy(mext.at[pl.ds(T, 8), :], halo_b, {"dp": lax.rem(dp + 1, n_dp)}, behind).start()

    @pl.when(dp > 0)
    def _():
        links.copy(mext.at[pl.ds(T, 8), :], halo_b, {"dp": lax.rem(dp + 1, n_dp)}, behind).wait_recv()
        mext[0:8, :] = halo_b[...]

    @pl.when(dp == 0)
    def _():
        mext[0:8, :] = jnp.zeros((8, Uc), F32)

    cot_relay()
    cot_line.start(3)
    CH = B // 2

    def masks_of(at):
        count = jnp.concatenate([reach[at, :]] * (Uc // 128), axis=1)
        return jnp.minimum(count, 1.0), jnp.maximum(count - 1.0, 0.0)

    for i in range(T // CH):
        at = pl.ds(i * CH, CH)
        x = mext[pl.ds(i * CH, CH + 8), :]
        m1, m2 = masks_of(at)
        y = cw[0:1, :] * x[8 : 8 + CH]
        y = y + cw[1:2, :] * m1 * x[7 : 7 + CH]
        y = y + cw[2:3, :] * m2 * x[6 : 6 + CH]
        cout[at, :] = y
        gat[col, i * CH // B, i * CH % B : i * CH % B + CH, :] = (proj_o[1, at, :] * y).astype(BF)
    gated_in = links.send(gat.at[col], gat.at[col], to_col)
    cot_second()
    gated_in.wait_recv()

    loaded("out")
    n1_out.wait()
    all_sent()

    def out_partial(blk, other_blk, put):
        x = [two(gat.at[c], blk, other_blk) for c in range(2)]
        for n0 in range(0, Dl, Dl // 4):
            n = slice(n0, n0 + Dl // 4)
            put(n0, nn(x[0], w_out_v[0, :, n]) + nn(x[1], w_out_v[1, :, n]))

    sent = row_sum(rs_s, rs_r, out_partial)

    def residual(r0):
        at = pl.ds(r0, 32)
        x = tok[at, :].astype(F32) + row_total(rs_r, at)
        resid[at, :] = x
        ss_s[1, at, :] = lanes(jnp.sum(x * x, axis=1, keepdims=True))

    cot_third()
    cot_far.start(1)
    rows_loop(B, 32, residual)
    links.sent(*sent)
    col_total(1)

    def normed_two(r0):
        at = pl.ds(r0, 32)
        xall[row, at, :] = (resid[at, :] * scale_of(1, at) * g2[...]).astype(BF)

    rows_loop(B, 32, normed_two)
    relay, second_in, third_in, all_sent = gather(xall)
    n2_line.start(1)

    loaded("dn")
    ga_step = min(Fc, 256)

    def ga_other(i, carry):
        n = pl.ds(pl.multiple_of(i * ga_step, ga_step), ga_step)
        y = nt(call[...].reshape(T, Dl), w_dn_v[other, n, :]).astype(BF)
        act[col, :, :, n] = y.reshape(R, B, ga_step)
        return carry

    def ga_own(i, carry):
        n = pl.ds(pl.multiple_of(i * ga_step, ga_step), ga_step)
        ga_o[:, :, n] = nt(call[...].reshape(T, Dl), w_dn_v[col, n, :]).reshape(R, B, ga_step)
        return carry

    lax.fori_loop(0, Fc // ga_step, ga_other, 0)
    ga_sent = links.send(act.at[col], ga_r, to_col)
    relay()
    lax.fori_loop(0, Fc // ga_step, ga_own, 0)
    cot_out = local(call, cotz.at[dp])
    n2_line.start(2)
    cot_far.start(2)

    def hidden_other(blk, other_blk):
        def one(k, carry):
            x = two(xall, blk, other_blk)
            for n0 in range(0, Fc, Fc // 2):
                n = slice(n0, n0 + Fc // 2)
                y = nn(x, w_gu_v[other, k, :, n]).astype(BF)
                gh[col, blk, k, :, n] = y[:B]
                gh[col, other_blk, k, :, n] = y[B:]
            return carry

        lax.fori_loop(0, 2, one, 0)
        return [links.send(gh.at[col, b], hid_r.at[b], to_col) for b in (blk, other_blk)]

    loaded("gu")
    hid_sent = hidden_other(row, row_a)
    second_in()
    third_in()
    hid_sent += hidden_other(row_b, row_d)
    n2_out = local(xall, n2z.at[dp])
    cot_line.plane(*range(1, n_dp))
    n2_far.start(1)

    gh_in = {}
    ga_sent.wait_recv()
    links.sent(ga_sent)
    H = Fc // 2
    for blks, mine_at, theirs_at in (((row_d, row_a), (3, 1), (3, 2)), ((row_b, row), (2, 0), (1, 0))):
        for h in range(2):

            def one(k, carry, h=h, blks=blks):
                y = nn(two(xall, *blks), w_gu_v[col, k, :, h * H : h * H + H])
                hid_o[k, :, :H] = y[:B]
                hid_o[k, :, H:] = y[B:]
                return carry

            lax.fori_loop(0, 2, one, 0)
            for i, blk in enumerate(blks):
                if h == 0:
                    hid_sent[theirs_at[i]].wait_recv()
                    links.sent(hid_sent[mine_at[i]])

                def activate(r0, blk=blk, i=i, h=h):
                    at = pl.ds(r0, 32)
                    n = slice(h * H, h * H + H)
                    own = slice(i * H, i * H + H)
                    gate = hid_o[0, at, own] + hid_r[blk, 0, at, n].astype(F32)
                    up = hid_o[1, at, own] + hid_r[blk, 1, at, n].astype(F32)
                    ga = ga_o[blk, at, n] + ga_r[blk, at, n].astype(F32)
                    s = jax.nn.sigmoid(gate)
                    silu = gate * s
                    act[col, blk, at, n] = (silu * up).astype(BF)
                    gh[col, blk, 0, at, n] = (ga * up * s * (1.0 + gate * (1.0 - s))).astype(BF)
                    gh[col, blk, 1, at, n] = (ga * silu).astype(BF)

                rows_loop(B, 32, activate)
                if h == 1:
                    gh_in[mine_at[i]] = (
                        links.send(gh.at[col, blk], gh.at[col, blk], to_col),
                        links.send(act.at[col, blk], act.at[col, blk], to_col),
                    )
    cot_far.start(3)
    n2_far.start(2)
    for pair in gh_in.values():
        for c in pair:
            c.wait_recv()
    size = actz.shape[-1]
    mine = pl.ds(pl.multiple_of(lax.rem(dp, half) * size, size), size)
    kept_units = [
        local(act.at[holder, :, :, mine], actz.at[dp]),
        local(gh.at[holder, :, :, :, mine], ghz.at[dp]),
    ]
    kept = []
    n2_out.wait()
    n2_line.start(3)
    n2_line.sent(1)
    n2_far.sent(1)
    all_sent()

    def gu_partial(blk, other_blk, put):
        for n0 in range(0, Dl, Dl // 4):
            n = slice(n0, n0 + Dl // 4)
            total = None
            for c in range(2):
                for k in range(2):
                    part = nt(two(gh.at[c, :, k], blk, other_blk), w_gu_v[c, k, n, :])
                    total = part if total is None else total + part
            put(n0, total)

    sent = row_sum(rs_s, rs_r, gu_partial)

    def back_two(r0):
        at = pl.ds(r0, 32)
        g = row_total(rs_r, at)
        gres[at, :] = g
        ss_s[2, at, :] = lanes(jnp.sum(g * g2[...] * resid[at, :], axis=1, keepdims=True))

    rows_loop(B, 32, back_two)
    links.sent(*sent)
    col_total(2)

    def inner_of(place, at):
        return (ss_s[place, at, :] + ss_r[place, at, :])[:, :1]

    def branch(i, gain):
        at = pl.ds(pl.multiple_of(i * 32, 32), 32)
        g = gres[at, :]
        x = resid[at, :]
        s = scale_of(1, at)
        y = cot[at, :].astype(F32) + s * g2[...] * g - x * (s * s * s) * inner_of(2, at) / width
        gres[at, :] = y
        xall[row, at, :] = y.astype(BF)
        return gain + jnp.sum(g * x * s, axis=0, keepdims=True)

    n2_far.start(3)
    cot_out.wait()
    cot_all_sent()
    cot_far.sent(1)
    n1_back = local(n1_h, call)
    gain_two = lax.fori_loop(0, B // 32, branch, jnp.zeros((1, Dl), F32))
    relay, second_in, third_in, all_sent = gather(xall)

    def down_partial(blk, other_blk, put):
        x = [two(act.at[c], blk, other_blk) for c in range(2)]
        for n0 in range(0, Dl, Dl // 4):
            n = slice(n0, n0 + Dl // 4)
            put(n0, nn(x[0], w_dn_v[0, :, n]) + nn(x[1], w_dn_v[1, :, n]))

    down_partial(row_d, row_a, both(put_to(rt_s.at[0]), put_to(rt_s.at[1])))

    def gated_other(blk, other_blk):
        x = two(xall, blk, other_blk)
        y = nt(x, w_out_v[other]).astype(BF)
        gg_s[blk] = y[:B]
        gg_s[other_blk] = y[B:]
        copies = [links.send(gg_s.at[b], gg_r.at[b], to_col) for b in (blk, other_blk)]
        y = nt(x, w_out_v[col])
        gg_o[blk] = y[:B]
        gg_o[other_blk] = y[B:]
        return copies

    relay()
    sent = gated_other(row, row_a)
    down_partial(row_b, row, both(put_to(rt_s.at[2]), put_to(down_o)))
    second_in()
    third_in()
    sent += gated_other(row_b, row_d)
    n2_line.plane(1)

    for blk, c in zip((row, row_b, row_a, row_d), sent):
        c.wait_recv()
        base = blk * B

        def conv_grad(r0, blk=blk, base=base):
            at = pl.ds(r0, 32)
            to = pl.ds(pl.multiple_of(base + r0, 32), 32)
            g = gg_o[blk, at, :] + gg_r[blk, at, :].astype(F32)
            gext[to, :] = g * proj_o[1, to, :]
            gp[col, blk, 1, at, :] = (g * cout[to, :]).astype(BF)

        rows_loop(B, 32, conv_grad)

    ahead = links.slot()

    @pl.when(dp > 0)
    def _():
        links.copy(gext.at[pl.ds(0, 8), :], halo_a, {"dp": lax.rem(dp + n_dp - 1, n_dp)}, ahead).start()

    @pl.when(dp < n_dp - 1)
    def _():
        links.copy(gext.at[pl.ds(0, 8), :], halo_a, {"dp": lax.rem(dp + n_dp - 1, n_dp)}, ahead).wait_recv()
        gext[T : T + 8, :] = halo_a[...]

    @pl.when(dp == n_dp - 1)
    def _():
        gext[T : T + 8, :] = jnp.zeros((8, Uc), F32)

    terms = [jnp.zeros((1, Uc), F32) for _ in range(3)]
    for i in range(T // CH):
        at = pl.ds(i * CH, CH)
        more = pl.ds(i * CH, CH + 8)
        x = mext[more, :]
        g = gext[more, :]
        m1, m2 = masks_of(more)
        now = g[:CH]
        terms[0] = terms[0] + jnp.sum(now * x[8 : 8 + CH], axis=0, keepdims=True)
        terms[1] = terms[1] + jnp.sum(m1[:CH] * now * x[7 : 7 + CH], axis=0, keepdims=True)
        terms[2] = terms[2] + jnp.sum(m2[:CH] * now * x[6 : 6 + CH], axis=0, keepdims=True)
        y = cw[0:1, :] * now
        y = y + cw[1:2, :] * (m1 * g)[1 : 1 + CH]
        y = y + cw[2:3, :] * (m2 * g)[2 : 2 + CH]
        blk, to = i * CH // B, slice(i * CH % B, i * CH % B + CH)
        gp[col, blk, 0, to, :] = (y * proj_o[2, at, :]).astype(BF)
        gp[col, blk, 2, to, :] = (y * proj_o[0, at, :]).astype(BF)
    red_s[...] = jnp.zeros_like(red_s)
    for k in range(3):
        red_s[2 + k : 3 + k, :Uc] = terms[k]
    gp_in = links.send(gp.at[col], gp.at[col], to_col)
    gp_in.wait_recv()
    if not split_in:
        kept.append(local(gp, d_in))

    def in_partial(blk, other_blk, put):
        for n0 in range(0, Dl, Dl // 4):
            n = slice(n0, n0 + Dl // 4)
            total = None
            for c in range(2):
                for k in range(3):
                    part = nt(two(gp.at[c, :, k], blk, other_blk), w_in_v[c, k, n, :])
                    total = part if total is None else total + part
            put(n0, total)

    po_all = []

    rows = po_r.shape[1]

    def out_chunk(z):
        return (z // half, pl.ds(pl.multiple_of(lax.rem(z, half) * rows, rows), rows), slice(None))

    def out_weights():
        for z in range(n_dp):
            at = pl.ds(z % half * rows, rows)
            g = lax.dot_general(
                gat[z // half, :, :, at].reshape(T, rows), xall[...].reshape(T, Dl),
                (((0,), (0,)), ((), ())), preferred_element_type=F32,
            )
            w_out_v[z // half, at, :] = g.astype(BF)
        for k in range(1, n_dp):
            po_all.append(links.send(w_out_v.at[out_chunk(peers[k])], po_r.at[dp], {"dp": peers[k]}))

    up_slots = [links.slot() for _ in range(n_dp)][0]
    down_slots = [links.slot() for _ in range(n_dp)][0]
    unit = 2 * Uc // n_dp

    def in_chunk(z):
        at = pl.ds(pl.multiple_of(lax.rem(z, half) * unit, unit), unit)
        return (z // half, slice(None), slice(None), at)

    def go_up(z):
        return links.copy(w_in_v.at[in_chunk(z)], in_up.at[z], {"dp": peers[1]}, up_slots + z)

    def go_down(z):
        return links.copy(w_in_v.at[in_chunk(z)], in_dn.at[z], {"dp": sources[1]}, down_slots + z)

    def in_weights():
        n1_back.wait()
        x = call[...].reshape(T, Dl)
        units = [(c, k) for c in range(2) for k in range(3)]
        g = jnp.concatenate([gp[c, :, k].reshape(T, Uc) for c, k in units], axis=1)
        for m0 in range(0, Dl, Dl // 4):
            m = slice(m0, m0 + Dl // 4)
            y = lax.dot_general(x[:, m], g, (((0,), (0,)), ((), ())), preferred_element_type=F32)
            for u, (c, k) in enumerate(units):
                w_in_v[c, k, m, :] = y[:, u * Uc : u * Uc + Uc].astype(BF)
        for z in range(n_dp - 1, 0, -1):

            @pl.when(dp == 0)
            def _(z=z):
                go_up(z).start()

        for z in range(n_dp - 1):

            @pl.when(dp == n_dp - 1)
            def _(z=z):
                go_down(z).start()

    def take(src, z):
        c = pltpu.make_async_copy(src, in_add, local_sems.at[local_sems.shape[0] - 1])
        c.start()
        c.wait()
        at = in_chunk(z)
        for k in range(3):
            here = (at[0], k, slice(None), at[3])
            w_in_v[here] = (w_in_v[here].astype(F32) + in_add[k].astype(F32)).astype(BF)

    def in_step(step):
        up = n_dp - 1 - step + dp

        @pl.when((dp > 0) & (dp <= step))
        def _():
            go_up(up).wait_recv()
            take(in_up.at[up], up)
            go_up(up).start()

        down = step - (n_dp - 1 - dp)

        @pl.when((dp < n_dp - 1) & (down >= 0))
        def _():
            go_down(down).wait_recv()
            take(in_dn.at[down], down)
            go_down(down).start()

    def in_end():
        @pl.when(dp > 0)
        def _():
            go_up(dp).wait_recv()
            take(in_up.at[dp], dp)

        @pl.when(dp < n_dp - 1)
        def _():
            go_down(dp).wait_recv()
            take(in_dn.at[dp], dp)

        out = local(w_in_v.at[in_chunk(dp)], d_in)
        for z in range(1, n_dp):

            @pl.when(dp < z)
            def _(z=z):
                go_up(z).wait_send()

        for z in range(n_dp - 1):

            @pl.when(dp > z)
            def _(z=z):
                go_down(z).wait_send()

        out.wait()

    def weights_wait():
        if split_in:
            in_weights()
        else:
            n1_back.wait()
        out_weights()

    sent_in = row_sum(rs_s, rs_r, in_partial, filler=weights_wait)
    n2_line.plane(*range(2, n_dp))
    down_sent = [
        links.send(rt_s.at[0], rt_r.at[0], to_a),
        links.send(rt_s.at[1], rt_r.at[1], to_a),
    ]

    def fetch(k):
        n2_line.finish(k)
        return [local(n2z.at[peers[k]], xall), local(cotz.at[peers[k]], call)]

    cot_far.rest()
    n2_far.rest()
    cot_line.finish(*range(1, n_dp))
    all_sent()
    fetched = {1: fetch(1)}

    def back_one(r0):
        at = pl.ds(r0, 32)
        g = row_total(rs_r, at)
        acc_o[at, :] = g
        ss_s[3, at, :] = lanes(
            jnp.sum(g * g1[...] * tok[at, :].astype(F32), axis=1, keepdims=True)
        )

    rows_loop(B, 32, back_one)
    col_total(3)

    def token_grad(i, gain):
        at = pl.ds(pl.multiple_of(i * 32, 32), 32)
        g = acc_o[at, :]
        x = tok[at, :].astype(F32)
        s = scale_of(0, at)
        y = gres[at, :] + s * g1[...] * g - x * (s * s * s) * inner_of(3, at) / width
        gres[at, :] = y
        return gain + jnp.sum(g * x * s, axis=0, keepdims=True)

    gain_one = lax.fori_loop(0, B // 32, token_grad, jnp.zeros((1, Dl), F32))

    kept.append(local(gres, d_tok))

    red_s[0:1, :] = gain_one
    red_s[1:2, :] = gain_two
    c0 = links.send(red_s, red_r.at[0], to_a)
    for c in kept_units:
        c.wait()
    for pair in gh_in.values():
        links.sent(*pair)

    slots = Fc // size

    def place(k, r, rank):
        q = (k - 1) * 2 + r
        lanes_at = slice(q % slots * size, q % slots * size + size)
        return (q // slots, *([slice(None)] * (rank - 2)), lanes_at)

    def again(k):
        z = peers[k]
        for c in fetched[k]:
            c.wait()
        copies = []
        for core, keep in ((other, False), (col, True)):
            x = xall[pl.ds(core * 2, 2)].reshape(2 * B, Dl)
            for j in range(2):
                h = nn(x, w_gu_v[holder, j, :, mine])
                for r in range(2):
                    if keep:
                        hid_o[j, :, r * size : r * size + size] = h[r * B : r * B + B]
                    else:
                        q, _, _, n = place(k, r, 4)
                        gh[0, q, j, :, n] = h[r * B : r * B + B].astype(BF)
            y = call[pl.ds(core * 2, 2)].reshape(2 * B, Dl)
            g = nt(y, w_dn_v[holder, mine, :])
            for r in range(2):
                if keep:
                    ga_o[r, :, :size] = g[r * B : r * B + B]
                else:
                    q, _, n = place(k, r, 3)
                    act[0, q, :, n] = g[r * B : r * B + B].astype(BF)
            if not keep:
                for r in range(2):
                    h_at, g_at = place(k, r, 4), place(k, r, 3)
                    copies.append(links.send(gh.at[0].at[h_at], hid_r.at[h_at], to_col))
                    copies.append(links.send(act.at[0].at[g_at], ga_r.at[g_at], to_col))
        if k + 1 < n_dp:
            fetched[k + 1] = fetch(k + 1)
        for c in copies:
            c.wait_recv()
        done = []
        for r in range(2):
            q, _, n = place(k, r, 3)

            def finish(r0, r=r, q=q, n=n):
                at = pl.ds(r0, 32)
                own = slice(r * size, r * size + size)
                gate = hid_o[0, at, own] + hid_r[q, 0, at, n].astype(F32)
                up = hid_o[1, at, own] + hid_r[q, 1, at, n].astype(F32)
                ga = ga_o[r, at, :size] + ga_r[q, at, n].astype(F32)
                s = jax.nn.sigmoid(gate)
                silu = gate * s
                act[1, q, at, n] = (silu * up).astype(BF)
                gh[1, q, 0, at, n] = (ga * up * s * (1.0 + gate * (1.0 - s))).astype(BF)
                gh[1, q, 1, at, n] = (ga * silu).astype(BF)

            rows_loop(B, 32, finish)
            blk = col * 2 + r
            h_src, a_src = gh.at[1].at[place(k, r, 4)], act.at[1].at[place(k, r, 3)]
            done.append(links.send(h_src, ghz.at[z, blk], to_col))
            done.append(links.send(a_src, actz.at[z, blk], to_col))
            kept.append(local(h_src, ghz.at[z, blk]))
            kept.append(local(a_src, actz.at[z, blk]))
        return done

    again_in = again(1)
    if split_in:
        in_step(1)

    down_sent[0].wait_recv()

    def down_combine(r0):
        at = pl.ds(r0, 16)
        rt_s[2, at, :] = (rt_s[2, at, :].astype(F32) + rt_r[0, at, :].astype(F32)).astype(BF)

    rows_loop(B, 16, down_combine)
    down_sent.append(links.send(rt_s.at[2], rt_r.at[2], to_b))
    c0.wait_recv()
    links.sent(c0)
    red_s[0:2, :] = red_s[0:2, :] + red_r[0, 0:2, :]
    c1 = links.send(red_s, red_r.at[1], to_b)
    again_in += again(2)
    if split_in:
        for step in range(2, n_dp - 1):
            in_step(step)
    c1.wait_recv()
    red_z[dp] = red_s[...]
    red_z[dp, 0:2, :] = red_s[0:2, :] + red_r[1, 0:2, :]
    arrived = []
    for k in range(1, n_dp):
        arrived.append(links.send(red_z.at[dp], red_z.at[dp], {"dp": lax.rem(dp + k, n_dp)}))
    for k in range(3, n_dp):
        again_in += again(k)
    for c in down_sent[1:]:
        c.wait_recv()

    def block_rows(r0):
        at = pl.ds(r0, 16)
        total = down_o[at, :] + rt_r[1, at, :].astype(F32) + rt_r[2, at, :].astype(F32)
        block_out[at, :] = (resid[at, :] + total).astype(BF)

    rows_loop(B, 16, block_rows)
    for c in arrived:
        c.wait_recv()
    total = red_z[0]
    for k in range(1, n_dp):
        total = total + red_z[k]
    d_gain[...] = total
    d_conv[...] = total[:, :Uc]

    @pl.when(dp < n_dp - 1)
    def _():
        links.copy(mext.at[pl.ds(T, 8), :], halo_b, {"dp": lax.rem(dp + 1, n_dp)}, behind).wait_send()

    @pl.when(dp > 0)
    def _():
        links.copy(gext.at[pl.ds(0, 8), :], halo_a, {"dp": lax.rem(dp + n_dp - 1, n_dp)}, ahead).wait_send()

    for c in again_in:
        c.wait_recv()
    for c in po_all:
        c.wait_recv()
    out_total = w_out_v[out_chunk(dp)].astype(F32)
    for k in range(1, n_dp):
        out_total = out_total + po_r[peers[k]].astype(F32)
    acc_b[:rows, :] = out_total
    kept.append(local(acc_b.at[pl.ds(0, rows), :], d_out))
    if split_in:
        in_end()
    cot_line.sent(1)
    for hop in range(2, n_dp):
        for line in (cot_line, cot_far, n2_line, n2_far):
            line.sent(hop)
    for c in kept:
        c.wait()
    assert links.count <= send_sems.shape[0]
    links.close()


def run_block(n_dp, width, split_in, tok, g1, w_in, cw, w_out, g2, w_gu, w_dn, cot, lengths):
    B, Dl = tok.shape
    R = 4
    T = R * B
    Uc = w_out.shape[0] // 2
    Fc = w_dn.shape[0] // 2
    vm = lambda shape, kind=BF: pltpu.VMEM(shape, kind)
    any_spec, vmem_spec = pl.BlockSpec(memory_space=pl.ANY), pl.BlockSpec(memory_space=pltpu.VMEM)
    shape = jax.ShapeDtypeStruct
    rows = shape((n_dp, R, B, Dl), BF)
    return pl.pallas_call(
        functools.partial(block_kernel, n_dp, width, split_in),
        out_shape=(
            shape((B, Dl), BF),
            shape((B, Dl), F32),
            shape((8, Dl), F32),
            shape((8, Uc), F32),
            shape((2 * Uc // n_dp, Dl), F32),
            shape((R, B, Dl), BF),
            rows,
            rows,
            shape((n_dp, R, B, 2 * Fc // n_dp), BF),
            shape((n_dp, R, 2, B, 2 * Fc // n_dp), BF),
            shape((3, Dl, 2 * Uc // n_dp) if split_in else (2, R, 3, B, Uc), BF),
            shape((n_dp, 3, Dl, 2 * Uc // n_dp), BF),
            shape((n_dp, 3, Dl, 2 * Uc // n_dp), BF),
        ),
        in_specs=[
            vmem_spec, vmem_spec, any_spec, vmem_spec, any_spec, vmem_spec,
            any_spec, any_spec, vmem_spec, pl.BlockSpec(memory_space=pltpu.SMEM),
        ],
        out_specs=[vmem_spec, any_spec, vmem_spec, vmem_spec] + [any_spec] * 9,
        scratch_shapes=[
            vm((2, 3, Dl, Uc)), vm((2, Uc, Dl)), vm((2, 2, Dl, Fc)), vm((2, Fc, Dl)),
            vm((R, B, Dl)), vm((R, B, Dl)),
            vm((2, R, B, Uc)), vm((2, R, B, Fc)), vm((2, R, 2, B, Fc)), vm((2, R, 3, B, Uc)),
            vm((3, T, Uc), F32), vm((R, 3, B, Uc)), vm((T + 8, Uc), F32), vm((8, Uc), F32),
            vm((T, Uc), F32), vm((T + 8, Uc), F32), vm((8, Uc), F32),
            vm((R, B, Uc)), vm((R, B, Uc)), vm((R, B, Uc), F32),
            vm((2, B, Fc), F32), vm((R, 2, B, Fc)), vm((R, B, Fc), F32), vm((R, B, Fc)),
            vm((3, B, Dl)), vm((3, B, Dl)), vm((3, B, Dl)), vm((3, B, Dl)),
            vm((B, Dl), F32), vm((B, Dl), F32), vm((B, Dl), F32),
            vm((B, Dl), F32), vm((B, Dl), F32),
            vm((4, B, 128), F32), vm((4, B, 128), F32),
            vm((8, Dl), F32), vm((2, 8, Dl), F32), vm((n_dp, 8, Dl), F32),
            vm((n_dp, 2 * Uc // n_dp, Dl)),
            vm((1, Dl), F32), vm((1, Dl), F32), vm((3, Uc), F32),
            vm((T + 16, 128), F32), vm((3, Dl, 2 * Uc // n_dp)),
            pltpu.SemaphoreType.DMA((96 + 48 * n_dp,)), pltpu.SemaphoreType.DMA((96 + 48 * n_dp,)),
            pltpu.SemaphoreType.DMA((32 + 6 * n_dp,)),
        ],
        compiler_params=pltpu.CompilerParams(
            collective_id=0, has_side_effects=True, vmem_limit_bytes=VMEM_LIMIT
        ),
        name="block",
    )(tok, g1, w_in, cw, w_out, g2, w_gu, w_dn, cot, lengths)


def weights_kernel(split_in, n2, cot, act, gh, d_in, gu_out, dn_out, in_out, gu_acc):
    _, R, B, Dl = n2.shape
    T, size = R * B, act.shape[-1]
    step = pl.program_id(0)

    def tn(a, b):
        return lax.dot_general(a, b, (((0,), (0,)), ((), ())), preferred_element_type=F32)

    @pl.when(step == 0)
    def _():
        gu_acc[...] = jnp.zeros_like(gu_acc)
        dn_out[...] = jnp.zeros_like(dn_out)
        if split_in:
            for k in range(3):
                in_out[pl.ds(k, Dl, stride=3), :] = d_in[k].astype(F32)
        else:
            in_out[...] = jnp.zeros_like(in_out)

    g = jnp.concatenate([gh[0, :, k].reshape(T, size) for k in range(2)], axis=1)
    gu_acc[...] += tn(n2[0].reshape(T, Dl), g)
    dn_out[...] += tn(act[0].reshape(T, size), cot[0].reshape(T, Dl))

    @pl.when(step == pl.num_programs(0) - 1)
    def _():
        parts = 2 * size // 128
        for p in range(parts):
            gu_out[pl.ds(p, Dl, stride=parts), :] = gu_acc[:, p * 128 : p * 128 + 128]


def run_weights(split_in, n2, cot, act, gh, d_in):
    n_dp, R, B, Dl = n2.shape
    size = act.shape[-1]
    whole = lambda *shape: pl.BlockSpec(shape, lambda z: (0,) * len(shape))
    one = lambda a: pl.BlockSpec((1, *a.shape[1:]), lambda z: (z,) + (0,) * (len(a.shape) - 1))
    out = ((Dl * 2 * size // 128, 128), (size, Dl), (Dl * 3, 128) if split_in else (8, 128))
    return pl.pallas_call(
        functools.partial(weights_kernel, split_in),
        grid=(n_dp,),
        out_shape=[jax.ShapeDtypeStruct(o, F32) for o in out],
        in_specs=[
            one(n2), one(cot), one(act), one(gh),
            whole(*d_in.shape) if split_in else pl.BlockSpec(memory_space=pl.ANY),
        ],
        out_specs=[whole(*o) for o in out],
        scratch_shapes=[pltpu.VMEM((Dl, 2 * size), F32)],
        compiler_params=pltpu.CompilerParams(vmem_limit_bytes=VMEM_LIMIT),
        name="weights",
    )(n2, cot, act, gh, d_in)


def on_device(
    tokens, gain_one, in_weight, conv_weight, out_weight, gain_two, gate_up_weight, down_weight,
    cotangent, lengths,
):
    n_dp = lax.axis_size("dp")
    B, Dl = tokens.shape
    width = Dl * lax.axis_size("col")
    chunk = in_weight.shape[2] // n_dp
    split_in = chunk == 128
    block_out, d_tok, d_gain, d_conv, d_out, n1, n2, cot, act, gh, d_in, _, _ = run_block(
        n_dp,
        float(width),
        split_in,
        tokens,
        gain_one[None, :],
        jnp.transpose(in_weight, (1, 0, 2)),
        conv_weight,
        out_weight,
        gain_two[None, :],
        jnp.transpose(gate_up_weight, (1, 0, 2)),
        down_weight,
        cotangent,
        lengths,
    )
    d_gu, d_down, in_rows = run_weights(split_in, n2, cot, act, gh, d_in)
    if split_in:
        d_in = in_rows
    else:
        d_in = lax.psum_scatter(
            jnp.einsum("rti,crktu->ikcu", n1, d_in, preferred_element_type=F32)
            .reshape(Dl, 3, -1)
            .astype(BF),
            "dp",
            scatter_dimension=2,
            tiled=True,
        ).astype(F32)
    part = d_conv.shape[1] * 1 // n_dp
    mine = lax.dynamic_slice(d_conv, (2, lax.axis_index("dp") * part), (3, part))
    return (
        block_out,
        d_tok,
        d_gain[0],
        d_in.reshape(Dl, 3, 1, 1, -1),
        mine.reshape(3, 1, 1, part),
        d_out.reshape(1, 1, -1, Dl),
        d_gain[1],
        d_gu.reshape(Dl, 2, 1, 1, -1),
        d_down.reshape(1, 1, -1, Dl),
    )


def solution(mesh):
    placed = (
        P(("dp", "row"), "col"),
        P("col"),
        P("col", None, "row"),
        P(None, ("row", "col")),
        P("row", "col"),
        P("col"),
        P("col", None, "row"),
        P("row", "col"),
        P(("dp", "row"), "col"),
        P(),
    )
    return jax.shard_map(
        on_device,
        mesh=mesh,
        in_specs=placed,
        out_specs=(
            P(("dp", "row"), "col"),
            P(("dp", "row"), "col"),
            P("col"),
            P("col", None, "row", "dp", None),
            P(None, ("row", "col"), "dp", None),
            P("row", "dp", None, "col"),
            P("col"),
            P("col", None, "row", "dp", None),
            P("row", "dp", None, "col"),
        ),
        check_vma=False,
    )
```

```python
import functools

import jax
import jax.numpy as jnp
from jax import lax
from jax.experimental import pallas as pl
from jax.experimental.pallas import tpu as pltpu
from jax.sharding import PartitionSpec as P

MESH = pl.DeviceIdType.MESH
BF = jnp.bfloat16
F32 = jnp.float32
EPS = 1e-05
VMEM_LIMIT = 63 * 2**20


def nn(a, b):
    return lax.dot_general(a, b, (((1,), (0,)), ((), ())), preferred_element_type=F32)


def nt(a, b):
    return lax.dot_general(a, b, (((1,), (1,)), ((), ())), preferred_element_type=F32)


class Links:
    def __init__(self, send_sems, recv_sems):
        self.send_sems, self.recv_sems = send_sems, recv_sems
        self.count = 0
        self.open = []

    def slot(self):
        self.count += 1
        return self.count - 1

    def copy(self, src, dst, to, slot=None):
        if slot is None:
            slot = self.slot()
        return pltpu.make_async_remote_copy(
            src_ref=src,
            dst_ref=dst,
            send_sem=self.send_sems.at[slot],
            recv_sem=self.recv_sems.at[slot],
            device_id=to,
            device_id_type=MESH,
        )

    def send(self, src, dst, to):
        c = self.copy(src, dst, to)
        c.start()
        self.open.append(c)
        return c

    def sent(self, *copies):
        for c in copies:
            c.wait_send()
            self.open = [o for o in self.open if o is not c]

    def close(self):
        for c in self.open:
            c.wait_send()
        self.open = []


def rows_loop(count, step, body):
    def one(i, carry):
        body(pl.multiple_of(i * step, step))
        return carry

    lax.fori_loop(0, count // step, one, 0)


def block_kernel(n_dp, width, split_in, *refs):
    (
        tok, g1_in, w_in, cw_in, w_out, g2_in, w_gu, w_dn, cot, lengths,
        block_out, d_tok, d_gain, d_conv, d_out, n1_h, n2z, cotz, actz, ghz, d_in, in_up, in_dn,
        w_in_v, w_out_v, w_gu_v, w_dn_v,
        xall, call, gat, act, gh, gp,
        proj_o, proj_r, mext, halo_b, cout, gext, halo_a, gg_s, gg_r, gg_o,
        hid_o, hid_r, ga_o, ga_r,
        rs_s, rs_r, rt_s, rt_r, acc_b, acc_o, down_o,
        resid, gres, ss_s, ss_r, red_s, red_r, red_z, po_r,
        g1, g2, cw, reach, in_add,
        send_sems, recv_sems, local_sems,
    ) = refs
    R, B, Dl = xall.shape
    Uc = w_out_v.shape[1]
    Fc = w_dn_v.shape[1]
    T = R * B
    dp, row, col = lax.axis_index("dp"), lax.axis_index("row"), lax.axis_index("col")
    other = 1 - col
    low = row + 1 - 2 * lax.rem(row, 2)
    high = row + 2 - 4 * lax.rem(row // 2, 2)
    row_a = low * other + high * col
    row_b = high * other + low * col
    row_d = low + high - row
    to_a, to_b, to_col = {"row": row_a}, {"row": row_b}, {"col": other}
    links = Links(send_sems, recv_sems)
    half = n_dp // 2
    holder = dp // half
    peers = [lax.rem(dp + k, n_dp) for k in range(n_dp)]
    sources = [lax.rem(dp + n_dp - k, n_dp) for k in range(n_dp)]

    loads = {"in": [], "out": [], "gu": [], "dn": []}
    n_local = 0

    def local(src, dst):
        nonlocal n_local
        c = pltpu.make_async_copy(src, dst, local_sems.at[n_local])
        n_local += 1
        c.start()
        return c

    for c in range(2):
        for k in range(3):
            loads["in"].append(local(w_in.at[k, :, pl.ds(c * Uc, Uc)], w_in_v.at[c, k]))
    for c in range(2):
        loads["dn"].append(local(w_dn.at[pl.ds(c * Fc, Fc), :], w_dn_v.at[c]))
        loads["out"].append(local(w_out.at[pl.ds(c * Uc, Uc), :], w_out_v.at[c]))
    for c in range(2):
        for k in range(2):
            loads["gu"].append(local(w_gu.at[k, :, pl.ds(c * Fc, Fc)], w_gu_v.at[c, k]))

    def loaded(name):
        for c in loads[name]:
            c.wait()

    barrier = pltpu.get_barrier_semaphore()
    for to in (to_col, {"row": low}, {"row": high}):
        pl.semaphore_signal(barrier, inc=1, device_id=to, device_id_type=MESH)
    for k in range(1, n_dp):
        pl.semaphore_signal(
            barrier, inc=1, device_id={"dp": lax.rem(dp + k, n_dp)}, device_id_type=MESH
        )

    def col_total(place):
        c = links.send(ss_s.at[place], ss_r.at[place], to_col)
        c.wait_recv()

    def gather(buf):
        first = links.send(buf.at[row], buf.at[row], to_a)
        second = links.send(buf.at[row], buf.at[row], to_b)
        state = {}

        def relay():
            first.wait_recv()
            state["third"] = links.send(buf.at[row_a], buf.at[row_a], to_b)

        def second_in():
            second.wait_recv()

        def third_in():
            state["third"].wait_recv()

        def all_sent():
            links.sent(first, second, state["third"])

        return relay, second_in, third_in, all_sent

    class Line:
        def __init__(self, first, dst, block=None):
            self.first, self.dst, self.block = first, dst, row if block is None else block
            self.up = [links.slot() for _ in range(n_dp + 1)]
            self.down = [links.slot() for _ in range(n_dp + 1)]
            self.sent_to = {}

        def at(self, z):
            return self.dst.at[z, self.block]

        def up_copy(self, hop):
            at = self.at(lax.rem(dp + n_dp - (hop - 1), n_dp))
            src = self.first if hop == 1 else at
            return links.copy(src, at, {"dp": peers[1]}, self.up[hop])

        def down_copy(self, hop):
            at = self.at(lax.rem(dp + hop - 1, n_dp))
            src = self.first if hop == 1 else at
            return links.copy(src, at, {"dp": sources[1]}, self.down[hop])

        def arrived(self, hop):
            @pl.when(dp >= hop)
            def _():
                self.up_copy(hop).wait_recv()

            @pl.when(dp + hop < n_dp)
            def _():
                self.down_copy(hop).wait_recv()

        def start(self, hop):
            if hop > 1:
                self.arrived(hop - 1)

            @pl.when((dp + 1 < n_dp) & (dp >= hop - 1))
            def _():
                self.up_copy(hop).start()

            @pl.when((dp >= 1) & (dp + hop - 1 < n_dp))
            def _():
                self.down_copy(hop).start()

        def sent(self, hop):
            @pl.when((dp + 1 < n_dp) & (dp >= hop - 1))
            def _():
                self.up_copy(hop).wait_send()

            @pl.when((dp >= 1) & (dp + hop - 1 < n_dp))
            def _():
                self.down_copy(hop).wait_send()

        def rest(self):
            for hop in range(4, n_dp):
                self.start(hop)
            self.arrived(n_dp - 1)

        def plane(self, *ks):
            if not self.sent_to:
                self.rest()
            for k in ks:
                at = self.dst.at[peers[k], row]
                self.sent_to[k] = (links.send(at, at, to_a), links.send(at, at, to_b))

        def finish(self, *ks):
            for k in ks:
                for c in self.sent_to[k]:
                    c.wait_recv()

    def put_to(ref):
        def put(n0, value):
            ref[:, n0 : n0 + value.shape[1]] = value.astype(ref.dtype)

        return put

    def both(first, second):
        def put(n0, value):
            first(n0, value[:B])
            second(n0, value[B:])

        return put

    def two(buf, blk, other_blk):
        return jnp.concatenate([buf[blk], buf[other_blk]], axis=0)

    def row_sum(sends, recvs, partial, filler=None):
        partial(row_d, row_a, both(put_to(sends.at[0]), put_to(sends.at[1])))
        c0 = links.send(sends.at[0], recvs.at[0], to_a)
        c1 = links.send(sends.at[1], recvs.at[1], to_a)
        partial(row_b, row, both(put_to(acc_b), put_to(acc_o)))
        c0.wait_recv()

        def combine(r0):
            at = pl.ds(r0, 32)
            sends[2, at, :] = (acc_b[at, :] + recvs[0, at, :].astype(F32)).astype(BF)

        rows_loop(B, 32, combine)
        c2 = links.send(sends.at[2], recvs.at[2], to_b)
        if filler is not None:
            filler()
        c1.wait_recv()
        c2.wait_recv()
        return c0, c1, c2

    def row_total(recvs, at):
        return acc_o[at, :] + recvs[1, at, :].astype(F32) + recvs[2, at, :].astype(F32)

    def lanes(x):
        return jnp.broadcast_to(x, (x.shape[0], 128))

    g1[...] = g1_in[...].astype(F32)
    g2[...] = g2_in[...].astype(F32)
    cw[...] = cw_in[...].astype(F32)
    starts = [jnp.int32(0)]
    for i in range(lengths.shape[0] - 1):
        starts.append(starts[-1] + lengths[i])

    def masks(r0):
        t = dp * T + r0 + lax.broadcasted_iota(jnp.int32, (16, 128), 0)
        count = jnp.full((16, 128), 2.0, F32)
        for start in starts:
            away = t - start
            count = jnp.where((away >= 0) & (away < 2), away.astype(F32), count)
        reach[pl.ds(r0, 16), :] = count

    rows_loop(T + 16, 16, masks)

    def squares(r0):
        at = pl.ds(r0, 32)
        x = tok[at, :].astype(F32)
        ss_s[0, at, :] = lanes(jnp.sum(x * x, axis=1, keepdims=True))

    rows_loop(B, 32, squares)
    pl.semaphore_wait(barrier, 3 + n_dp - 1)
    cot_line = Line(cot, cotz)
    cot_far = Line(call.at[row_d], cotz, row_d)
    n2_line = Line(xall.at[row], n2z)
    n2_far = Line(xall.at[row_d], n2z, row_d)
    cot_line.start(1)
    col_total(0)

    def scale_of(place, at):
        return lax.rsqrt((ss_s[place, at, :] + ss_r[place, at, :]) / width + EPS)[:, :1]

    def normed_one(r0):
        at = pl.ds(r0, 32)
        x = tok[at, :].astype(F32)
        xall[row, at, :] = (x * scale_of(0, at) * g1[...]).astype(BF)

    rows_loop(B, 32, normed_one)
    relay, second_in, third_in, all_sent = gather(xall)

    def project(blk, other_blk):
        x = two(xall, blk, other_blk)
        for k in range(3):
            y = nn(x, w_in_v[other, k]).astype(BF)
            gp[col, blk, k] = y[:B]
            gp[col, other_blk, k] = y[B:]
        copies = [links.send(gp.at[col, b], proj_r.at[b], to_col) for b in (blk, other_blk)]
        for k in range(3):
            y = nn(x, w_in_v[col, k])
            proj_o[k, pl.ds(pl.multiple_of(blk * B, B), B), :] = y[:B]
            proj_o[k, pl.ds(pl.multiple_of(other_blk * B, B), B), :] = y[B:]
        return copies

    loaded("in")
    relay()
    sent = project(row, row_a)
    cot_line.start(2)
    second_in()
    third_in()
    call[row] = cot[...]
    cot_relay, cot_second, cot_third, cot_all_sent = gather(call)
    sent += project(row_b, row_d)
    n1_out = local(xall, n1_h)

    for blk, c in zip((row, row_b, row_a, row_d), sent):
        c.wait_recv()
        base = blk * B

        def add(r0, blk=blk, base=base):
            at = pl.ds(r0, 32)
            to = pl.ds(pl.multiple_of(base + r0, 32), 32)
            g = [proj_o[k, to, :] + proj_r[blk, k, at, :].astype(F32) for k in range(3)]
            for k in range(3):
                proj_o[k, to, :] = g[k]
            mext[pl.ds(pl.multiple_of(base + r0 + 8, 8), 32), :] = g[0] * g[2]

        rows_loop(B, 32, add)
    links.sent(*sent)

    behind = links.slot()

    @pl.when(dp < n_dp - 1)
    def _():
        links.copy(mext.at[pl.ds(T, 8), :], halo_b, {"dp": lax.rem(dp + 1, n_dp)}, behind).start()

    @pl.when(dp > 0)
    def _():
        links.copy(mext.at[pl.ds(T, 8), :], halo_b, {"dp": lax.rem(dp + 1, n_dp)}, behind).wait_recv()
        mext[0:8, :] = halo_b[...]

    @pl.when(dp == 0)
    def _():
        mext[0:8, :] = jnp.zeros((8, Uc), F32)

    cot_relay()
    cot_line.start(3)
    CH = B // 2

    def masks_of(at):
        count = jnp.concatenate([reach[at, :]] * (Uc // 128), axis=1)
        return jnp.minimum(count, 1.0), jnp.maximum(count - 1.0, 0.0)

    for i in range(T // CH):
        at = pl.ds(i * CH, CH)
        x = mext[pl.ds(i * CH, CH + 8), :]
        m1, m2 = masks_of(at)
        y = cw[0:1, :] * x[8 : 8 + CH]
        y = y + cw[1:2, :] * m1 * x[7 : 7 + CH]
        y = y + cw[2:3, :] * m2 * x[6 : 6 + CH]
        cout[at, :] = y
        gat[col, i * CH // B, i * CH % B : i * CH % B + CH, :] = (proj_o[1, at, :] * y).astype(BF)
    gated_in = links.send(gat.at[col], gat.at[col], to_col)
    cot_second()
    gated_in.wait_recv()

    loaded("out")
    n1_out.wait()
    all_sent()

    def out_partial(blk, other_blk, put):
        x = [two(gat.at[c], blk, other_blk) for c in range(2)]
        for n0 in range(0, Dl, Dl // 4):
            n = slice(n0, n0 + Dl // 4)
            put(n0, nn(x[0], w_out_v[0, :, n]) + nn(x[1], w_out_v[1, :, n]))

    sent = row_sum(rs_s, rs_r, out_partial)

    def residual(r0):
        at = pl.ds(r0, 32)
        x = tok[at, :].astype(F32) + row_total(rs_r, at)
        resid[at, :] = x
        ss_s[1, at, :] = lanes(jnp.sum(x * x, axis=1, keepdims=True))

    cot_third()
    cot_far.start(1)
    rows_loop(B, 32, residual)
    links.sent(*sent)
    col_total(1)

    def normed_two(r0):
        at = pl.ds(r0, 32)
        xall[row, at, :] = (resid[at, :] * scale_of(1, at) * g2[...]).astype(BF)

    rows_loop(B, 32, normed_two)
    relay, second_in, third_in, all_sent = gather(xall)
    n2_line.start(1)

    loaded("dn")
    ga_step = min(Fc, 256)

    def ga_other(i, carry):
        n = pl.ds(pl.multiple_of(i * ga_step, ga_step), ga_step)
        y = nt(call[...].reshape(T, Dl), w_dn_v[other, n, :]).astype(BF)
        act[col, :, :, n] = y.reshape(R, B, ga_step)
        return carry

    def ga_own(i, carry):
        n = pl.ds(pl.multiple_of(i * ga_step, ga_step), ga_step)
        ga_o[:, :, n] = nt(call[...].reshape(T, Dl), w_dn_v[col, n, :]).reshape(R, B, ga_step)
        return carry

    lax.fori_loop(0, Fc // ga_step, ga_other, 0)
    ga_sent = links.send(act.at[col], ga_r, to_col)
    relay()
    lax.fori_loop(0, Fc // ga_step, ga_own, 0)
    cot_out = local(call, cotz.at[dp])
    n2_line.start(2)
    cot_far.start(2)

    def hidden_other(blk, other_blk):
        def one(k, carry):
            x = two(xall, blk, other_blk)
            for n0 in range(0, Fc, Fc // 2):
                n = slice(n0, n0 + Fc // 2)
                y = nn(x, w_gu_v[other, k, :, n]).astype(BF)
                gh[col, blk, k, :, n] = y[:B]
                gh[col, other_blk, k, :, n] = y[B:]
            return carry

        lax.fori_loop(0, 2, one, 0)
        return [links.send(gh.at[col, b], hid_r.at[b], to_col) for b in (blk, other_blk)]

    loaded("gu")
    hid_sent = hidden_other(row, row_a)
    second_in()
    third_in()
    hid_sent += hidden_other(row_b, row_d)
    n2_out = local(xall, n2z.at[dp])
    cot_line.plane(*range(1, n_dp))
    n2_far.start(1)

    gh_in = {}
    ga_sent.wait_recv()
    links.sent(ga_sent)
    H = Fc // 2
    for blks, mine_at, theirs_at in (((row_d, row_a), (3, 1), (3, 2)), ((row_b, row), (2, 0), (1, 0))):
        for h in range(2):

            def one(k, carry, h=h, blks=blks):
                y = nn(two(xall, *blks), w_gu_v[col, k, :, h * H : h * H + H])
                hid_o[k, :, :H] = y[:B]
                hid_o[k, :, H:] = y[B:]
                return carry

            lax.fori_loop(0, 2, one, 0)
            for i, blk in enumerate(blks):
                if h == 0:
                    hid_sent[theirs_at[i]].wait_recv()
                    links.sent(hid_sent[mine_at[i]])

                def activate(r0, blk=blk, i=i, h=h):
                    at = pl.ds(r0, 32)
                    n = slice(h * H, h * H + H)
                    own = slice(i * H, i * H + H)
                    gate = hid_o[0, at, own] + hid_r[blk, 0, at, n].astype(F32)
                    up = hid_o[1, at, own] + hid_r[blk, 1, at, n].astype(F32)
                    ga = ga_o[blk, at, n] + ga_r[blk, at, n].astype(F32)
                    s = jax.nn.sigmoid(gate)
                    silu = gate * s
                    act[col, blk, at, n] = (silu * up).astype(BF)
                    gh[col, blk, 0, at, n] = (ga * up * s * (1.0 + gate * (1.0 - s))).astype(BF)
                    gh[col, blk, 1, at, n] = (ga * silu).astype(BF)

                rows_loop(B, 32, activate)
                if h == 1:
                    gh_in[mine_at[i]] = (
                        links.send(gh.at[col, blk], gh.at[col, blk], to_col),
                        links.send(act.at[col, blk], act.at[col, blk], to_col),
                    )
    cot_far.start(3)
    n2_far.start(2)
    for pair in gh_in.values():
        for c in pair:
            c.wait_recv()
    size = actz.shape[-1]
    mine = pl.ds(pl.multiple_of(lax.rem(dp, half) * size, size), size)
    kept_units = [
        local(act.at[holder, :, :, mine], actz.at[dp]),
        local(gh.at[holder, :, :, :, mine], ghz.at[dp]),
    ]
    kept = []
    n2_out.wait()
    n2_line.start(3)
    n2_line.sent(1)
    n2_far.sent(1)
    all_sent()

    def gu_partial(blk, other_blk, put):
        for n0 in range(0, Dl, Dl // 4):
            n = slice(n0, n0 + Dl // 4)
            total = None
            for c in range(2):
                for k in range(2):
                    part = nt(two(gh.at[c, :, k], blk, other_blk), w_gu_v[c, k, n, :])
                    total = part if total is None else total + part
            put(n0, total)

    sent = row_sum(rs_s, rs_r, gu_partial)

    def back_two(r0):
        at = pl.ds(r0, 32)
        g = row_total(rs_r, at)
        gres[at, :] = g
        ss_s[2, at, :] = lanes(jnp.sum(g * g2[...] * resid[at, :], axis=1, keepdims=True))

    rows_loop(B, 32, back_two)
    links.sent(*sent)
    col_total(2)

    def inner_of(place, at):
        return (ss_s[place, at, :] + ss_r[place, at, :])[:, :1]

    def branch(i, gain):
        at = pl.ds(pl.multiple_of(i * 32, 32), 32)
        g = gres[at, :]
        x = resid[at, :]
        s = scale_of(1, at)
        y = cot[at, :].astype(F32) + s * g2[...] * g - x * (s * s * s) * inner_of(2, at) / width
        gres[at, :] = y
        xall[row, at, :] = y.astype(BF)
        return gain + jnp.sum(g * x * s, axis=0, keepdims=True)

    n2_far.start(3)
    cot_out.wait()
    cot_all_sent()
    cot_far.sent(1)
    n1_back = local(n1_h, call)
    gain_two = lax.fori_loop(0, B // 32, branch, jnp.zeros((1, Dl), F32))
    relay, second_in, third_in, all_sent = gather(xall)

    def down_partial(blk, other_blk, put):
        x = [two(act.at[c], blk, other_blk) for c in range(2)]
        for n0 in range(0, Dl, Dl // 4):
            n = slice(n0, n0 + Dl // 4)
            put(n0, nn(x[0], w_dn_v[0, :, n]) + nn(x[1], w_dn_v[1, :, n]))

    down_partial(row_d, row_a, both(put_to(rt_s.at[0]), put_to(rt_s.at[1])))

    def gated_other(blk, other_blk):
        x = two(xall, blk, other_blk)
        y = nt(x, w_out_v[other]).astype(BF)
        gg_s[blk] = y[:B]
        gg_s[other_blk] = y[B:]
        copies = [links.send(gg_s.at[b], gg_r.at[b], to_col) for b in (blk, other_blk)]
        y = nt(x, w_out_v[col])
        gg_o[blk] = y[:B]
        gg_o[other_blk] = y[B:]
        return copies

    relay()
    sent = gated_other(row, row_a)
    down_partial(row_b, row, both(put_to(rt_s.at[2]), put_to(down_o)))
    second_in()
    third_in()
    sent += gated_other(row_b, row_d)
    n2_line.plane(1)

    po_all = []

    rows = po_r.shape[1]

    def out_chunk(z):
        return (z // half, pl.ds(pl.multiple_of(lax.rem(z, half) * rows, rows), rows), slice(None))

    def out_weights():
        for z in range(n_dp):
            at = pl.ds(z % half * rows, rows)
            g = lax.dot_general(
                gat[z // half, :, :, at].reshape(T, rows), xall[...].reshape(T, Dl),
                (((0,), (0,)), ((), ())), preferred_element_type=F32,
            )
            w_out_v[z // half, at, :] = g.astype(BF)
        for k in range(1, n_dp):
            po_all.append(links.send(w_out_v.at[out_chunk(peers[k])], po_r.at[dp], {"dp": peers[k]}))

    out_weights()

    for blk, c in zip((row, row_b, row_a, row_d), sent):
        c.wait_recv()
        base = blk * B

        def conv_grad(r0, blk=blk, base=base):
            at = pl.ds(r0, 32)
            to = pl.ds(pl.multiple_of(base + r0, 32), 32)
            g = gg_o[blk, at, :] + gg_r[blk, at, :].astype(F32)
            gext[to, :] = g * proj_o[1, to, :]
            gp[col, blk, 1, at, :] = (g * cout[to, :]).astype(BF)

        rows_loop(B, 32, conv_grad)

    ahead = links.slot()

    @pl.when(dp > 0)
    def _():
        links.copy(gext.at[pl.ds(0, 8), :], halo_a, {"dp": lax.rem(dp + n_dp - 1, n_dp)}, ahead).start()

    @pl.when(dp < n_dp - 1)
    def _():
        links.copy(gext.at[pl.ds(0, 8), :], halo_a, {"dp": lax.rem(dp + n_dp - 1, n_dp)}, ahead).wait_recv()
        gext[T : T + 8, :] = halo_a[...]

    @pl.when(dp == n_dp - 1)
    def _():
        gext[T : T + 8, :] = jnp.zeros((8, Uc), F32)

    terms = [jnp.zeros((1, Uc), F32) for _ in range(3)]
    for i in range(T // CH):
        at = pl.ds(i * CH, CH)
        more = pl.ds(i * CH, CH + 8)
        x = mext[more, :]
        g = gext[more, :]
        m1, m2 = masks_of(more)
        now = g[:CH]
        terms[0] = terms[0] + jnp.sum(now * x[8 : 8 + CH], axis=0, keepdims=True)
        terms[1] = terms[1] + jnp.sum(m1[:CH] * now * x[7 : 7 + CH], axis=0, keepdims=True)
        terms[2] = terms[2] + jnp.sum(m2[:CH] * now * x[6 : 6 + CH], axis=0, keepdims=True)
        y = cw[0:1, :] * now
        y = y + cw[1:2, :] * (m1 * g)[1 : 1 + CH]
        y = y + cw[2:3, :] * (m2 * g)[2 : 2 + CH]
        blk, to = i * CH // B, slice(i * CH % B, i * CH % B + CH)
        gp[col, blk, 0, to, :] = (y * proj_o[2, at, :]).astype(BF)
        gp[col, blk, 2, to, :] = (y * proj_o[0, at, :]).astype(BF)
    red_s[...] = jnp.zeros_like(red_s)
    for k in range(3):
        red_s[2 + k : 3 + k, :Uc] = terms[k]
    gp_in = links.send(gp.at[col], gp.at[col], to_col)
    gp_in.wait_recv()
    if not split_in:
        kept.append(local(gp, d_in))

    def in_partial(blk, other_blk, put):
        for n0 in range(0, Dl, Dl // 4):
            n = slice(n0, n0 + Dl // 4)
            total = None
            for c in range(2):
                for k in range(3):
                    part = nt(two(gp.at[c, :, k], blk, other_blk), w_in_v[c, k, n, :])
                    total = part if total is None else total + part
            put(n0, total)

    up_slots = [links.slot() for _ in range(n_dp)][0]
    down_slots = [links.slot() for _ in range(n_dp)][0]
    unit = 2 * Uc // n_dp

    def in_chunk(z):
        at = pl.ds(pl.multiple_of(lax.rem(z, half) * unit, unit), unit)
        return (z // half, slice(None), slice(None), at)

    def go_up(z):
        return links.copy(w_in_v.at[in_chunk(z)], in_up.at[z], {"dp": peers[1]}, up_slots + z)

    def go_down(z):
        return links.copy(w_in_v.at[in_chunk(z)], in_dn.at[z], {"dp": sources[1]}, down_slots + z)

    def in_weights():
        n1_back.wait()
        x = call[...].reshape(T, Dl)
        units = [(c, k) for c in range(2) for k in range(3)]
        g = jnp.concatenate([gp[c, :, k].reshape(T, Uc) for c, k in units], axis=1)
        for m0 in range(0, Dl, Dl // 4):
            m = slice(m0, m0 + Dl // 4)
            y = lax.dot_general(x[:, m], g, (((0,), (0,)), ((), ())), preferred_element_type=F32)
            for u, (c, k) in enumerate(units):
                w_in_v[c, k, m, :] = y[:, u * Uc : u * Uc + Uc].astype(BF)
        for z in range(n_dp - 1, 0, -1):

            @pl.when(dp == 0)
            def _(z=z):
                go_up(z).start()

        for z in range(n_dp - 1):

            @pl.when(dp == n_dp - 1)
            def _(z=z):
                go_down(z).start()

    def take(src, z):
        c = pltpu.make_async_copy(src, in_add, local_sems.at[local_sems.shape[0] - 1])
        c.start()
        c.wait()
        at = in_chunk(z)
        for k in range(3):
            here = (at[0], k, slice(None), at[3])
            w_in_v[here] = (w_in_v[here].astype(F32) + in_add[k].astype(F32)).astype(BF)

    def in_step(step):
        up = n_dp - 1 - step + dp

        @pl.when((dp > 0) & (dp <= step))
        def _():
            go_up(up).wait_recv()
            take(in_up.at[up], up)
            go_up(up).start()

        down = step - (n_dp - 1 - dp)

        @pl.when((dp < n_dp - 1) & (down >= 0))
        def _():
            go_down(down).wait_recv()
            take(in_dn.at[down], down)
            go_down(down).start()

    def in_end():
        @pl.when(dp > 0)
        def _():
            go_up(dp).wait_recv()
            take(in_up.at[dp], dp)

        @pl.when(dp < n_dp - 1)
        def _():
            go_down(dp).wait_recv()
            take(in_dn.at[dp], dp)

        out = local(w_in_v.at[in_chunk(dp)], d_in)
        for z in range(1, n_dp):

            @pl.when(dp < z)
            def _(z=z):
                go_up(z).wait_send()

        for z in range(n_dp - 1):

            @pl.when(dp > z)
            def _(z=z):
                go_down(z).wait_send()

        out.wait()

    def weights_wait():
        if split_in:
            in_weights()
        else:
            n1_back.wait()

    sent_in = row_sum(rs_s, rs_r, in_partial, filler=weights_wait)
    n2_line.plane(*range(2, n_dp))
    down_sent = [
        links.send(rt_s.at[0], rt_r.at[0], to_a),
        links.send(rt_s.at[1], rt_r.at[1], to_a),
    ]

    def fetch(k):
        n2_line.finish(k)
        return [local(n2z.at[peers[k]], xall), local(cotz.at[peers[k]], call)]

    cot_far.rest()
    n2_far.rest()
    cot_line.finish(*range(1, n_dp))
    all_sent()
    fetched = {1: fetch(1)}

    def back_one(r0):
        at = pl.ds(r0, 32)
        g = row_total(rs_r, at)
        acc_o[at, :] = g
        ss_s[3, at, :] = lanes(
            jnp.sum(g * g1[...] * tok[at, :].astype(F32), axis=1, keepdims=True)
        )

    rows_loop(B, 32, back_one)
    col_total(3)

    def token_grad(i, gain):
        at = pl.ds(pl.multiple_of(i * 32, 32), 32)
        g = acc_o[at, :]
        x = tok[at, :].astype(F32)
        s = scale_of(0, at)
        y = gres[at, :] + s * g1[...] * g - x * (s * s * s) * inner_of(3, at) / width
        gres[at, :] = y
        return gain + jnp.sum(g * x * s, axis=0, keepdims=True)

    gain_one = lax.fori_loop(0, B // 32, token_grad, jnp.zeros((1, Dl), F32))

    kept.append(local(gres, d_tok))

    red_s[0:1, :] = gain_one
    red_s[1:2, :] = gain_two
    c0 = links.send(red_s, red_r.at[0], to_a)
    for c in kept_units:
        c.wait()
    for pair in gh_in.values():
        links.sent(*pair)

    slots = Fc // size

    def place(k, r, rank):
        q = (k - 1) * 2 + r
        lanes_at = slice(q % slots * size, q % slots * size + size)
        return (q // slots, *([slice(None)] * (rank - 2)), lanes_at)

    def again(k):
        z = peers[k]
        for c in fetched[k]:
            c.wait()
        copies = []
        for core, keep in ((other, False), (col, True)):
            x = xall[pl.ds(core * 2, 2)].reshape(2 * B, Dl)
            for j in range(2):
                h = nn(x, w_gu_v[holder, j, :, mine])
                for r in range(2):
                    if keep:
                        hid_o[j, :, r * size : r * size + size] = h[r * B : r * B + B]
                    else:
                        q, _, _, n = place(k, r, 4)
                        gh[0, q, j, :, n] = h[r * B : r * B + B].astype(BF)
            y = call[pl.ds(core * 2, 2)].reshape(2 * B, Dl)
            g = nt(y, w_dn_v[holder, mine, :])
            for r in range(2):
                if keep:
                    ga_o[r, :, :size] = g[r * B : r * B + B]
                else:
                    q, _, n = place(k, r, 3)
                    act[0, q, :, n] = g[r * B : r * B + B].astype(BF)
            if not keep:
                for r in range(2):
                    h_at, g_at = place(k, r, 4), place(k, r, 3)
                    copies.append(links.send(gh.at[0].at[h_at], hid_r.at[h_at], to_col))
                    copies.append(links.send(act.at[0].at[g_at], ga_r.at[g_at], to_col))
        if k + 1 < n_dp:
            fetched[k + 1] = fetch(k + 1)
        for c in copies:
            c.wait_recv()
        done = []
        for r in range(2):
            q, _, n = place(k, r, 3)

            def finish(r0, r=r, q=q, n=n):
                at = pl.ds(r0, 32)
                own = slice(r * size, r * size + size)
                gate = hid_o[0, at, own] + hid_r[q, 0, at, n].astype(F32)
                up = hid_o[1, at, own] + hid_r[q, 1, at, n].astype(F32)
                ga = ga_o[r, at, :size] + ga_r[q, at, n].astype(F32)
                s = jax.nn.sigmoid(gate)
                silu = gate * s
                act[1, q, at, n] = (silu * up).astype(BF)
                gh[1, q, 0, at, n] = (ga * up * s * (1.0 + gate * (1.0 - s))).astype(BF)
                gh[1, q, 1, at, n] = (ga * silu).astype(BF)

            rows_loop(B, 32, finish)
            blk = col * 2 + r
            h_src, a_src = gh.at[1].at[place(k, r, 4)], act.at[1].at[place(k, r, 3)]
            done.append(links.send(h_src, ghz.at[z, blk], to_col))
            done.append(links.send(a_src, actz.at[z, blk], to_col))
            kept.append(local(h_src, ghz.at[z, blk]))
            kept.append(local(a_src, actz.at[z, blk]))
        return done

    again_in = again(1)
    if split_in:
        in_step(1)

    down_sent[0].wait_recv()

    def down_combine(r0):
        at = pl.ds(r0, 16)
        rt_s[2, at, :] = (rt_s[2, at, :].astype(F32) + rt_r[0, at, :].astype(F32)).astype(BF)

    rows_loop(B, 16, down_combine)
    down_sent.append(links.send(rt_s.at[2], rt_r.at[2], to_b))
    c0.wait_recv()
    links.sent(c0)
    red_s[0:2, :] = red_s[0:2, :] + red_r[0, 0:2, :]
    c1 = links.send(red_s, red_r.at[1], to_b)
    again_in += again(2)
    c1.wait_recv()
    red_z[dp] = red_s[...]
    red_z[dp, 0:2, :] = red_s[0:2, :] + red_r[1, 0:2, :]
    arrived = []
    for k in range(1, n_dp):
        arrived.append(links.send(red_z.at[dp], red_z.at[dp], {"dp": lax.rem(dp + k, n_dp)}))
    for k in range(3, n_dp):
        again_in += again(k)
    for c in down_sent[1:]:
        c.wait_recv()

    def block_rows(r0):
        at = pl.ds(r0, 16)
        total = down_o[at, :] + rt_r[1, at, :].astype(F32) + rt_r[2, at, :].astype(F32)
        block_out[at, :] = (resid[at, :] + total).astype(BF)

    rows_loop(B, 16, block_rows)
    if split_in:
        for step in range(2, n_dp - 1):
            in_step(step)
    for c in arrived:
        c.wait_recv()
    total = red_z[0]
    for k in range(1, n_dp):
        total = total + red_z[k]
    d_gain[...] = total
    d_conv[...] = total[:, :Uc]

    @pl.when(dp < n_dp - 1)
    def _():
        links.copy(mext.at[pl.ds(T, 8), :], halo_b, {"dp": lax.rem(dp + 1, n_dp)}, behind).wait_send()

    @pl.when(dp > 0)
    def _():
        links.copy(gext.at[pl.ds(0, 8), :], halo_a, {"dp": lax.rem(dp + n_dp - 1, n_dp)}, ahead).wait_send()

    for c in again_in:
        c.wait_recv()
    for c in po_all:
        c.wait_recv()
    out_total = w_out_v[out_chunk(dp)].astype(F32)
    for k in range(1, n_dp):
        out_total = out_total + po_r[peers[k]].astype(F32)
    acc_b[:rows, :] = out_total
    kept.append(local(acc_b.at[pl.ds(0, rows), :], d_out))
    if split_in:
        in_end()
    cot_line.sent(1)
    for hop in range(2, n_dp):
        for line in (cot_line, cot_far, n2_line, n2_far):
            line.sent(hop)
    for c in kept:
        c.wait()
    assert links.count <= send_sems.shape[0]
    links.close()


def run_block(n_dp, width, split_in, tok, g1, w_in, cw, w_out, g2, w_gu, w_dn, cot, lengths):
    B, Dl = tok.shape
    R = 4
    T = R * B
    Uc = w_out.shape[0] // 2
    Fc = w_dn.shape[0] // 2
    vm = lambda shape, kind=BF: pltpu.VMEM(shape, kind)
    any_spec, vmem_spec = pl.BlockSpec(memory_space=pl.ANY), pl.BlockSpec(memory_space=pltpu.VMEM)
    shape = jax.ShapeDtypeStruct
    rows = shape((n_dp, R, B, Dl), BF)
    return pl.pallas_call(
        functools.partial(block_kernel, n_dp, width, split_in),
        out_shape=(
            shape((B, Dl), BF),
            shape((B, Dl), F32),
            shape((8, Dl), F32),
            shape((8, Uc), F32),
            shape((2 * Uc // n_dp, Dl), F32),
            shape((R, B, Dl), BF),
            rows,
            rows,
            shape((n_dp, R, B, 2 * Fc // n_dp), BF),
            shape((n_dp, R, 2, B, 2 * Fc // n_dp), BF),
            shape((3, Dl, 2 * Uc // n_dp) if split_in else (2, R, 3, B, Uc), BF),
            shape((n_dp, 3, Dl, 2 * Uc // n_dp), BF),
            shape((n_dp, 3, Dl, 2 * Uc // n_dp), BF),
        ),
        in_specs=[
            vmem_spec, vmem_spec, any_spec, vmem_spec, any_spec, vmem_spec,
            any_spec, any_spec, vmem_spec, pl.BlockSpec(memory_space=pltpu.SMEM),
        ],
        out_specs=[vmem_spec, any_spec, vmem_spec, vmem_spec] + [any_spec] * 9,
        scratch_shapes=[
            vm((2, 3, Dl, Uc)), vm((2, Uc, Dl)), vm((2, 2, Dl, Fc)), vm((2, Fc, Dl)),
            vm((R, B, Dl)), vm((R, B, Dl)),
            vm((2, R, B, Uc)), vm((2, R, B, Fc)), vm((2, R, 2, B, Fc)), vm((2, R, 3, B, Uc)),
            vm((3, T, Uc), F32), vm((R, 3, B, Uc)), vm((T + 8, Uc), F32), vm((8, Uc), F32),
            vm((T, Uc), F32), vm((T + 8, Uc), F32), vm((8, Uc), F32),
            vm((R, B, Uc)), vm((R, B, Uc)), vm((R, B, Uc), F32),
            vm((2, B, Fc), F32), vm((R, 2, B, Fc)), vm((R, B, Fc), F32), vm((R, B, Fc)),
            vm((3, B, Dl)), vm((3, B, Dl)), vm((3, B, Dl)), vm((3, B, Dl)),
            vm((B, Dl), F32), vm((B, Dl), F32), vm((B, Dl), F32),
            vm((B, Dl), F32), vm((B, Dl), F32),
            vm((4, B, 128), F32), vm((4, B, 128), F32),
            vm((8, Dl), F32), vm((2, 8, Dl), F32), vm((n_dp, 8, Dl), F32),
            vm((n_dp, 2 * Uc // n_dp, Dl)),
            vm((1, Dl), F32), vm((1, Dl), F32), vm((3, Uc), F32),
            vm((T + 16, 128), F32), vm((3, Dl, 2 * Uc // n_dp)),
            pltpu.SemaphoreType.DMA((96 + 48 * n_dp,)), pltpu.SemaphoreType.DMA((96 + 48 * n_dp,)),
            pltpu.SemaphoreType.DMA((32 + 6 * n_dp,)),
        ],
        compiler_params=pltpu.CompilerParams(
            collective_id=0, has_side_effects=True, vmem_limit_bytes=VMEM_LIMIT
        ),
        name="block",
    )(tok, g1, w_in, cw, w_out, g2, w_gu, w_dn, cot, lengths)


def weights_kernel(split_in, n2, cot, act, gh, d_in, gu_out, dn_out, in_out, gu_acc):
    _, R, B, Dl = n2.shape
    T, size = R * B, act.shape[-1]
    step = pl.program_id(0)

    def tn(a, b):
        return lax.dot_general(a, b, (((0,), (0,)), ((), ())), preferred_element_type=F32)

    @pl.when(step == 0)
    def _():
        gu_acc[...] = jnp.zeros_like(gu_acc)
        dn_out[...] = jnp.zeros_like(dn_out)
        if split_in:
            for k in range(3):
                in_out[pl.ds(k, Dl, stride=3), :] = d_in[k].astype(F32)
        else:
            in_out[...] = jnp.zeros_like(in_out)

    g = jnp.concatenate([gh[0, :, k].reshape(T, size) for k in range(2)], axis=1)
    gu_acc[...] += tn(n2[0].reshape(T, Dl), g)
    dn_out[...] += tn(act[0].reshape(T, size), cot[0].reshape(T, Dl))

    @pl.when(step == pl.num_programs(0) - 1)
    def _():
        parts = 2 * size // 128
        for p in range(parts):
            gu_out[pl.ds(p, Dl, stride=parts), :] = gu_acc[:, p * 128 : p * 128 + 128]


def run_weights(split_in, n2, cot, act, gh, d_in):
    n_dp, R, B, Dl = n2.shape
    size = act.shape[-1]
    whole = lambda *shape: pl.BlockSpec(shape, lambda z: (0,) * len(shape))
    one = lambda a: pl.BlockSpec((1, *a.shape[1:]), lambda z: (z,) + (0,) * (len(a.shape) - 1))
    out = ((Dl * 2 * size // 128, 128), (size, Dl), (Dl * 3, 128) if split_in else (8, 128))
    return pl.pallas_call(
        functools.partial(weights_kernel, split_in),
        grid=(n_dp,),
        out_shape=[jax.ShapeDtypeStruct(o, F32) for o in out],
        in_specs=[
            one(n2), one(cot), one(act), one(gh),
            whole(*d_in.shape) if split_in else pl.BlockSpec(memory_space=pl.ANY),
        ],
        out_specs=[whole(*o) for o in out],
        scratch_shapes=[pltpu.VMEM((Dl, 2 * size), F32)],
        compiler_params=pltpu.CompilerParams(vmem_limit_bytes=VMEM_LIMIT),
        name="weights",
    )(n2, cot, act, gh, d_in)


def on_device(
    tokens, gain_one, in_weight, conv_weight, out_weight, gain_two, gate_up_weight, down_weight,
    cotangent, lengths,
):
    n_dp = lax.axis_size("dp")
    B, Dl = tokens.shape
    width = Dl * lax.axis_size("col")
    chunk = in_weight.shape[2] // n_dp
    split_in = chunk == 128
    block_out, d_tok, d_gain, d_conv, d_out, n1, n2, cot, act, gh, d_in, _, _ = run_block(
        n_dp,
        float(width),
        split_in,
        tokens,
        gain_one[None, :],
        jnp.transpose(in_weight, (1, 0, 2)),
        conv_weight,
        out_weight,
        gain_two[None, :],
        jnp.transpose(gate_up_weight, (1, 0, 2)),
        down_weight,
        cotangent,
        lengths,
    )
    d_gu, d_down, in_rows = run_weights(split_in, n2, cot, act, gh, d_in)
    if split_in:
        d_in = in_rows
    else:
        d_in = lax.psum_scatter(
            jnp.einsum("rti,crktu->ikcu", n1, d_in, preferred_element_type=F32)
            .reshape(Dl, 3, -1)
            .astype(BF),
            "dp",
            scatter_dimension=2,
            tiled=True,
        ).astype(F32)
    part = d_conv.shape[1] * 1 // n_dp
    mine = lax.dynamic_slice(d_conv, (2, lax.axis_index("dp") * part), (3, part))
    return (
        block_out,
        d_tok,
        d_gain[0],
        d_in.reshape(Dl, 3, 1, 1, -1),
        mine.reshape(3, 1, 1, part),
        d_out.reshape(1, 1, -1, Dl),
        d_gain[1],
        d_gu.reshape(Dl, 2, 1, 1, -1),
        d_down.reshape(1, 1, -1, Dl),
    )


def solution(mesh):
    placed = (
        P(("dp", "row"), "col"),
        P("col"),
        P("col", None, "row"),
        P(None, ("row", "col")),
        P("row", "col"),
        P("col"),
        P("col", None, "row"),
        P("row", "col"),
        P(("dp", "row"), "col"),
        P(),
    )
    return jax.shard_map(
        on_device,
        mesh=mesh,
        in_specs=placed,
        out_specs=(
            P(("dp", "row"), "col"),
            P(("dp", "row"), "col"),
            P("col"),
            P("col", None, "row", "dp", None),
            P(None, ("row", "col"), "dp", None),
            P("row", "dp", None, "col"),
            P("col"),
            P("col", None, "row", "dp", None),
            P("row", "dp", None, "col"),
        ),
        check_vma=False,
    )
```
